32 devices in a mesh: sector: 16 (over z, y, core), span: 2 (over x).
Axes of the slice: x: 2, y: 2, z: 4, core: 2. Of those that a mesh axis runs over, the one named last changes fastest.
Arguments:
- rhs: float32 [11, 7, 32, 16, 128], P(None, None, 'sector', 'span'), may hold values from -6 to 6
- diag_coef: float32 [32, 16, 128], P('sector', 'span'), may hold values from 2 to 4
- face_coef: float32 [3, 32, 16, 128], P(None, 'sector', 'span'), may hold values from 0.2 to 0.6
- time_coef: float32 [32, 16, 128], P('sector', 'span'), may hold values from 0.05 to 0.4
- jac_up: float32 [3, 7, 7], replicated, may hold values from -1.5 to 1.5
- jac_down: float32 [3, 7, 7], replicated, may hold values from -1.5 to 1.5
- wall_mask: int32 [32, 16, 128], P('sector', 'span'), may hold values 0 or 1
- stator_adj: float32 [11, 7, 64, 16], P(None, None, 'sector', 'span'), may hold values from -6 to 6
- owner: int32 [11, 32, 16], P(None, 'sector', 'span'), may hold values from 0 to 62, as said below
- first_panel_share: float32 [11, 32, 16], P(None, 'sector', 'span'), may hold values from 0 to 1
Outputs:
- adjoint_out: float32 [11, 7, 32, 16, 128], P(None, None, 'sector', 'span')
- stator_sens: float32 [11, 7, 64, 16], P(None, None, 'sector', 'span')
The draws below stay inside these ranges and needn't reach their ends.
Inputs may be any that keep to these rules, and one draw needn't show every extreme that they name: For instance t and an inlet cell in azimuthal block b (cells b * 2 to (b + 1) * 2 - 1), owner and owner + 1 both lie in panel block q = (b + (t * 16) // 10 - t // 10) mod 16, that is between q * 4 and (q + 1) * 4 - 1.
All inputs are finite; a program needn't handle non-finite values. No bound on the sum of `wall_mask` on one device may be relied on, other than what follows from the above.
Results may differ from the reference program's by a relative error of at most 0.0001.
Values sent between devices are 32-bit elements; how exact they have to be, the bound alone decides.
No kernel may reach another device: no remote copies, remote signals or barrier semaphores. Data moves between devices by JAX's collectives and lax.ppermute only.
A program may use at most 64 MiB of HBM per device.

```python
import math
import jax
import jax.numpy as jnp
from jax import lax

HB_SNAPSHOTS = 11
FLD = 7
CT = 2
NAX = 128
SWEEPS = 4
PT = 4
NTH = 32
NR = 16
NPT = 64


def draw_owner(key, part):
    period_samples = jnp.arange(HB_SNAPSHOTS)[:, None, None]
    azimuth = jnp.arange(NTH)[None, :, None]
    wheel_passage_count = NTH // CT
    cell_groups = azimuth // CT
    turned = period_samples * wheel_passage_count // (HB_SNAPSHOTS - 1) - period_samples // (HB_SNAPSHOTS - 1)
    destination_solution = jnp.mod(cell_groups + turned, wheel_passage_count)
    nearby_leading = jax.random.randint(key, (HB_SNAPSHOTS, NTH, NR), 0, PT - 1)
    nearby_leading = nearby_leading.at[0, 0, 0].set(0)
    nearby_leading = nearby_leading.at[0, NTH - 1, 0].set(PT - 2)
    return (destination_solution * PT + nearby_leading).astype(jnp.int32)


def with_ends(array, key, low, largest):
    longest = array.shape.index(max(array.shape))
    spots = []
    for shift in (0, 1):
        where = [jax.random.randint(jax.random.fold_in(key, axis), (), 0, length) for axis, length in enumerate(array.shape)]
        where[longest] = (where[longest] + shift) % array.shape[longest]
        spots.append(tuple(where))
    return array.at[spots[0]].set(low).at[spots[1]].set(largest)


def steps_of(own_key, extent, split, smallest, largest):
    def one(axis_at, shards_of):
        steps = jax.random.uniform(jax.random.fold_in(jax.random.fold_in(own_key, 6), axis_at), (shards_of,), jnp.float32, smallest / len(split), largest / len(split))
        return jnp.repeat(jnp.exp(steps), extent[axis_at] // shards_of).reshape((-1,) + (1,) * (len(extent) - axis_at - 1))

    factor_of = one(*split[0])
    for cut in split[1:]:
        factor_of = factor_of * one(*cut)
    return factor_of


def centred(key, shape, scale, bound, cuts=(), held_as=jnp.bfloat16):
    drawn = scale * jax.random.normal(key, shape, jnp.float32)
    if cuts:
        drawn = drawn * steps_of(key, shape, cuts, -0.22, 0.18)
    return jnp.clip(drawn, -bound, bound).astype(held_as)


def setup_inputs(seed: int = 0) -> dict:
    keys = jax.random.split(jax.random.key(seed), 11)
    rhs = centred(keys[0], (HB_SNAPSHOTS, FLD, NTH, NR, NAX), 1.0, 6.0, ((2, 16), (3, 2)), jnp.float32)
    diag_coef = jnp.clip(jnp.exp(math.log(4.0) - 0.6931472 * jax.random.uniform(keys[1], (NTH, NR, NAX), jnp.float32) ** steps_of(keys[1], (NTH, NR, NAX), ((0, 16), (1, 2)), -0.2, 0.2)), 2.0, 4.0)
    face_coef = jnp.clip(jnp.exp(math.log(0.6) - 1.0986123 * jax.random.uniform(keys[2], (3, NTH, NR, NAX), jnp.float32) ** steps_of(keys[2], (3, NTH, NR, NAX), ((1, 16), (2, 2)), -0.2, 0.2)), 0.2, 0.6)
    time_coef = jnp.clip(jnp.exp(math.log(0.4) - 2.0794415 * jax.random.uniform(keys[3], (NTH, NR, NAX), jnp.float32) ** steps_of(keys[3], (NTH, NR, NAX), ((0, 16), (1, 2)), -0.2, 0.2)), 0.05, 0.4)
    jac_up = centred(keys[4], (3, FLD, FLD), (2 * FLD) ** -0.5, 1.5, (), jnp.float32)
    jac_down = centred(keys[5], (3, FLD, FLD), (2 * FLD) ** -0.5, 1.5, (), jnp.float32)
    wall_mask = with_ends((jax.random.randint(keys[6], (NTH, NR, NAX), 0, 8) < 7).astype(jnp.int32), jax.random.fold_in(keys[6], 1), 0, 1)
    stator_adj = centred(keys[7], (HB_SNAPSHOTS, FLD, NPT, NR), 1.0, 6.0, ((2, 16), (3, 2)), jnp.float32)
    owner = draw_owner(jax.random.fold_in(keys[10], 71), 0)
    first_panel_share = jnp.clip(1.0 * jax.random.uniform(keys[9], (HB_SNAPSHOTS, NTH, NR), jnp.float32) ** steps_of(keys[9], (HB_SNAPSHOTS, NTH, NR), ((1, 16), (2, 2)), -0.2, 0.2), 0.0, 1.0)
    return {"rhs": rhs, "diag_coef": diag_coef, "face_coef": face_coef, "time_coef": time_coef, "jac_up": jac_up, "jac_down": jac_down, "wall_mask": wall_mask, "stator_adj": stator_adj, "owner": owner, "first_panel_share": first_panel_share}


def spectral_table(count):
    positions = jnp.arange(count)
    offsets = positions[:, None] - positions[None, :]
    sweep_parity = 1.0 - 2.0 * jnp.mod(offsets, 2).astype(jnp.float32)
    angles = math.pi * offsets.astype(jnp.float32) / count
    sines = jnp.where(offsets == 0, 1.0, jnp.sin(angles))
    return jnp.where(offsets == 0, 0.0, 0.5 * sweep_parity / sines).astype(jnp.float32)


def apply_block(matrix, field):
    return jnp.einsum('ef,tfabc->teabc', matrix, field, precision=lax.Precision.HIGHEST)


def couple(field, face_coef, time_coef, jac_up, jac_down, spectral_matrix):
    coupled = time_coef * jnp.einsum('st,sfabc->tfabc', spectral_matrix, field, precision=lax.Precision.HIGHEST)
    theta = (jnp.roll(field, -1, axis=2), jnp.roll(field, 1, axis=2))
    radial_padding = jnp.pad(field, ((0, 0), (0, 0), (0, 0), (1, 1), (0, 0)))
    radial = (radial_padding[:, :, :, 2:, :], radial_padding[:, :, :, :-2, :])
    axial_pad = jnp.pad(field, ((0, 0), (0, 0), (0, 0), (0, 0), (1, 1)))
    axial = (axial_pad[..., 2:], axial_pad[..., :-2])
    sides = (theta, radial, axial)
    for direction in range(3):
        forward_side, backward_side = sides[direction]
        coupled = coupled + face_coef[direction] * (apply_block(jac_up[direction], forward_side) + apply_block(jac_down[direction], backward_side))
    return coupled


def reference(rhs, diag_coef, face_coef, time_coef, jac_up, jac_down, wall_mask, stator_adj, owner, first_panel_share):
    spectral_matrix = spectral_table(HB_SNAPSHOTS)
    radial_index = jnp.arange(NR)[None, :]
    pieces = []
    for inst in range(HB_SNAPSHOTS):
        panels = stator_adj[inst]
        first = owner[inst]
        weight = first_panel_share[inst]
        pieces.append(weight * panels[:, first, radial_index] + (1.0 - weight) * panels[:, first + 1, radial_index])
    rotor_stator_seam = jnp.stack(pieces)
    forcing = rhs.at[..., 0].add(rotor_stator_seam)
    mask_float = wall_mask.astype(jnp.float32)
    adjoint_field = mask_float * forcing / diag_coef
    for sweep in range(SWEEPS):
        coupled = couple(adjoint_field, face_coef, time_coef, jac_up, jac_down, spectral_matrix)
        adjoint_field = mask_float * (forcing - coupled) / diag_coef
    inlet_plane = adjoint_field[..., 0]
    results = []
    for inst in range(HB_SNAPSHOTS):
        first = owner[inst]
        weight = first_panel_share[inst]
        accum = jnp.zeros((FLD, NPT, NR), jnp.float32)
        accum = accum.at[:, first, radial_index].add(weight * inlet_plane[inst])
        accum = accum.at[:, first + 1, radial_index].add((1.0 - weight) * inlet_plane[inst])
        results.append(accum)
    return adjoint_field, jnp.stack(results)
```

```python
import functools

import jax
import jax.numpy as jnp
import ml_dtypes
import numpy as np
from jax import lax
from jax.experimental import pallas as pl
from jax.experimental.pallas import tpu as pltpu
from jax.sharding import PartitionSpec as P

SWEEPS = 4
LANES = 128
CHUNK = 256
HIGHEST = lax.Precision.HIGHEST
DOWN_AZ, SPECTRAL, UP_SP, DOWN_SP, UP_AX, DOWN_AX, UP_AZ = range(7)
C_TIME, C_AZ, C_SP, C_UP, C_DOWN, C_MASK = range(6)


class Plan:
    def __init__(self, rhs, stator_adj, sectors, spans):
        self.insts, self.fields, self.ct, self.rows, self.nax = rhs.shape
        assert self.ct == 2 and self.nax == LANES
        self.panels = stator_adj.shape[2]
        self.sectors, self.spans = sectors, spans
        self.tf = self.insts * self.fields
        self.pad = -(-self.tf // 16) * 16
        self.cells = self.ct * self.rows
        self.slab = self.rows * LANES
        self.shift = [
            ((t * sectors) // (self.insts - 1) - t // (self.insts - 1)) % sectors for t in range(self.insts)
        ]
        assert len(set(self.shift)) == self.insts
        assert self.slab % CHUNK == 0 and 3 * self.pad <= 256 and self.cells * self.panels <= LANES

    def spectral(self):
        t = np.arange(self.insts)
        off = t[:, None] - t[None, :]
        sines = np.where(off == 0, 1.0, np.sin(np.pi * off / self.insts))
        table = np.where(off == 0, 0.0, 0.5 * (1.0 - 2.0 * (off % 2)) / sines).astype(np.float32)
        full = np.zeros((self.pad, self.pad), np.float32)
        full[: self.tf, : self.tf] = np.kron(table.T, np.eye(self.fields, dtype=np.float32))
        hi = full.astype(ml_dtypes.bfloat16)
        lo = (full - hi.astype(np.float32)).astype(ml_dtypes.bfloat16)
        return np.concatenate([hi, lo, hi], axis=1)

    def field_rows(self):
        out = np.zeros((self.pad, self.fields), np.float32)
        out[np.arange(self.tf), np.arange(self.tf) % self.fields] = 1.0
        return out

    def field_lanes(self):
        return np.tile(self.field_rows().T, (1, 3))

    def block_diagonal(self):
        block = np.full(self.pad, -1)
        block[: self.tf] = np.arange(self.tf) // self.fields
        same = (block[:, None] == block[None, :]) & (block[:, None] >= 0)
        return np.tile(same.astype(np.float32), (1, 3))

    def inst_rows(self):
        out = np.zeros((self.pad, self.insts), np.float32)
        out[np.arange(self.tf), np.arange(self.tf) // self.fields] = 1.0
        return out

    def cell_lanes(self):
        out = np.zeros((self.ct, self.rows, self.ct, self.panels, self.rows), np.float32)
        for a in range(self.ct):
            for r in range(self.rows):
                out[a, r, a, :, r] = 1.0
        return out.reshape(self.cells, -1)

    def panel_lanes(self):
        lane = np.arange(self.cells * self.panels)
        return ((lane // self.rows) % self.panels).astype(np.float32)[None]

    def panel_sum(self):
        return np.tile(np.eye(self.panels * self.rows, dtype=np.float32), (self.ct, 1))


def call(kernel, out, scratch=(), flops=2_000_000, nbytes=1_000_000):
    return pl.pallas_call(
        kernel,
        out_shape=out,
        scratch_shapes=list(scratch),
        compiler_params=pltpu.CompilerParams(vmem_limit_bytes=40 * 1024 * 1024),
        cost_estimate=pl.CostEstimate(flops=flops, bytes_accessed=nbytes, transcendentals=0),
    )


def f32(*shape):
    return jax.ShapeDtypeStruct(shape, jnp.float32)


def split3(x):
    hi = x.astype(jnp.bfloat16)
    lo = (x - hi.astype(jnp.float32)).astype(jnp.bfloat16)
    return jnp.concatenate([hi, hi, lo], axis=0)


def dot3(w, x):
    return jnp.dot(w, split3(x), preferred_element_type=jnp.float32)


def dot_full(a, b):
    return jnp.dot(a, b, precision=HIGHEST, preferred_element_type=jnp.float32)


def lane_index(rows):
    return lax.broadcasted_iota(jnp.int32, (rows, LANES), 1)


def send_panels(plan, stator_ref, out_ref):
    me = lax.axis_index("sector")
    width = plan.panels * plan.rows
    out_ref[...] = jnp.zeros_like(out_ref)
    for t in range(plan.insts):
        to = lax.rem(me + (plan.sectors - plan.shift[t]), plan.sectors)
        out_ref[to, : plan.fields, :width] = stator_ref[t]


def panel_weights(plan, owner_ref, share_ref, inst_rows, cell_lanes, panel_lanes):
    local = lax.rem(owner_ref[...], plan.panels).astype(jnp.float32)
    first = dot_full(dot_full(inst_rows[...], local), cell_lanes[...])
    share = dot_full(dot_full(inst_rows[...], share_ref[...]), cell_lanes[...])
    panel = panel_lanes[...]
    lower = (jnp.abs(first - panel) < 0.5).astype(jnp.float32)
    upper = (jnp.abs(first + 1.0 - panel) < 0.5).astype(jnp.float32)
    return share * lower + (1.0 - share) * upper


def prepare(
    plan, rhs_ref, diag_ref, face_ref, time_ref, mask_ref, got_ref, owner_ref, share_ref,
    inst_rows, cell_lanes, panel_lanes,
    x0_ref, x1_ref, edge_ref, coef_ref, weight_ref, panels_ref,
):
    me = lax.axis_index("sector")
    cells = plan.cells
    scale = mask_ref[...].astype(jnp.float32) / diag_ref[...]
    lane = lane_index(cells)
    coef_ref[C_TIME] = scale * time_ref[...]
    coef_ref[C_AZ] = scale * face_ref[0]
    coef_ref[C_SP] = scale * face_ref[1]
    axial = scale * face_ref[2]
    coef_ref[C_UP] = jnp.where(lane < LANES - 1, axial, 0.0)
    coef_ref[C_DOWN] = jnp.where(lane > 0, axial, 0.0)
    coef_ref[C_MASK] = scale

    weight = panel_weights(plan, owner_ref, share_ref, inst_rows, cell_lanes, panel_lanes)
    weight_ref[...] = weight
    width = plan.panels * plan.rows
    panels_ref[...] = jnp.zeros_like(panels_ref)
    for t in range(plan.insts):
        source = lax.rem(me + plan.shift[t], plan.sectors)
        panels_ref[t * plan.fields : (t + 1) * plan.fields, :width] = got_ref[source, : plan.fields, :width]
    panels = panels_ref[:, :width]
    terms = jnp.concatenate([panels] * plan.ct, axis=1) * weight
    seam = dot_full(terms, jnp.transpose(cell_lanes[...]))
    seam = jnp.concatenate([seam, jnp.zeros((plan.pad, LANES - cells), jnp.float32)], axis=1)

    inlet = lane_index(plan.pad) == 0
    tail = jnp.zeros((plan.pad - plan.tf, LANES), jnp.float32)
    for cell in range(cells):
        a, r = divmod(cell, plan.rows)
        field = jnp.concatenate([rhs_ref[pl.ds(cell, plan.tf, stride=cells), :], tail], axis=0)
        here = pltpu.roll(seam, (LANES - cell) % LANES, axis=1)
        field = (field + jnp.where(inlet, here, 0.0)) * coef_ref[C_MASK, cell : cell + 1, :]
        (x0_ref, x1_ref)[a][:, r * LANES : (r + 1) * LANES] = field
    write_edges(plan, (x0_ref, x1_ref), edge_ref)


def write_edges(plan, x_refs, edge_ref):
    last = plan.slab - LANES
    for a in range(plan.ct):
        low = x_refs[a][:, :LANES]
        high = x_refs[a][:, last:]
        if plan.spans == 2:
            first = lax.axis_index("span") == 0
            edge_ref[0, :, a * LANES : (a + 1) * LANES] = jnp.where(first, high, low)
        else:
            edge_ref[0, :, a * LANES : (a + 1) * LANES] = low
            edge_ref[1, :, a * LANES : (a + 1) * LANES] = high


def stack_matrices(plan, up_ref, down_ref, spectral_ref, rows_ref, lanes_ref, diagonal_ref, out_ref):
    pad = plan.pad
    lane = lax.broadcasted_iota(jnp.int32, (pad, 3 * pad), 1)
    second = (lane >= pad) & (lane < 2 * pad)
    out_ref[SPECTRAL * pad : (SPECTRAL + 1) * pad, :] = spectral_ref[...]
    for block, ref, direction in (
        (DOWN_AZ, down_ref, 0), (UP_SP, up_ref, 1), (DOWN_SP, down_ref, 1),
        (UP_AX, up_ref, 2), (DOWN_AX, down_ref, 2), (UP_AZ, up_ref, 0),
    ):
        full = dot_full(dot_full(rows_ref[...], ref[direction]), lanes_ref[...]) * diagonal_ref[...]
        hi = full.astype(jnp.bfloat16).astype(jnp.float32)
        out_ref[block * pad : (block + 1) * pad, :] = jnp.where(second, full - hi, hi).astype(jnp.bfloat16)


def inner(plan, w_ref, x0_ref, x1_ref, f0_ref, f1_ref, coef_ref, g0_ref, g1_ref, p0_ref, p1_ref):
    pad = plan.pad
    start = (DOWN_AZ, SPECTRAL)
    for a, (x_ref, p_ref) in enumerate(((x0_ref, p0_ref), (x1_ref, p1_ref))):
        for c in range(plan.slab // CHUNK):
            at = slice(c * CHUNK, (c + 1) * CHUNK)
            p_ref[:, at] = dot3(w_ref[start[a] * pad : (start[a] + 6) * pad, :], x_ref[:, at])

    def product(block, a, r):
        row = (block - start[a]) * pad
        return (p0_ref, p1_ref)[a][row : row + pad, r * LANES : (r + 1) * LANES]

    for a in range(plan.ct):
        for r in range(plan.rows):
            cell = a * plan.rows + r

            def coef(which):
                return coef_ref[which, cell : cell + 1, :]

            total = coef(C_TIME) * product(SPECTRAL, a, r)
            other = product(UP_AZ, 1, r) if a == 0 else product(DOWN_AZ, 0, r)
            total = total + coef(C_AZ) * other
            beside = []
            if r + 1 < plan.rows:
                beside.append(product(UP_SP, a, r + 1))
            if r > 0:
                beside.append(product(DOWN_SP, a, r - 1))
            total = total + coef(C_SP) * sum(beside[1:], beside[0])
            total = total + coef(C_UP) * pltpu.roll(product(UP_AX, a, r), LANES - 1, axis=1)
            total = total + coef(C_DOWN) * pltpu.roll(product(DOWN_AX, a, r), 1, axis=1)
            at = slice(r * LANES, (r + 1) * LANES)
            (g0_ref, g1_ref)[a][:, at] = (f0_ref, f1_ref)[a][:, at] - total


def outer_terms(plan, w_ref, low_ref, high_ref, side_ref, coef_ref, g_refs, put):
    pad = plan.pad

    def matrix(block):
        return w_ref[block * pad : (block + 1) * pad, :]

    span = lax.axis_index("span")
    keep_high = jnp.where(span < plan.spans - 1, 1.0, 0.0)
    keep_low = jnp.where(span > 0, 1.0, 0.0)
    above = dot3(matrix(UP_SP), side_ref[0]) * keep_high
    below = dot3(matrix(DOWN_SP), side_ref[side_ref.shape[0] - 1]) * keep_low
    for a, (block, ref) in enumerate(((DOWN_AZ, low_ref), (UP_AZ, high_ref))):
        for c in range(plan.slab // CHUNK):
            terms = dot3(matrix(block), ref[:, c * CHUNK : (c + 1) * CHUNK])
            for part in range(CHUNK // LANES):
                r = c * (CHUNK // LANES) + part
                cell = a * plan.rows + r
                value = g_refs[a][:, r * LANES : (r + 1) * LANES]
                value = value - coef_ref[C_AZ, cell : cell + 1, :] * terms[:, part * LANES : (part + 1) * LANES]
                mine = slice(a * LANES, (a + 1) * LANES)
                if r == 0:
                    value = value - coef_ref[C_SP, cell : cell + 1, :] * below[:, mine]
                if r == plan.rows - 1:
                    value = value - coef_ref[C_SP, cell : cell + 1, :] * above[:, mine]
                put(a, r, value)


def outer(plan, w_ref, low_ref, high_ref, side_ref, coef_ref, g0_ref, g1_ref, x0_ref, x1_ref, edge_ref):
    def put(a, r, value):
        (x0_ref, x1_ref)[a][:, r * LANES : (r + 1) * LANES] = value

    outer_terms(plan, w_ref, low_ref, high_ref, side_ref, coef_ref, (g0_ref, g1_ref), put)
    write_edges(plan, (x0_ref, x1_ref), edge_ref)


def outer_last(
    plan, w_ref, low_ref, high_ref, side_ref, coef_ref, g0_ref, g1_ref, weight_ref, cell_lanes, panel_sum,
    out_ref, send_ref, inlet_ref,
):
    lane = lane_index(plan.pad)
    inlet_ref[...] = jnp.zeros_like(inlet_ref)

    def put(a, r, value):
        cell = a * plan.rows + r
        out_ref[pl.ds(cell, plan.tf, stride=plan.cells), :] = value[: plan.tf]
        inlet_ref[...] = jnp.where(lane == cell, pltpu.roll(value, cell, axis=1) if cell else value, inlet_ref[...])

    outer_terms(plan, w_ref, low_ref, high_ref, side_ref, coef_ref, (g0_ref, g1_ref), put)
    me = lax.axis_index("sector")
    spread = dot_full(inlet_ref[:, : plan.cells], cell_lanes[...]) * weight_ref[...]
    back = dot_full(spread, panel_sum[...])
    width = plan.panels * plan.rows
    send_ref[...] = jnp.zeros_like(send_ref)
    for t in range(plan.insts):
        to = lax.rem(me + plan.shift[t], plan.sectors)
        send_ref[to, : plan.fields, :width] = back[t * plan.fields : (t + 1) * plan.fields]


def collect_panels(plan, got_ref, out_ref):
    me = lax.axis_index("sector")
    width = plan.panels * plan.rows
    for t in range(plan.insts):
        source = lax.rem(me + (plan.sectors - plan.shift[t]), plan.sectors)
        out_ref[t] = got_ref[source, : plan.fields, :width]


def exchange(plan, x0, x1, edge):
    count = plan.sectors
    forward = [(i, (i + 1) % count) for i in range(count)]
    backward = [(target, source) for source, target in forward]
    low = lax.ppermute(x1, "sector", forward)
    high = lax.ppermute(x0, "sector", backward)
    if plan.spans == 2:
        side = lax.ppermute(edge, "span", [(0, 1), (1, 0)])
    else:
        up = [(i, i + 1) for i in range(plan.spans - 1)]
        above = lax.ppermute(edge[0:1], "span", [(target, source) for source, target in up])
        below = lax.ppermute(edge[1:2], "span", up)
        side = jnp.concatenate([above, below], axis=0)
    return low, high, side


def on_device(
    sectors, spans,
    rhs, diag_coef, face_coef, time_coef, jac_up, jac_down, wall_mask, stator_adj, owner, first_panel_share,
):
    plan = Plan(rhs, stator_adj, sectors, spans)
    pad, cells, slab, insts = plan.pad, plan.cells, plan.slab, plan.insts
    width = plan.panels * plan.rows
    edges = 1 if spans == 2 else 2
    bind = functools.partial
    tile = f32(sectors, 8, LANES)
    block = f32(pad, slab)
    edge_shape = f32(edges, pad, plan.ct * LANES)

    sent = call(bind(send_panels, plan), tile)(stator_adj.reshape(insts, plan.fields, width))
    got = lax.all_to_all(sent, "sector", 0, 0, tiled=True)
    cell_lanes = plan.cell_lanes()
    x0, x1, edge, coef, weight = call(
        bind(prepare, plan),
        (block, block, edge_shape, f32(6, cells, LANES), f32(pad, cells * plan.panels)),
        (pltpu.VMEM((pad, LANES), jnp.float32),),
    )(
        rhs.reshape(plan.tf * cells, LANES), diag_coef.reshape(cells, LANES), face_coef.reshape(3, cells, LANES),
        time_coef.reshape(cells, LANES), wall_mask.reshape(cells, LANES), got,
        owner.reshape(insts, cells), first_panel_share.reshape(insts, cells),
        plan.inst_rows(), cell_lanes, plan.panel_lanes(),
    )
    first0, first1 = x0, x1
    matrices = call(
        bind(stack_matrices, plan), jax.ShapeDtypeStruct((7 * pad, 3 * pad), jnp.bfloat16)
    )(jac_up, jac_down, plan.spectral(), plan.field_rows(), plan.field_lanes(), plan.block_diagonal())

    for sweep in range(SWEEPS):
        low, high, side = exchange(plan, x0, x1, edge)
        g0, g1 = call(
            bind(inner, plan), (block, block), (pltpu.VMEM((6 * pad, slab), jnp.float32),) * 2, flops=2_000_000_000
        )(matrices, x0, x1, first0, first1, coef)
        if sweep + 1 < SWEEPS:
            x0, x1, edge = call(bind(outer, plan), (block, block, edge_shape))(
                matrices, low, high, side, coef, g0, g1
            )
    out, sent = call(
        bind(outer_last, plan), (f32(plan.tf * cells, LANES), tile), (pltpu.VMEM((pad, LANES), jnp.float32),)
    )(matrices, low, high, side, coef, g0, g1, weight, cell_lanes, plan.panel_sum())
    got = lax.all_to_all(sent, "sector", 0, 0, tiled=True)
    sens = call(bind(collect_panels, plan), f32(insts, plan.fields, width))(got)
    return out.reshape(rhs.shape), sens.reshape(stator_adj.shape)


def solution(mesh):
    in_specs = (
        P(None, None, "sector", "span", None),
        P("sector", "span", None),
        P(None, "sector", "span", None),
        P("sector", "span", None),
        P(),
        P(),
        P("sector", "span", None),
        P(None, None, "sector", "span"),
        P(None, "sector", "span"),
        P(None, "sector", "span"),
    )
    out_specs = (P(None, None, "sector", "span", None), P(None, None, "sector", "span"))
    return jax.shard_map(
        functools.partial(on_device, mesh.shape["sector"], mesh.shape["span"]),
        mesh=mesh, in_specs=in_specs, out_specs=out_specs, check_vma=False,
    )
```

```python
import functools

import jax
import jax.numpy as jnp
import ml_dtypes
import numpy as np
from jax import lax
from jax.experimental import pallas as pl
from jax.experimental.pallas import tpu as pltpu
from jax.sharding import PartitionSpec as P

SWEEPS = 4
LANES = 128
CHUNK = 256
WINDOW = 8
DEPTH = SWEEPS + 1
SEAM_LANE = 6
HIGHEST = lax.Precision.HIGHEST
DOWN_AZ, SPECTRAL, UP_SP, DOWN_SP, UP_AX, DOWN_AX, UP_AZ = range(7)
C_TIME, C_AZ, C_SP, C_UP, C_DOWN, C_MASK = range(6)


class Plan:
    def __init__(self, rhs, stator_adj, sectors, spans):
        self.insts, self.fields, self.ct, self.rows, self.nax = rhs.shape
        assert self.ct == 2 and self.nax == LANES
        self.panels = stator_adj.shape[2]
        self.sectors, self.spans = sectors, spans
        self.tf = self.insts * self.fields
        self.pad = -(-self.tf // 16) * 16
        self.cells = self.ct * self.rows
        self.slab = self.rows * LANES
        self.shift = [
            ((t * sectors) // (self.insts - 1) - t // (self.insts - 1)) % sectors for t in range(self.insts)
        ]
        assert len(set(self.shift)) == self.insts
        assert self.slab % CHUNK == 0 and 3 * self.pad <= 256 and self.cells * self.panels <= LANES

    def spectral(self):
        t = np.arange(self.insts)
        off = t[:, None] - t[None, :]
        sines = np.where(off == 0, 1.0, np.sin(np.pi * off / self.insts))
        table = np.where(off == 0, 0.0, 0.5 * (1.0 - 2.0 * (off % 2)) / sines).astype(np.float32)
        full = np.zeros((self.pad, self.pad), np.float32)
        full[: self.tf, : self.tf] = np.kron(table.T, np.eye(self.fields, dtype=np.float32))
        hi = full.astype(ml_dtypes.bfloat16)
        lo = (full - hi.astype(np.float32)).astype(ml_dtypes.bfloat16)
        return np.concatenate([hi, lo, hi], axis=1)

    def field_rows(self):
        out = np.zeros((self.pad, self.fields), np.float32)
        out[np.arange(self.tf), np.arange(self.tf) % self.fields] = 1.0
        return out

    def field_lanes(self):
        return np.tile(self.field_rows().T, (1, 3))

    def block_diagonal(self):
        block = np.full(self.pad, -1)
        block[: self.tf] = np.arange(self.tf) // self.fields
        same = (block[:, None] == block[None, :]) & (block[:, None] >= 0)
        return np.tile(same.astype(np.float32), (1, 3))

    def inst_rows(self):
        out = np.zeros((self.pad, self.insts), np.float32)
        out[np.arange(self.tf), np.arange(self.tf) // self.fields] = 1.0
        return out

    def cell_lanes(self):
        out = np.zeros((self.ct, self.rows, self.ct, self.panels, self.rows), np.float32)
        for a in range(self.ct):
            for r in range(self.rows):
                out[a, r, a, :, r] = 1.0
        return out.reshape(self.cells, -1)

    def window_lanes(self):
        out = np.zeros((self.ct, self.panels, self.rows, self.cells, WINDOW), np.float32)
        for a in range(self.ct):
            for r in range(self.rows):
                out[a, :, r, a * self.rows + r, 0] = 1.0
        return out.reshape(self.cells * self.panels, LANES)

    def panel_lanes(self):
        lane = np.arange(self.cells * self.panels)
        return ((lane // self.rows) % self.panels).astype(np.float32)[None]

    def panel_sum(self):
        return np.tile(np.eye(self.panels * self.rows, dtype=np.float32), (self.ct, 1))


def call(kernel, out, scratch=(), flops=2_000_000, nbytes=1_000_000):
    return pl.pallas_call(
        kernel,
        out_shape=out,
        scratch_shapes=list(scratch),
        compiler_params=pltpu.CompilerParams(vmem_limit_bytes=40 * 1024 * 1024),
        cost_estimate=pl.CostEstimate(flops=flops, bytes_accessed=nbytes, transcendentals=0),
    )


def f32(*shape):
    return jax.ShapeDtypeStruct(shape, jnp.float32)


def split3(x):
    hi = x.astype(jnp.bfloat16)
    lo = (x - hi.astype(jnp.float32)).astype(jnp.bfloat16)
    return jnp.concatenate([hi, hi, lo], axis=0)


def dot3(w, x):
    return jnp.dot(w, split3(x), preferred_element_type=jnp.float32)


def dot_full(a, b):
    return jnp.dot(a, b, precision=HIGHEST, preferred_element_type=jnp.float32)


def lane_index(rows):
    return lax.broadcasted_iota(jnp.int32, (rows, LANES), 1)


def send_panels(plan, stator_ref, out_ref):
    me = lax.axis_index("sector")
    width = plan.panels * plan.rows
    out_ref[...] = jnp.zeros_like(out_ref)
    for t in range(plan.insts):
        to = lax.rem(me + (plan.sectors - plan.shift[t]), plan.sectors)
        out_ref[to, : plan.fields, :width] = stator_ref[t]


def panel_weights(plan, owner_ref, share_ref, inst_rows, cell_lanes, panel_lanes):
    local = lax.rem(owner_ref[...], plan.panels).astype(jnp.float32)
    first = dot_full(dot_full(inst_rows[...], local), cell_lanes[...])
    share = dot_full(dot_full(inst_rows[...], share_ref[...]), cell_lanes[...])
    panel = panel_lanes[...]
    lower = (jnp.abs(first - panel) < 0.5).astype(jnp.float32)
    upper = (jnp.abs(first + 1.0 - panel) < 0.5).astype(jnp.float32)
    return share * lower + (1.0 - share) * upper


def prepare(plan, rhs_ref, diag_ref, face_ref, time_ref, mask_ref, x0_ref, x1_ref, edge_ref, coef_ref):
    cells = plan.cells
    scale = mask_ref[...].astype(jnp.float32) / diag_ref[...]
    lane = lane_index(cells)
    coef_ref[C_TIME] = scale * time_ref[...]
    coef_ref[C_AZ] = scale * face_ref[0]
    coef_ref[C_SP] = scale * face_ref[1]
    axial = scale * face_ref[2]
    coef_ref[C_UP] = jnp.where(lane < LANES - 1, axial, 0.0)
    coef_ref[C_DOWN] = jnp.where(lane > 0, axial, 0.0)
    coef_ref[C_MASK] = scale
    tail = jnp.zeros((plan.pad - plan.tf, LANES), jnp.float32)
    for cell in range(cells):
        a, r = divmod(cell, plan.rows)
        field = jnp.concatenate([rhs_ref[pl.ds(cell, plan.tf, stride=cells), :], tail], axis=0)
        (x0_ref, x1_ref)[a][:, r * LANES : (r + 1) * LANES] = field * coef_ref[C_MASK, cell : cell + 1, :]
    write_edges(plan, (x0_ref, x1_ref), edge_ref)


def window_message(
    plan, got_ref, owner_ref, share_ref, x0_ref, x1_ref, coef_ref, inst_rows, cell_lanes, panel_lanes, window_lanes,
    message_ref, weight_ref, panels_ref,
):
    me = lax.axis_index("sector")
    weight = panel_weights(plan, owner_ref, share_ref, inst_rows, cell_lanes, panel_lanes)
    weight_ref[...] = weight
    width = plan.panels * plan.rows
    panels_ref[...] = jnp.zeros_like(panels_ref)
    for t in range(plan.insts):
        source = lax.rem(me + plan.shift[t], plan.sectors)
        panels_ref[t * plan.fields : (t + 1) * plan.fields, :width] = got_ref[source, : plan.fields, :width]
    terms = jnp.concatenate([panels_ref[:, :width]] * plan.ct, axis=1) * weight
    seam = dot_full(terms, window_lanes[...])

    def packed(rows, tile_of):
        lane = lane_index(rows)
        out = jnp.zeros((rows, LANES), jnp.float32)
        for cell in range(plan.cells):
            at = cell * WINDOW
            tile = tile_of(cell)
            tile = pltpu.roll(tile, at, axis=1) if at else tile
            out = jnp.where((lane >= at) & (lane < at + DEPTH), tile, out)
        return out

    def field(cell):
        a, r = divmod(cell, plan.rows)
        return (x0_ref, x1_ref)[a][:, r * LANES : (r + 1) * LANES]

    def coefs(cell):
        return jnp.concatenate([coef_ref[which, cell : cell + 1, :] for which in range(6)] + [zeros], axis=0)

    zeros = jnp.zeros((2, LANES), jnp.float32)
    rates = packed(8, coefs)
    seam = seam * rates[C_MASK : C_MASK + 1, :]
    message_ref[: plan.pad, :] = packed(plan.pad, field) + seam + pltpu.roll(seam, SEAM_LANE, axis=1)
    message_ref[plan.pad :, :] = rates


def window_sweeps(
    plan, w_ref, *refs
):
    sides = 1 if plan.spans == 2 else 2
    block_refs = refs[:5]
    side_refs = refs[5 : 5 + sides]
    weight_ref, window_lanes, panel_sum, inlet_ref, send_ref, force_ref, state_ref, product_ref = refs[5 + sides :]
    pad, rows = plan.pad, plan.rows
    span = lax.axis_index("span")
    keep_high = jnp.where(span < plan.spans - 1, 1.0, 0.0)
    keep_low = jnp.where(span > 0, 1.0, 0.0)
    lane = lane_index(pad)
    cell_at = lax.rem(lane, WINDOW)
    row_at = lax.rem(lax.div(lane, WINDOW), rows)
    half = plan.rows * WINDOW
    blocks, beside = range(-2, 3), range(-1, 2)

    def at(k, x, which):
        start = (((k + 2) * 3 + x + 1) * 2 + which) * LANES
        return slice(start, start + LANES)

    def both(k, x):
        return slice(at(k, x, 0).start, at(k, x, 1).stop)

    rates = {}
    for k in blocks:
        for x in beside:
            if x == 0:
                message = block_refs[k + 2][...]
            elif x > 0:
                message = side_refs[0][k + 2] * keep_high
            else:
                message = side_refs[-1][k + 2] * keep_low
            field = message[:pad]
            force_ref[:, at(k, x, 0)] = jnp.where(cell_at < DEPTH, field, 0.0)
            force_ref[:, at(k, x, 1)] = jnp.where(cell_at == 0, pltpu.roll(field, LANES - SEAM_LANE, axis=1), 0.0)
            rates[k, x] = message[pad:]
    state_ref[...] = force_ref[...]

    def multiply(k, x, low, high):
        product_ref[low * pad : high * pad, both(k, x)] = dot3(
            w_ref[low * pad : high * pad, :], state_ref[:, both(k, x)]
        )

    def product(block, k, x, which):
        if k not in blocks or x not in beside:
            return jnp.zeros((pad, LANES), jnp.float32)
        return product_ref[block * pad : (block + 1) * pad, at(k, x, which)]

    def rate(which, k, x):
        return rates[k, x][which : which + 1, :]

    def update(k, x, which):
        up = pltpu.roll(jnp.where(lane >= half, product(UP_AZ, k, x, which), product(UP_AZ, k + 1, x, which)), half, axis=1)
        down = pltpu.roll(
            jnp.where(lane < half, product(DOWN_AZ, k, x, which), product(DOWN_AZ, k - 1, x, which)), half, axis=1
        )
        total = rate(C_AZ, k, x) * (up + down)
        step = (rows - 1) * WINDOW
        up = jnp.where(
            row_at < rows - 1,
            pltpu.roll(product(UP_SP, k, x, which), LANES - WINDOW, axis=1),
            pltpu.roll(product(UP_SP, k, x + 1, which), step, axis=1),
        )
        down = jnp.where(
            row_at > 0,
            pltpu.roll(product(DOWN_SP, k, x, which), WINDOW, axis=1),
            pltpu.roll(product(DOWN_SP, k, x - 1, which), LANES - step, axis=1),
        )
        total = total + rate(C_SP, k, x) * (up + down)
        total = total + rate(C_TIME, k, x) * product(SPECTRAL, k, x, which)
        total = total + rate(C_UP, k, x) * pltpu.roll(product(UP_AX, k, x, which), LANES - 1, axis=1)
        total = total + rate(C_DOWN, k, x) * pltpu.roll(product(DOWN_AX, k, x, which), 1, axis=1)
        state_ref[:, at(k, x, which)] = force_ref[:, at(k, x, which)] - total

    everything = (DOWN_AZ, UP_AZ + 1)
    for sweep in range(SWEEPS):
        left = SWEEPS - 1 - sweep
        reach = -(-left // plan.ct)
        targets = [(k, x) for k in range(-reach, reach + 1) for x in beside if left or x == 0]
        for k in blocks:
            for x in beside:
                if (k, x) in targets:
                    multiply(k, x, *everything)
                elif (k + 1, x) in targets and left % plan.ct == 0:
                    multiply(k, x, DOWN_AZ, DOWN_AZ + 1)
                elif (k - 1, x) in targets and left % plan.ct == 0:
                    multiply(k, x, UP_AZ, UP_AZ + 1)
                elif (k, x - 1) in targets or (k, x + 1) in targets:
                    multiply(k, x, UP_SP, DOWN_SP + 1)
        for k, x in targets:
            for which in range(2):
                update(k, x, which)
    inlet_ref[...] = state_ref[:, at(0, 0, 1)]

    me = lax.axis_index("sector")
    spread = dot_full(state_ref[:, at(0, 0, 0)], jnp.transpose(window_lanes[...])) * weight_ref[...]
    back = dot_full(spread, panel_sum[...])
    width = plan.panels * plan.rows
    send_ref[...] = jnp.zeros_like(send_ref)
    for t in range(plan.insts):
        to = lax.rem(me + plan.shift[t], plan.sectors)
        send_ref[to, : plan.fields, :width] = back[t * plan.fields : (t + 1) * plan.fields]


def write_edges(plan, x_refs, edge_ref):
    last = plan.slab - LANES
    for a in range(plan.ct):
        low = x_refs[a][:, :LANES]
        high = x_refs[a][:, last:]
        if plan.spans == 2:
            first = lax.axis_index("span") == 0
            edge_ref[0, :, a * LANES : (a + 1) * LANES] = jnp.where(first, high, low)
        else:
            edge_ref[0, :, a * LANES : (a + 1) * LANES] = low
            edge_ref[1, :, a * LANES : (a + 1) * LANES] = high


def stack_matrices(plan, up_ref, down_ref, spectral_ref, rows_ref, lanes_ref, diagonal_ref, out_ref):
    pad = plan.pad
    lane = lax.broadcasted_iota(jnp.int32, (pad, 3 * pad), 1)
    second = (lane >= pad) & (lane < 2 * pad)
    out_ref[SPECTRAL * pad : (SPECTRAL + 1) * pad, :] = spectral_ref[...]
    for block, ref, direction in (
        (DOWN_AZ, down_ref, 0), (UP_SP, up_ref, 1), (DOWN_SP, down_ref, 1),
        (UP_AX, up_ref, 2), (DOWN_AX, down_ref, 2), (UP_AZ, up_ref, 0),
    ):
        full = dot_full(dot_full(rows_ref[...], ref[direction]), lanes_ref[...]) * diagonal_ref[...]
        hi = full.astype(jnp.bfloat16).astype(jnp.float32)
        out_ref[block * pad : (block + 1) * pad, :] = jnp.where(second, full - hi, hi).astype(jnp.bfloat16)


def inner(plan, w_ref, x0_ref, x1_ref, f0_ref, f1_ref, coef_ref, g0_ref, g1_ref, p0_ref, p1_ref):
    pad = plan.pad
    start = (DOWN_AZ, SPECTRAL)
    for a, (x_ref, p_ref) in enumerate(((x0_ref, p0_ref), (x1_ref, p1_ref))):
        for c in range(plan.slab // CHUNK):
            at = slice(c * CHUNK, (c + 1) * CHUNK)
            p_ref[:, at] = dot3(w_ref[start[a] * pad : (start[a] + 6) * pad, :], x_ref[:, at])

    def product(block, a, r):
        row = (block - start[a]) * pad
        return (p0_ref, p1_ref)[a][row : row + pad, r * LANES : (r + 1) * LANES]

    for a in range(plan.ct):
        for r in range(plan.rows):
            cell = a * plan.rows + r

            def coef(which):
                return coef_ref[which, cell : cell + 1, :]

            total = coef(C_TIME) * product(SPECTRAL, a, r)
            other = product(UP_AZ, 1, r) if a == 0 else product(DOWN_AZ, 0, r)
            total = total + coef(C_AZ) * other
            beside = []
            if r + 1 < plan.rows:
                beside.append(product(UP_SP, a, r + 1))
            if r > 0:
                beside.append(product(DOWN_SP, a, r - 1))
            total = total + coef(C_SP) * sum(beside[1:], beside[0])
            total = total + coef(C_UP) * pltpu.roll(product(UP_AX, a, r), LANES - 1, axis=1)
            total = total + coef(C_DOWN) * pltpu.roll(product(DOWN_AX, a, r), 1, axis=1)
            at = slice(r * LANES, (r + 1) * LANES)
            (g0_ref, g1_ref)[a][:, at] = (f0_ref, f1_ref)[a][:, at] - total


def outer_terms(plan, w_ref, low_ref, high_ref, side_ref, coef_ref, g_refs, put):
    pad = plan.pad

    def matrix(block):
        return w_ref[block * pad : (block + 1) * pad, :]

    span = lax.axis_index("span")
    keep_high = jnp.where(span < plan.spans - 1, 1.0, 0.0)
    keep_low = jnp.where(span > 0, 1.0, 0.0)
    above = dot3(matrix(UP_SP), side_ref[0]) * keep_high
    below = dot3(matrix(DOWN_SP), side_ref[side_ref.shape[0] - 1]) * keep_low
    for a, (block, ref) in enumerate(((DOWN_AZ, low_ref), (UP_AZ, high_ref))):
        for c in range(plan.slab // CHUNK):
            terms = dot3(matrix(block), ref[:, c * CHUNK : (c + 1) * CHUNK])
            for part in range(CHUNK // LANES):
                r = c * (CHUNK // LANES) + part
                cell = a * plan.rows + r
                value = g_refs[a][:, r * LANES : (r + 1) * LANES]
                value = value - coef_ref[C_AZ, cell : cell + 1, :] * terms[:, part * LANES : (part + 1) * LANES]
                mine = slice(a * LANES, (a + 1) * LANES)
                if r == 0:
                    value = value - coef_ref[C_SP, cell : cell + 1, :] * below[:, mine]
                if r == plan.rows - 1:
                    value = value - coef_ref[C_SP, cell : cell + 1, :] * above[:, mine]
                put(a, r, value)


def outer(plan, w_ref, low_ref, high_ref, side_ref, coef_ref, g0_ref, g1_ref, x0_ref, x1_ref, edge_ref):
    def put(a, r, value):
        (x0_ref, x1_ref)[a][:, r * LANES : (r + 1) * LANES] = value

    outer_terms(plan, w_ref, low_ref, high_ref, side_ref, coef_ref, (g0_ref, g1_ref), put)
    write_edges(plan, (x0_ref, x1_ref), edge_ref)


def outer_last(plan, w_ref, low_ref, high_ref, side_ref, coef_ref, g0_ref, g1_ref, inlet_ref, out_ref):
    lane = lane_index(plan.pad)

    def put(a, r, value):
        cell = a * plan.rows + r
        seam = inlet_ref[...]
        seam = pltpu.roll(seam, LANES - cell * WINDOW, axis=1) if cell else seam
        value = value + jnp.where(lane < DEPTH, seam, 0.0)
        out_ref[pl.ds(cell, plan.tf, stride=plan.cells), :] = value[: plan.tf]

    outer_terms(plan, w_ref, low_ref, high_ref, side_ref, coef_ref, (g0_ref, g1_ref), put)


def collect_panels(plan, got_ref, out_ref):
    me = lax.axis_index("sector")
    width = plan.panels * plan.rows
    for t in range(plan.insts):
        source = lax.rem(me + (plan.sectors - plan.shift[t]), plan.sectors)
        out_ref[t] = got_ref[source, : plan.fields, :width]


def exchange(plan, x0, x1, edge):
    count = plan.sectors
    forward = [(i, (i + 1) % count) for i in range(count)]
    backward = [(target, source) for source, target in forward]
    low = lax.ppermute(x1, "sector", forward)
    high = lax.ppermute(x0, "sector", backward)
    if plan.spans == 2:
        side = lax.ppermute(edge, "span", [(0, 1), (1, 0)])
    else:
        up = [(i, i + 1) for i in range(plan.spans - 1)]
        above = lax.ppermute(edge[0:1], "span", [(target, source) for source, target in up])
        below = lax.ppermute(edge[1:2], "span", up)
        side = jnp.concatenate([above, below], axis=0)
    return low, high, side


def exchange_window(plan, message):
    count = plan.sectors

    def from_block(k):
        if k == 0:
            return message
        return lax.ppermute(message, "sector", [(i, (i - k) % count) for i in range(count)])

    blocks = [from_block(k) for k in range(-2, 3)]
    stack = jnp.stack(blocks)
    if plan.spans == 2:
        return blocks, [lax.ppermute(stack, "span", [(0, 1), (1, 0)])]
    up = [(i, i + 1) for i in range(plan.spans - 1)]
    above = lax.ppermute(stack, "span", [(target, source) for source, target in up])
    return blocks, [above, lax.ppermute(stack, "span", up)]


def on_device(
    sectors, spans,
    rhs, diag_coef, face_coef, time_coef, jac_up, jac_down, wall_mask, stator_adj, owner, first_panel_share,
):
    plan = Plan(rhs, stator_adj, sectors, spans)
    pad, cells, slab, insts = plan.pad, plan.cells, plan.slab, plan.insts
    width = plan.panels * plan.rows
    edges = 1 if spans == 2 else 2
    bind = functools.partial
    tile = f32(sectors, 8, LANES)
    block = f32(pad, slab)
    edge_shape = f32(edges, pad, plan.ct * LANES)

    sent = call(bind(send_panels, plan), tile)(stator_adj.reshape(insts, plan.fields, width))
    got = lax.all_to_all(sent, "sector", 0, 0, tiled=True)
    x0, x1, edge, coef = call(bind(prepare, plan), (block, block, edge_shape, f32(6, cells, LANES)))(
        rhs.reshape(plan.tf * cells, LANES), diag_coef.reshape(cells, LANES), face_coef.reshape(3, cells, LANES),
        time_coef.reshape(cells, LANES), wall_mask.reshape(cells, LANES),
    )
    first0, first1 = x0, x1
    matrices = call(
        bind(stack_matrices, plan), jax.ShapeDtypeStruct((7 * pad, 3 * pad), jnp.bfloat16)
    )(jac_up, jac_down, plan.spectral(), plan.field_rows(), plan.field_lanes(), plan.block_diagonal())

    message, weight = call(
        bind(window_message, plan), (f32(pad + 8, LANES), f32(pad, cells * plan.panels)),
        (pltpu.VMEM((pad, LANES), jnp.float32),),
    )(
        got, owner.reshape(insts, cells), first_panel_share.reshape(insts, cells), x0, x1, coef,
        plan.inst_rows(), plan.cell_lanes(), plan.panel_lanes(), plan.window_lanes(),
    )
    blocks, beside = exchange_window(plan, message)
    lanes = 5 * 3 * 2 * LANES
    inlet, back = call(
        bind(window_sweeps, plan), (f32(pad, LANES), tile),
        (
            pltpu.VMEM((pad, lanes), jnp.float32), pltpu.VMEM((pad, lanes), jnp.float32),
            pltpu.VMEM((7 * pad, lanes), jnp.float32),
        ),
        flops=10_000_000_000,
    )(matrices, *blocks, *beside, weight, plan.window_lanes(), plan.panel_sum())
    returned = lax.all_to_all(back, "sector", 0, 0, tiled=True)
    sens = call(bind(collect_panels, plan), f32(insts, plan.fields, width))(returned)

    for sweep in range(SWEEPS):
        low, high, side = exchange(plan, x0, x1, edge)
        g0, g1 = call(
            bind(inner, plan), (block, block), (pltpu.VMEM((6 * pad, slab), jnp.float32),) * 2, flops=2_000_000_000
        )(matrices, x0, x1, first0, first1, coef)
        if sweep + 1 < SWEEPS:
            x0, x1, edge = call(bind(outer, plan), (block, block, edge_shape))(
                matrices, low, high, side, coef, g0, g1
            )
    out = call(bind(outer_last, plan), f32(plan.tf * cells, LANES))(matrices, low, high, side, coef, g0, g1, inlet)
    return out.reshape(rhs.shape), sens.reshape(stator_adj.shape)


def solution(mesh):
    in_specs = (
        P(None, None, "sector", "span", None),
        P("sector", "span", None),
        P(None, "sector", "span", None),
        P("sector", "span", None),
        P(),
        P(),
        P("sector", "span", None),
        P(None, None, "sector", "span"),
        P(None, "sector", "span"),
        P(None, "sector", "span"),
    )
    out_specs = (P(None, None, "sector", "span", None), P(None, None, "sector", "span"))
    return jax.shard_map(
        functools.partial(on_device, mesh.shape["sector"], mesh.shape["span"]),
        mesh=mesh, in_specs=in_specs, out_specs=out_specs, check_vma=False,
    )
```

```python
import functools

import jax
import jax.numpy as jnp
import ml_dtypes
import numpy as np
from jax import lax
from jax.experimental import pallas as pl
from jax.experimental.pallas import tpu as pltpu
from jax.sharding import PartitionSpec as P

SWEEPS = 4
DEPTH = 2
LANES = 128
CHUNK = 256
WINDOW = 8
INLET = SWEEPS + 1
HIGHEST = lax.Precision.HIGHEST
DOWN_AZ, SPECTRAL, UP_SP, DOWN_SP, UP_AX, DOWN_AX, UP_AZ = range(7)
C_TIME, C_AZ, C_SP, C_UP, C_DOWN, C_MASK = range(6)
RATES = 8
AXES = ("sector", "span")


class Plan:
    def __init__(self, rhs, stator_adj, sectors, spans):
        self.insts, self.fields, self.ct, self.rows, self.nax = rhs.shape
        self.panels = stator_adj.shape[2]
        self.sectors, self.spans = sectors, spans
        self.tf = self.insts * self.fields
        self.pad = -(-self.tf // 16) * 16
        self.cells = self.ct * self.rows
        self.slab = self.rows * LANES
        self.width = self.panels * self.rows
        self.shift = [
            ((t * sectors) // (self.insts - 1) - t // (self.insts - 1)) % sectors for t in range(self.insts)
        ]
        assert self.ct == 2 and self.nax == LANES and SWEEPS % DEPTH == 0 and spans > 1
        assert len(set(self.shift)) == self.insts and self.cells * WINDOW == LANES and self.rows >= SWEEPS
        assert self.slab % CHUNK == 0 and 3 * self.pad <= 256 and 2 * self.width <= LANES
        self.blocks = list(range(-2, 3))
        self.halves = [0, 1] if spans == 2 else [-1, 0, 1]
        self.tiles = [(k, x) for k in self.blocks for x in self.halves]
        self.slots = [
            [t for t in range(self.insts) if any((k + self.shift[t]) % sectors == o for k in self.blocks)]
            for o in range(sectors)
        ]
        assert max(map(len, self.slots)) * self.width <= LANES

    def spectral(self):
        t = np.arange(self.insts)
        off = t[:, None] - t[None, :]
        sines = np.where(off == 0, 1.0, np.sin(np.pi * off / self.insts))
        table = np.where(off == 0, 0.0, 0.5 * (1.0 - 2.0 * (off % 2)) / sines).astype(np.float32)
        full = np.zeros((self.pad, self.pad), np.float32)
        full[: self.tf, : self.tf] = np.kron(table.T, np.eye(self.fields, dtype=np.float32))
        hi = full.astype(ml_dtypes.bfloat16)
        lo = (full - hi.astype(np.float32)).astype(ml_dtypes.bfloat16)
        return np.concatenate([hi, lo, hi], axis=1)

    def field_rows(self):
        out = np.zeros((self.pad, self.fields), np.float32)
        out[np.arange(self.tf), np.arange(self.tf) % self.fields] = 1.0
        return out

    def field_lanes(self):
        return np.tile(self.field_rows().T, (1, 3))

    def block_diagonal(self):
        block = np.full(self.pad, -1)
        block[: self.tf] = np.arange(self.tf) // self.fields
        same = (block[:, None] == block[None, :]) & (block[:, None] >= 0)
        return np.tile(same.astype(np.float32), (1, 3))

    def inst_rows(self):
        out = np.zeros((self.pad, 16), np.float32)
        out[np.arange(self.tf), np.arange(self.tf) // self.fields] = 1.0
        return out

    def cell_lanes(self):
        out = np.zeros((self.ct, self.rows, self.ct, self.panels, self.rows), np.float32)
        for a in range(self.ct):
            for r in range(self.rows):
                out[a, r, a, :, r] = 1.0
        out = out.reshape(self.cells, -1)
        return np.pad(out, ((0, 0), (0, LANES - out.shape[1])))

    def window_lanes(self):
        out = np.zeros((LANES, LANES), np.float32)
        out[:, ::WINDOW] = self.cell_lanes().T
        return out

    def twice(self, table):
        return np.concatenate([table, table]).astype(ml_dtypes.bfloat16)

    def panel_lanes(self):
        lane = np.arange(LANES)
        return np.where(lane < self.ct * self.width, (lane // self.rows) % self.panels, -9).astype(np.float32)[None]


def call(kernel, out, scratch=(), flops=2_000_000, nbytes=1_000_000):
    return pl.pallas_call(
        kernel,
        out_shape=out,
        scratch_shapes=list(scratch),
        compiler_params=pltpu.CompilerParams(vmem_limit_bytes=40 * 1024 * 1024),
        cost_estimate=pl.CostEstimate(flops=flops, bytes_accessed=nbytes, transcendentals=0),
    )


def f32(*shape):
    return jax.ShapeDtypeStruct(shape, jnp.float32)


def vmem(*shape):
    return pltpu.VMEM(shape, jnp.float32)


def halves_of(x):
    hi = x.astype(jnp.bfloat16)
    return hi, (x - hi.astype(jnp.float32)).astype(jnp.bfloat16)


def dot3(w, x):
    hi, lo = halves_of(x)
    return jnp.dot(w, jnp.concatenate([hi, hi, lo], axis=0), preferred_element_type=jnp.float32)


def pick(x, table2):
    return jnp.dot(jnp.concatenate(halves_of(x), axis=1), table2, preferred_element_type=jnp.float32)


def dot_full(a, b):
    return jnp.dot(a, b, precision=HIGHEST, preferred_element_type=jnp.float32)


def lane_index(rows):
    return lax.broadcasted_iota(jnp.int32, (rows, LANES), 1)


def rolled(x, by):
    by %= LANES
    return pltpu.roll(x, by, axis=1) if by else x


def at(r, count=1):
    return slice(r * LANES, (r + count) * LANES)


def has_sides(plan):
    span = lax.axis_index("span")
    return jnp.where(span < plan.spans - 1, 1.0, 0.0), jnp.where(span > 0, 1.0, 0.0)


def prepare(
    plan, rhs_ref, diag_ref, face_ref, time_ref, mask_ref, m0_ref, m1_ref, x0_ref, x1_ref, side_ref, c0_ref, c1_ref,
):
    pad = plan.pad
    lane = lane_index(1)
    tail = jnp.zeros((pad - plan.tf, LANES), jnp.float32)
    for cell in range(plan.cells):
        a, r = divmod(cell, plan.rows)
        one = slice(cell, cell + 1)
        scale = mask_ref[one, :].astype(jnp.float32) / diag_ref[one, :]
        axial = scale * face_ref[2, one, :]
        rates = [
            scale * time_ref[one, :], scale * face_ref[0, one, :], scale * face_ref[1, one, :],
            jnp.where(lane < LANES - 1, axial, 0.0), jnp.where(lane > 0, axial, 0.0), scale,
            jnp.zeros((RATES - 6, LANES), jnp.float32),
        ]
        field = jnp.concatenate([rhs_ref[pl.ds(cell, plan.tf, stride=plan.cells), :], tail], axis=0) * scale
        (m0_ref, m1_ref)[a][pad:, at(r)] = jnp.concatenate(rates, axis=0)
        (m0_ref, m1_ref)[a][:pad, at(r)] = field
        (x0_ref, x1_ref)[a][:, at(r)] = field
    write_edges(plan, (m0_ref, m1_ref), side_ref, (c0_ref, c1_ref))


def write_edges(plan, x_refs, side_ref, c_refs):
    last = plan.rows - 1
    first = lax.axis_index("span") == 0
    for a in range(plan.ct):
        for e in range(DEPTH):
            low, high = x_refs[a][:, at(e)], x_refs[a][:, at(last - e)]
            ends = [jnp.where(first, high, low)] if plan.spans == 2 else [low, high]
            for n, end in enumerate(ends):
                side_ref[n, :, at(e * plan.ct + a)] = end
                if e == 0:
                    c_refs[a][n] = end[: plan.pad]


def stack_matrices(plan, up_ref, down_ref, spectral_ref, rows_ref, lanes_ref, diagonal_ref, out_ref):
    pad = plan.pad
    lane = lax.broadcasted_iota(jnp.int32, (pad, 3 * pad), 1)
    second = (lane >= pad) & (lane < 2 * pad)
    out_ref[SPECTRAL * pad : (SPECTRAL + 1) * pad, :] = spectral_ref[...]
    for block, ref, direction in (
        (DOWN_AZ, down_ref, 0), (UP_SP, up_ref, 1), (DOWN_SP, down_ref, 1),
        (UP_AX, up_ref, 2), (DOWN_AX, down_ref, 2), (UP_AZ, up_ref, 0),
    ):
        full = dot_full(dot_full(rows_ref[...], ref[direction]), lanes_ref[...]) * diagonal_ref[...]
        hi = full.astype(jnp.bfloat16).astype(jnp.float32)
        out_ref[block * pad : (block + 1) * pad, :] = jnp.where(second, full - hi, hi).astype(jnp.bfloat16)


class Slab:
    def __init__(self, plan, w_ref, p_ref, rates_ref, first):
        self.plan, self.w, self.p, self.rates, self.first = plan, w_ref, p_ref, rates_ref, first

    def multiply(self, x_ref):
        pad = self.plan.pad
        for c in range(self.plan.slab // CHUNK):
            lanes = slice(c * CHUNK, (c + 1) * CHUNK)
            self.p[:, lanes] = dot3(self.w[self.first * pad : (self.first + 6) * pad, :], x_ref[:pad, lanes])

    def product(self, block, r):
        pad = self.plan.pad
        row = (block - self.first) * pad
        return self.p[row : row + pad, at(r)]

    def rate(self, which, r):
        row = self.plan.pad + which
        return self.rates[row : row + 1, at(r)]

    def own_terms(self, r):
        total = self.rate(C_TIME, r) * self.product(SPECTRAL, r)
        beside = []
        if r + 1 < self.plan.rows:
            beside.append(self.product(UP_SP, r + 1))
        if r > 0:
            beside.append(self.product(DOWN_SP, r - 1))
        total = total + self.rate(C_SP, r) * sum(beside[1:], beside[0])
        total = total + self.rate(C_UP, r) * rolled(self.product(UP_AX, r), -1)
        return total + self.rate(C_DOWN, r) * rolled(self.product(DOWN_AX, r), 1)


def matrix(plan, w_ref, block, count=1):
    return w_ref[block * plan.pad : (block + count) * plan.pad, :]


def inner(plan, w_ref, x0_ref, x1_ref, m0_ref, m1_ref, g0_ref, g1_ref, p0_ref, p1_ref):
    slabs = Slab(plan, w_ref, p0_ref, m0_ref, DOWN_AZ), Slab(plan, w_ref, p1_ref, m1_ref, SPECTRAL)
    slabs[0].multiply(x0_ref)
    slabs[1].multiply(x1_ref)
    inner_rows(plan, slabs, (m0_ref, m1_ref), (g0_ref, g1_ref))


def inner_rows(plan, slabs, force_refs, g_refs):
    for r in range(plan.rows):
        other = slabs[1].product(UP_AZ, r), slabs[0].product(DOWN_AZ, r)
        for a, slab in enumerate(slabs):
            total = slab.own_terms(r) + slab.rate(C_AZ, r) * other[a]
            g_refs[a][:, at(r)] = force_refs[a][: plan.pad, at(r)] - total


def azimuthal(plan, w_ref, block, chunk_of, take):
    for c in range(plan.slab // CHUNK):
        terms = dot3(matrix(plan, w_ref, block), chunk_of(slice(c * CHUNK, (c + 1) * CHUNK)))
        for part in range(CHUNK // LANES):
            take(c * (CHUNK // LANES) + part, terms[:, at(part)])


def middle(
    plan, w_ref, x0_ref, x1_ref, m0_ref, m1_ref, g0_ref, g1_ref, low_ref, high_ref, low_first, high_first,
    side_ref, side_first, c_low, c_high, h0_ref, h1_ref, n_low_ref, n_high_ref, p0_ref, p1_ref, y0_ref, y1_ref,
):
    pad, rows, ct = plan.pad, plan.rows, plan.ct
    outward, inward, last = (UP_SP, DOWN_SP), (DOWN_SP, UP_SP), (rows - 1, 0)
    edge_terms, edge_new, corner_terms = [], [], []
    for n, keep in enumerate(has_sides(plan)):
        i = 0 if plan.spans == 2 else n
        first = side_ref[i, :pad, at(0, ct)] * keep
        second = side_ref[i, :pad, at(ct, ct)] * keep
        corner = [c[i] * keep for c in (c_low, c_high)]
        every = dot3(w_ref[...], first)
        edge_terms.append(every[outward[n] * pad : (outward[n] + 1) * pad])
        corner_terms.append([dot3(matrix(plan, w_ref, outward[n]), c) for c in corner])
        beyond = dot3(matrix(plan, w_ref, outward[n]), second)
        edges_own = jnp.concatenate([x_ref[:, at(last[n])] for x_ref in (x0_ref, x1_ref)], axis=1)
        within = dot3(matrix(plan, w_ref, inward[n]), edges_own)
        from_low = dot3(matrix(plan, w_ref, DOWN_AZ), corner[0])
        from_high = dot3(matrix(plan, w_ref, UP_AZ), corner[1])
        new = []
        for a in range(ct):

            def rate(which):
                return side_first[i, pad + which : pad + which + 1, at(a)] * keep

            def part(block, b=a):
                return every[block * pad : (block + 1) * pad, at(b)]

            around = part(UP_AZ, 1) + from_low if a == 0 else from_high + part(DOWN_AZ, 0)
            total = rate(C_TIME) * part(SPECTRAL) + rate(C_AZ) * around
            total = total + rate(C_SP) * (beyond[:, at(a)] + within[:, at(a)])
            total = total + rate(C_UP) * rolled(part(UP_AX), -1) + rate(C_DOWN) * rolled(part(DOWN_AX), 1)
            new.append(side_first[i, :pad, at(a)] * keep - total)
        edge_new.append(dot3(matrix(plan, w_ref, outward[n]), jnp.concatenate(new, axis=1)))

    near = Slab(plan, w_ref, p0_ref, low_first, DOWN_AZ), Slab(plan, w_ref, p1_ref, high_first, SPECTRAL)
    own = Slab(plan, w_ref, p0_ref, m0_ref, DOWN_AZ), Slab(plan, w_ref, p1_ref, m1_ref, SPECTRAL)
    near[0].multiply(low_ref)
    near[1].multiply(high_ref)
    for a, (near_ref, first_ref, n_ref, x_ref, to_own, to_near) in enumerate((
        (low_ref, low_first, n_low_ref, x0_ref, DOWN_AZ, UP_AZ), (high_ref, high_first, n_high_ref, x1_ref, UP_AZ, DOWN_AZ),
    )):

        def take(r, terms):
            total = near[a].own_terms(r) + near[a].rate(C_AZ, r) * terms
            mine = own[a].rate(C_AZ, r) * near[a].product(to_own, r)
            for n in range(2):
                if r == last[n]:
                    total = total + near[a].rate(C_SP, r) * corner_terms[n][a]
                    mine = mine + own[a].rate(C_SP, r) * edge_terms[n][:, at(a)]
            n_ref[:, at(r)] = first_ref[:pad, at(r)] - total
            (y0_ref, y1_ref)[a][:, at(r)] = (g0_ref, g1_ref)[a][:, at(r)] - mine

        azimuthal(plan, w_ref, to_near, lambda lanes: x_ref[:pad, lanes], take)

    own[0].multiply(y0_ref)
    own[1].multiply(y1_ref)
    inner_rows(plan, own, (m0_ref, m1_ref), (h0_ref, h1_ref))
    for a, h_ref in enumerate((h0_ref, h1_ref)):
        for n in range(2):
            h_ref[:, at(last[n])] -= own[a].rate(C_SP, last[n]) * edge_new[n][:, at(a)]


def outer_rows(plan, w_ref, low_ref, high_ref, n_low_ref, n_high_ref, low_first, high_first, m0_ref, m1_ref, h0_ref, h1_ref, put):
    pad = plan.pad
    for a, (block, far_ref, n_ref, first_ref, m_ref, h_ref) in enumerate((
        (DOWN_AZ, low_ref, n_low_ref, low_first, m0_ref, h0_ref), (UP_AZ, high_ref, n_high_ref, high_first, m1_ref, h1_ref),
    )):

        def near_rows(lanes):
            terms = dot3(matrix(plan, w_ref, block), far_ref[:pad, lanes])
            return n_ref[:, lanes] - first_ref[pad + C_AZ : pad + C_AZ + 1, lanes] * terms

        def take(r, terms):
            put(a, r, h_ref[:, at(r)] - m_ref[pad + C_AZ : pad + C_AZ + 1, at(r)] * terms)

        azimuthal(plan, w_ref, block, near_rows, take)


def outer(plan, *refs):
    x0_ref, x1_ref, side_ref, c0_ref, c1_ref = refs[-5:]

    def put(a, r, value):
        (x0_ref, x1_ref)[a][:, at(r)] = value

    outer_rows(plan, *refs[:-5], put)
    write_edges(plan, (x0_ref, x1_ref), side_ref, (c0_ref, c1_ref))


def outer_last(plan, *refs):
    inlet_ref, out_ref = refs[-2:]
    lane = lane_index(plan.pad)

    def put(a, r, value):
        cell = a * plan.rows + r
        value = value + jnp.where(lane < INLET, rolled(inlet_ref[...], -cell * WINDOW), 0.0)
        out_ref[pl.ds(cell, plan.tf, stride=plan.cells), :] = value[: plan.tf]

    outer_rows(plan, *refs[:-2], put)


def along(array, axis, pairs):
    return lax.ppermute(array, axis, pairs)


def ring(plan, by):
    return [(i, (i + by) % plan.sectors) for i in range(plan.sectors)]


def beside(plan, array, by=0):
    def pairs(step):
        out = []
        for s in range(plan.sectors):
            for x in range(plan.spans):
                to = 1 - x if plan.spans == 2 else x + step
                if 0 <= to < plan.spans:
                    out.append((s * plan.spans + x, (s + by) % plan.sectors * plan.spans + to))
        return out

    if plan.spans == 2:
        return along(array, AXES, pairs(0))
    return jnp.concatenate([along(array[:1], AXES, pairs(-1)), along(array[1:], AXES, pairs(1))])


def send_panels(plan, stator_ref, out_ref, panels_ref):
    me = lax.axis_index("sector")
    for f in range(plan.fields):
        panels_ref[pl.ds(f, plan.insts, stride=RATES), : plan.width] = jnp.transpose(stator_ref[f])
    out_ref[...] = jnp.zeros_like(out_ref)
    for o, slots in enumerate(plan.slots):
        to = lax.rem(me + (plan.sectors - o), plan.sectors) * plan.spans
        for slot, t in enumerate(slots):
            lanes = slice(slot * plan.width, (slot + 1) * plan.width)
            panels = panels_ref[t * RATES : t * RATES + plan.fields, : plan.width]
            for x in range(plan.spans):
                out_ref[to + x, : plan.fields, lanes] = panels


def window_message(
    plan, m0_ref, m1_ref, owner_ref, share_ref, cell_lanes, panel_lanes, message_ref,
):
    pad = plan.pad
    lane = lane_index(pad + RATES)
    out = jnp.zeros((pad + RATES, LANES), jnp.float32)
    for cell in range(plan.cells):
        a, r = divmod(cell, plan.rows)
        start = cell * WINDOW
        tile = rolled((m0_ref, m1_ref)[a][:, at(r)], start)
        out = jnp.where((lane >= start) & (lane < start + INLET), tile, out)
    message_ref[: pad + RATES, :] = out

    first = dot_full(lax.rem(owner_ref[...], plan.panels).astype(jnp.float32), cell_lanes[...])
    share = dot_full(share_ref[...], cell_lanes[...])
    panel = panel_lanes[...]
    lower = (jnp.abs(first - panel) < 0.5).astype(jnp.float32)
    upper = (jnp.abs(first + 1.0 - panel) < 0.5).astype(jnp.float32)
    weight = share * lower + (1.0 - share) * upper
    message_ref[pad + RATES :, :] = jnp.concatenate([weight, jnp.zeros((16 - plan.insts, LANES), jnp.float32)], axis=0)


def window_sweeps(plan, w_ref, got_ref, inst_rows, sum_table, spread_table, *refs):
    sides = 1 if plan.spans == 2 else 2
    block_refs, side_refs = refs[:5], refs[5 : 5 + sides]
    inlet_ref, send_ref, force_ref, state_ref, product_ref, panels_ref, terms_ref = refs[5 + sides :]
    pad, rows, insts, fields = plan.pad, plan.rows, plan.insts, plan.fields
    me, span = lax.axis_index("sector"), lax.axis_index("span")
    is_first = span == 0
    keep_high, keep_low = has_sides(plan)
    lane = lane_index(pad)
    row_at = lax.rem(lax.div(lane, WINDOW), rows)
    half = rows * WINDOW
    tiles = plan.tiles

    messages = []
    for k, x in tiles:
        mine = block_refs[k + 2][...]
        if plan.spans == 2:
            theirs = side_refs[0][k + 2]
            messages.append(jnp.where(is_first, mine, theirs) if x == 0 else jnp.where(is_first, theirs, mine))
        elif x == 0:
            messages.append(mine)
        else:
            messages.append(side_refs[0][k + 2] * keep_high if x > 0 else side_refs[1][k + 2] * keep_low)

    panels_ref[...] = jnp.zeros_like(panels_ref)
    for n, (k, x) in enumerate(tiles):
        at_span = x if plan.spans == 2 else jnp.clip(span + x, 0, plan.spans - 1)
        for t in range(insts):
            o = (k + plan.shift[t]) % plan.sectors
            source = lax.rem(me + o, plan.sectors) * plan.spans + at_span
            tile = rolled(got_ref[source], -plan.slots[o].index(t) * plan.width)
            panels_ref[t * fields : (t + 1) * fields, n * LANES : n * LANES + plan.width] = tile[:fields, : plan.width]
    weights = dot_full(inst_rows[...], jnp.concatenate([m[pad + RATES :] for m in messages], axis=1))
    for n in range(len(tiles)):
        panels = panels_ref[:, at(n)]
        terms_ref[n * pad : (n + 1) * pad, :] = (panels + rolled(panels, plan.width)) * weights[:, at(n)]
    seams = pick(terms_ref[...], sum_table[...])

    def lanes_of(k, x, which=0, count=1):
        start = ((tiles.index((k, x))) * 2 + which) * LANES
        return slice(start, start + count * LANES)

    for n, (k, x) in enumerate(tiles):
        seam = seams[n * pad : (n + 1) * pad] * messages[n][pad + C_MASK : pad + C_MASK + 1]
        force_ref[:, lanes_of(k, x, 0)] = messages[n][:pad] + seam
        force_ref[:, lanes_of(k, x, 1)] = seam
    state_ref[...] = force_ref[...]

    def multiply(k, x, low, high):
        product_ref[low * pad : high * pad, lanes_of(k, x, 0, 2)] = dot3(
            w_ref[low * pad : high * pad, :], state_ref[:, lanes_of(k, x, 0, 2)]
        )

    def product(block, k, x, which):
        if (k, x) not in tiles:
            return jnp.zeros((pad, LANES), jnp.float32)
        return product_ref[block * pad : (block + 1) * pad, lanes_of(k, x, which)]

    def update(k, x, which):
        def rate(row):
            return messages[tiles.index((k, x))][pad + row : pad + row + 1]

        up = rolled(jnp.where(lane >= half, product(UP_AZ, k, x, which), product(UP_AZ, k + 1, x, which)), half)
        down = rolled(jnp.where(lane < half, product(DOWN_AZ, k, x, which), product(DOWN_AZ, k - 1, x, which)), half)
        total = rate(C_AZ) * (up + down)
        step = (rows - 1) * WINDOW
        up = jnp.where(
            row_at < rows - 1,
            rolled(product(UP_SP, k, x, which), -WINDOW), rolled(product(UP_SP, k, x + 1, which), step),
        )
        down = jnp.where(
            row_at > 0,
            rolled(product(DOWN_SP, k, x, which), WINDOW), rolled(product(DOWN_SP, k, x - 1, which), -step),
        )
        total = total + rate(C_SP) * (up + down)
        total = total + rate(C_TIME) * product(SPECTRAL, k, x, which)
        total = total + rate(C_UP) * rolled(product(UP_AX, k, x, which), -1)
        total = total + rate(C_DOWN) * rolled(product(DOWN_AX, k, x, which), 1)
        state_ref[:, lanes_of(k, x, which)] = force_ref[:, lanes_of(k, x, which)] - total

    for sweep in range(SWEEPS):
        left = SWEEPS - 1 - sweep
        reach = -(-left // plan.ct)
        targets = [(k, x) for k, x in tiles if abs(k) <= reach and (left or plan.spans == 2 or x == 0)]
        for k, x in tiles:
            if (k, x) in targets:
                multiply(k, x, DOWN_AZ, UP_AZ + 1)
            elif (k + 1, x) in targets and left % plan.ct == 0:
                multiply(k, x, DOWN_AZ, DOWN_AZ + 1)
            elif (k - 1, x) in targets and left % plan.ct == 0:
                multiply(k, x, UP_AZ, UP_AZ + 1)
            elif (k, x - 1) in targets or (k, x + 1) in targets:
                multiply(k, x, UP_SP, DOWN_SP + 1)
        for k, x in targets:
            for which in range(2):
                update(k, x, which)

    def own(read):
        if plan.spans == 2:
            return jnp.where(is_first, read(tiles.index((0, 0))), read(tiles.index((0, 1))))
        return read(tiles.index((0, 0)))

    inlet_ref[...] = own(lambda n: state_ref[:, at(2 * n + 1)])
    back = pick(own(lambda n: state_ref[:, at(2 * n)]), spread_table[...]) * own(lambda n: weights[:, at(n)])
    back = back + rolled(back, -plan.width)
    send_ref[...] = jnp.zeros_like(send_ref)
    for t in range(insts):
        to = lax.rem(me + plan.shift[t], plan.sectors)
        send_ref[to, :fields, : plan.width] = back[t * fields : (t + 1) * fields, : plan.width]


def collect_panels(plan, got_ref, out_ref, panels_ref):
    me = lax.axis_index("sector")
    for t in range(plan.insts):
        source = lax.rem(me + (plan.sectors - plan.shift[t]), plan.sectors)
        panels_ref[t * RATES : (t + 1) * RATES, :] = got_ref[source]
    for f in range(plan.fields):
        tile = panels_ref[pl.ds(f, plan.insts, stride=RATES), : plan.width]
        out_ref[f] = jnp.transpose(tile)


def on_device(
    sectors, spans,
    rhs, diag_coef, face_coef, time_coef, jac_up, jac_down, wall_mask, stator_adj, owner, first_panel_share,
):
    plan = Plan(rhs, stator_adj, sectors, spans)
    pad, cells, slab, insts, fields = plan.pad, plan.cells, plan.slab, plan.insts, plan.fields
    ends = 1 if spans == 2 else 2
    bind = functools.partial
    block, message = f32(pad, slab), f32(pad + RATES, slab)
    corner = f32(ends, pad, LANES)

    m0, m1, x0, x1, side, c0, c1 = call(
        bind(prepare, plan),
        (message, message, block, block, f32(ends, pad + RATES, DEPTH * plan.ct * LANES), corner, corner),
    )(
        rhs.reshape(plan.tf * cells, LANES), diag_coef.reshape(cells, LANES), face_coef.reshape(3, cells, LANES),
        time_coef.reshape(cells, LANES), wall_mask.reshape(cells, LANES),
    )
    matrices = call(
        bind(stack_matrices, plan), jax.ShapeDtypeStruct((7 * pad, 3 * pad), jnp.bfloat16)
    )(jac_up, jac_down, plan.spectral(), plan.field_rows(), plan.field_lanes(), plan.block_diagonal())

    stator = jnp.transpose(stator_adj, (1, 2, 3, 0)).reshape(fields, plan.width, insts)
    sent = call(bind(send_panels, plan), f32(sectors * spans, RATES, LANES), (vmem(insts * RATES, LANES),))(stator)
    got = lax.all_to_all(sent, AXES, 0, 0, tiled=True)
    window = call(bind(window_message, plan), f32(pad + RATES + 16, LANES))(
        m0, m1, owner.reshape(insts, cells), first_panel_share.reshape(insts, cells),
        plan.cell_lanes(), plan.panel_lanes(),
    )
    windows = [window if k == 0 else along(window, "sector", ring(plan, -k)) for k in plan.blocks]
    stack = jnp.stack(windows)
    if spans == 2:
        others = [along(stack, "span", [(0, 1), (1, 0)])]
    else:
        up = [(i, i + 1) for i in range(spans - 1)]
        others = [along(stack, "span", [(target, source) for source, target in up]), along(stack, "span", up)]
    lanes = len(plan.tiles) * LANES
    sums, spreads = plan.twice(plan.window_lanes()), plan.twice(plan.window_lanes().T)
    inlet, back = call(
        bind(window_sweeps, plan), (f32(pad, LANES), f32(sectors, RATES, LANES)),
        (
            vmem(pad, 2 * lanes), vmem(pad, 2 * lanes), vmem(7 * pad, 2 * lanes), vmem(pad, lanes),
            vmem(len(plan.tiles) * pad, LANES),
        ),
        flops=10_000_000_000,
    )(matrices, got, plan.inst_rows(), sums, spreads, *windows, *others)
    returned = lax.all_to_all(back, "sector", 0, 0, tiled=True)
    sens = call(bind(collect_panels, plan), f32(fields, plan.width, insts), (vmem(insts * RATES, LANES),))(returned)

    firsts = None
    for half in range(SWEEPS // DEPTH):
        low = along(m1 if half == 0 else x1, "sector", ring(plan, 1))
        high = along(m0 if half == 0 else x0, "sector", ring(plan, -1))
        sides = beside(plan, side)
        c_low, c_high = beside(plan, c1, 1), beside(plan, c0, -1)
        far_low = along(x0, "sector", ring(plan, 1))
        far_high = along(x1, "sector", ring(plan, -1))
        firsts = firsts or (low, high, sides)
        products = (vmem(6 * pad, slab),) * 2
        g0, g1 = call(bind(inner, plan), (block, block), products, flops=2_000_000_000)(matrices, x0, x1, m0, m1)
        h0, h1, n_low, n_high = call(
            bind(middle, plan), (block,) * 4, products + (vmem(pad, slab),) * 2, flops=4_000_000_000
        )(
            matrices, x0, x1, m0, m1, g0, g1, low, high, firsts[0], firsts[1], sides, firsts[2], c_low, c_high
        )
        operands = (matrices, far_low, far_high, n_low, n_high, firsts[0], firsts[1], m0, m1, h0, h1)
        if half + 1 < SWEEPS // DEPTH:
            x0, x1, side, c0, c1 = call(
                bind(outer, plan), (block, block, f32(ends, pad, DEPTH * plan.ct * LANES), corner, corner)
            )(*operands)
    out = call(bind(outer_last, plan), f32(plan.tf * cells, LANES))(*operands, inlet)
    sens = jnp.transpose(sens.reshape(fields, plan.panels, plan.rows, insts), (3, 0, 1, 2))
    return out.reshape(rhs.shape), sens


def solution(mesh):
    in_specs = (
        P(None, None, "sector", "span", None),
        P("sector", "span", None),
        P(None, "sector", "span", None),
        P("sector", "span", None),
        P(),
        P(),
        P("sector", "span", None),
        P(None, None, "sector", "span"),
        P(None, "sector", "span"),
        P(None, "sector", "span"),
    )
    out_specs = (P(None, None, "sector", "span", None), P(None, None, "sector", "span"))
    return jax.shard_map(
        functools.partial(on_device, mesh.shape["sector"], mesh.shape["span"]),
        mesh=mesh, in_specs=in_specs, out_specs=out_specs, check_vma=False,
    )
```

```python
import functools

import jax
import jax.numpy as jnp
import ml_dtypes
import numpy as np
from jax import lax
from jax.experimental import pallas as pl
from jax.experimental.pallas import tpu as pltpu
from jax.sharding import PartitionSpec as P

SWEEPS = 4
DEPTH = 2
LANES = 128
CHUNK = 256
WINDOW = 8
HIGHEST = lax.Precision.HIGHEST
DOWN_AZ, SPECTRAL, UP_SP, DOWN_SP, UP_AX, DOWN_AX, UP_AZ = range(7)
C_TIME, C_AZ, C_SP, C_UP, C_DOWN, C_MASK = range(6)
RATES = 8
GROUP = 3
AXES = ("sector", "span")


class Plan:
    def __init__(self, rhs, stator_adj, sectors, spans):
        self.insts, self.fields, self.ct, self.rows, self.nax = rhs.shape
        self.panels = stator_adj.shape[2]
        self.sectors, self.spans = sectors, spans
        self.tf = self.insts * self.fields
        self.pad = -(-self.tf // 16) * 16
        self.cells = self.ct * self.rows
        self.slab = self.rows * LANES
        self.width = self.panels * self.rows
        self.shift = [
            ((t * sectors) // (self.insts - 1) - t // (self.insts - 1)) % sectors for t in range(self.insts)
        ]
        assert self.ct == 2 and self.nax == LANES and SWEEPS % DEPTH == 0 and spans > 1
        assert len(set(self.shift)) == self.insts and self.cells * WINDOW == LANES and self.rows >= SWEEPS
        assert self.slab % CHUNK == 0 and 3 * self.pad <= 256 and 2 * self.ct * self.width == LANES
        assert sectors % 2 == 0
        self.ends = 1 if spans == 2 else 2
        self.blocks = [-1, 0, 1]
        self.halves = [0, 1] if spans == 2 else [-1, 0, 1]
        self.tiles = [(k, x) for k in self.blocks for x in self.halves]
        self.slots = [
            [t for t in range(self.insts) if any((k + self.shift[t]) % sectors == o for k in self.blocks)]
            for o in range(sectors)
        ]
        assert max(map(len, self.slots)) * self.width <= LANES

    def spectral(self):
        t = np.arange(self.insts)
        off = t[:, None] - t[None, :]
        sines = np.where(off == 0, 1.0, np.sin(np.pi * off / self.insts))
        table = np.where(off == 0, 0.0, 0.5 * (1.0 - 2.0 * (off % 2)) / sines).astype(np.float32)
        full = np.zeros((self.pad, self.pad), np.float32)
        full[: self.tf, : self.tf] = np.kron(table.T, np.eye(self.fields, dtype=np.float32))
        hi = full.astype(ml_dtypes.bfloat16)
        lo = (full - hi.astype(np.float32)).astype(ml_dtypes.bfloat16)
        return np.concatenate([hi, lo, hi], axis=1)

    def field_rows(self):
        out = np.zeros((self.pad, self.fields), np.float32)
        out[np.arange(self.tf), np.arange(self.tf) % self.fields] = 1.0
        return out

    def field_lanes(self):
        return np.tile(self.field_rows().T, (1, 3))

    def block_diagonal(self):
        block = np.full(self.pad, -1)
        block[: self.tf] = np.arange(self.tf) // self.fields
        same = (block[:, None] == block[None, :]) & (block[:, None] >= 0)
        return np.tile(same.astype(np.float32), (1, 3))

    def inst_rows(self):
        out = np.zeros((self.pad, 16), np.float32)
        out[np.arange(self.tf), np.arange(self.tf) // self.fields] = 1.0
        return out

    def cell_lanes(self):
        out = np.zeros((self.ct, self.rows, self.ct, self.panels, self.rows), np.float32)
        for a in range(self.ct):
            for r in range(self.rows):
                out[a, r, a, :, r] = 1.0
        out = out.reshape(self.cells, -1)
        return np.pad(out, ((0, 0), (0, LANES - out.shape[1])))

    def window_lanes(self):
        out = np.zeros((LANES, LANES), np.float32)
        out[:, ::WINDOW] = self.cell_lanes().T
        return out

    def twice(self, table):
        return np.concatenate([table, table]).astype(ml_dtypes.bfloat16)

    def weight_lanes(self):
        out = np.zeros((LANES, LANES), np.float32)
        half = self.ct * self.width
        out[: self.cells, :half] = self.cell_lanes()[:, :half]
        out[self.cells : 2 * self.cells, half:] = self.cell_lanes()[:, :half]
        return out

    def panel_lanes(self):
        lane = np.arange(LANES)
        return np.where(lane < self.ct * self.width, (lane // self.rows) % self.panels, -9).astype(np.float32)[None]


def call(kernel, out, scratch=(), flops=2_000_000, nbytes=1_000_000):
    return pl.pallas_call(
        kernel,
        out_shape=out,
        scratch_shapes=list(scratch),
        compiler_params=pltpu.CompilerParams(vmem_limit_bytes=40 * 1024 * 1024),
        cost_estimate=pl.CostEstimate(flops=flops, bytes_accessed=nbytes, transcendentals=0),
    )


def f32(*shape):
    return jax.ShapeDtypeStruct(shape, jnp.float32)


def vmem(*shape):
    return pltpu.VMEM(shape, jnp.float32)


def halves_of(x):
    hi = x.astype(jnp.bfloat16)
    return hi, (x - hi.astype(jnp.float32)).astype(jnp.bfloat16)


def dot3(w, x):
    hi, lo = halves_of(x)
    return jnp.dot(w, jnp.concatenate([hi, hi, lo], axis=0), preferred_element_type=jnp.float32)


def pick(x, table2):
    return jnp.dot(jnp.concatenate(halves_of(x), axis=1), table2, preferred_element_type=jnp.float32)


def dot_full(a, b):
    return jnp.dot(a, b, precision=HIGHEST, preferred_element_type=jnp.float32)


def lane_index(rows):
    return lax.broadcasted_iota(jnp.int32, (rows, LANES), 1)


def rolled(x, by):
    by %= LANES
    return pltpu.roll(x, by, axis=1) if by else x


def at(r, count=1, start=0):
    return slice(start + r * LANES, start + (r + count) * LANES)


def parity():
    return lax.rem(lax.axis_index("sector"), 2)


def has_sides(plan):
    span = lax.axis_index("span")
    return jnp.where(span < plan.spans - 1, 1.0, 0.0), jnp.where(span > 0, 1.0, 0.0)


class Layer:
    def __init__(self, plan, ref, start=0, rates=None, seam=None, layer=0):
        self.plan, self.ref, self.start, self.seam, self.layer = plan, ref, start, seam, layer
        self.rates = rates or (ref, start)

    def rate(self, which, r, count=1):
        ref, start = self.rates
        row = self.plan.pad + which
        return ref[row : row + 1, at(r, count, start)]

    def row(self, r):
        value = self.ref[: self.plan.pad, at(r, 1, self.start)]
        if self.seam is None:
            return value
        return value + placed(self.seam, self.layer * self.plan.rows + r) * self.rate(C_MASK, r)

    def chunk(self, c):
        count = CHUNK // LANES
        if self.seam is None:
            return self.ref[: self.plan.pad, at(c * count, count, self.start)]
        return jnp.concatenate([self.row(c * count + part) for part in range(count)], axis=1)


def placed(tile, cell):
    return jnp.where(lane_index(tile.shape[0]) == 0, rolled(tile, -cell * WINDOW), 0.0)


class Products:
    def __init__(self, plan, w_ref, p_ref, first):
        self.plan, self.w, self.p, self.first = plan, w_ref, p_ref, first

    def fill(self, layer):
        for c in range(self.plan.slab // CHUNK):
            self.p[:, c * CHUNK : (c + 1) * CHUNK] = dot3(matrix(self.plan, self.w, self.first, 6), layer.chunk(c))
        self.layer = layer
        return self

    def get(self, block, r):
        row = (block - self.first) * self.plan.pad
        return self.p[row : row + self.plan.pad, at(r)]

    def own_terms(self, r):
        rate = self.layer.rate
        total = rate(C_TIME, r) * self.get(SPECTRAL, r)
        beside = []
        if r + 1 < self.plan.rows:
            beside.append(self.get(UP_SP, r + 1))
        if r > 0:
            beside.append(self.get(DOWN_SP, r - 1))
        total = total + rate(C_SP, r) * sum(beside[1:], beside[0])
        total = total + rate(C_UP, r) * rolled(self.get(UP_AX, r), -1)
        return total + rate(C_DOWN, r) * rolled(self.get(DOWN_AX, r), 1)


def matrix(plan, w_ref, block, count=1):
    return w_ref[block * plan.pad : (block + count) * plan.pad, :]


def two_layers(plan, ref, rates=None, seam=None):
    return [
        Layer(plan, ref, a * plan.slab, (rates, a * plan.slab) if rates is not None else None, seam, a)
        for a in range(plan.ct)
    ]


def inner_rows(plan, w_ref, p_refs, layers, force, g_ref):
    first = Products(plan, w_ref, p_refs[0], DOWN_AZ).fill(layers[0])
    second = Products(plan, w_ref, p_refs[1], SPECTRAL).fill(layers[1])
    for r in range(plan.rows):
        other = second.get(UP_AZ, r), first.get(DOWN_AZ, r)
        for a, products in enumerate((first, second)):
            total = products.own_terms(r) + layers[a].rate(C_AZ, r) * other[a]
            g_ref[:, at(r, 1, a * plan.slab)] = force[a].row(r) - total


def azimuthal(plan, w_ref, block, chunk_of, take):
    for c in range(plan.slab // CHUNK):
        terms = dot3(matrix(plan, w_ref, block), chunk_of(c))
        for part in range(CHUNK // LANES):
            take(c * (CHUNK // LANES) + part, terms[:, at(part)])


def middle_rows(plan, w_ref, p_refs, own, own_force, g_ref, near, near_force, side, corner, y_ref, h_ref, n_refs):
    pad, rows, ct = plan.pad, plan.rows, plan.ct
    outward, inward, last = (UP_SP, DOWN_SP), (DOWN_SP, UP_SP), (rows - 1, 0)
    edge_terms, edge_new, corner_terms = [], [], []
    for n in range(2):
        first, second, edge_force, edge_rate = side(n)
        corners = corner(n)
        every = dot3(w_ref[...], first)
        edge_terms.append(every[outward[n] * pad : (outward[n] + 1) * pad])
        corner_terms.append([dot3(matrix(plan, w_ref, outward[n]), c) for c in corners])
        beyond = dot3(matrix(plan, w_ref, outward[n]), second)
        within = dot3(matrix(plan, w_ref, inward[n]), jnp.concatenate([x.row(last[n]) for x in own], axis=1))
        from_low = dot3(matrix(plan, w_ref, DOWN_AZ), corners[0])
        from_high = dot3(matrix(plan, w_ref, UP_AZ), corners[1])
        new = []
        for a in range(ct):

            def part(block, b=a):
                return every[block * pad : (block + 1) * pad, at(b)]

            around = part(UP_AZ, 1) + from_low if a == 0 else from_high + part(DOWN_AZ, 0)
            total = edge_rate(C_TIME, a) * part(SPECTRAL) + edge_rate(C_AZ, a) * around
            total = total + edge_rate(C_SP, a) * (beyond[:, at(a)] + within[:, at(a)])
            total = total + edge_rate(C_UP, a) * rolled(part(UP_AX), -1)
            total = total + edge_rate(C_DOWN, a) * rolled(part(DOWN_AX), 1)
            new.append(edge_force[:, at(a)] - total)
        edge_new.append(dot3(matrix(plan, w_ref, outward[n]), jnp.concatenate(new, axis=1)))

    products = (
        Products(plan, w_ref, p_refs[0], DOWN_AZ).fill(near[0]), Products(plan, w_ref, p_refs[1], SPECTRAL).fill(near[1]),
    )
    for a, (to_own, to_near) in enumerate(((DOWN_AZ, UP_AZ), (UP_AZ, DOWN_AZ))):

        def take(r, terms):
            total = products[a].own_terms(r) + near[a].rate(C_AZ, r) * terms
            mine = own[a].rate(C_AZ, r) * products[a].get(to_own, r)
            for n in range(2):
                if r == last[n]:
                    total = total + near[a].rate(C_SP, r) * corner_terms[n][a]
                    mine = mine + own[a].rate(C_SP, r) * edge_terms[n][:, at(a)]
            n_refs[a][:, at(r)] = near_force[a].row(r) - total
            lanes = at(r, 1, a * plan.slab)
            y_ref[:, lanes] = g_ref[:, lanes] - mine

        azimuthal(plan, w_ref, to_near, own[a].chunk, take)

    after = [Layer(plan, y_ref, a * plan.slab, own[a].rates) for a in range(ct)]
    inner_rows(plan, w_ref, p_refs, after, own_force, h_ref)
    for a in range(ct):
        for n in range(2):
            lanes = at(last[n], 1, a * plan.slab)
            h_ref[:, lanes] -= own[a].rate(C_SP, last[n]) * edge_new[n][:, at(a)]


def outer_rows(plan, w_ref, own, near, far_chunks, n_refs, h_ref, put):
    count = CHUNK // LANES
    for a, block in enumerate((DOWN_AZ, UP_AZ)):

        def near_chunk(c):
            terms = dot3(matrix(plan, w_ref, block), far_chunks[a](c))
            return n_refs[a][:, at(c * count, count)] - near[a].rate(C_AZ, c * count, count) * terms

        def take(r, terms):
            put(a, r, h_ref[:, at(r, 1, a * plan.slab)] - own[a].rate(C_AZ, r) * terms)

        azimuthal(plan, w_ref, block, near_chunk, take)


def sides_of(plan, side_ref, force_ref, seams_ref):
    pad, ct = plan.pad, plan.ct
    keeps = has_sides(plan)

    def read(n, ref, e, seam):
        i = n if plan.ends == 2 else 0
        value = ref[i, :pad, at(e * ct, ct)]
        if seam:
            r = e if n == 0 else plan.rows - 1 - e
            tile = seams_ref[1, 1 + i]
            scale = ref[i, pad + C_MASK : pad + C_MASK + 1, at(e * ct, ct)]
            value = value + jnp.concatenate([placed(tile, a * plan.rows + r) for a in range(ct)], axis=1) * scale
        return value * keeps[n]

    def side(n):
        i = n if plan.ends == 2 else 0
        same = side_ref is force_ref

        def rate(which, a):
            return force_ref[i, pad + which : pad + which + 1, at(a)] * keeps[n]

        force = read(n, force_ref, 0, True)
        first = force if same else read(n, side_ref, 0, False)
        return first, read(n, side_ref, 1, same), force, rate

    return side


def corners_of(plan, c_refs, seams_ref):
    keeps = has_sides(plan)

    def corner(n):
        i = n if plan.ends == 2 else 0
        out = []
        for a, c_ref in enumerate(c_refs):
            value = c_ref[i, : plan.pad]
            if seams_ref is not None:
                r = 0 if n == 0 else plan.rows - 1
                scale = c_ref[i, plan.pad + C_MASK : plan.pad + C_MASK + 1]
                value = value + placed(seams_ref[2 * a, 1 + i], a * plan.rows + r) * scale
            out.append(value * keeps[n])
        return out

    return corner


def prepare(plan, rhs_ref, diag_ref, face_ref, time_ref, mask_ref, m_ref, side_ref, c0_ref, c1_ref):
    pad = plan.pad
    lane = lane_index(1)
    tail = jnp.zeros((pad - plan.tf, LANES), jnp.float32)
    mirror = parity()
    for cell in range(plan.cells):
        a, r = divmod(cell, plan.rows)
        there = jnp.where(mirror == 0, a, plan.ct - 1 - a) * plan.rows + r
        one = pl.ds(there, 1)
        scale = mask_ref[one, :].astype(jnp.float32) / diag_ref[one, :]
        axial = scale * face_ref[2, one, :]
        rates = [
            scale * time_ref[one, :], scale * face_ref[0, one, :], scale * face_ref[1, one, :],
            jnp.where(lane < LANES - 1, axial, 0.0), jnp.where(lane > 0, axial, 0.0), scale,
            jnp.zeros((RATES - 6, LANES), jnp.float32),
        ]
        field = jnp.concatenate([rhs_ref[pl.ds(there, plan.tf, stride=plan.cells), :], tail], axis=0) * scale
        m_ref[:pad, at(cell)] = field
        m_ref[pad:, at(cell)] = jnp.concatenate(rates, axis=0)
    write_edges(plan, m_ref, side_ref, (c0_ref, c1_ref))


def write_edges(plan, x_ref, side_ref, c_refs):
    first = lax.axis_index("span") == 0
    for a in range(plan.ct):
        for e in range(DEPTH):
            low, high = x_ref[:, at(a * plan.rows + e)], x_ref[:, at((a + 1) * plan.rows - 1 - e)]
            ends = [jnp.where(first, high, low)] if plan.ends == 1 else [low, high]
            for n, end in enumerate(ends):
                side_ref[n, :, at(e * plan.ct + a)] = end
                if e == 0:
                    c_refs[a][n] = end


def stack_matrices(plan, up_ref, down_ref, spectral_ref, rows_ref, lanes_ref, diagonal_ref, out_ref):
    pad = plan.pad
    lane = lax.broadcasted_iota(jnp.int32, (pad, 3 * pad), 1)
    second = (lane >= pad) & (lane < 2 * pad)
    out_ref[SPECTRAL * pad : (SPECTRAL + 1) * pad, :] = spectral_ref[...]
    even = parity() == 0
    for block, small in (
        (DOWN_AZ, jnp.where(even, down_ref[0], up_ref[0])), (UP_AZ, jnp.where(even, up_ref[0], down_ref[0])),
        (UP_SP, up_ref[1]), (DOWN_SP, down_ref[1]), (UP_AX, up_ref[2]), (DOWN_AX, down_ref[2]),
    ):
        full = dot_full(dot_full(rows_ref[...], small), lanes_ref[...]) * diagonal_ref[...]
        hi = full.astype(jnp.bfloat16).astype(jnp.float32)
        out_ref[block * pad : (block + 1) * pad, :] = jnp.where(second, full - hi, hi).astype(jnp.bfloat16)


def send_panels(plan, stator_ref, owner_ref, share_ref, out_ref, panels_ref):
    me = lax.axis_index("sector")
    for f in range(plan.fields):
        panels_ref[pl.ds(f, plan.insts, stride=RATES), : plan.width] = jnp.transpose(stator_ref[f])
    out_ref[...] = jnp.zeros_like(out_ref)
    both = jnp.concatenate([lax.rem(owner_ref[...], plan.panels).astype(jnp.float32), share_ref[...]], axis=1)
    for t in range(plan.insts):
        group, row = divmod(t, GROUP)
        lanes = slice(group * 2 * plan.cells, (group + 1) * 2 * plan.cells)
        row += RATES
        out_ref[:, row : row + 1, lanes] = jnp.broadcast_to(both[t : t + 1][None], (out_ref.shape[0], 1, 2 * plan.cells))
    for o, slots in enumerate(plan.slots):
        to = lax.rem(me + (plan.sectors - o), plan.sectors) * plan.spans
        for slot, t in enumerate(slots):
            lanes = slice(slot * plan.width, (slot + 1) * plan.width)
            panels = panels_ref[t * RATES : t * RATES + plan.fields, : plan.width]
            for x in range(plan.spans):
                out_ref[to + x, : plan.fields, lanes] = panels


def begin(
    plan, w_ref, m_ref, got_ref, inst_rows, weight_table, panel_lanes, sum_table,
    seams_ref, weight_ref, x_ref, g_ref, panels_ref, terms_ref, rows_ref, p0_ref, p1_ref,
):
    pad, insts, fields = plan.pad, plan.insts, plan.fields
    me, span = lax.axis_index("sector"), lax.axis_index("span")
    tiles = plan.tiles
    panels_ref[...] = jnp.zeros_like(panels_ref)
    rows_ref[...] = jnp.zeros_like(rows_ref)
    wide = 2 * plan.cells
    for n, (k, x) in enumerate(tiles):
        at_span = x if plan.spans == 2 else jnp.clip(span + x, 0, plan.spans - 1)
        for t in range(insts):
            o = (k + plan.shift[t]) % plan.sectors
            source = lax.rem(me + o, plan.sectors) * plan.spans + at_span
            tile = rolled(got_ref[source, :RATES], -plan.slots[o].index(t) * plan.width)
            panels_ref[t * fields : (t + 1) * fields, n * LANES : n * LANES + plan.width] = tile[:fields, : plan.width]
        source = lax.rem(me + k + plan.sectors, plan.sectors) * plan.spans + at_span
        table = got_ref[source, RATES:]
        for group in range(-(-insts // GROUP)):
            shifted = rolled(table, -group * wide)
            rows_ref[group * GROUP : (group + 1) * GROUP, n * LANES : n * LANES + wide] = shifted[:GROUP, :wide]
    spread = dot_full(inst_rows[...], rows_ref[...])
    spread = pick(jnp.concatenate([spread[:, at(n)] for n in range(len(tiles))], axis=0), weight_table[...])
    first, share, panel = spread, rolled(spread, plan.ct * plan.width), panel_lanes[...]
    lower = (jnp.abs(first - panel) < 0.5).astype(jnp.float32)
    upper = (jnp.abs(first + 1.0 - panel) < 0.5).astype(jnp.float32)
    weights = share * lower + (1.0 - share) * upper
    for n in range(len(tiles)):
        panels = panels_ref[:, at(n)]
        terms_ref[n * pad : (n + 1) * pad, :] = panels + rolled(panels, plan.width)
    seams = pick(terms_ref[...] * weights, sum_table[...])

    even = parity() == 0
    is_first = span == 0

    def tile(values, k, x):
        n = tiles.index((k, x))
        return values[n * pad : (n + 1) * pad]

    def around(values, k):
        if plan.spans == 2:
            pair = tile(values, k, 0), tile(values, k, 1)
            return [jnp.where(is_first, pair[0], pair[1]), jnp.where(is_first, pair[1], pair[0])]
        return [tile(values, k, x) for x in (0, 1, -1)]

    def mirrored(value):
        return rolled(value, LANES // 2)

    here = around(seams, 0)
    behind, ahead = around(seams, -1), around(seams, 1)
    for i in range(1 + plan.ends):
        seams_ref[0, i] = jnp.where(even, mirrored(behind[i]), ahead[i])
        seams_ref[1, i] = jnp.where(even, here[i], mirrored(here[i]))
        seams_ref[2, i] = jnp.where(even, mirrored(ahead[i]), behind[i])
    weight_ref[...] = around(weights, 0)[0]

    for layer in two_layers(plan, m_ref, seam=seams_ref[1, 0]):
        for r in range(plan.rows):
            x_ref[:, at(r, 1, layer.start)] = layer.row(r)
    layers = two_layers(plan, x_ref, m_ref)
    inner_rows(plan, w_ref, (p0_ref, p1_ref), layers, layers, g_ref)


def first_half(
    plan, w_ref, m_ref, f_ref, g_ref, low_ref, high_ref, side_ref, c_low, c_high, seams_ref,
    x_ref, near_ref, side_out, c0_ref, c1_ref, p0_ref, p1_ref, y_ref, h_ref, n0_ref, n1_ref,
):
    own = two_layers(plan, f_ref, m_ref)
    low = two_layers(plan, low_ref, seam=seams_ref[0, 0])
    high = two_layers(plan, high_ref, seam=seams_ref[2, 0])
    near = low[0], high[1]
    n_refs = n0_ref, n1_ref
    middle_rows(
        plan, w_ref, (p0_ref, p1_ref), own, own, g_ref, near, near, sides_of(plan, side_ref, side_ref, seams_ref),
        corners_of(plan, (c_low, c_high), seams_ref), y_ref, h_ref, n_refs,
    )
    lane = lane_index(plan.pad)
    near_ref[:, plan.slab :] = jnp.zeros((plan.pad, LANES), jnp.float32)

    def put(a, r, value):
        x_ref[:, at(r, 1, a * plan.slab)] = value
        if a == 0:
            near_ref[:, at(r)] = value
        else:
            here = rolled(value, r * WINDOW)
            near_ref[:, plan.slab :] = jnp.where(lane == r * WINDOW, here, near_ref[:, plan.slab :])

    outer_rows(plan, w_ref, own, near, (low[1].chunk, high[0].chunk), n_refs, h_ref, put)
    write_edges(plan, x_ref, side_out, (c0_ref, c1_ref))


def inner(plan, w_ref, m_ref, f_ref, x_ref, c_low, c_high, g_ref, far_ref, p0_ref, p1_ref):
    far_ref[...] = x_ref[:, plan.slab :] + 0.0 * (c_low[0, 0:1, 0:1] + c_high[0, 0:1, 0:1])
    inner_rows(plan, w_ref, (p0_ref, p1_ref), two_layers(plan, x_ref, m_ref), two_layers(plan, f_ref, m_ref), g_ref)


def middle(
    plan, w_ref, m_ref, f_ref, x_ref, g_ref, low_ref, high_ref, side_ref, c_low, c_high,
    low_first, high_first, side_first, seams_ref, weight_ref, spread_table,
    h_ref, n0_ref, n1_ref, send_ref, p0_ref, p1_ref, y_ref, inlet_ref,
):
    pad = plan.pad
    own, force = two_layers(plan, x_ref, m_ref), two_layers(plan, f_ref, m_ref)
    low_force = Layer(plan, low_first, 0, None, seams_ref[0, 0], 0)
    high_force = Layer(plan, high_first, plan.slab, None, seams_ref[2, 0], 1)
    near = Layer(plan, low_ref, 0, low_force.rates), Layer(plan, high_ref, plan.slab, high_force.rates)
    n_refs = n0_ref, n1_ref
    middle_rows(
        plan, w_ref, (p0_ref, p1_ref), own, force, g_ref, near, (low_force, high_force),
        sides_of(plan, side_ref, side_first, seams_ref), corners_of(plan, (c_low, c_high), None), y_ref, h_ref, n_refs,
    )
    lane = lane_index(pad)
    inlet_ref[...] = jnp.zeros_like(inlet_ref)

    def put(a, r, value):
        cell = a * plan.rows + r
        inlet_ref[...] = jnp.where(lane == cell * WINDOW, rolled(value, cell * WINDOW), inlet_ref[...])

    def far_inlet(c):
        tile = low_ref[:, plan.slab :]
        count = CHUNK // LANES
        return jnp.concatenate([placed(tile, c * count + part) for part in range(count)], axis=1)

    outer_rows(plan, w_ref, own, near, (far_inlet, Layer(plan, high_ref).chunk), n_refs, h_ref, put)
    inlet = inlet_ref[...]
    inlet = jnp.where(parity() == 0, inlet, rolled(inlet, LANES // 2))
    back = pick(inlet, spread_table[...]) * weight_ref[...]
    back = back + rolled(back, -plan.width)
    me = lax.axis_index("sector")
    send_ref[...] = jnp.zeros_like(send_ref)
    for t in range(plan.insts):
        to = lax.rem(me + plan.shift[t], plan.sectors)
        send_ref[to, : plan.fields, : plan.width] = back[t * plan.fields : (t + 1) * plan.fields, : plan.width]


def outer(plan, w_ref, m_ref, low_first, high_first, n0_ref, n1_ref, h_ref, low_ref, high_ref, out_ref):
    mirror = parity()
    own = two_layers(plan, m_ref)
    near = Layer(plan, low_first), Layer(plan, high_first, plan.slab)

    def put(a, r, value):
        there = jnp.where(mirror == 0, a, plan.ct - 1 - a) * plan.rows + r
        out_ref[pl.ds(there, plan.tf, stride=plan.cells), :] = value[: plan.tf]

    far = Layer(plan, low_ref).chunk, Layer(plan, high_ref).chunk
    outer_rows(plan, w_ref, own, near, far, (n0_ref, n1_ref), h_ref, put)


def collect_panels(plan, got_ref, out_ref, panels_ref):
    me = lax.axis_index("sector")
    for t in range(plan.insts):
        source = lax.rem(me + (plan.sectors - plan.shift[t]), plan.sectors)
        panels_ref[t * RATES : (t + 1) * RATES, :] = got_ref[source]
    for f in range(plan.fields):
        tile = panels_ref[pl.ds(f, plan.insts, stride=RATES), : plan.width]
        out_ref[f] = jnp.transpose(tile)


def sibling(plan):
    return [s ^ 1 for s in range(plan.sectors)]


def outside(plan):
    return [(s - 1 if s % 2 == 0 else s + 1) % plan.sectors for s in range(plan.sectors)]


def swap(array, partner):
    return lax.ppermute(array, "sector", list(enumerate(partner)))


def beside(plan, array, partner):
    def pairs(step):
        out = []
        for s in range(plan.sectors):
            for x in range(plan.spans):
                to = 1 - x if plan.ends == 1 else x + step
                if 0 <= to < plan.spans:
                    out.append((s * plan.spans + x, partner[s] * plan.spans + to))
        return out

    if plan.ends == 1:
        return lax.ppermute(array, AXES, pairs(0))
    return jnp.concatenate([lax.ppermute(array[:1], AXES, pairs(-1)), lax.ppermute(array[1:], AXES, pairs(1))])


def on_device(
    sectors, spans,
    rhs, diag_coef, face_coef, time_coef, jac_up, jac_down, wall_mask, stator_adj, owner, first_panel_share,
):
    plan = Plan(rhs, stator_adj, sectors, spans)
    pad, cells, slab, insts, fields, ends = plan.pad, plan.cells, plan.slab, plan.insts, plan.fields, plan.ends
    bind = functools.partial
    whole, half = f32(pad, plan.ct * slab), f32(pad, slab)
    products = (vmem(6 * pad, slab),) * 2
    alone, next_chip, next_core = list(range(sectors)), outside(plan), sibling(plan)

    def edges(rows):
        return f32(ends, rows, DEPTH * plan.ct * LANES), f32(ends, rows, LANES), f32(ends, rows, LANES)

    stator = jnp.transpose(stator_adj, (1, 2, 3, 0)).reshape(fields, plan.width, insts)
    sent = call(bind(send_panels, plan), f32(sectors * spans, 2 * RATES, LANES), (vmem(insts * RATES, LANES),))(
        stator, owner.reshape(insts, cells), first_panel_share.reshape(insts, cells)
    )
    got = lax.all_to_all(sent, AXES, 0, 0, tiled=True)
    m, side, c0, c1 = call(bind(prepare, plan), (f32(pad + RATES, plan.ct * slab),) + edges(pad + RATES))(
        rhs.reshape(plan.tf * cells, LANES), diag_coef.reshape(cells, LANES), face_coef.reshape(3, cells, LANES),
        time_coef.reshape(cells, LANES), wall_mask.reshape(cells, LANES),
    )
    low_first, high_first = swap(m, next_chip), swap(m, next_core)
    side_first = beside(plan, side, alone)
    c_low, c_high = beside(plan, c0, next_chip), beside(plan, c1, next_core)
    matrices = call(
        bind(stack_matrices, plan), jax.ShapeDtypeStruct((7 * pad, 3 * pad), jnp.bfloat16)
    )(jac_up, jac_down, plan.spectral(), plan.field_rows(), plan.field_lanes(), plan.block_diagonal())
    tiles = len(plan.tiles)
    seams, weight, force, g = call(
        bind(begin, plan), (f32(3, 1 + ends, pad, LANES), f32(pad, LANES), whole, whole),
        (vmem(pad, tiles * LANES), vmem(tiles * pad, LANES), vmem(16, tiles * LANES)) + products,
        flops=2_000_000_000,
    )(
        matrices, m, got, plan.inst_rows(), plan.twice(plan.weight_lanes()), plan.panel_lanes(),
        plan.twice(plan.window_lanes()),
    )
    x, near, side, c0, c1 = call(
        bind(first_half, plan), (whole, f32(pad, slab + LANES)) + edges(pad),
        products + (vmem(pad, 2 * slab), vmem(pad, 2 * slab), vmem(pad, slab), vmem(pad, slab)), flops=4_000_000_000,
    )(matrices, m, force, g, low_first, high_first, side_first, c_low, c_high, seams)

    low, high = swap(near, next_chip), swap(x, next_core)
    side = beside(plan, side, alone)
    c_low, c_high = beside(plan, c0, next_chip), beside(plan, c1, next_core)
    g, far = call(bind(inner, plan), (whole, half), products, flops=2_000_000_000)(
        matrices, m, force, x, c_low, c_high
    )
    far_low = swap(far, next_chip)
    h, n0, n1, back = call(
        bind(middle, plan), (whole, half, half, f32(sectors, RATES, LANES)),
        products + (vmem(pad, 2 * slab), vmem(pad, LANES)), flops=4_000_000_000,
    )(
        matrices, m, force, x, g, low, high, side, c_low, c_high, low_first, high_first, side_first, seams, weight,
        plan.twice(plan.window_lanes().T),
    )
    returned = lax.all_to_all(back, "sector", 0, 0, tiled=True)
    sens = call(bind(collect_panels, plan), f32(fields, plan.width, insts), (vmem(insts * RATES, LANES),))(returned)
    out = call(bind(outer, plan), f32(plan.tf * cells, LANES))(
        matrices, m, low_first, high_first, n0, n1, h, far_low, high
    )
    sens = jnp.transpose(sens.reshape(fields, plan.panels, plan.rows, insts), (3, 0, 1, 2))
    return out.reshape(rhs.shape), sens


def solution(mesh):
    in_specs = (
        P(None, None, "sector", "span", None),
        P("sector", "span", None),
        P(None, "sector", "span", None),
        P("sector", "span", None),
        P(),
        P(),
        P("sector", "span", None),
        P(None, None, "sector", "span"),
        P(None, "sector", "span"),
        P(None, "sector", "span"),
    )
    out_specs = (P(None, None, "sector", "span", None), P(None, None, "sector", "span"))
    return jax.shard_map(
        functools.partial(on_device, mesh.shape["sector"], mesh.shape["span"]),
        mesh=mesh, in_specs=in_specs, out_specs=out_specs, check_vma=False,
    )
```

```python
import functools

import jax
import jax.numpy as jnp
import ml_dtypes
import numpy as np
from jax import lax
from jax.experimental import pallas as pl
from jax.experimental.pallas import tpu as pltpu
from jax.sharding import PartitionSpec as P

SWEEPS = 4
DEPTH = 2
LANES = 128
CHUNK = 256
WINDOW = 8
HIGHEST = lax.Precision.HIGHEST
DOWN_AZ, SPECTRAL, UP_SP, DOWN_SP, UP_AX, DOWN_AX, UP_AZ = range(7)
C_TIME, C_AZ, C_SP, C_UP, C_DOWN, C_MASK, C_OTHER = range(7)
RATES = 8
GROUP = 3
AXES = ("sector", "span")


class Plan:
    def __init__(self, rhs, stator_adj, sectors, spans):
        self.insts, self.fields, self.ct, self.rows, self.nax = rhs.shape
        self.panels = stator_adj.shape[2]
        self.sectors, self.spans = sectors, spans
        self.tf = self.insts * self.fields
        self.pad = -(-self.tf // 16) * 16
        self.cells = self.ct * self.rows
        self.slab = self.rows * LANES
        self.width = self.panels * self.rows
        self.shift = [
            ((t * sectors) // (self.insts - 1) - t // (self.insts - 1)) % sectors for t in range(self.insts)
        ]
        assert self.ct == 2 and self.nax == LANES and SWEEPS % DEPTH == 0 and spans > 1
        assert len(set(self.shift)) == self.insts and self.cells * WINDOW == LANES and self.rows >= SWEEPS
        assert self.slab % CHUNK == 0 and 3 * self.pad <= 256 and 2 * self.ct * self.width == LANES
        assert sectors % 2 == 0
        self.ends = 1 if spans == 2 else 2
        self.blocks = [-1, 0, 1]
        self.halves = [0, 1] if spans == 2 else [-1, 0, 1]
        self.tiles = [(k, x) for k in self.blocks for x in self.halves]
        self.slots = [
            [t for t in range(self.insts) if any((k + self.shift[t]) % sectors == o for k in self.blocks)]
            for o in range(sectors)
        ]
        assert max(map(len, self.slots)) * self.width <= LANES

    def spectral(self):
        t = np.arange(self.insts)
        off = t[:, None] - t[None, :]
        sines = np.where(off == 0, 1.0, np.sin(np.pi * off / self.insts))
        table = np.where(off == 0, 0.0, 0.5 * (1.0 - 2.0 * (off % 2)) / sines).astype(np.float32)
        full = np.zeros((self.pad, self.pad), np.float32)
        full[: self.tf, : self.tf] = np.kron(table.T, np.eye(self.fields, dtype=np.float32))
        hi = full.astype(ml_dtypes.bfloat16)
        lo = (full - hi.astype(np.float32)).astype(ml_dtypes.bfloat16)
        return np.concatenate([hi, lo, hi], axis=1)

    def field_rows(self):
        out = np.zeros((self.pad, self.fields), np.float32)
        out[np.arange(self.tf), np.arange(self.tf) % self.fields] = 1.0
        return out

    def field_lanes(self):
        return np.tile(self.field_rows().T, (1, 3))

    def block_diagonal(self):
        block = np.full(self.pad, -1)
        block[: self.tf] = np.arange(self.tf) // self.fields
        same = (block[:, None] == block[None, :]) & (block[:, None] >= 0)
        return np.tile(same.astype(np.float32), (1, 3))

    def inst_rows(self):
        out = np.zeros((self.pad, 16), np.float32)
        out[np.arange(self.tf), np.arange(self.tf) // self.fields] = 1.0
        return out

    def cell_lanes(self):
        out = np.zeros((self.ct, self.rows, self.ct, self.panels, self.rows), np.float32)
        for a in range(self.ct):
            for r in range(self.rows):
                out[a, r, a, :, r] = 1.0
        out = out.reshape(self.cells, -1)
        return np.pad(out, ((0, 0), (0, LANES - out.shape[1])))

    def window_lanes(self):
        out = np.zeros((LANES, LANES), np.float32)
        out[:, ::WINDOW] = self.cell_lanes().T
        return out

    def twice(self, table):
        return np.concatenate([table, table]).astype(ml_dtypes.bfloat16)

    def weight_lanes(self):
        out = np.zeros((LANES, LANES), np.float32)
        half = self.ct * self.width
        out[: self.cells, :half] = self.cell_lanes()[:, :half]
        out[self.cells : 2 * self.cells, half:] = self.cell_lanes()[:, :half]
        return out

    def panel_lanes(self):
        lane = np.arange(LANES)
        return np.where(lane < self.ct * self.width, (lane // self.rows) % self.panels, -9).astype(np.float32)[None]


def call(kernel, out, scratch=(), flops=2_000_000, nbytes=1_000_000, **specs):
    return pl.pallas_call(
        kernel,
        out_shape=out,
        scratch_shapes=list(scratch),
        compiler_params=pltpu.CompilerParams(vmem_limit_bytes=20 * 1024 * 1024),
        cost_estimate=pl.CostEstimate(flops=flops, bytes_accessed=nbytes, transcendentals=0),
        **specs,
    )


def places(count, far=()):
    return [pl.BlockSpec(memory_space=pltpu.HBM if i in far else pltpu.VMEM) for i in range(count)]


def copies(pairs, sems):
    out = [pltpu.make_async_copy(source, target, sems.at[i]) for i, (source, target) in enumerate(pairs)]
    for one in out:
        one.start()
    return out


def f32(*shape):
    return jax.ShapeDtypeStruct(shape, jnp.float32)


def vmem(*shape):
    return pltpu.VMEM(shape, jnp.float32)


def halves_of(x):
    hi = x.astype(jnp.bfloat16)
    return hi, (x - hi.astype(jnp.float32)).astype(jnp.bfloat16)


def dot3(w, x):
    hi, lo = halves_of(x)
    return jnp.dot(w, jnp.concatenate([hi, hi, lo], axis=0), preferred_element_type=jnp.float32)


def pick(x, table2):
    return jnp.dot(jnp.concatenate(halves_of(x), axis=1), table2, preferred_element_type=jnp.float32)


def dot_full(a, b):
    return jnp.dot(a, b, precision=HIGHEST, preferred_element_type=jnp.float32)


def lane_index(rows):
    return lax.broadcasted_iota(jnp.int32, (rows, LANES), 1)


def rolled(x, by):
    by %= LANES
    return pltpu.roll(x, by, axis=1) if by else x


def at(r, count=1, start=0):
    return slice(start + r * LANES, start + (r + count) * LANES)


def parity():
    return lax.rem(lax.axis_index("sector"), 2)


def has_sides(plan):
    span = lax.axis_index("span")
    return jnp.where(span < plan.spans - 1, 1.0, 0.0), jnp.where(span > 0, 1.0, 0.0)


class Layer:
    def __init__(self, plan, ref, start=0, rates=None, seam=None, layer=0, scale=C_MASK):
        self.plan, self.ref, self.start, self.seam, self.layer, self.scale = plan, ref, start, seam, layer, scale
        self.rates = rates or (ref, start)

    def rate(self, which, r, count=1):
        ref, start = self.rates
        row = self.plan.pad + which
        return ref[row : row + 1, at(r, count, start)]

    def row(self, r):
        value = self.ref[: self.plan.pad, at(r, 1, self.start)]
        if self.seam is None:
            return value
        return value + placed(self.seam, self.layer * self.plan.rows + r) * self.rate(self.scale, r)

    def chunk(self, c):
        count = CHUNK // LANES
        if self.seam is None:
            return self.ref[: self.plan.pad, at(c * count, count, self.start)]
        return jnp.concatenate([self.row(c * count + part) for part in range(count)], axis=1)


def placed(tile, cell):
    return jnp.where(lane_index(tile.shape[0]) == 0, rolled(tile, -cell * WINDOW), 0.0)


class Products:
    def __init__(self, plan, w_ref, p_ref, first):
        self.plan, self.w, self.p, self.first = plan, w_ref, p_ref, first

    def fill(self, layer):
        for c in range(self.plan.slab // CHUNK):
            self.p[:, c * CHUNK : (c + 1) * CHUNK] = dot3(matrix(self.plan, self.w, self.first, 6), layer.chunk(c))
        self.layer = layer
        return self

    def get(self, block, r):
        row = (block - self.first) * self.plan.pad
        return self.p[row : row + self.plan.pad, at(r)]

    def own_terms(self, r):
        rate = self.layer.rate
        total = rate(C_TIME, r) * self.get(SPECTRAL, r)
        beside = []
        if r + 1 < self.plan.rows:
            beside.append(self.get(UP_SP, r + 1))
        if r > 0:
            beside.append(self.get(DOWN_SP, r - 1))
        total = total + rate(C_SP, r) * sum(beside[1:], beside[0])
        total = total + rate(C_UP, r) * rolled(self.get(UP_AX, r), -1)
        return total + rate(C_DOWN, r) * rolled(self.get(DOWN_AX, r), 1)


def matrix(plan, w_ref, block, count=1):
    return w_ref[block * plan.pad : (block + count) * plan.pad, :]


def two_layers(plan, ref, rates=None, seam=None):
    return [
        Layer(plan, ref, a * plan.slab, (rates, a * plan.slab) if rates is not None else None, seam, a)
        for a in range(plan.ct)
    ]


def inner_rows(plan, w_ref, p_refs, layers, force, g_ref):
    first = Products(plan, w_ref, p_refs[0], DOWN_AZ).fill(layers[0])
    second = Products(plan, w_ref, p_refs[1], SPECTRAL).fill(layers[1])
    for r in range(plan.rows):
        other = second.get(UP_AZ, r), first.get(DOWN_AZ, r)
        for a, products in enumerate((first, second)):
            total = products.own_terms(r) + layers[a].rate(C_AZ, r) * other[a]
            g_ref[:, at(r, 1, a * plan.slab)] = force[a].row(r) - total


def azimuthal(plan, w_ref, block, chunk_of, take):
    for c in range(plan.slab // CHUNK):
        terms = dot3(matrix(plan, w_ref, block), chunk_of(c))
        for part in range(CHUNK // LANES):
            take(c * (CHUNK // LANES) + part, terms[:, at(part)])


def middle_rows(plan, w_ref, p_refs, own, own_force, g_ref, near, near_force, side, corner, y_ref, h_ref, n_refs):
    pad, rows, ct = plan.pad, plan.rows, plan.ct
    outward, inward, last = (UP_SP, DOWN_SP), (DOWN_SP, UP_SP), (rows - 1, 0)
    edge_terms, edge_new, corner_terms = [], [], []
    for n in range(2):
        first, second, edge_force, edge_rate = side(n)
        corners = corner(n)
        every = dot3(w_ref[...], first)
        edge_terms.append(every[outward[n] * pad : (outward[n] + 1) * pad])
        corner_terms.append([dot3(matrix(plan, w_ref, outward[n]), c) for c in corners])
        beyond = dot3(matrix(plan, w_ref, outward[n]), second)
        within = dot3(matrix(plan, w_ref, inward[n]), jnp.concatenate([x.row(last[n]) for x in own], axis=1))
        from_low = dot3(matrix(plan, w_ref, DOWN_AZ), corners[0])
        from_high = dot3(matrix(plan, w_ref, UP_AZ), corners[1])
        new = []
        for a in range(ct):

            def part(block, b=a):
                return every[block * pad : (block + 1) * pad, at(b)]

            around = part(UP_AZ, 1) + from_low if a == 0 else from_high + part(DOWN_AZ, 0)
            total = edge_rate(C_TIME, a) * part(SPECTRAL) + edge_rate(C_AZ, a) * around
            total = total + edge_rate(C_SP, a) * (beyond[:, at(a)] + within[:, at(a)])
            total = total + edge_rate(C_UP, a) * rolled(part(UP_AX), -1)
            total = total + edge_rate(C_DOWN, a) * rolled(part(DOWN_AX), 1)
            new.append(edge_force[:, at(a)] - total)
        edge_new.append(dot3(matrix(plan, w_ref, outward[n]), jnp.concatenate(new, axis=1)))

    products = (
        Products(plan, w_ref, p_refs[0], DOWN_AZ).fill(near[0]), Products(plan, w_ref, p_refs[1], SPECTRAL).fill(near[1]),
    )
    for a, (to_own, to_near) in enumerate(((DOWN_AZ, UP_AZ), (UP_AZ, DOWN_AZ))):

        def take(r, terms):
            total = products[a].own_terms(r) + near[a].rate(C_AZ, r) * terms
            mine = own[a].rate(C_AZ, r) * products[a].get(to_own, r)
            for n in range(2):
                if r == last[n]:
                    total = total + near[a].rate(C_SP, r) * corner_terms[n][a]
                    mine = mine + own[a].rate(C_SP, r) * edge_terms[n][:, at(a)]
            n_refs[a][:, at(r)] = near_force[a].row(r) - total
            lanes = at(r, 1, a * plan.slab)
            y_ref[:, lanes] = g_ref[:, lanes] - mine

        azimuthal(plan, w_ref, to_near, own[a].chunk, take)

    after = [Layer(plan, y_ref, a * plan.slab, own[a].rates) for a in range(ct)]
    inner_rows(plan, w_ref, p_refs, after, own_force, h_ref)
    for a in range(ct):
        for n in range(2):
            lanes = at(last[n], 1, a * plan.slab)
            h_ref[:, lanes] -= own[a].rate(C_SP, last[n]) * edge_new[n][:, at(a)]


def outer_rows(plan, w_ref, own, near, far_chunks, n_refs, h_ref, put):
    count = CHUNK // LANES
    for a, block in enumerate((DOWN_AZ, UP_AZ)):

        def near_chunk(c):
            terms = dot3(matrix(plan, w_ref, block), far_chunks[a](c))
            return n_refs[a][:, at(c * count, count)] - near[a].rate(C_AZ, c * count, count) * terms

        def take(r, terms):
            put(a, r, h_ref[:, at(r, 1, a * plan.slab)] - own[a].rate(C_AZ, r) * terms)

        azimuthal(plan, w_ref, block, near_chunk, take)


def sides_of(plan, side_ref, force_ref, seams_ref):
    pad, ct = plan.pad, plan.ct
    keeps = has_sides(plan)

    def read(n, ref, e, seam):
        i = n if plan.ends == 2 else 0
        value = ref[i, :pad, at(e * ct, ct)]
        if seam:
            r = e if n == 0 else plan.rows - 1 - e
            tile = seams_ref[1, 1 + i]
            scale = ref[i, pad + C_MASK : pad + C_MASK + 1, at(e * ct, ct)]
            value = value + jnp.concatenate([placed(tile, a * plan.rows + r) for a in range(ct)], axis=1) * scale
        return value * keeps[n]

    def side(n):
        i = n if plan.ends == 2 else 0
        same = side_ref is force_ref

        def rate(which, a):
            return force_ref[i, pad + which : pad + which + 1, at(a)] * keeps[n]

        force = read(n, force_ref, 0, True)
        first = force if same else read(n, side_ref, 0, False)
        return first, read(n, side_ref, 1, same), force, rate

    return side


def corners_of(plan, c_refs, seams_ref):
    keeps = has_sides(plan)

    def corner(n):
        i = n if plan.ends == 2 else 0
        out = []
        for a, c_ref in enumerate(c_refs):
            value = c_ref[i, : plan.pad]
            if seams_ref is not None:
                r = 0 if n == 0 else plan.rows - 1
                scale = c_ref[i, plan.pad + C_MASK : plan.pad + C_MASK + 1]
                value = value + placed(seams_ref[2 * a, 1 + i], a * plan.rows + r) * scale
            out.append(value * keeps[n])
        return out

    return corner


def prepare(
    plan, rhs_hbm, diag_hbm, face_hbm, time_hbm, mask_hbm, m_ref, near_ref, side_ref, c0_ref, c1_ref,
    rhs_ref, diag_ref, face_ref, time_ref, mask_ref, sems,
):
    pad = plan.pad
    for one in copies((
        (rhs_hbm, rhs_ref), (diag_hbm, diag_ref), (face_hbm, face_ref), (time_hbm, time_ref), (mask_hbm, mask_ref),
    ), sems):
        one.wait()
    lane = lane_index(1)
    tail = jnp.zeros((pad - plan.tf, LANES), jnp.float32)
    mirror = parity()

    def places_of(a, r):
        return jnp.where(mirror == 0, a, plan.ct - 1 - a) * plan.rows + r

    def scale_of(a, r):
        one = pl.ds(places_of(a, r), 1)
        return mask_ref[one, :].astype(jnp.float32) / diag_ref[one, :]

    for r in range(plan.rows):
        scales = [scale_of(a, r) for a in range(plan.ct)]
        for a, scale in enumerate(scales):
            there = places_of(a, r)
            one = pl.ds(there, 1)
            axial = scale * face_ref[2, one, :]
            rates = jnp.concatenate([
                scale * time_ref[one, :], scale * face_ref[0, one, :], scale * face_ref[1, one, :],
                jnp.where(lane < LANES - 1, axial, 0.0), jnp.where(lane > 0, axial, 0.0), scale, scales[1 - a],
                jnp.zeros((RATES - 7, LANES), jnp.float32),
            ], axis=0)
            field = jnp.concatenate([rhs_ref[pl.ds(there, plan.tf, stride=plan.cells), :], tail], axis=0) * scale
            lanes = at(a * plan.rows + r)
            m_ref[:pad, lanes] = field
            m_ref[pad:, lanes] = rates
            if a == 0:
                near_ref[:pad, lanes] = field
                near_ref[pad:, lanes] = rates
    write_edges(plan, m_ref, side_ref, (c0_ref, c1_ref))


def write_edges(plan, x_ref, side_ref, c_refs):
    first = lax.axis_index("span") == 0
    for a in range(plan.ct):
        for e in range(DEPTH):
            low, high = x_ref[:, at(a * plan.rows + e)], x_ref[:, at((a + 1) * plan.rows - 1 - e)]
            ends = [jnp.where(first, high, low)] if plan.ends == 1 else [low, high]
            for n, end in enumerate(ends):
                side_ref[n, :, at(e * plan.ct + a)] = end
                if e == 0:
                    c_refs[a][n] = end


def after(value, *refs):
    return value + 0.0 * sum(ref[0, 0:1, 0:1] for ref in refs)


def stack_matrices(plan, m_ref, side_ref, c_high, up_ref, down_ref, spectral_ref, rows_ref, lanes_ref, diagonal_ref, *refs):
    pad = plan.pad
    out_ref, far_ref = refs[len(refs) // 2 - 1 : len(refs) // 2 + 1]
    far_ref[...] = after(m_ref[:pad, plan.slab :], side_ref, c_high)
    for source, target in zip(refs[: len(refs) // 2 - 1], refs[len(refs) // 2 + 1 :]):
        target[...] = source[...]
    lane = lax.broadcasted_iota(jnp.int32, (pad, 3 * pad), 1)
    second = (lane >= pad) & (lane < 2 * pad)
    out_ref[SPECTRAL * pad : (SPECTRAL + 1) * pad, :] = spectral_ref[...]
    even = parity() == 0
    for block, small in (
        (DOWN_AZ, jnp.where(even, down_ref[0], up_ref[0])), (UP_AZ, jnp.where(even, up_ref[0], down_ref[0])),
        (UP_SP, up_ref[1]), (DOWN_SP, down_ref[1]), (UP_AX, up_ref[2]), (DOWN_AX, down_ref[2]),
    ):
        full = dot_full(dot_full(rows_ref[...], small), lanes_ref[...]) * diagonal_ref[...]
        hi = full.astype(jnp.bfloat16).astype(jnp.float32)
        out_ref[block * pad : (block + 1) * pad, :] = jnp.where(second, full - hi, hi).astype(jnp.bfloat16)


def send_panels(plan, stator_ref, owner_ref, share_ref, out_ref, panels_ref):
    me = lax.axis_index("sector")
    for f in range(plan.fields):
        panels_ref[pl.ds(f, plan.insts, stride=RATES), : plan.width] = jnp.transpose(stator_ref[f])
    out_ref[...] = jnp.zeros_like(out_ref)
    both = jnp.concatenate([lax.rem(owner_ref[...], plan.panels).astype(jnp.float32), share_ref[...]], axis=1)
    for t in range(plan.insts):
        group, row = divmod(t, GROUP)
        lanes = slice(group * 2 * plan.cells, (group + 1) * 2 * plan.cells)
        row += RATES
        out_ref[:, row : row + 1, lanes] = jnp.broadcast_to(both[t : t + 1][None], (out_ref.shape[0], 1, 2 * plan.cells))
    for o, slots in enumerate(plan.slots):
        to = lax.rem(me + (plan.sectors - o), plan.sectors) * plan.spans
        for slot, t in enumerate(slots):
            lanes = slice(slot * plan.width, (slot + 1) * plan.width)
            panels = panels_ref[t * RATES : t * RATES + plan.fields, : plan.width]
            for x in range(plan.spans):
                out_ref[to + x, : plan.fields, lanes] = panels


def begin(
    plan, w_ref, m_ref, got_ref, inst_rows, weight_table, panel_lanes, sum_table,
    seams_ref, weight_ref, x_ref, g_ref, panels_ref, terms_ref, rows_ref, p0_ref, p1_ref,
):
    pad, insts, fields = plan.pad, plan.insts, plan.fields
    me, span = lax.axis_index("sector"), lax.axis_index("span")
    tiles = plan.tiles
    panels_ref[...] = jnp.zeros_like(panels_ref)
    rows_ref[...] = jnp.zeros_like(rows_ref)
    wide = 2 * plan.cells
    for n, (k, x) in enumerate(tiles):
        at_span = x if plan.spans == 2 else jnp.clip(span + x, 0, plan.spans - 1)
        for t in range(insts):
            o = (k + plan.shift[t]) % plan.sectors
            source = lax.rem(me + o, plan.sectors) * plan.spans + at_span
            tile = rolled(got_ref[source, :RATES], -plan.slots[o].index(t) * plan.width)
            panels_ref[t * fields : (t + 1) * fields, n * LANES : n * LANES + plan.width] = tile[:fields, : plan.width]
        source = lax.rem(me + k + plan.sectors, plan.sectors) * plan.spans + at_span
        table = got_ref[source, RATES:]
        for group in range(-(-insts // GROUP)):
            shifted = rolled(table, -group * wide)
            rows_ref[group * GROUP : (group + 1) * GROUP, n * LANES : n * LANES + wide] = shifted[:GROUP, :wide]
    spread = dot_full(inst_rows[...], rows_ref[...])
    spread = pick(jnp.concatenate([spread[:, at(n)] for n in range(len(tiles))], axis=0), weight_table[...])
    first, share, panel = spread, rolled(spread, plan.ct * plan.width), panel_lanes[...]
    lower = (jnp.abs(first - panel) < 0.5).astype(jnp.float32)
    upper = (jnp.abs(first + 1.0 - panel) < 0.5).astype(jnp.float32)
    weights = share * lower + (1.0 - share) * upper
    for n in range(len(tiles)):
        panels = panels_ref[:, at(n)]
        terms_ref[n * pad : (n + 1) * pad, :] = panels + rolled(panels, plan.width)
    seams = pick(terms_ref[...] * weights, sum_table[...])

    even = parity() == 0
    is_first = span == 0

    def tile(values, k, x):
        n = tiles.index((k, x))
        return values[n * pad : (n + 1) * pad]

    def around(values, k):
        if plan.spans == 2:
            pair = tile(values, k, 0), tile(values, k, 1)
            return [jnp.where(is_first, pair[0], pair[1]), jnp.where(is_first, pair[1], pair[0])]
        return [tile(values, k, x) for x in (0, 1, -1)]

    def mirrored(value):
        return rolled(value, LANES // 2)

    here = around(seams, 0)
    behind, ahead = around(seams, -1), around(seams, 1)
    for i in range(1 + plan.ends):
        seams_ref[0, i] = jnp.where(even, mirrored(behind[i]), ahead[i])
        seams_ref[1, i] = jnp.where(even, here[i], mirrored(here[i]))
        seams_ref[2, i] = jnp.where(even, mirrored(ahead[i]), behind[i])
    weight_ref[...] = around(weights, 0)[0]

    for layer in two_layers(plan, m_ref, seam=seams_ref[1, 0]):
        for r in range(plan.rows):
            x_ref[:, at(r, 1, layer.start)] = layer.row(r)
    layers = two_layers(plan, x_ref, m_ref)
    inner_rows(plan, w_ref, (p0_ref, p1_ref), layers, layers, g_ref)


def middle_first(
    plan, w_ref, m_ref, f_ref, g_ref, low_ref, high_ref, side_ref, c_low, c_high, seams_ref,
    h_ref, n0_ref, n1_ref, p0_ref, p1_ref, y_ref,
):
    own = two_layers(plan, f_ref, m_ref)
    near = (
        Layer(plan, low_ref, 0, None, seams_ref[0, 0], 0), Layer(plan, high_ref, plan.slab, None, seams_ref[2, 0], 1),
    )
    middle_rows(
        plan, w_ref, (p0_ref, p1_ref), own, own, g_ref, near, near, sides_of(plan, side_ref, side_ref, seams_ref),
        corners_of(plan, (c_low, c_high), seams_ref), y_ref, h_ref, (n0_ref, n1_ref),
    )


def outer_first(
    plan, w_ref, m_ref, low_first, high_first, n0_ref, n1_ref, h_ref, far_ref, seams_ref,
    x_ref, near_ref, side_out, c0_ref, c1_ref,
):
    own = two_layers(plan, m_ref)
    near = Layer(plan, low_first), Layer(plan, high_first, plan.slab)
    far_low = Layer(plan, far_ref, 0, (low_first, 0), seams_ref[0, 0], 1, C_OTHER)
    far_high = Layer(plan, high_first, 0, None, seams_ref[2, 0], 0)
    lane = lane_index(plan.pad)
    near_ref[:, plan.slab :] = jnp.zeros((plan.pad, LANES), jnp.float32)

    def put(a, r, value):
        x_ref[:, at(r, 1, a * plan.slab)] = value
        if a == 0:
            near_ref[:, at(r)] = value
        else:
            here = rolled(value, r * WINDOW)
            near_ref[:, plan.slab :] = jnp.where(lane == r * WINDOW, here, near_ref[:, plan.slab :])

    outer_rows(plan, w_ref, own, near, (far_low.chunk, far_high.chunk), (n0_ref, n1_ref), h_ref, put)
    write_edges(plan, x_ref, side_out, (c0_ref, c1_ref))


def inner(plan, w_ref, m_ref, f_ref, x_ref, side_ref, c_high, g_ref, far_ref, p0_ref, p1_ref):
    far_ref[...] = after(x_ref[:, plan.slab :], side_ref, c_high)
    inner_rows(plan, w_ref, (p0_ref, p1_ref), two_layers(plan, x_ref, m_ref), two_layers(plan, f_ref, m_ref), g_ref)


def middle(
    plan, w_ref, m_ref, f_ref, x_ref, g_ref, low_ref, high_ref, side_ref, c_low, c_high,
    low_first, high_first, side_first, seams_ref, weight_ref, spread_table,
    h_hbm, n0_hbm, n1_hbm, send_hbm, h_ref, n0_ref, n1_ref, send_ref, p0_ref, p1_ref, y_ref, inlet_ref, sems,
):
    pad = plan.pad
    own, force = two_layers(plan, x_ref, m_ref), two_layers(plan, f_ref, m_ref)
    low_force = Layer(plan, low_first, 0, None, seams_ref[0, 0], 0)
    high_force = Layer(plan, high_first, plan.slab, None, seams_ref[2, 0], 1)
    near = Layer(plan, low_ref, 0, low_force.rates), Layer(plan, high_ref, plan.slab, high_force.rates)
    n_refs = n0_ref, n1_ref
    middle_rows(
        plan, w_ref, (p0_ref, p1_ref), own, force, g_ref, near, (low_force, high_force),
        sides_of(plan, side_ref, side_first, seams_ref), corners_of(plan, (c_low, c_high), None), y_ref, h_ref, n_refs,
    )
    started = copies(((h_ref, h_hbm), (n0_ref, n0_hbm), (n1_ref, n1_hbm)), sems)
    lane = lane_index(pad)
    inlet_ref[...] = jnp.zeros_like(inlet_ref)

    def put(a, r, value):
        cell = a * plan.rows + r
        inlet_ref[...] = jnp.where(lane == cell * WINDOW, rolled(value, cell * WINDOW), inlet_ref[...])

    def far_inlet(c):
        tile = low_ref[:, plan.slab :]
        count = CHUNK // LANES
        return jnp.concatenate([placed(tile, c * count + part) for part in range(count)], axis=1)

    outer_rows(plan, w_ref, own, near, (far_inlet, Layer(plan, high_ref).chunk), n_refs, h_ref, put)
    inlet = inlet_ref[...]
    inlet = jnp.where(parity() == 0, inlet, rolled(inlet, LANES // 2))
    back = pick(inlet, spread_table[...]) * weight_ref[...]
    back = back + rolled(back, -plan.width)
    me = lax.axis_index("sector")
    send_ref[...] = jnp.zeros_like(send_ref)
    for t in range(plan.insts):
        to = lax.rem(me + plan.shift[t], plan.sectors)
        send_ref[to, : plan.fields, : plan.width] = back[t * plan.fields : (t + 1) * plan.fields, : plan.width]
    started.append(pltpu.make_async_copy(send_ref, send_hbm, sems.at[3]))
    started[-1].start()
    for one in started:
        one.wait()


def outer(
    plan, w_ref, m_ref, low_first, high_first, n0_hbm, n1_hbm, h_hbm, low_ref, high_ref, out_ref,
    n0_ref, n1_ref, h_ref, sems,
):
    for one in copies(((n0_hbm, n0_ref), (n1_hbm, n1_ref), (h_hbm, h_ref)), sems):
        one.wait()
    mirror = parity()
    own = two_layers(plan, m_ref)
    near = Layer(plan, low_first), Layer(plan, high_first, plan.slab)

    def put(a, r, value):
        there = jnp.where(mirror == 0, a, plan.ct - 1 - a) * plan.rows + r
        out_ref[pl.ds(there, plan.tf, stride=plan.cells), :] = value[: plan.tf]

    far = Layer(plan, low_ref).chunk, Layer(plan, high_ref).chunk
    outer_rows(plan, w_ref, own, near, far, (n0_ref, n1_ref), h_ref, put)


def collect_panels(plan, got_ref, out_ref, panels_ref):
    me = lax.axis_index("sector")
    for t in range(plan.insts):
        source = lax.rem(me + (plan.sectors - plan.shift[t]), plan.sectors)
        panels_ref[t * RATES : (t + 1) * RATES, :] = got_ref[source]
    for f in range(plan.fields):
        tile = panels_ref[pl.ds(f, plan.insts, stride=RATES), : plan.width]
        out_ref[f] = jnp.transpose(tile)


def sibling(plan):
    return [s ^ 1 for s in range(plan.sectors)]


def outside(plan):
    return [(s - 1 if s % 2 == 0 else s + 1) % plan.sectors for s in range(plan.sectors)]


def swap(array, partner):
    return lax.ppermute(array, "sector", list(enumerate(partner)))


def beside(plan, array, partner):
    def pairs(step):
        out = []
        for s in range(plan.sectors):
            for x in range(plan.spans):
                to = 1 - x if plan.ends == 1 else x + step
                if 0 <= to < plan.spans:
                    out.append((s * plan.spans + x, partner[s] * plan.spans + to))
        return out

    if plan.ends == 1:
        return lax.ppermute(array, AXES, pairs(0))
    return jnp.concatenate([lax.ppermute(array[:1], AXES, pairs(-1)), lax.ppermute(array[1:], AXES, pairs(1))])


def on_device(
    sectors, spans,
    rhs, diag_coef, face_coef, time_coef, jac_up, jac_down, wall_mask, stator_adj, owner, first_panel_share,
):
    plan = Plan(rhs, stator_adj, sectors, spans)
    pad, cells, slab, insts, fields, ends = plan.pad, plan.cells, plan.slab, plan.insts, plan.fields, plan.ends
    bind = functools.partial
    whole, half = f32(pad, plan.ct * slab), f32(pad, slab)
    products = (vmem(6 * pad, slab),) * 2
    alone, next_chip, next_core = list(range(sectors)), outside(plan), sibling(plan)

    def edges(rows):
        return f32(ends, rows, DEPTH * plan.ct * LANES), f32(ends, rows, LANES), f32(ends, rows, LANES)

    stator = jnp.transpose(stator_adj, (1, 2, 3, 0)).reshape(fields, plan.width, insts)
    sent = call(bind(send_panels, plan), f32(sectors * spans, 2 * RATES, LANES), (vmem(insts * RATES, LANES),))(
        stator, owner.reshape(insts, cells), first_panel_share.reshape(insts, cells)
    )
    got = lax.all_to_all(sent, AXES, 0, 0, tiled=True)
    m, near, side, c0, c1 = call(
        bind(prepare, plan), (f32(pad + RATES, plan.ct * slab), f32(pad + RATES, slab)) + edges(pad + RATES),
        (
            vmem(plan.tf * cells, LANES), vmem(cells, LANES), vmem(3, cells, LANES), vmem(cells, LANES),
            pltpu.VMEM((cells, LANES), jnp.int32), pltpu.SemaphoreType.DMA((5,)),
        ),
        in_specs=places(5, range(5)),
    )(
        rhs.reshape(plan.tf * cells, LANES), diag_coef.reshape(cells, LANES), face_coef.reshape(3, cells, LANES),
        time_coef.reshape(cells, LANES), wall_mask.reshape(cells, LANES),
    )
    low_first, high_first = swap(near, next_chip), swap(m, next_core)
    side_first = beside(plan, side, alone)
    c_low, c_high = beside(plan, c0, next_chip), beside(plan, c1, next_core)
    tables = (
        plan.inst_rows(), plan.twice(plan.weight_lanes()), plan.panel_lanes(), plan.twice(plan.window_lanes()),
        plan.twice(plan.window_lanes().T),
    )
    matrices, far, *tables = call(
        bind(stack_matrices, plan),
        [jax.ShapeDtypeStruct((7 * pad, 3 * pad), jnp.bfloat16), half]
        + [jax.ShapeDtypeStruct(table.shape, table.dtype) for table in tables],
    )(m, side_first, c_high, jac_up, jac_down, plan.spectral(), plan.field_rows(), plan.field_lanes(), plan.block_diagonal(), *tables)
    far_low = swap(far, next_chip)
    tiles = len(plan.tiles)
    seams, weight, force, g = call(
        bind(begin, plan), (f32(3, 1 + ends, pad, LANES), f32(pad, LANES), whole, whole),
        (vmem(pad, tiles * LANES), vmem(tiles * pad, LANES), vmem(16, tiles * LANES)) + products,
        flops=2_000_000_000,
    )(matrices, m, got, *tables[:4])
    h, n0, n1 = call(
        bind(middle_first, plan), (whole, half, half), products + (vmem(pad, 2 * slab),), flops=4_000_000_000
    )(matrices, m, force, g, low_first, high_first, side_first, c_low, c_high, seams)
    x, near, side, c0, c1 = call(bind(outer_first, plan), (whole, f32(pad, slab + LANES)) + edges(pad))(
        matrices, m, low_first, high_first, n0, n1, h, far_low, seams
    )

    low, high = swap(near, next_chip), swap(x, next_core)
    side = beside(plan, side, alone)
    c_low, c_high = beside(plan, c0, next_chip), beside(plan, c1, next_core)
    g, far = call(bind(inner, plan), (whole, half), products, flops=2_000_000_000)(
        matrices, m, force, x, side, c_high
    )
    far_low = swap(far, next_chip)
    copied = (vmem(pad, 2 * slab), vmem(pad, slab), vmem(pad, slab))
    h, n0, n1, back = call(
        bind(middle, plan), (whole, half, half, f32(sectors, RATES, LANES)),
        copied + (vmem(sectors, RATES, LANES),) + products
        + (vmem(pad, 2 * slab), vmem(pad, LANES), pltpu.SemaphoreType.DMA((4,))),
        flops=4_000_000_000, out_specs=places(4, range(4)),
    )(
        matrices, m, force, x, g, low, high, side, c_low, c_high, low_first, high_first, side_first, seams, weight,
        tables[4],
    )
    returned = lax.all_to_all(back, "sector", 0, 0, tiled=True)
    sens = call(bind(collect_panels, plan), f32(fields, plan.width, insts), (vmem(insts * RATES, LANES),))(returned)
    out = call(
        bind(outer, plan), f32(plan.tf * cells, LANES),
        (vmem(pad, slab), vmem(pad, slab), vmem(pad, 2 * slab), pltpu.SemaphoreType.DMA((3,))),
        in_specs=places(9, (4, 5, 6)),
    )(matrices, m, low_first, high_first, n0, n1, h, far_low, high)
    sens = jnp.transpose(sens.reshape(fields, plan.panels, plan.rows, insts), (3, 0, 1, 2))
    return out.reshape(rhs.shape), sens


def solution(mesh):
    in_specs = (
        P(None, None, "sector", "span", None),
        P("sector", "span", None),
        P(None, "sector", "span", None),
        P("sector", "span", None),
        P(),
        P(),
        P("sector", "span", None),
        P(None, None, "sector", "span"),
        P(None, "sector", "span"),
        P(None, "sector", "span"),
    )
    out_specs = (P(None, None, "sector", "span", None), P(None, None, "sector", "span"))
    return jax.shard_map(
        functools.partial(on_device, mesh.shape["sector"], mesh.shape["span"]),
        mesh=mesh, in_specs=in_specs, out_specs=out_specs, check_vma=False,
    )
```

```python
import functools

import jax
import jax.numpy as jnp
import ml_dtypes
import numpy as np
from jax import lax
from jax.experimental import pallas as pl
from jax.experimental.pallas import tpu as pltpu
from jax.sharding import PartitionSpec as P

SWEEPS = 4
DEPTH = 2
LANES = 128
CHUNK = 256
WINDOW = 8
HIGHEST = lax.Precision.HIGHEST
DOWN_AZ, SPECTRAL, UP_SP, DOWN_SP, UP_AX, DOWN_AX, UP_AZ = range(7)
C_TIME, C_AZ, C_SP, C_UP, C_DOWN, C_MASK = range(6)
RATES = 8
GROUP = 3
AXES = ("sector", "span")


class Plan:
    def __init__(self, rhs, stator_adj, sectors, spans):
        self.insts, self.fields, self.ct, self.rows, self.nax = rhs.shape
        self.panels = stator_adj.shape[2]
        self.sectors, self.spans = sectors, spans
        self.tf = self.insts * self.fields
        self.pad = -(-self.tf // 16) * 16
        self.cells = self.ct * self.rows
        self.slab = self.rows * LANES
        self.width = self.panels * self.rows
        self.shift = [
            ((t * sectors) // (self.insts - 1) - t // (self.insts - 1)) % sectors for t in range(self.insts)
        ]
        assert self.ct == 2 and self.nax == LANES and SWEEPS % DEPTH == 0 and spans > 1
        assert len(set(self.shift)) == self.insts and self.cells * WINDOW == LANES and self.rows >= SWEEPS
        assert self.slab % CHUNK == 0 and 3 * self.pad <= 256 and 2 * self.ct * self.width == LANES
        assert sectors % 2 == 0
        self.ends = 1 if spans == 2 else 2
        self.blocks = [-1, 0, 1]
        self.halves = [0, 1] if spans == 2 else [-1, 0, 1]
        self.tiles = [(k, x) for k in self.blocks for x in self.halves]
        self.slots = [
            [t for t in range(self.insts) if any((k + self.shift[t]) % sectors == o for k in self.blocks)]
            for o in range(sectors)
        ]
        assert max(map(len, self.slots)) * self.width <= LANES

    def spectral(self):
        t = np.arange(self.insts)
        off = t[:, None] - t[None, :]
        sines = np.where(off == 0, 1.0, np.sin(np.pi * off / self.insts))
        table = np.where(off == 0, 0.0, 0.5 * (1.0 - 2.0 * (off % 2)) / sines).astype(np.float32)
        full = np.zeros((self.pad, self.pad), np.float32)
        full[: self.tf, : self.tf] = np.kron(table.T, np.eye(self.fields, dtype=np.float32))
        hi = full.astype(ml_dtypes.bfloat16)
        lo = (full - hi.astype(np.float32)).astype(ml_dtypes.bfloat16)
        return np.concatenate([hi, lo, hi], axis=1)

    def field_rows(self):
        out = np.zeros((self.pad, self.fields), np.float32)
        out[np.arange(self.tf), np.arange(self.tf) % self.fields] = 1.0
        return out

    def field_lanes(self):
        return np.tile(self.field_rows().T, (1, 3))

    def block_diagonal(self):
        block = np.full(self.pad, -1)
        block[: self.tf] = np.arange(self.tf) // self.fields
        same = (block[:, None] == block[None, :]) & (block[:, None] >= 0)
        return np.tile(same.astype(np.float32), (1, 3))


    def inst_rows(self):
        row, inst = table_index(self.pad, 16)
        return ((row >= inst * self.fields) & (row < (inst + 1) * self.fields)).astype(jnp.float32)

    def cell_of(self, lane):
        return lax.div(lane, self.width) * self.rows + lax.rem(lane, self.rows)

    def window_lanes(self):
        lane, to = table_index(LANES, LANES)
        return (lane < self.ct * self.width) & (to == self.cell_of(lane) * WINDOW)

    def window_spread(self):
        to, lane = table_index(LANES, LANES)
        return (lane < self.ct * self.width) & (to == self.cell_of(lane) * WINDOW)

    def weight_lanes(self):
        cell, lane = table_index(LANES, LANES)
        half = self.ct * self.width
        wanted = jnp.where(lane < half, self.cell_of(lane), self.cells + self.cell_of(lane - half))
        return cell == wanted

    def panel_lanes(self):
        lane = lane_index(1)
        panel = lax.rem(lax.div(lane, self.rows), self.panels)
        return jnp.where(lane < self.ct * self.width, panel, -9).astype(jnp.float32)


def table_index(rows, columns):
    return [lax.broadcasted_iota(jnp.int32, (rows, columns), axis) for axis in (0, 1)]


def call(kernel, out, scratch=(), flops=2_000_000, nbytes=1_000_000):
    return pl.pallas_call(
        kernel,
        out_shape=out,
        scratch_shapes=list(scratch),
        compiler_params=pltpu.CompilerParams(vmem_limit_bytes=20 * 1024 * 1024),
        cost_estimate=pl.CostEstimate(flops=flops, bytes_accessed=nbytes, transcendentals=0),
    )


def f32(*shape):
    return jax.ShapeDtypeStruct(shape, jnp.float32)


def vmem(*shape):
    return pltpu.VMEM(shape, jnp.float32)


def halves_of(x):
    hi = x.astype(jnp.bfloat16)
    return hi, (x - hi.astype(jnp.float32)).astype(jnp.bfloat16)


def dot3(w, x):
    hi, lo = halves_of(x)
    return jnp.dot(w, jnp.concatenate([hi, hi, lo], axis=0), preferred_element_type=jnp.float32)


def pick(x, table):
    table = table.astype(jnp.float32).astype(jnp.bfloat16)
    table = jnp.concatenate([table, table], axis=0)
    return jnp.dot(jnp.concatenate(halves_of(x), axis=1), table, preferred_element_type=jnp.float32)


def dot_full(a, b):
    return jnp.dot(a, b, precision=HIGHEST, preferred_element_type=jnp.float32)


def lane_index(rows):
    return lax.broadcasted_iota(jnp.int32, (rows, LANES), 1)


def rolled(x, by):
    by %= LANES
    return pltpu.roll(x, by, axis=1) if by else x


def at(r, count=1, start=0):
    return slice(start + r * LANES, start + (r + count) * LANES)


def parity():
    return lax.rem(lax.axis_index("sector"), 2)


def has_sides(plan):
    span = lax.axis_index("span")
    return jnp.where(span < plan.spans - 1, 1.0, 0.0), jnp.where(span > 0, 1.0, 0.0)


class Layer:
    def __init__(self, plan, ref, start=0, rates=None, seam=None, layer=0):
        self.plan, self.ref, self.start, self.seam, self.layer = plan, ref, start, seam, layer
        self.rates = rates or (ref, start)

    def rate(self, which, r, count=1):
        ref, start = self.rates
        row = self.plan.pad + which
        return ref[row : row + 1, at(r, count, start)]

    def row(self, r):
        value = self.ref[: self.plan.pad, at(r, 1, self.start)]
        if self.seam is None:
            return value
        return value + placed(self.seam, self.layer * self.plan.rows + r) * self.rate(C_MASK, r)

    def chunk(self, c):
        count = CHUNK // LANES
        if self.seam is None:
            return self.ref[: self.plan.pad, at(c * count, count, self.start)]
        return jnp.concatenate([self.row(c * count + part) for part in range(count)], axis=1)


def placed(tile, cell):
    return jnp.where(lane_index(tile.shape[0]) == 0, rolled(tile, -cell * WINDOW), 0.0)


class Products:
    def __init__(self, plan, w_ref, p_ref, first):
        self.plan, self.w, self.p, self.first = plan, w_ref, p_ref, first

    def fill(self, layer):
        for c in range(self.plan.slab // CHUNK):
            self.p[:, c * CHUNK : (c + 1) * CHUNK] = dot3(matrix(self.plan, self.w, self.first, 6), layer.chunk(c))
        self.layer = layer
        return self

    def get(self, block, r):
        row = (block - self.first) * self.plan.pad
        return self.p[row : row + self.plan.pad, at(r)]

    def own_terms(self, r):
        rate = self.layer.rate
        total = rate(C_TIME, r) * self.get(SPECTRAL, r)
        beside = []
        if r + 1 < self.plan.rows:
            beside.append(self.get(UP_SP, r + 1))
        if r > 0:
            beside.append(self.get(DOWN_SP, r - 1))
        total = total + rate(C_SP, r) * sum(beside[1:], beside[0])
        total = total + rate(C_UP, r) * rolled(self.get(UP_AX, r), -1)
        return total + rate(C_DOWN, r) * rolled(self.get(DOWN_AX, r), 1)


def matrix(plan, w_ref, block, count=1):
    return w_ref[block * plan.pad : (block + count) * plan.pad, :]


def two_layers(plan, ref, rates=None, seam=None):
    return [
        Layer(plan, ref, a * plan.slab, (rates, a * plan.slab) if rates is not None else None, seam, a)
        for a in range(plan.ct)
    ]


def inner_rows(plan, w_ref, p_refs, layers, force, g_ref):
    first = Products(plan, w_ref, p_refs[0], DOWN_AZ).fill(layers[0])
    second = Products(plan, w_ref, p_refs[1], SPECTRAL).fill(layers[1])
    for r in range(plan.rows):
        other = second.get(UP_AZ, r), first.get(DOWN_AZ, r)
        for a, products in enumerate((first, second)):
            total = products.own_terms(r) + layers[a].rate(C_AZ, r) * other[a]
            g_ref[:, at(r, 1, a * plan.slab)] = force[a].row(r) - total


def azimuthal(plan, w_ref, block, chunk_of, take):
    for c in range(plan.slab // CHUNK):
        terms = dot3(matrix(plan, w_ref, block), chunk_of(c))
        for part in range(CHUNK // LANES):
            take(c * (CHUNK // LANES) + part, terms[:, at(part)])


def middle_rows(plan, w_ref, p_refs, own, own_force, g_ref, near, near_force, side, corner, y_ref, h_ref, n_refs):
    pad, rows, ct = plan.pad, plan.rows, plan.ct
    outward, inward, last = (UP_SP, DOWN_SP), (DOWN_SP, UP_SP), (rows - 1, 0)
    edge_terms, edge_new, corner_terms = [], [], []
    for n in range(2):
        first, second, edge_force, edge_rate = side(n)
        corners = corner(n)
        every = dot3(w_ref[...], first)
        edge_terms.append(every[outward[n] * pad : (outward[n] + 1) * pad])
        corner_terms.append([dot3(matrix(plan, w_ref, outward[n]), c) for c in corners])
        beyond = dot3(matrix(plan, w_ref, outward[n]), second)
        within = dot3(matrix(plan, w_ref, inward[n]), jnp.concatenate([x.row(last[n]) for x in own], axis=1))
        from_low = dot3(matrix(plan, w_ref, DOWN_AZ), corners[0])
        from_high = dot3(matrix(plan, w_ref, UP_AZ), corners[1])
        new = []
        for a in range(ct):

            def part(block, b=a):
                return every[block * pad : (block + 1) * pad, at(b)]

            around = part(UP_AZ, 1) + from_low if a == 0 else from_high + part(DOWN_AZ, 0)
            total = edge_rate(C_TIME, a) * part(SPECTRAL) + edge_rate(C_AZ, a) * around
            total = total + edge_rate(C_SP, a) * (beyond[:, at(a)] + within[:, at(a)])
            total = total + edge_rate(C_UP, a) * rolled(part(UP_AX), -1)
            total = total + edge_rate(C_DOWN, a) * rolled(part(DOWN_AX), 1)
            new.append(edge_force[:, at(a)] - total)
        edge_new.append(dot3(matrix(plan, w_ref, outward[n]), jnp.concatenate(new, axis=1)))

    products = (
        Products(plan, w_ref, p_refs[0], DOWN_AZ).fill(near[0]), Products(plan, w_ref, p_refs[1], SPECTRAL).fill(near[1]),
    )
    for a, (to_own, to_near) in enumerate(((DOWN_AZ, UP_AZ), (UP_AZ, DOWN_AZ))):

        def take(r, terms):
            total = products[a].own_terms(r) + near[a].rate(C_AZ, r) * terms
            mine = own[a].rate(C_AZ, r) * products[a].get(to_own, r)
            for n in range(2):
                if r == last[n]:
                    total = total + near[a].rate(C_SP, r) * corner_terms[n][a]
                    mine = mine + own[a].rate(C_SP, r) * edge_terms[n][:, at(a)]
            n_refs[a][:, at(r)] = near_force[a].row(r) - total
            lanes = at(r, 1, a * plan.slab)
            y_ref[:, lanes] = g_ref[:, lanes] - mine

        azimuthal(plan, w_ref, to_near, own[a].chunk, take)

    after = [Layer(plan, y_ref, a * plan.slab, own[a].rates) for a in range(ct)]
    inner_rows(plan, w_ref, p_refs, after, own_force, h_ref)
    for a in range(ct):
        for n in range(2):
            lanes = at(last[n], 1, a * plan.slab)
            h_ref[:, lanes] -= own[a].rate(C_SP, last[n]) * edge_new[n][:, at(a)]


def outer_rows(plan, w_ref, own, near, far_chunks, n_refs, h_ref, put, layers=(0, 1)):
    count = CHUNK // LANES
    for a in layers:
        block = (DOWN_AZ, UP_AZ)[a]

        def near_chunk(c):
            terms = dot3(matrix(plan, w_ref, block), far_chunks[a](c))
            return n_refs[a][:, at(c * count, count)] - near[a].rate(C_AZ, c * count, count) * terms

        def take(r, terms):
            put(a, r, h_ref[:, at(r, 1, a * plan.slab)] - own[a].rate(C_AZ, r) * terms)

        azimuthal(plan, w_ref, block, near_chunk, take)


def sides_of(plan, side_ref, force_ref, seams_ref):
    pad, ct = plan.pad, plan.ct
    keeps = has_sides(plan)

    def read(n, ref, e, seam):
        i = n if plan.ends == 2 else 0
        value = ref[i, :pad, at(e * ct, ct)]
        if seam:
            r = e if n == 0 else plan.rows - 1 - e
            tile = seams_ref[1, 1 + i]
            scale = ref[i, pad + C_MASK : pad + C_MASK + 1, at(e * ct, ct)]
            value = value + jnp.concatenate([placed(tile, a * plan.rows + r) for a in range(ct)], axis=1) * scale
        return value * keeps[n]

    def side(n):
        i = n if plan.ends == 2 else 0
        same = side_ref is force_ref

        def rate(which, a):
            return force_ref[i, pad + which : pad + which + 1, at(a)] * keeps[n]

        force = read(n, force_ref, 0, True)
        first = force if same else read(n, side_ref, 0, False)
        return first, read(n, side_ref, 1, same), force, rate

    return side


def corners_of(plan, c_refs, seams_ref):
    keeps = has_sides(plan)

    def corner(n):
        i = n if plan.ends == 2 else 0
        out = []
        for a, c_ref in enumerate(c_refs):
            value = c_ref[i, : plan.pad]
            if seams_ref is not None:
                r = 0 if n == 0 else plan.rows - 1
                scale = c_ref[i, plan.pad + C_MASK : plan.pad + C_MASK + 1]
                value = value + placed(seams_ref[2 * a, 1 + i], a * plan.rows + r) * scale
            out.append(value * keeps[n])
        return out

    return corner


def prepare(plan, rhs_ref, coef_ref, m_ref, side_ref, c0_ref, c1_ref):
    pad = plan.pad
    lane = lane_index(1)
    tail = jnp.zeros((pad - plan.tf, LANES), jnp.float32)
    mirror = parity()
    for cell in range(plan.cells):
        a, r = divmod(cell, plan.rows)
        there = jnp.where(mirror == 0, a, plan.ct - 1 - a) * plan.rows + r
        mask, diag, time, *face = [coef_ref[pl.ds(there + plan.cells * i, 1), :] for i in range(6)]
        scale = mask / diag
        axial = scale * face[2]
        rates = [
            scale * time, scale * face[0], scale * face[1],
            jnp.where(lane < LANES - 1, axial, 0.0), jnp.where(lane > 0, axial, 0.0), scale,
            jnp.zeros((RATES - 6, LANES), jnp.float32),
        ]
        field = jnp.concatenate([rhs_ref[pl.ds(there, plan.tf, stride=plan.cells), :], tail], axis=0) * scale
        m_ref[:pad, at(cell)] = field
        m_ref[pad:, at(cell)] = jnp.concatenate(rates, axis=0)
    write_edges(plan, m_ref, side_ref, (c0_ref, c1_ref))


def write_edges(plan, x_ref, side_ref, c_refs):
    first = lax.axis_index("span") == 0
    for a in range(plan.ct):
        for e in range(DEPTH):
            low, high = x_ref[:, at(a * plan.rows + e)], x_ref[:, at((a + 1) * plan.rows - 1 - e)]
            ends = [jnp.where(first, high, low)] if plan.ends == 1 else [low, high]
            for n, end in enumerate(ends):
                side_ref[n, :, at(e * plan.ct + a)] = end
                if e == 0:
                    c_refs[a][n] = end


def stack_matrices(plan, up_ref, down_ref, spectral_ref, rows_ref, lanes_ref, diagonal_ref, out_ref, down_out):
    pad = plan.pad
    lane = lax.broadcasted_iota(jnp.int32, (pad, 3 * pad), 1)
    second = (lane >= pad) & (lane < 2 * pad)
    out_ref[SPECTRAL * pad : (SPECTRAL + 1) * pad, :] = spectral_ref[...]
    even = parity() == 0
    for block, small in (
        (DOWN_AZ, jnp.where(even, down_ref[0], up_ref[0])), (UP_AZ, jnp.where(even, up_ref[0], down_ref[0])),
        (UP_SP, up_ref[1]), (DOWN_SP, down_ref[1]), (UP_AX, up_ref[2]), (DOWN_AX, down_ref[2]),
    ):
        full = dot_full(dot_full(rows_ref[...], small), lanes_ref[...]) * diagonal_ref[...]
        hi = full.astype(jnp.bfloat16).astype(jnp.float32)
        out_ref[block * pad : (block + 1) * pad, :] = jnp.where(second, full - hi, hi).astype(jnp.bfloat16)
    down_out[...] = matrix(plan, out_ref, DOWN_AZ)


def send_panels(plan, stator_ref, both_ref, out_ref, panels_ref):
    me = lax.axis_index("sector")
    for f in range(plan.fields):
        panels_ref[pl.ds(f, plan.insts, stride=RATES), : plan.width] = jnp.transpose(stator_ref[f])
    out_ref[...] = jnp.zeros_like(out_ref)
    both = both_ref[...]
    for t in range(plan.insts):
        group, row = divmod(t, GROUP)
        lanes = slice(group * 2 * plan.cells, (group + 1) * 2 * plan.cells)
        row += RATES
        out_ref[:, row : row + 1, lanes] = jnp.broadcast_to(both[t : t + 1][None], (out_ref.shape[0], 1, 2 * plan.cells))
    for o, slots in enumerate(plan.slots):
        to = lax.rem(me + (plan.sectors - o), plan.sectors) * plan.spans
        for slot, t in enumerate(slots):
            lanes = slice(slot * plan.width, (slot + 1) * plan.width)
            panels = panels_ref[t * RATES : t * RATES + plan.fields, : plan.width]
            for x in range(plan.spans):
                out_ref[to + x, : plan.fields, lanes] = panels


def begin(
    plan, w_ref, m_ref, got_ref,
    seams_ref, weight_ref, x_ref, g_ref, panels_ref, terms_ref, rows_ref, p0_ref, p1_ref,
):
    pad, insts, fields = plan.pad, plan.insts, plan.fields
    me, span = lax.axis_index("sector"), lax.axis_index("span")
    tiles = plan.tiles
    panels_ref[...] = jnp.zeros_like(panels_ref)
    rows_ref[...] = jnp.zeros_like(rows_ref)
    wide = 2 * plan.cells
    for n, (k, x) in enumerate(tiles):
        at_span = x if plan.spans == 2 else jnp.clip(span + x, 0, plan.spans - 1)
        for t in range(insts):
            o = (k + plan.shift[t]) % plan.sectors
            source = lax.rem(me + o, plan.sectors) * plan.spans + at_span
            tile = rolled(got_ref[source, :RATES], -plan.slots[o].index(t) * plan.width)
            panels_ref[t * fields : (t + 1) * fields, n * LANES : n * LANES + plan.width] = tile[:fields, : plan.width]
        source = lax.rem(me + k + plan.sectors, plan.sectors) * plan.spans + at_span
        table = got_ref[source, RATES:]
        for group in range(-(-insts // GROUP)):
            shifted = rolled(table, -group * wide)
            rows_ref[group * GROUP : (group + 1) * GROUP, n * LANES : n * LANES + wide] = shifted[:GROUP, :wide]
    spread = dot_full(plan.inst_rows(), rows_ref[...])
    spread = pick(jnp.concatenate([spread[:, at(n)] for n in range(len(tiles))], axis=0), plan.weight_lanes())
    first, share, panel = spread, rolled(spread, plan.ct * plan.width), plan.panel_lanes()
    lower = (jnp.abs(first - panel) < 0.5).astype(jnp.float32)
    upper = (jnp.abs(first + 1.0 - panel) < 0.5).astype(jnp.float32)
    weights = share * lower + (1.0 - share) * upper
    for n in range(len(tiles)):
        panels = panels_ref[:, at(n)]
        terms_ref[n * pad : (n + 1) * pad, :] = panels + rolled(panels, plan.width)
    seams = pick(terms_ref[...] * weights, plan.window_lanes())

    even = parity() == 0
    is_first = span == 0

    def tile(values, k, x):
        n = tiles.index((k, x))
        return values[n * pad : (n + 1) * pad]

    def around(values, k):
        if plan.spans == 2:
            pair = tile(values, k, 0), tile(values, k, 1)
            return [jnp.where(is_first, pair[0], pair[1]), jnp.where(is_first, pair[1], pair[0])]
        return [tile(values, k, x) for x in (0, 1, -1)]

    def mirrored(value):
        return rolled(value, LANES // 2)

    here = around(seams, 0)
    behind, ahead = around(seams, -1), around(seams, 1)
    for i in range(1 + plan.ends):
        seams_ref[0, i] = jnp.where(even, mirrored(behind[i]), ahead[i])
        seams_ref[1, i] = jnp.where(even, here[i], mirrored(here[i]))
        seams_ref[2, i] = jnp.where(even, mirrored(ahead[i]), behind[i])
    weight_ref[...] = around(weights, 0)[0]

    for layer in two_layers(plan, m_ref, seam=seams_ref[1, 0]):
        for r in range(plan.rows):
            x_ref[:, at(r, 1, layer.start)] = layer.row(r)
    layers = two_layers(plan, x_ref, m_ref)
    inner_rows(plan, w_ref, (p0_ref, p1_ref), layers, layers, g_ref)


def first_half(
    plan, w_ref, m_ref, f_ref, g_ref, low_ref, high_ref, side_ref, c_low, c_high, seams_ref,
    x_ref, near_ref, side_out, c0_ref, c1_ref, p0_ref, p1_ref, y_ref, h_ref, n0_ref, n1_ref,
):
    own = two_layers(plan, f_ref, m_ref)
    low = two_layers(plan, low_ref, seam=seams_ref[0, 0])
    high = two_layers(plan, high_ref, seam=seams_ref[2, 0])
    near = low[0], high[1]
    n_refs = n0_ref, n1_ref
    middle_rows(
        plan, w_ref, (p0_ref, p1_ref), own, own, g_ref, near, near, sides_of(plan, side_ref, side_ref, seams_ref),
        corners_of(plan, (c_low, c_high), seams_ref), y_ref, h_ref, n_refs,
    )
    lane = lane_index(plan.pad)
    near_ref[:, plan.slab :] = jnp.zeros((plan.pad, LANES), jnp.float32)

    def put(a, r, value):
        x_ref[:, at(r, 1, a * plan.slab)] = value
        if a == 0:
            near_ref[:, at(r)] = value
        else:
            here = rolled(value, r * WINDOW)
            near_ref[:, plan.slab :] = jnp.where(lane == r * WINDOW, here, near_ref[:, plan.slab :])

    outer_rows(plan, w_ref, own, near, (low[1].chunk, high[0].chunk), n_refs, h_ref, put)
    write_edges(plan, x_ref, side_out, (c0_ref, c1_ref))


def inner(plan, w_ref, m_ref, f_ref, x_ref, side_ref, g_ref, far_ref, p0_ref, p1_ref):
    far_ref[...] = x_ref[:, plan.slab :] + 0.0 * side_ref[0, 0:1, 0:1]
    inner_rows(plan, w_ref, (p0_ref, p1_ref), two_layers(plan, x_ref, m_ref), two_layers(plan, f_ref, m_ref), g_ref)


def middle(
    plan, w_ref, m_ref, f_ref, x_ref, g_ref, low_ref, high_ref, side_ref, c_low, c_high,
    low_first, high_first, side_first, seams_ref, weight_ref,
    send_ref, n0_ref, h0_ref, x1_ref, rates_ref, p0_ref, p1_ref, y_ref, inlet_ref, h_ref, n1_ref,
):
    pad = plan.pad
    own, force = two_layers(plan, x_ref, m_ref), two_layers(plan, f_ref, m_ref)
    low_force = Layer(plan, low_first, 0, None, seams_ref[0, 0], 0)
    high_force = Layer(plan, high_first, plan.slab, None, seams_ref[2, 0], 1)
    near = Layer(plan, low_ref, 0, low_force.rates), Layer(plan, high_ref, plan.slab, high_force.rates)
    n_refs = n0_ref, n1_ref
    middle_rows(
        plan, w_ref, (p0_ref, p1_ref), own, force, g_ref, near, (low_force, high_force),
        sides_of(plan, side_ref, side_first, seams_ref), corners_of(plan, (c_low, c_high), None), y_ref, h_ref, n_refs,
    )
    lane = lane_index(pad)
    inlet_ref[...] = jnp.zeros_like(inlet_ref)

    def put(a, r, value):
        cell = a * plan.rows + r
        inlet_ref[...] = jnp.where(lane == cell * WINDOW, rolled(value, cell * WINDOW), inlet_ref[...])
        if a == 1:
            x1_ref[:, at(r)] = value

    def far_inlet(c):
        tile = low_ref[:, plan.slab :]
        count = CHUNK // LANES
        return jnp.concatenate([placed(tile, c * count + part) for part in range(count)], axis=1)

    outer_rows(plan, w_ref, own, near, (far_inlet, Layer(plan, high_ref).chunk), n_refs, h_ref, put)
    inlet = inlet_ref[...]
    inlet = jnp.where(parity() == 0, inlet, rolled(inlet, LANES // 2))
    back = pick(inlet, plan.window_spread()) * weight_ref[...]
    back = back + rolled(back, -plan.width)
    me = lax.axis_index("sector")
    send_ref[...] = jnp.zeros_like(send_ref)
    for t in range(plan.insts):
        to = lax.rem(me + plan.shift[t], plan.sectors)
        send_ref[to, : plan.fields, : plan.width] = back[t * plan.fields : (t + 1) * plan.fields, : plan.width]
    h0_ref[...] = h_ref[:, : plan.slab]
    for r in range(plan.rows):
        rest = jnp.zeros((RATES - 2, LANES), jnp.float32)
        rates_ref[:, at(r)] = jnp.concatenate([near[0].rate(C_AZ, r), own[0].rate(C_AZ, r), rest], axis=0)


def outer(plan, w_ref, rates_ref, n0_ref, h0_ref, x1_ref, far_ref, out_ref):
    mirror = parity()

    def put(a, r, value):
        there = jnp.where(mirror == 0, a, plan.ct - 1 - a) * plan.rows + r
        out_ref[pl.ds(there, plan.tf, stride=plan.cells), :] = value[: plan.tf]

    for r in range(plan.rows):
        put(1, r, x1_ref[:, at(r)])

    def near_chunk(c):
        lanes = slice(c * CHUNK, (c + 1) * CHUNK)
        return n0_ref[:, lanes] - rates_ref[0:1, lanes] * dot3(w_ref[...], far_ref[:, lanes])

    azimuthal(plan, w_ref, 0, near_chunk, lambda r, terms: put(0, r, h0_ref[:, at(r)] - rates_ref[1:2, at(r)] * terms))


def collect_panels(plan, got_ref, out_ref, panels_ref):
    me = lax.axis_index("sector")
    for t in range(plan.insts):
        source = lax.rem(me + (plan.sectors - plan.shift[t]), plan.sectors)
        panels_ref[t * RATES : (t + 1) * RATES, :] = got_ref[source]
    for f in range(plan.fields):
        tile = panels_ref[pl.ds(f, plan.insts, stride=RATES), : plan.width]
        out_ref[f] = jnp.transpose(tile)


def sibling(plan):
    return [s ^ 1 for s in range(plan.sectors)]


def outside(plan):
    return [(s - 1 if s % 2 == 0 else s + 1) % plan.sectors for s in range(plan.sectors)]


def swap(array, partner):
    return lax.ppermute(array, "sector", list(enumerate(partner)))


def beside(plan, array, partner):
    def pairs(step):
        out = []
        for s in range(plan.sectors):
            for x in range(plan.spans):
                to = 1 - x if plan.ends == 1 else x + step
                if 0 <= to < plan.spans:
                    out.append((s * plan.spans + x, partner[s] * plan.spans + to))
        return out

    if plan.ends == 1:
        return lax.ppermute(array, AXES, pairs(0))
    return jnp.concatenate([lax.ppermute(array[:1], AXES, pairs(-1)), lax.ppermute(array[1:], AXES, pairs(1))])


def on_device(
    sectors, spans,
    rhs, diag_coef, face_coef, time_coef, jac_up, jac_down, wall_mask, stator_adj, owner, first_panel_share,
):
    plan = Plan(rhs, stator_adj, sectors, spans)
    pad, cells, slab, insts, fields, ends = plan.pad, plan.cells, plan.slab, plan.insts, plan.fields, plan.ends
    bind = functools.partial
    whole, half = f32(pad, plan.ct * slab), f32(pad, slab)
    products = (vmem(6 * pad, slab),) * 2
    alone, next_chip, next_core = list(range(sectors)), outside(plan), sibling(plan)

    def edges(rows):
        return f32(ends, rows, DEPTH * plan.ct * LANES), f32(ends, rows, LANES), f32(ends, rows, LANES)

    stator = jnp.transpose(stator_adj, (1, 2, 3, 0)).reshape(fields, plan.width, insts)
    sent = call(bind(send_panels, plan), f32(sectors * spans, 2 * RATES, LANES), (vmem(insts * RATES, LANES),))(
        stator,
        jnp.concatenate([
            lax.rem(owner, plan.panels).astype(jnp.float32).reshape(insts, cells), first_panel_share.reshape(insts, cells),
        ], axis=1),
    )
    got = lax.all_to_all(sent, AXES, 0, 0, tiled=True)
    m, side, c0, c1 = call(bind(prepare, plan), (f32(pad + RATES, plan.ct * slab),) + edges(pad + RATES))(
        rhs.reshape(plan.tf * cells, LANES),
        jnp.concatenate([
            wall_mask.astype(jnp.float32).reshape(cells, LANES), diag_coef.reshape(cells, LANES),
            time_coef.reshape(cells, LANES), face_coef.reshape(3 * cells, LANES),
        ]),
    )
    low_first, high_first = swap(m, next_chip), swap(m, next_core)
    side_first = beside(plan, side, alone)
    c_low, c_high = beside(plan, c0, next_chip), beside(plan, c1, next_core)
    matrices, down = call(
        bind(stack_matrices, plan),
        [jax.ShapeDtypeStruct((count * pad, 3 * pad), jnp.bfloat16) for count in (7, 1)],
    )(jac_up, jac_down, plan.spectral(), plan.field_rows(), plan.field_lanes(), plan.block_diagonal())
    tiles = len(plan.tiles)
    seams, weight, force, g = call(
        bind(begin, plan), (f32(3, 1 + ends, pad, LANES), f32(pad, LANES), whole, whole),
        (vmem(pad, tiles * LANES), vmem(tiles * pad, LANES), vmem(16, tiles * LANES)) + products,
        flops=2_000_000_000,
    )(matrices, m, got)
    x, near, side, c0, c1 = call(
        bind(first_half, plan), (whole, f32(pad, slab + LANES)) + edges(pad),
        products + (vmem(pad, 2 * slab), vmem(pad, 2 * slab), vmem(pad, slab), vmem(pad, slab)), flops=4_000_000_000,
    )(matrices, m, force, g, low_first, high_first, side_first, c_low, c_high, seams)

    low, high = swap(near, next_chip), swap(x, next_core)
    side = beside(plan, side, alone)
    c_low, c_high = beside(plan, c0, next_chip), beside(plan, c1, next_core)
    g, far = call(bind(inner, plan), (whole, half), products, flops=2_000_000_000)(
        matrices, m, force, x, side
    )
    far_low = swap(far, next_chip)
    back, n0, h0, x1, rates = call(
        bind(middle, plan), (f32(sectors, RATES, LANES), half, half, half, f32(RATES, slab)),
        products + (vmem(pad, 2 * slab), vmem(pad, LANES), vmem(pad, 2 * slab), vmem(pad, slab)), flops=4_000_000_000,
    )(
        matrices, m, force, x, g, low, high, side, c_low, c_high, low_first, high_first, side_first, seams, weight
    )
    returned = lax.all_to_all(back, "sector", 0, 0, tiled=True)
    sens = call(bind(collect_panels, plan), f32(fields, plan.width, insts), (vmem(insts * RATES, LANES),))(returned)
    out = call(bind(outer, plan), f32(plan.tf * cells, LANES))(down, rates, n0, h0, x1, far_low)
    sens = jnp.transpose(sens.reshape(fields, plan.panels, plan.rows, insts), (3, 0, 1, 2))
    return out.reshape(rhs.shape), sens


def solution(mesh):
    in_specs = (
        P(None, None, "sector", "span", None),
        P("sector", "span", None),
        P(None, "sector", "span", None),
        P("sector", "span", None),
        P(),
        P(),
        P("sector", "span", None),
        P(None, None, "sector", "span"),
        P(None, "sector", "span"),
        P(None, "sector", "span"),
    )
    out_specs = (P(None, None, "sector", "span", None), P(None, None, "sector", "span"))
    return jax.shard_map(
        functools.partial(on_device, mesh.shape["sector"], mesh.shape["span"]),
        mesh=mesh, in_specs=in_specs, out_specs=out_specs, check_vma=False,
    )
```

```python
import functools

import jax
import jax.numpy as jnp
import ml_dtypes
import numpy as np
from jax import lax
from jax.experimental import pallas as pl
from jax.experimental.pallas import tpu as pltpu
from jax.sharding import PartitionSpec as P

SWEEPS = 4
DEPTH = 2
LANES = 128
CHUNK = 256
WINDOW = 8
HIGHEST = lax.Precision.HIGHEST
DOWN_AZ, SPECTRAL, UP_SP, DOWN_SP, UP_AX, DOWN_AX, UP_AZ = range(7)
C_TIME, C_AZ, C_SP, C_UP, C_DOWN, C_MASK, C_OTHER = range(7)
RATES = 8
GROUP = 3
AXES = ("sector", "span")


class Plan:
    def __init__(self, rhs, stator_adj, sectors, spans):
        self.insts, self.fields, self.ct, self.rows, self.nax = rhs.shape
        self.panels = stator_adj.shape[2]
        self.sectors, self.spans = sectors, spans
        self.tf = self.insts * self.fields
        self.pad = -(-self.tf // 16) * 16
        self.cells = self.ct * self.rows
        self.slab = self.rows * LANES
        self.width = self.panels * self.rows
        self.shift = [
            ((t * sectors) // (self.insts - 1) - t // (self.insts - 1)) % sectors for t in range(self.insts)
        ]
        assert self.ct == 2 and self.nax == LANES and SWEEPS % DEPTH == 0 and spans > 1
        assert len(set(self.shift)) == self.insts and self.cells * WINDOW == LANES and self.rows >= SWEEPS
        assert self.slab % CHUNK == 0 and 3 * self.pad <= 256 and 2 * self.ct * self.width == LANES
        assert sectors % 2 == 0
        self.ends = 1 if spans == 2 else 2
        self.blocks = [-1, 0, 1]
        self.halves = [0, 1] if spans == 2 else [-1, 0, 1]
        self.tiles = [(k, x) for k in self.blocks for x in self.halves]
        self.slots = [
            [t for t in range(self.insts) if any((k + self.shift[t]) % sectors == o for k in self.blocks)]
            for o in range(sectors)
        ]
        assert max(map(len, self.slots)) * self.width <= LANES

    def spectral(self):
        t = np.arange(self.insts)
        off = t[:, None] - t[None, :]
        sines = np.where(off == 0, 1.0, np.sin(np.pi * off / self.insts))
        table = np.where(off == 0, 0.0, 0.5 * (1.0 - 2.0 * (off % 2)) / sines).astype(np.float32)
        full = np.zeros((self.pad, self.pad), np.float32)
        full[: self.tf, : self.tf] = np.kron(table.T, np.eye(self.fields, dtype=np.float32))
        hi = full.astype(ml_dtypes.bfloat16)
        lo = (full - hi.astype(np.float32)).astype(ml_dtypes.bfloat16)
        return np.concatenate([hi, lo, hi], axis=1)

    def field_rows(self):
        out = np.zeros((self.pad, self.fields), np.float32)
        out[np.arange(self.tf), np.arange(self.tf) % self.fields] = 1.0
        return out

    def field_lanes(self):
        return np.tile(self.field_rows().T, (1, 3))

    def block_diagonal(self):
        block = np.full(self.pad, -1)
        block[: self.tf] = np.arange(self.tf) // self.fields
        same = (block[:, None] == block[None, :]) & (block[:, None] >= 0)
        return np.tile(same.astype(np.float32), (1, 3))


    def inst_rows(self):
        row, inst = table_index(self.pad, 16)
        return ((row >= inst * self.fields) & (row < (inst + 1) * self.fields)).astype(jnp.float32)

    def cell_of(self, lane):
        return lax.div(lane, self.width) * self.rows + lax.rem(lane, self.rows)

    def window_lanes(self):
        lane, to = table_index(LANES, LANES)
        return (lane < self.ct * self.width) & (to == self.cell_of(lane) * WINDOW)

    def window_spread(self):
        to, lane = table_index(LANES, LANES)
        return (lane < self.ct * self.width) & (to == self.cell_of(lane) * WINDOW)

    def weight_lanes(self):
        cell, lane = table_index(LANES, LANES)
        half = self.ct * self.width
        wanted = jnp.where(lane < half, self.cell_of(lane), self.cells + self.cell_of(lane - half))
        return cell == wanted

    def panel_lanes(self):
        lane = lane_index(1)
        panel = lax.rem(lax.div(lane, self.rows), self.panels)
        return jnp.where(lane < self.ct * self.width, panel, -9).astype(jnp.float32)


def table_index(rows, columns):
    return [lax.broadcasted_iota(jnp.int32, (rows, columns), axis) for axis in (0, 1)]


def call(kernel, out, scratch=(), flops=2_000_000, nbytes=1_000_000):
    return pl.pallas_call(
        kernel,
        out_shape=out,
        scratch_shapes=list(scratch),
        compiler_params=pltpu.CompilerParams(vmem_limit_bytes=20 * 1024 * 1024),
        cost_estimate=pl.CostEstimate(flops=flops, bytes_accessed=nbytes, transcendentals=0),
    )


def f32(*shape):
    return jax.ShapeDtypeStruct(shape, jnp.float32)


def vmem(*shape):
    return pltpu.VMEM(shape, jnp.float32)


def halves_of(x):
    hi = x.astype(jnp.bfloat16)
    return hi, (x - hi.astype(jnp.float32)).astype(jnp.bfloat16)


def dot3(w, x):
    hi, lo = halves_of(x)
    return jnp.dot(w, jnp.concatenate([hi, hi, lo], axis=0), preferred_element_type=jnp.float32)


def pick(x, table):
    table = table.astype(jnp.float32).astype(jnp.bfloat16)
    table = jnp.concatenate([table, table], axis=0)
    return jnp.dot(jnp.concatenate(halves_of(x), axis=1), table, preferred_element_type=jnp.float32)


def dot_full(a, b):
    return jnp.dot(a, b, precision=HIGHEST, preferred_element_type=jnp.float32)


def lane_index(rows):
    return lax.broadcasted_iota(jnp.int32, (rows, LANES), 1)


def rolled(x, by):
    by %= LANES
    return pltpu.roll(x, by, axis=1) if by else x


def at(r, count=1, start=0):
    return slice(start + r * LANES, start + (r + count) * LANES)


def parity():
    return lax.rem(lax.axis_index("sector"), 2)


def has_sides(plan):
    span = lax.axis_index("span")
    return jnp.where(span < plan.spans - 1, 1.0, 0.0), jnp.where(span > 0, 1.0, 0.0)


class Layer:
    def __init__(self, plan, ref, start=0, rates=None, seam=None, layer=0, scale=C_MASK):
        self.plan, self.ref, self.start, self.seam, self.layer, self.scale = plan, ref, start, seam, layer, scale
        self.rates = rates or (ref, start)

    def rate(self, which, r, count=1):
        ref, start = self.rates
        row = self.plan.pad + which
        return ref[row : row + 1, at(r, count, start)]

    def row(self, r):
        value = self.ref[: self.plan.pad, at(r, 1, self.start)]
        if self.seam is None:
            return value
        return value + placed(self.seam, self.layer * self.plan.rows + r) * self.rate(self.scale, r)

    def chunk(self, c):
        count = CHUNK // LANES
        if self.seam is None:
            return self.ref[: self.plan.pad, at(c * count, count, self.start)]
        return jnp.concatenate([self.row(c * count + part) for part in range(count)], axis=1)


def placed(tile, cell):
    return jnp.where(lane_index(tile.shape[0]) == 0, rolled(tile, -cell * WINDOW), 0.0)


class Products:
    def __init__(self, plan, w_ref, p_ref, first):
        self.plan, self.w, self.p, self.first = plan, w_ref, p_ref, first

    def fill(self, layer):
        for c in range(self.plan.slab // CHUNK):
            self.p[:, c * CHUNK : (c + 1) * CHUNK] = dot3(matrix(self.plan, self.w, self.first, 6), layer.chunk(c))
        self.layer = layer
        return self

    def get(self, block, r):
        row = (block - self.first) * self.plan.pad
        return self.p[row : row + self.plan.pad, at(r)]

    def own_terms(self, r):
        rate = self.layer.rate
        total = rate(C_TIME, r) * self.get(SPECTRAL, r)
        beside = []
        if r + 1 < self.plan.rows:
            beside.append(self.get(UP_SP, r + 1))
        if r > 0:
            beside.append(self.get(DOWN_SP, r - 1))
        total = total + rate(C_SP, r) * sum(beside[1:], beside[0])
        total = total + rate(C_UP, r) * rolled(self.get(UP_AX, r), -1)
        return total + rate(C_DOWN, r) * rolled(self.get(DOWN_AX, r), 1)


def matrix(plan, w_ref, block, count=1):
    return w_ref[block * plan.pad : (block + count) * plan.pad, :]


def two_layers(plan, ref, rates=None, seam=None):
    return [
        Layer(plan, ref, a * plan.slab, (rates, a * plan.slab) if rates is not None else None, seam, a)
        for a in range(plan.ct)
    ]


def inner_rows(plan, w_ref, p_refs, layers, force, g_ref):
    first = Products(plan, w_ref, p_refs[0], DOWN_AZ).fill(layers[0])
    second = Products(plan, w_ref, p_refs[1], SPECTRAL).fill(layers[1])
    for r in range(plan.rows):
        other = second.get(UP_AZ, r), first.get(DOWN_AZ, r)
        for a, products in enumerate((first, second)):
            total = products.own_terms(r) + layers[a].rate(C_AZ, r) * other[a]
            g_ref[:, at(r, 1, a * plan.slab)] = force[a].row(r) - total


def azimuthal(plan, w_ref, block, chunk_of, take):
    for c in range(plan.slab // CHUNK):
        terms = dot3(matrix(plan, w_ref, block), chunk_of(c))
        for part in range(CHUNK // LANES):
            take(c * (CHUNK // LANES) + part, terms[:, at(part)])


def middle_rows(plan, w_ref, p_refs, own, own_force, g_ref, near, near_force, side, corner, y_ref, h_ref, n_refs):
    pad, rows, ct = plan.pad, plan.rows, plan.ct
    outward, inward, last = (UP_SP, DOWN_SP), (DOWN_SP, UP_SP), (rows - 1, 0)
    edge_terms, edge_new, corner_terms = [], [], []
    for n in range(2):
        first, second, edge_force, edge_rate = side(n)
        corners = corner(n)
        every = dot3(w_ref[...], first)
        edge_terms.append(every[outward[n] * pad : (outward[n] + 1) * pad])
        corner_terms.append([dot3(matrix(plan, w_ref, outward[n]), c) for c in corners])
        beyond = dot3(matrix(plan, w_ref, outward[n]), second)
        within = dot3(matrix(plan, w_ref, inward[n]), jnp.concatenate([x.row(last[n]) for x in own], axis=1))
        from_low = dot3(matrix(plan, w_ref, DOWN_AZ), corners[0])
        from_high = dot3(matrix(plan, w_ref, UP_AZ), corners[1])
        new = []
        for a in range(ct):

            def part(block, b=a):
                return every[block * pad : (block + 1) * pad, at(b)]

            around = part(UP_AZ, 1) + from_low if a == 0 else from_high + part(DOWN_AZ, 0)
            total = edge_rate(C_TIME, a) * part(SPECTRAL) + edge_rate(C_AZ, a) * around
            total = total + edge_rate(C_SP, a) * (beyond[:, at(a)] + within[:, at(a)])
            total = total + edge_rate(C_UP, a) * rolled(part(UP_AX), -1)
            total = total + edge_rate(C_DOWN, a) * rolled(part(DOWN_AX), 1)
            new.append(edge_force[:, at(a)] - total)
        edge_new.append(dot3(matrix(plan, w_ref, outward[n]), jnp.concatenate(new, axis=1)))

    products = (
        Products(plan, w_ref, p_refs[0], DOWN_AZ).fill(near[0]), Products(plan, w_ref, p_refs[1], SPECTRAL).fill(near[1]),
    )
    for a, (to_own, to_near) in enumerate(((DOWN_AZ, UP_AZ), (UP_AZ, DOWN_AZ))):

        def take(r, terms):
            total = products[a].own_terms(r) + near[a].rate(C_AZ, r) * terms
            mine = own[a].rate(C_AZ, r) * products[a].get(to_own, r)
            for n in range(2):
                if r == last[n]:
                    total = total + near[a].rate(C_SP, r) * corner_terms[n][a]
                    mine = mine + own[a].rate(C_SP, r) * edge_terms[n][:, at(a)]
            n_refs[a][:, at(r)] = near_force[a].row(r) - total
            lanes = at(r, 1, a * plan.slab)
            y_ref[:, lanes] = g_ref[:, lanes] - mine

        azimuthal(plan, w_ref, to_near, own[a].chunk, take)

    after = [Layer(plan, y_ref, a * plan.slab, own[a].rates) for a in range(ct)]
    inner_rows(plan, w_ref, p_refs, after, own_force, h_ref)
    for a in range(ct):
        for n in range(2):
            lanes = at(last[n], 1, a * plan.slab)
            h_ref[:, lanes] -= own[a].rate(C_SP, last[n]) * edge_new[n][:, at(a)]


def outer_rows(plan, w_ref, own, near, far_chunks, n_refs, h_ref, put, layers=(0, 1)):
    count = CHUNK // LANES
    for a in layers:
        block = (DOWN_AZ, UP_AZ)[a]

        def near_chunk(c):
            terms = dot3(matrix(plan, w_ref, block), far_chunks[a](c))
            return n_refs[a][:, at(c * count, count)] - near[a].rate(C_AZ, c * count, count) * terms

        def take(r, terms):
            put(a, r, h_ref[:, at(r, 1, a * plan.slab)] - own[a].rate(C_AZ, r) * terms)

        azimuthal(plan, w_ref, block, near_chunk, take)


def sides_of(plan, side_ref, force_ref, seams_ref):
    pad, ct = plan.pad, plan.ct
    keeps = has_sides(plan)

    def read(n, ref, e, seam):
        i = n if plan.ends == 2 else 0
        value = ref[i, :pad, at(e * ct, ct)]
        if seam:
            r = e if n == 0 else plan.rows - 1 - e
            tile = seams_ref[1, 1 + i]
            scale = ref[i, pad + C_MASK : pad + C_MASK + 1, at(e * ct, ct)]
            value = value + jnp.concatenate([placed(tile, a * plan.rows + r) for a in range(ct)], axis=1) * scale
        return value * keeps[n]

    def side(n):
        i = n if plan.ends == 2 else 0
        same = side_ref is force_ref

        def rate(which, a):
            return force_ref[i, pad + which : pad + which + 1, at(a)] * keeps[n]

        force = read(n, force_ref, 0, True)
        first = force if same else read(n, side_ref, 0, False)
        return first, read(n, side_ref, 1, same), force, rate

    return side


def corners_of(plan, c_refs, seams_ref):
    keeps = has_sides(plan)

    def corner(n):
        i = n if plan.ends == 2 else 0
        out = []
        for a, c_ref in enumerate(c_refs):
            value = c_ref[i, : plan.pad]
            if seams_ref is not None:
                r = 0 if n == 0 else plan.rows - 1
                scale = c_ref[i, plan.pad + C_MASK : plan.pad + C_MASK + 1]
                value = value + placed(seams_ref[2 * a, 1 + i], a * plan.rows + r) * scale
            out.append(value * keeps[n])
        return out

    return corner


def prepare(plan, rhs_ref, coef_ref, m_ref, near_ref, side_ref, c0_ref, c1_ref):
    pad = plan.pad
    lane = lane_index(1)
    tail = jnp.zeros((pad - plan.tf, LANES), jnp.float32)
    mirror = parity()

    def coefs(a, r):
        there = jnp.where(mirror == 0, a, plan.ct - 1 - a) * plan.rows + r
        mask, diag, *rest = [coef_ref[pl.ds(there + plan.cells * i, 1), :] for i in range(6)]
        return there, mask / diag, rest

    for r in range(plan.rows):
        scales = [coefs(a, r)[1] for a in range(plan.ct)]
        for a in range(plan.ct):
            there, scale, (time, *face) = coefs(a, r)
            axial = scale * face[2]
            rates = jnp.concatenate([
                scale * time, scale * face[0], scale * face[1],
                jnp.where(lane < LANES - 1, axial, 0.0), jnp.where(lane > 0, axial, 0.0), scale, scales[1 - a],
                jnp.zeros((RATES - 7, LANES), jnp.float32),
            ], axis=0)
            field = jnp.concatenate([rhs_ref[pl.ds(there, plan.tf, stride=plan.cells), :], tail], axis=0) * scale
            lanes = at(a * plan.rows + r)
            m_ref[:pad, lanes] = field
            m_ref[pad:, lanes] = rates
            if a == 0:
                near_ref[:pad, lanes] = field
                near_ref[pad:, lanes] = rates
    write_edges(plan, m_ref, side_ref, (c0_ref, c1_ref))


def write_edges(plan, x_ref, side_ref, c_refs):
    first = lax.axis_index("span") == 0
    for a in range(plan.ct):
        for e in range(DEPTH):
            low, high = x_ref[:, at(a * plan.rows + e)], x_ref[:, at((a + 1) * plan.rows - 1 - e)]
            ends = [jnp.where(first, high, low)] if plan.ends == 1 else [low, high]
            for n, end in enumerate(ends):
                side_ref[n, :, at(e * plan.ct + a)] = end
                if e == 0:
                    c_refs[a][n] = end


def stack_matrices(plan, m_ref, high_ref, up_ref, down_ref, spectral_ref, rows_ref, lanes_ref, diagonal_ref, out_ref, down_out, far_ref):
    pad = plan.pad
    far_ref[...] = m_ref[:pad, plan.slab :] + 0.0 * high_ref[0:1, 0:1]
    lane = lax.broadcasted_iota(jnp.int32, (pad, 3 * pad), 1)
    second = (lane >= pad) & (lane < 2 * pad)
    out_ref[SPECTRAL * pad : (SPECTRAL + 1) * pad, :] = spectral_ref[...]
    even = parity() == 0
    for block, small in (
        (DOWN_AZ, jnp.where(even, down_ref[0], up_ref[0])), (UP_AZ, jnp.where(even, up_ref[0], down_ref[0])),
        (UP_SP, up_ref[1]), (DOWN_SP, down_ref[1]), (UP_AX, up_ref[2]), (DOWN_AX, down_ref[2]),
    ):
        full = dot_full(dot_full(rows_ref[...], small), lanes_ref[...]) * diagonal_ref[...]
        hi = full.astype(jnp.bfloat16).astype(jnp.float32)
        out_ref[block * pad : (block + 1) * pad, :] = jnp.where(second, full - hi, hi).astype(jnp.bfloat16)
    down_out[...] = matrix(plan, out_ref, DOWN_AZ)


def send_panels(plan, stator_ref, both_ref, out_ref, panels_ref):
    me = lax.axis_index("sector")
    for f in range(plan.fields):
        panels_ref[pl.ds(f, plan.insts, stride=RATES), : plan.width] = jnp.transpose(stator_ref[f])
    out_ref[...] = jnp.zeros_like(out_ref)
    both = both_ref[...]
    for t in range(plan.insts):
        group, row = divmod(t, GROUP)
        lanes = slice(group * 2 * plan.cells, (group + 1) * 2 * plan.cells)
        row += RATES
        out_ref[:, row : row + 1, lanes] = jnp.broadcast_to(both[t : t + 1][None], (out_ref.shape[0], 1, 2 * plan.cells))
    for o, slots in enumerate(plan.slots):
        to = lax.rem(me + (plan.sectors - o), plan.sectors) * plan.spans
        for slot, t in enumerate(slots):
            lanes = slice(slot * plan.width, (slot + 1) * plan.width)
            panels = panels_ref[t * RATES : t * RATES + plan.fields, : plan.width]
            for x in range(plan.spans):
                out_ref[to + x, : plan.fields, lanes] = panels


def begin(
    plan, w_ref, m_ref, got_ref,
    seams_ref, weight_ref, x_ref, g_ref, panels_ref, terms_ref, rows_ref, p0_ref, p1_ref,
):
    pad, insts, fields = plan.pad, plan.insts, plan.fields
    me, span = lax.axis_index("sector"), lax.axis_index("span")
    tiles = plan.tiles
    panels_ref[...] = jnp.zeros_like(panels_ref)
    rows_ref[...] = jnp.zeros_like(rows_ref)
    wide = 2 * plan.cells
    for n, (k, x) in enumerate(tiles):
        at_span = x if plan.spans == 2 else jnp.clip(span + x, 0, plan.spans - 1)
        for t in range(insts):
            o = (k + plan.shift[t]) % plan.sectors
            source = lax.rem(me + o, plan.sectors) * plan.spans + at_span
            tile = rolled(got_ref[source, :RATES], -plan.slots[o].index(t) * plan.width)
            panels_ref[t * fields : (t + 1) * fields, n * LANES : n * LANES + plan.width] = tile[:fields, : plan.width]
        source = lax.rem(me + k + plan.sectors, plan.sectors) * plan.spans + at_span
        table = got_ref[source, RATES:]
        for group in range(-(-insts // GROUP)):
            shifted = rolled(table, -group * wide)
            rows_ref[group * GROUP : (group + 1) * GROUP, n * LANES : n * LANES + wide] = shifted[:GROUP, :wide]
    spread = dot_full(plan.inst_rows(), rows_ref[...])
    spread = pick(jnp.concatenate([spread[:, at(n)] for n in range(len(tiles))], axis=0), plan.weight_lanes())
    first, share, panel = spread, rolled(spread, plan.ct * plan.width), plan.panel_lanes()
    lower = (jnp.abs(first - panel) < 0.5).astype(jnp.float32)
    upper = (jnp.abs(first + 1.0 - panel) < 0.5).astype(jnp.float32)
    weights = share * lower + (1.0 - share) * upper
    for n in range(len(tiles)):
        panels = panels_ref[:, at(n)]
        terms_ref[n * pad : (n + 1) * pad, :] = panels + rolled(panels, plan.width)
    seams = pick(terms_ref[...] * weights, plan.window_lanes())

    even = parity() == 0
    is_first = span == 0

    def tile(values, k, x):
        n = tiles.index((k, x))
        return values[n * pad : (n + 1) * pad]

    def around(values, k):
        if plan.spans == 2:
            pair = tile(values, k, 0), tile(values, k, 1)
            return [jnp.where(is_first, pair[0], pair[1]), jnp.where(is_first, pair[1], pair[0])]
        return [tile(values, k, x) for x in (0, 1, -1)]

    def mirrored(value):
        return rolled(value, LANES // 2)

    here = around(seams, 0)
    behind, ahead = around(seams, -1), around(seams, 1)
    for i in range(1 + plan.ends):
        seams_ref[0, i] = jnp.where(even, mirrored(behind[i]), ahead[i])
        seams_ref[1, i] = jnp.where(even, here[i], mirrored(here[i]))
        seams_ref[2, i] = jnp.where(even, mirrored(ahead[i]), behind[i])
    weight_ref[...] = around(weights, 0)[0]

    for layer in two_layers(plan, m_ref, seam=seams_ref[1, 0]):
        for r in range(plan.rows):
            x_ref[:, at(r, 1, layer.start)] = layer.row(r)
    layers = two_layers(plan, x_ref, m_ref)
    inner_rows(plan, w_ref, (p0_ref, p1_ref), layers, layers, g_ref)


def middle_first(
    plan, w_ref, m_ref, f_ref, g_ref, low_ref, high_ref, side_ref, c_low, c_high, seams_ref,
    h_ref, n0_ref, n1_ref, p0_ref, p1_ref, y_ref,
):
    own = two_layers(plan, f_ref, m_ref)
    near = (
        Layer(plan, low_ref, 0, None, seams_ref[0, 0], 0), Layer(plan, high_ref, plan.slab, None, seams_ref[2, 0], 1),
    )
    middle_rows(
        plan, w_ref, (p0_ref, p1_ref), own, own, g_ref, near, near, sides_of(plan, side_ref, side_ref, seams_ref),
        corners_of(plan, (c_low, c_high), seams_ref), y_ref, h_ref, (n0_ref, n1_ref),
    )


def outer_first(
    plan, w_ref, m_ref, low_first, high_first, n0_ref, n1_ref, h_ref, far_ref, seams_ref,
    x_ref, near_ref, side_out, c0_ref, c1_ref,
):
    own = two_layers(plan, m_ref)
    near = Layer(plan, low_first), Layer(plan, high_first, plan.slab)
    far_low = Layer(plan, far_ref, 0, (low_first, 0), seams_ref[0, 0], 1, C_OTHER)
    far_high = Layer(plan, high_first, 0, None, seams_ref[2, 0], 0)
    lane = lane_index(plan.pad)
    near_ref[:, plan.slab :] = jnp.zeros((plan.pad, LANES), jnp.float32)

    def put(a, r, value):
        x_ref[:, at(r, 1, a * plan.slab)] = value
        if a == 0:
            near_ref[:, at(r)] = value
        else:
            here = rolled(value, r * WINDOW)
            near_ref[:, plan.slab :] = jnp.where(lane == r * WINDOW, here, near_ref[:, plan.slab :])

    outer_rows(plan, w_ref, own, near, (far_low.chunk, far_high.chunk), (n0_ref, n1_ref), h_ref, put)
    write_edges(plan, x_ref, side_out, (c0_ref, c1_ref))


def inner(plan, w_ref, m_ref, f_ref, x_ref, side_ref, g_ref, far_ref, p0_ref, p1_ref):
    far_ref[...] = x_ref[:, plan.slab :] + 0.0 * side_ref[0, 0:1, 0:1]
    inner_rows(plan, w_ref, (p0_ref, p1_ref), two_layers(plan, x_ref, m_ref), two_layers(plan, f_ref, m_ref), g_ref)


def middle(
    plan, w_ref, m_ref, f_ref, x_ref, g_ref, low_ref, high_ref, side_ref, c_low, c_high,
    low_first, high_first, side_first, seams_ref, weight_ref,
    send_ref, n0_ref, h0_ref, x1_ref, rates_ref, p0_ref, p1_ref, y_ref, inlet_ref, h_ref, n1_ref,
):
    pad = plan.pad
    own, force = two_layers(plan, x_ref, m_ref), two_layers(plan, f_ref, m_ref)
    low_force = Layer(plan, low_first, 0, None, seams_ref[0, 0], 0)
    high_force = Layer(plan, high_first, plan.slab, None, seams_ref[2, 0], 1)
    near = Layer(plan, low_ref, 0, low_force.rates), Layer(plan, high_ref, plan.slab, high_force.rates)
    n_refs = n0_ref, n1_ref
    middle_rows(
        plan, w_ref, (p0_ref, p1_ref), own, force, g_ref, near, (low_force, high_force),
        sides_of(plan, side_ref, side_first, seams_ref), corners_of(plan, (c_low, c_high), None), y_ref, h_ref, n_refs,
    )
    lane = lane_index(pad)
    inlet_ref[...] = jnp.zeros_like(inlet_ref)

    def put(a, r, value):
        cell = a * plan.rows + r
        inlet_ref[...] = jnp.where(lane == cell * WINDOW, rolled(value, cell * WINDOW), inlet_ref[...])
        if a == 1:
            x1_ref[:, at(r)] = value

    def far_inlet(c):
        tile = low_ref[:, plan.slab :]
        count = CHUNK // LANES
        return jnp.concatenate([placed(tile, c * count + part) for part in range(count)], axis=1)

    outer_rows(plan, w_ref, own, near, (far_inlet, Layer(plan, high_ref).chunk), n_refs, h_ref, put)
    inlet = inlet_ref[...]
    inlet = jnp.where(parity() == 0, inlet, rolled(inlet, LANES // 2))
    back = pick(inlet, plan.window_spread()) * weight_ref[...]
    back = back + rolled(back, -plan.width)
    me = lax.axis_index("sector")
    send_ref[...] = jnp.zeros_like(send_ref)
    for t in range(plan.insts):
        to = lax.rem(me + plan.shift[t], plan.sectors)
        send_ref[to, : plan.fields, : plan.width] = back[t * plan.fields : (t + 1) * plan.fields, : plan.width]
    h0_ref[...] = h_ref[:, : plan.slab]
    for r in range(plan.rows):
        rest = jnp.zeros((RATES - 2, LANES), jnp.float32)
        rates_ref[:, at(r)] = jnp.concatenate([near[0].rate(C_AZ, r), own[0].rate(C_AZ, r), rest], axis=0)


def outer(plan, w_ref, rates_ref, n0_ref, h0_ref, x1_ref, far_ref, out_ref):
    mirror = parity()

    def put(a, r, value):
        there = jnp.where(mirror == 0, a, plan.ct - 1 - a) * plan.rows + r
        out_ref[pl.ds(there, plan.tf, stride=plan.cells), :] = value[: plan.tf]

    for r in range(plan.rows):
        put(1, r, x1_ref[:, at(r)])

    def near_chunk(c):
        lanes = slice(c * CHUNK, (c + 1) * CHUNK)
        return n0_ref[:, lanes] - rates_ref[0:1, lanes] * dot3(w_ref[...], far_ref[:, lanes])

    azimuthal(plan, w_ref, 0, near_chunk, lambda r, terms: put(0, r, h0_ref[:, at(r)] - rates_ref[1:2, at(r)] * terms))


def collect_panels(plan, got_ref, out_ref, panels_ref):
    me = lax.axis_index("sector")
    for t in range(plan.insts):
        source = lax.rem(me + (plan.sectors - plan.shift[t]), plan.sectors)
        panels_ref[t * RATES : (t + 1) * RATES, :] = got_ref[source]
    for f in range(plan.fields):
        tile = panels_ref[pl.ds(f, plan.insts, stride=RATES), : plan.width]
        out_ref[f] = jnp.transpose(tile)


def sibling(plan):
    return [s ^ 1 for s in range(plan.sectors)]


def outside(plan):
    return [(s - 1 if s % 2 == 0 else s + 1) % plan.sectors for s in range(plan.sectors)]


def swap(array, partner):
    return lax.ppermute(array, "sector", list(enumerate(partner)))


def beside(plan, array, partner):
    def pairs(step):
        out = []
        for s in range(plan.sectors):
            for x in range(plan.spans):
                to = 1 - x if plan.ends == 1 else x + step
                if 0 <= to < plan.spans:
                    out.append((s * plan.spans + x, partner[s] * plan.spans + to))
        return out

    if plan.ends == 1:
        return lax.ppermute(array, AXES, pairs(0))
    return jnp.concatenate([lax.ppermute(array[:1], AXES, pairs(-1)), lax.ppermute(array[1:], AXES, pairs(1))])


def on_device(
    sectors, spans,
    rhs, diag_coef, face_coef, time_coef, jac_up, jac_down, wall_mask, stator_adj, owner, first_panel_share,
):
    plan = Plan(rhs, stator_adj, sectors, spans)
    pad, cells, slab, insts, fields, ends = plan.pad, plan.cells, plan.slab, plan.insts, plan.fields, plan.ends
    bind = functools.partial
    whole, half = f32(pad, plan.ct * slab), f32(pad, slab)
    products = (vmem(6 * pad, slab),) * 2
    alone, next_chip, next_core = list(range(sectors)), outside(plan), sibling(plan)

    def edges(rows):
        return f32(ends, rows, DEPTH * plan.ct * LANES), f32(ends, rows, LANES), f32(ends, rows, LANES)

    stator = jnp.transpose(stator_adj, (1, 2, 3, 0)).reshape(fields, plan.width, insts)
    sent = call(bind(send_panels, plan), f32(sectors * spans, 2 * RATES, LANES), (vmem(insts * RATES, LANES),))(
        stator,
        jnp.concatenate([
            lax.rem(owner, plan.panels).astype(jnp.float32).reshape(insts, cells), first_panel_share.reshape(insts, cells),
        ], axis=1),
    )
    got = lax.all_to_all(sent, AXES, 0, 0, tiled=True)
    m, near, side, c0, c1 = call(
        bind(prepare, plan), (f32(pad + RATES, plan.ct * slab), f32(pad + RATES, slab)) + edges(pad + RATES)
    )(
        rhs.reshape(plan.tf * cells, LANES),
        jnp.concatenate([
            wall_mask.astype(jnp.float32).reshape(cells, LANES), diag_coef.reshape(cells, LANES),
            time_coef.reshape(cells, LANES), face_coef.reshape(3 * cells, LANES),
        ]),
    )
    low_first, high_first = swap(near, next_chip), swap(m, next_core)
    side_first = beside(plan, side, alone)
    c_low, c_high = beside(plan, c0, next_chip), beside(plan, c1, next_core)
    matrices, down, far = call(
        bind(stack_matrices, plan),
        [jax.ShapeDtypeStruct((count * pad, 3 * pad), jnp.bfloat16) for count in (7, 1)] + [half],
    )(m, high_first, jac_up, jac_down, plan.spectral(), plan.field_rows(), plan.field_lanes(), plan.block_diagonal())
    far_low = swap(far, next_chip)
    tiles = len(plan.tiles)
    seams, weight, force, g = call(
        bind(begin, plan), (f32(3, 1 + ends, pad, LANES), f32(pad, LANES), whole, whole),
        (vmem(pad, tiles * LANES), vmem(tiles * pad, LANES), vmem(16, tiles * LANES)) + products,
    )(matrices, m, got)
    h, n0, n1 = call(bind(middle_first, plan), (whole, half, half), products + (vmem(pad, 2 * slab),))(
        matrices, m, force, g, low_first, high_first, side_first, c_low, c_high, seams
    )
    x, near, side, c0, c1 = call(bind(outer_first, plan), (whole, f32(pad, slab + LANES)) + edges(pad))(
        matrices, m, low_first, high_first, n0, n1, h, far_low, seams
    )

    low, high = swap(near, next_chip), swap(x, next_core)
    side = beside(plan, side, alone)
    c_low, c_high = beside(plan, c0, next_chip), beside(plan, c1, next_core)
    g, far = call(bind(inner, plan), (whole, half), products, flops=2_000_000_000)(
        matrices, m, force, x, side
    )
    far_low = swap(far, next_chip)
    back, n0, h0, x1, rates = call(
        bind(middle, plan), (f32(sectors, RATES, LANES), half, half, half, f32(RATES, slab)),
        products + (vmem(pad, 2 * slab), vmem(pad, LANES), vmem(pad, 2 * slab), vmem(pad, slab)), flops=4_000_000_000,
    )(
        matrices, m, force, x, g, low, high, side, c_low, c_high, low_first, high_first, side_first, seams, weight
    )
    returned = lax.all_to_all(back, "sector", 0, 0, tiled=True)
    sens = call(bind(collect_panels, plan), f32(fields, plan.width, insts), (vmem(insts * RATES, LANES),))(returned)
    out = call(bind(outer, plan), f32(plan.tf * cells, LANES))(down, rates, n0, h0, x1, far_low)
    sens = jnp.transpose(sens.reshape(fields, plan.panels, plan.rows, insts), (3, 0, 1, 2))
    return out.reshape(rhs.shape), sens


def solution(mesh):
    in_specs = (
        P(None, None, "sector", "span", None),
        P("sector", "span", None),
        P(None, "sector", "span", None),
        P("sector", "span", None),
        P(),
        P(),
        P("sector", "span", None),
        P(None, None, "sector", "span"),
        P(None, "sector", "span"),
        P(None, "sector", "span"),
    )
    out_specs = (P(None, None, "sector", "span", None), P(None, None, "sector", "span"))
    return jax.shard_map(
        functools.partial(on_device, mesh.shape["sector"], mesh.shape["span"]),
        mesh=mesh, in_specs=in_specs, out_specs=out_specs, check_vma=False,
    )
```

```python
import functools

import jax
import jax.numpy as jnp
import ml_dtypes
import numpy as np
from jax import lax
from jax.experimental import pallas as pl
from jax.experimental.pallas import tpu as pltpu
from jax.sharding import PartitionSpec as P

SWEEPS = 4
DEPTH = 2
LANES = 128
CHUNK = 256
WINDOW = 8
HIGHEST = lax.Precision.HIGHEST
DOWN_AZ, SPECTRAL, UP_SP, DOWN_SP, UP_AX, DOWN_AX, UP_AZ = range(7)
C_TIME, C_AZ, C_SP, C_UP, C_DOWN, C_MASK, C_OTHER = range(7)
RATES = 8
GROUP = 3
AXES = ("sector", "span")


class Plan:
    def __init__(self, rhs, stator_adj, sectors, spans):
        self.insts, self.fields, self.ct, self.rows, self.nax = rhs.shape
        self.panels = stator_adj.shape[2]
        self.sectors, self.spans = sectors, spans
        self.tf = self.insts * self.fields
        self.pad = -(-self.tf // 16) * 16
        self.cells = self.ct * self.rows
        self.slab = self.rows * LANES
        self.width = self.panels * self.rows
        self.shift = [
            ((t * sectors) // (self.insts - 1) - t // (self.insts - 1)) % sectors for t in range(self.insts)
        ]
        assert self.ct == 2 and self.nax == LANES and SWEEPS % DEPTH == 0 and spans > 1
        assert len(set(self.shift)) == self.insts and self.cells * WINDOW == LANES and self.rows >= SWEEPS
        assert self.slab % CHUNK == 0 and 3 * self.pad <= 256 and 2 * self.ct * self.width == LANES
        assert sectors % 2 == 0
        self.ends = 1 if spans == 2 else 2
        self.blocks = [-1, 0, 1]
        self.halves = [0, 1] if spans == 2 else [-1, 0, 1]
        self.tiles = [(k, x) for k in self.blocks for x in self.halves]
        self.slots = [
            [t for t in range(self.insts) if any((k + self.shift[t]) % sectors == o for k in self.blocks)]
            for o in range(sectors)
        ]
        assert max(map(len, self.slots)) * self.width <= LANES

    def spectral(self):
        t = np.arange(self.insts)
        off = t[:, None] - t[None, :]
        sines = np.where(off == 0, 1.0, np.sin(np.pi * off / self.insts))
        table = np.where(off == 0, 0.0, 0.5 * (1.0 - 2.0 * (off % 2)) / sines).astype(np.float32)
        full = np.zeros((self.pad, self.pad), np.float32)
        full[: self.tf, : self.tf] = np.kron(table.T, np.eye(self.fields, dtype=np.float32))
        hi = full.astype(ml_dtypes.bfloat16)
        lo = (full - hi.astype(np.float32)).astype(ml_dtypes.bfloat16)
        return np.concatenate([hi, lo, hi], axis=1)

    def field_rows(self):
        out = np.zeros((self.pad, self.fields), np.float32)
        out[np.arange(self.tf), np.arange(self.tf) % self.fields] = 1.0
        return out

    def field_lanes(self):
        return np.tile(self.field_rows().T, (1, 3))

    def block_diagonal(self):
        block = np.full(self.pad, -1)
        block[: self.tf] = np.arange(self.tf) // self.fields
        same = (block[:, None] == block[None, :]) & (block[:, None] >= 0)
        return np.tile(same.astype(np.float32), (1, 3))


    def inst_rows(self):
        row, inst = table_index(self.pad, 16)
        return ((row >= inst * self.fields) & (row < (inst + 1) * self.fields)).astype(jnp.float32)

    def cell_of(self, lane):
        return lax.div(lane, self.width) * self.rows + lax.rem(lane, self.rows)

    def window_lanes(self):
        lane, to = table_index(LANES, LANES)
        return (lane < self.ct * self.width) & (to == self.cell_of(lane) * WINDOW)

    def window_spread(self):
        to, lane = table_index(LANES, LANES)
        return (lane < self.ct * self.width) & (to == self.cell_of(lane) * WINDOW)

    def weight_lanes(self):
        cell, lane = table_index(LANES, LANES)
        half = self.ct * self.width
        wanted = jnp.where(lane < half, self.cell_of(lane), self.cells + self.cell_of(lane - half))
        return cell == wanted

    def panel_lanes(self):
        lane = lane_index(1)
        panel = lax.rem(lax.div(lane, self.rows), self.panels)
        return jnp.where(lane < self.ct * self.width, panel, -9).astype(jnp.float32)


def table_index(rows, columns):
    return [lax.broadcasted_iota(jnp.int32, (rows, columns), axis) for axis in (0, 1)]


def call(kernel, out, scratch=(), flops=2_000_000, nbytes=1_000_000):
    return pl.pallas_call(
        kernel,
        out_shape=out,
        scratch_shapes=list(scratch),
        compiler_params=pltpu.CompilerParams(vmem_limit_bytes=20 * 1024 * 1024),
        cost_estimate=pl.CostEstimate(flops=flops, bytes_accessed=nbytes, transcendentals=0),
    )


def f32(*shape):
    return jax.ShapeDtypeStruct(shape, jnp.float32)


def vmem(*shape):
    return pltpu.VMEM(shape, jnp.float32)


def halves_of(x):
    hi = x.astype(jnp.bfloat16)
    return hi, (x - hi.astype(jnp.float32)).astype(jnp.bfloat16)


def dot3(w, x):
    hi, lo = halves_of(x)
    return jnp.dot(w, jnp.concatenate([hi, hi, lo], axis=0), preferred_element_type=jnp.float32)


def pick(x, table):
    table = table.astype(jnp.float32).astype(jnp.bfloat16)
    table = jnp.concatenate([table, table], axis=0)
    return jnp.dot(jnp.concatenate(halves_of(x), axis=1), table, preferred_element_type=jnp.float32)


def dot_full(a, b):
    return jnp.dot(a, b, precision=HIGHEST, preferred_element_type=jnp.float32)


def lane_index(rows):
    return lax.broadcasted_iota(jnp.int32, (rows, LANES), 1)


def rolled(x, by):
    by %= LANES
    return pltpu.roll(x, by, axis=1) if by else x


def at(r, count=1, start=0):
    return slice(start + r * LANES, start + (r + count) * LANES)


def parity():
    return lax.rem(lax.axis_index("sector"), 2)


def has_sides(plan):
    span = lax.axis_index("span")
    return jnp.where(span < plan.spans - 1, 1.0, 0.0), jnp.where(span > 0, 1.0, 0.0)


class Layer:
    def __init__(self, plan, ref, start=0, rates=None, seam=None, layer=0, scale=C_MASK):
        self.plan, self.ref, self.start, self.seam, self.layer, self.scale = plan, ref, start, seam, layer, scale
        self.rates = rates or (ref, start)

    def rate(self, which, r, count=1):
        ref, start = self.rates
        row = self.plan.pad + which
        return ref[row : row + 1, at(r, count, start)]

    def row(self, r):
        value = self.ref[: self.plan.pad, at(r, 1, self.start)]
        if self.seam is None:
            return value
        return value + placed(self.seam, self.layer * self.plan.rows + r) * self.rate(self.scale, r)

    def chunk(self, c):
        count = CHUNK // LANES
        if self.seam is None:
            return self.ref[: self.plan.pad, at(c * count, count, self.start)]
        return jnp.concatenate([self.row(c * count + part) for part in range(count)], axis=1)


def placed(tile, cell):
    return jnp.where(lane_index(tile.shape[0]) == 0, rolled(tile, -cell * WINDOW), 0.0)


class Products:
    def __init__(self, plan, w_ref, p_ref, first):
        self.plan, self.w, self.p, self.first = plan, w_ref, p_ref, first

    def fill(self, layer):
        for c in range(self.plan.slab // CHUNK):
            self.p[:, c * CHUNK : (c + 1) * CHUNK] = dot3(matrix(self.plan, self.w, self.first, 6), layer.chunk(c))
        self.layer = layer
        return self

    def get(self, block, r):
        row = (block - self.first) * self.plan.pad
        return self.p[row : row + self.plan.pad, at(r)]

    def own_terms(self, r):
        rate = self.layer.rate
        total = rate(C_TIME, r) * self.get(SPECTRAL, r)
        beside = []
        if r + 1 < self.plan.rows:
            beside.append(self.get(UP_SP, r + 1))
        if r > 0:
            beside.append(self.get(DOWN_SP, r - 1))
        total = total + rate(C_SP, r) * sum(beside[1:], beside[0])
        total = total + rate(C_UP, r) * rolled(self.get(UP_AX, r), -1)
        return total + rate(C_DOWN, r) * rolled(self.get(DOWN_AX, r), 1)


def matrix(plan, w_ref, block, count=1):
    return w_ref[block * plan.pad : (block + count) * plan.pad, :]


def two_layers(plan, ref, rates=None, seam=None):
    return [
        Layer(plan, ref, a * plan.slab, (rates, a * plan.slab) if rates is not None else None, seam, a)
        for a in range(plan.ct)
    ]


def inner_rows(plan, w_ref, p_refs, layers, force, g_ref):
    first = Products(plan, w_ref, p_refs[0], DOWN_AZ).fill(layers[0])
    second = Products(plan, w_ref, p_refs[1], SPECTRAL).fill(layers[1])
    for r in range(plan.rows):
        other = second.get(UP_AZ, r), first.get(DOWN_AZ, r)
        for a, products in enumerate((first, second)):
            total = products.own_terms(r) + layers[a].rate(C_AZ, r) * other[a]
            g_ref[:, at(r, 1, a * plan.slab)] = force[a].row(r) - total


def azimuthal(plan, w_ref, block, chunk_of, take):
    for c in range(plan.slab // CHUNK):
        terms = dot3(matrix(plan, w_ref, block), chunk_of(c))
        for part in range(CHUNK // LANES):
            take(c * (CHUNK // LANES) + part, terms[:, at(part)])


def middle_rows(plan, w_ref, p_refs, own, own_force, g_ref, near, near_force, side, corner, y_ref, h_ref, n_refs):
    pad, rows, ct = plan.pad, plan.rows, plan.ct
    outward, inward, last = (UP_SP, DOWN_SP), (DOWN_SP, UP_SP), (rows - 1, 0)
    edge_terms, edge_new, corner_terms = [], [], []
    for n in range(2):
        first, second, edge_force, edge_rate = side(n)
        corners = corner(n)
        every = dot3(w_ref[...], first)
        edge_terms.append(every[outward[n] * pad : (outward[n] + 1) * pad])
        corner_terms.append([dot3(matrix(plan, w_ref, outward[n]), c) for c in corners])
        beyond = dot3(matrix(plan, w_ref, outward[n]), second)
        within = dot3(matrix(plan, w_ref, inward[n]), jnp.concatenate([x.row(last[n]) for x in own], axis=1))
        from_low = dot3(matrix(plan, w_ref, DOWN_AZ), corners[0])
        from_high = dot3(matrix(plan, w_ref, UP_AZ), corners[1])
        new = []
        for a in range(ct):

            def part(block, b=a):
                return every[block * pad : (block + 1) * pad, at(b)]

            around = part(UP_AZ, 1) + from_low if a == 0 else from_high + part(DOWN_AZ, 0)
            total = edge_rate(C_TIME, a) * part(SPECTRAL) + edge_rate(C_AZ, a) * around
            total = total + edge_rate(C_SP, a) * (beyond[:, at(a)] + within[:, at(a)])
            total = total + edge_rate(C_UP, a) * rolled(part(UP_AX), -1)
            total = total + edge_rate(C_DOWN, a) * rolled(part(DOWN_AX), 1)
            new.append(edge_force[:, at(a)] - total)
        edge_new.append(dot3(matrix(plan, w_ref, outward[n]), jnp.concatenate(new, axis=1)))

    products = (
        Products(plan, w_ref, p_refs[0], DOWN_AZ).fill(near[0]), Products(plan, w_ref, p_refs[1], SPECTRAL).fill(near[1]),
    )
    for a, (to_own, to_near) in enumerate(((DOWN_AZ, UP_AZ), (UP_AZ, DOWN_AZ))):

        def take(r, terms):
            total = products[a].own_terms(r) + near[a].rate(C_AZ, r) * terms
            mine = own[a].rate(C_AZ, r) * products[a].get(to_own, r)
            for n in range(2):
                if r == last[n]:
                    total = total + near[a].rate(C_SP, r) * corner_terms[n][a]
                    mine = mine + own[a].rate(C_SP, r) * edge_terms[n][:, at(a)]
            n_refs[a][:, at(r)] = near_force[a].row(r) - total
            lanes = at(r, 1, a * plan.slab)
            y_ref[:, lanes] = g_ref[:, lanes] - mine

        azimuthal(plan, w_ref, to_near, own[a].chunk, take)

    after = [Layer(plan, y_ref, a * plan.slab, own[a].rates) for a in range(ct)]
    inner_rows(plan, w_ref, p_refs, after, own_force, h_ref)
    for a in range(ct):
        for n in range(2):
            lanes = at(last[n], 1, a * plan.slab)
            h_ref[:, lanes] -= own[a].rate(C_SP, last[n]) * edge_new[n][:, at(a)]


def outer_rows(plan, w_ref, own, near, far_chunks, n_refs, h_ref, put, layers=(0, 1)):
    count = CHUNK // LANES
    for a in layers:
        block = (DOWN_AZ, UP_AZ)[a]

        def near_chunk(c):
            terms = dot3(matrix(plan, w_ref, block), far_chunks[a](c))
            return n_refs[a][:, at(c * count, count)] - near[a].rate(C_AZ, c * count, count) * terms

        def take(r, terms):
            put(a, r, h_ref[:, at(r, 1, a * plan.slab)] - own[a].rate(C_AZ, r) * terms)

        azimuthal(plan, w_ref, block, near_chunk, take)


def sides_of(plan, side_ref, force_ref, seams_ref):
    pad, ct = plan.pad, plan.ct
    keeps = has_sides(plan)

    def read(n, ref, e, seam):
        i = n if plan.ends == 2 else 0
        value = ref[i, :pad, at(e * ct, ct)]
        if seam:
            r = e if n == 0 else plan.rows - 1 - e
            tile = seams_ref[1, 1 + i]
            scale = ref[i, pad + C_MASK : pad + C_MASK + 1, at(e * ct, ct)]
            value = value + jnp.concatenate([placed(tile, a * plan.rows + r) for a in range(ct)], axis=1) * scale
        return value * keeps[n]

    def side(n):
        i = n if plan.ends == 2 else 0
        same = side_ref is force_ref

        def rate(which, a):
            return force_ref[i, pad + which : pad + which + 1, at(a)] * keeps[n]

        force = read(n, force_ref, 0, True)
        first = force if same else read(n, side_ref, 0, False)
        return first, read(n, side_ref, 1, same), force, rate

    return side


def corners_of(plan, c_refs, seams_ref):
    keeps = has_sides(plan)

    def corner(n):
        i = n if plan.ends == 2 else 0
        out = []
        for a, c_ref in enumerate(c_refs):
            value = c_ref[i, : plan.pad]
            if seams_ref is not None:
                r = 0 if n == 0 else plan.rows - 1
                scale = c_ref[i, plan.pad + C_MASK : plan.pad + C_MASK + 1]
                value = value + placed(seams_ref[2 * a, 1 + i], a * plan.rows + r) * scale
            out.append(value * keeps[n])
        return out

    return corner


def prepare(plan, rhs_ref, coef_ref, m_ref, near_ref, side_ref, c0_ref, c1_ref):
    pad = plan.pad
    lane = lane_index(1)
    tail = jnp.zeros((pad - plan.tf, LANES), jnp.float32)
    mirror = parity()

    def coefs(a, r):
        there = jnp.where(mirror == 0, a, plan.ct - 1 - a) * plan.rows + r
        mask, diag, *rest = [coef_ref[pl.ds(there + plan.cells * i, 1), :] for i in range(6)]
        return there, mask / diag, rest

    for r in range(plan.rows):
        scales = [coefs(a, r)[1] for a in range(plan.ct)]
        for a in range(plan.ct):
            there, scale, (time, *face) = coefs(a, r)
            axial = scale * face[2]
            rates = jnp.concatenate([
                scale * time, scale * face[0], scale * face[1],
                jnp.where(lane < LANES - 1, axial, 0.0), jnp.where(lane > 0, axial, 0.0), scale, scales[1 - a],
                jnp.zeros((RATES - 7, LANES), jnp.float32),
            ], axis=0)
            field = jnp.concatenate([rhs_ref[pl.ds(there, plan.tf, stride=plan.cells), :], tail], axis=0) * scale
            lanes = at(a * plan.rows + r)
            m_ref[:pad, lanes] = field
            m_ref[pad:, lanes] = rates
            if a == 0:
                near_ref[:pad, lanes] = field
                near_ref[pad:, lanes] = rates
    write_edges(plan, m_ref, side_ref, (c0_ref, c1_ref))


def write_edges(plan, x_ref, side_ref, c_refs):
    first = lax.axis_index("span") == 0
    for a in range(plan.ct):
        for e in range(DEPTH):
            low, high = x_ref[:, at(a * plan.rows + e)], x_ref[:, at((a + 1) * plan.rows - 1 - e)]
            ends = [jnp.where(first, high, low)] if plan.ends == 1 else [low, high]
            for n, end in enumerate(ends):
                side_ref[n, :, at(e * plan.ct + a)] = end
                if e == 0:
                    c_refs[a][n] = end


def stack_matrices(plan, up_ref, down_ref, spectral_ref, rows_ref, lanes_ref, diagonal_ref, out_ref, down_out):
    pad = plan.pad
    lane = lax.broadcasted_iota(jnp.int32, (pad, 3 * pad), 1)
    second = (lane >= pad) & (lane < 2 * pad)
    out_ref[SPECTRAL * pad : (SPECTRAL + 1) * pad, :] = spectral_ref[...]
    even = parity() == 0
    for block, small in (
        (DOWN_AZ, jnp.where(even, down_ref[0], up_ref[0])), (UP_AZ, jnp.where(even, up_ref[0], down_ref[0])),
        (UP_SP, up_ref[1]), (DOWN_SP, down_ref[1]), (UP_AX, up_ref[2]), (DOWN_AX, down_ref[2]),
    ):
        full = dot_full(dot_full(rows_ref[...], small), lanes_ref[...]) * diagonal_ref[...]
        hi = full.astype(jnp.bfloat16).astype(jnp.float32)
        out_ref[block * pad : (block + 1) * pad, :] = jnp.where(second, full - hi, hi).astype(jnp.bfloat16)
    down_out[...] = matrix(plan, out_ref, DOWN_AZ)


def hold_far(plan, m_ref, low_ref, high_ref, far_ref):
    far_ref[...] = m_ref[: plan.pad, plan.slab :] + 0.0 * (low_ref[0:1, 0:1] + high_ref[0:1, 0:1])


def send_panels(plan, stator_ref, both_ref, out_ref, panels_ref):
    me = lax.axis_index("sector")
    for f in range(plan.fields):
        panels_ref[pl.ds(f, plan.insts, stride=RATES), : plan.width] = jnp.transpose(stator_ref[f])
    out_ref[...] = jnp.zeros_like(out_ref)
    both = both_ref[...]
    for t in range(plan.insts):
        group, row = divmod(t, GROUP)
        lanes = slice(group * 2 * plan.cells, (group + 1) * 2 * plan.cells)
        row += RATES
        out_ref[:, row : row + 1, lanes] = jnp.broadcast_to(both[t : t + 1][None], (out_ref.shape[0], 1, 2 * plan.cells))
    for o, slots in enumerate(plan.slots):
        to = lax.rem(me + (plan.sectors - o), plan.sectors) * plan.spans
        for slot, t in enumerate(slots):
            lanes = slice(slot * plan.width, (slot + 1) * plan.width)
            panels = panels_ref[t * RATES : t * RATES + plan.fields, : plan.width]
            for x in range(plan.spans):
                out_ref[to + x, : plan.fields, lanes] = panels


def begin(
    plan, w_ref, m_ref, got_ref,
    seams_ref, weight_ref, x_ref, g_ref, panels_ref, terms_ref, rows_ref, p0_ref, p1_ref,
):
    pad, insts, fields = plan.pad, plan.insts, plan.fields
    me, span = lax.axis_index("sector"), lax.axis_index("span")
    tiles = plan.tiles
    panels_ref[...] = jnp.zeros_like(panels_ref)
    rows_ref[...] = jnp.zeros_like(rows_ref)
    wide = 2 * plan.cells
    for n, (k, x) in enumerate(tiles):
        at_span = x if plan.spans == 2 else jnp.clip(span + x, 0, plan.spans - 1)
        for t in range(insts):
            o = (k + plan.shift[t]) % plan.sectors
            source = lax.rem(me + o, plan.sectors) * plan.spans + at_span
            tile = rolled(got_ref[source, :RATES], -plan.slots[o].index(t) * plan.width)
            panels_ref[t * fields : (t + 1) * fields, n * LANES : n * LANES + plan.width] = tile[:fields, : plan.width]
        source = lax.rem(me + k + plan.sectors, plan.sectors) * plan.spans + at_span
        table = got_ref[source, RATES:]
        for group in range(-(-insts // GROUP)):
            shifted = rolled(table, -group * wide)
            rows_ref[group * GROUP : (group + 1) * GROUP, n * LANES : n * LANES + wide] = shifted[:GROUP, :wide]
    spread = dot_full(plan.inst_rows(), rows_ref[...])
    spread = pick(jnp.concatenate([spread[:, at(n)] for n in range(len(tiles))], axis=0), plan.weight_lanes())
    first, share, panel = spread, rolled(spread, plan.ct * plan.width), plan.panel_lanes()
    lower = (jnp.abs(first - panel) < 0.5).astype(jnp.float32)
    upper = (jnp.abs(first + 1.0 - panel) < 0.5).astype(jnp.float32)
    weights = share * lower + (1.0 - share) * upper
    for n in range(len(tiles)):
        panels = panels_ref[:, at(n)]
        terms_ref[n * pad : (n + 1) * pad, :] = panels + rolled(panels, plan.width)
    seams = pick(terms_ref[...] * weights, plan.window_lanes())

    even = parity() == 0
    is_first = span == 0

    def tile(values, k, x):
        n = tiles.index((k, x))
        return values[n * pad : (n + 1) * pad]

    def around(values, k):
        if plan.spans == 2:
            pair = tile(values, k, 0), tile(values, k, 1)
            return [jnp.where(is_first, pair[0], pair[1]), jnp.where(is_first, pair[1], pair[0])]
        return [tile(values, k, x) for x in (0, 1, -1)]

    def mirrored(value):
        return rolled(value, LANES // 2)

    here = around(seams, 0)
    behind, ahead = around(seams, -1), around(seams, 1)
    for i in range(1 + plan.ends):
        seams_ref[0, i] = jnp.where(even, mirrored(behind[i]), ahead[i])
        seams_ref[1, i] = jnp.where(even, here[i], mirrored(here[i]))
        seams_ref[2, i] = jnp.where(even, mirrored(ahead[i]), behind[i])
    weight_ref[...] = around(weights, 0)[0]

    for layer in two_layers(plan, m_ref, seam=seams_ref[1, 0]):
        for r in range(plan.rows):
            x_ref[:, at(r, 1, layer.start)] = layer.row(r)
    layers = two_layers(plan, x_ref, m_ref)
    inner_rows(plan, w_ref, (p0_ref, p1_ref), layers, layers, g_ref)


def middle_first(
    plan, w_ref, m_ref, f_ref, g_ref, low_ref, high_ref, side_ref, c_low, c_high, seams_ref,
    h_ref, n0_ref, n1_ref, p0_ref, p1_ref, y_ref,
):
    own = two_layers(plan, f_ref, m_ref)
    near = (
        Layer(plan, low_ref, 0, None, seams_ref[0, 0], 0), Layer(plan, high_ref, plan.slab, None, seams_ref[2, 0], 1),
    )
    middle_rows(
        plan, w_ref, (p0_ref, p1_ref), own, own, g_ref, near, near, sides_of(plan, side_ref, side_ref, seams_ref),
        corners_of(plan, (c_low, c_high), seams_ref), y_ref, h_ref, (n0_ref, n1_ref),
    )


def outer_first(
    plan, w_ref, m_ref, low_first, high_first, n0_ref, n1_ref, h_ref, far_ref, seams_ref,
    x_ref, near_ref, side_out, c0_ref, c1_ref,
):
    own = two_layers(plan, m_ref)
    near = Layer(plan, low_first), Layer(plan, high_first, plan.slab)
    far_low = Layer(plan, far_ref, 0, (low_first, 0), seams_ref[0, 0], 1, C_OTHER)
    far_high = Layer(plan, high_first, 0, None, seams_ref[2, 0], 0)
    lane = lane_index(plan.pad)
    near_ref[:, plan.slab :] = jnp.zeros((plan.pad, LANES), jnp.float32)

    def put(a, r, value):
        x_ref[:, at(r, 1, a * plan.slab)] = value
        if a == 0:
            near_ref[:, at(r)] = value
        else:
            here = rolled(value, r * WINDOW)
            near_ref[:, plan.slab :] = jnp.where(lane == r * WINDOW, here, near_ref[:, plan.slab :])

    outer_rows(plan, w_ref, own, near, (far_low.chunk, far_high.chunk), (n0_ref, n1_ref), h_ref, put)
    write_edges(plan, x_ref, side_out, (c0_ref, c1_ref))


def inner(plan, w_ref, m_ref, f_ref, x_ref, side_ref, g_ref, far_ref, p0_ref, p1_ref):
    far_ref[...] = x_ref[:, plan.slab :] + 0.0 * side_ref[0, 0:1, 0:1]
    inner_rows(plan, w_ref, (p0_ref, p1_ref), two_layers(plan, x_ref, m_ref), two_layers(plan, f_ref, m_ref), g_ref)


def middle(
    plan, w_ref, m_ref, f_ref, x_ref, g_ref, low_ref, high_ref, side_ref, c_low, c_high,
    low_first, high_first, side_first, seams_ref, weight_ref,
    send_ref, n0_ref, h0_ref, x1_ref, rates_ref, p0_ref, p1_ref, y_ref, inlet_ref, h_ref, n1_ref,
):
    pad = plan.pad
    own, force = two_layers(plan, x_ref, m_ref), two_layers(plan, f_ref, m_ref)
    low_force = Layer(plan, low_first, 0, None, seams_ref[0, 0], 0)
    high_force = Layer(plan, high_first, plan.slab, None, seams_ref[2, 0], 1)
    near = Layer(plan, low_ref, 0, low_force.rates), Layer(plan, high_ref, plan.slab, high_force.rates)
    n_refs = n0_ref, n1_ref
    middle_rows(
        plan, w_ref, (p0_ref, p1_ref), own, force, g_ref, near, (low_force, high_force),
        sides_of(plan, side_ref, side_first, seams_ref), corners_of(plan, (c_low, c_high), None), y_ref, h_ref, n_refs,
    )
    lane = lane_index(pad)
    inlet_ref[...] = jnp.zeros_like(inlet_ref)

    def put(a, r, value):
        cell = a * plan.rows + r
        inlet_ref[...] = jnp.where(lane == cell * WINDOW, rolled(value, cell * WINDOW), inlet_ref[...])
        if a == 1:
            x1_ref[:, at(r)] = value

    def far_inlet(c):
        tile = low_ref[:, plan.slab :]
        count = CHUNK // LANES
        return jnp.concatenate([placed(tile, c * count + part) for part in range(count)], axis=1)

    outer_rows(plan, w_ref, own, near, (far_inlet, Layer(plan, high_ref).chunk), n_refs, h_ref, put)
    inlet = inlet_ref[...]
    inlet = jnp.where(parity() == 0, inlet, rolled(inlet, LANES // 2))
    back = pick(inlet, plan.window_spread()) * weight_ref[...]
    back = back + rolled(back, -plan.width)
    me = lax.axis_index("sector")
    send_ref[...] = jnp.zeros_like(send_ref)
    for t in range(plan.insts):
        to = lax.rem(me + plan.shift[t], plan.sectors)
        send_ref[to, : plan.fields, : plan.width] = back[t * plan.fields : (t + 1) * plan.fields, : plan.width]
    h0_ref[...] = h_ref[:, : plan.slab]
    for r in range(plan.rows):
        rest = jnp.zeros((RATES - 2, LANES), jnp.float32)
        rates_ref[:, at(r)] = jnp.concatenate([near[0].rate(C_AZ, r), own[0].rate(C_AZ, r), rest], axis=0)


def outer(plan, w_ref, rates_ref, n0_ref, h0_ref, x1_ref, far_ref, out_ref):
    mirror = parity()

    def put(a, r, value):
        there = jnp.where(mirror == 0, a, plan.ct - 1 - a) * plan.rows + r
        out_ref[pl.ds(there, plan.tf, stride=plan.cells), :] = value[: plan.tf]

    for r in range(plan.rows):
        put(1, r, x1_ref[:, at(r)])

    def near_chunk(c):
        lanes = slice(c * CHUNK, (c + 1) * CHUNK)
        return n0_ref[:, lanes] - rates_ref[0:1, lanes] * dot3(w_ref[...], far_ref[:, lanes])

    azimuthal(plan, w_ref, 0, near_chunk, lambda r, terms: put(0, r, h0_ref[:, at(r)] - rates_ref[1:2, at(r)] * terms))


def collect_panels(plan, got_ref, out_ref, panels_ref):
    me = lax.axis_index("sector")
    for t in range(plan.insts):
        source = lax.rem(me + (plan.sectors - plan.shift[t]), plan.sectors)
        panels_ref[t * RATES : (t + 1) * RATES, :] = got_ref[source]
    for f in range(plan.fields):
        tile = panels_ref[pl.ds(f, plan.insts, stride=RATES), : plan.width]
        out_ref[f] = jnp.transpose(tile)


def sibling(plan):
    return [s ^ 1 for s in range(plan.sectors)]


def outside(plan):
    return [(s - 1 if s % 2 == 0 else s + 1) % plan.sectors for s in range(plan.sectors)]


def swap(array, partner):
    return lax.ppermute(array, "sector", list(enumerate(partner)))


def beside(plan, array, partner):
    def pairs(step):
        out = []
        for s in range(plan.sectors):
            for x in range(plan.spans):
                to = 1 - x if plan.ends == 1 else x + step
                if 0 <= to < plan.spans:
                    out.append((s * plan.spans + x, partner[s] * plan.spans + to))
        return out

    if plan.ends == 1:
        return lax.ppermute(array, AXES, pairs(0))
    return jnp.concatenate([lax.ppermute(array[:1], AXES, pairs(-1)), lax.ppermute(array[1:], AXES, pairs(1))])


def on_device(
    sectors, spans,
    rhs, diag_coef, face_coef, time_coef, jac_up, jac_down, wall_mask, stator_adj, owner, first_panel_share,
):
    plan = Plan(rhs, stator_adj, sectors, spans)
    pad, cells, slab, insts, fields, ends = plan.pad, plan.cells, plan.slab, plan.insts, plan.fields, plan.ends
    bind = functools.partial
    whole, half = f32(pad, plan.ct * slab), f32(pad, slab)
    products = (vmem(6 * pad, slab),) * 2
    alone, next_chip, next_core = list(range(sectors)), outside(plan), sibling(plan)

    def edges(rows):
        return f32(ends, rows, DEPTH * plan.ct * LANES), f32(ends, rows, LANES), f32(ends, rows, LANES)

    stator = jnp.transpose(stator_adj, (1, 2, 3, 0)).reshape(fields, plan.width, insts)
    sent = call(bind(send_panels, plan), f32(sectors * spans, 2 * RATES, LANES), (vmem(insts * RATES, LANES),))(
        stator,
        jnp.concatenate([
            lax.rem(owner, plan.panels).astype(jnp.float32).reshape(insts, cells), first_panel_share.reshape(insts, cells),
        ], axis=1),
    )
    got = lax.all_to_all(sent, AXES, 0, 0, tiled=True)
    m, near, side, c0, c1 = call(
        bind(prepare, plan), (f32(pad + RATES, plan.ct * slab), f32(pad + RATES, slab)) + edges(pad + RATES)
    )(
        rhs.reshape(plan.tf * cells, LANES),
        jnp.concatenate([
            wall_mask.astype(jnp.float32).reshape(cells, LANES), diag_coef.reshape(cells, LANES),
            time_coef.reshape(cells, LANES), face_coef.reshape(3 * cells, LANES),
        ]),
    )
    low_first, high_first = swap(near, next_chip), swap(m, next_core)
    side_first = beside(plan, side, alone)
    c_low, c_high = beside(plan, c0, next_chip), beside(plan, c1, next_core)
    far_low = swap(call(bind(hold_far, plan), half)(m, low_first, high_first), next_chip)
    matrices, down = call(
        bind(stack_matrices, plan),
        [jax.ShapeDtypeStruct((count * pad, 3 * pad), jnp.bfloat16) for count in (7, 1)],
    )(jac_up, jac_down, plan.spectral(), plan.field_rows(), plan.field_lanes(), plan.block_diagonal())
    tiles = len(plan.tiles)
    seams, weight, force, g = call(
        bind(begin, plan), (f32(3, 1 + ends, pad, LANES), f32(pad, LANES), whole, whole),
        (vmem(pad, tiles * LANES), vmem(tiles * pad, LANES), vmem(16, tiles * LANES)) + products,
    )(matrices, m, got)
    h, n0, n1 = call(bind(middle_first, plan), (whole, half, half), products + (vmem(pad, 2 * slab),))(
        matrices, m, force, g, low_first, high_first, side_first, c_low, c_high, seams
    )
    x, near, side, c0, c1 = call(bind(outer_first, plan), (whole, f32(pad, slab + LANES)) + edges(pad))(
        matrices, m, low_first, high_first, n0, n1, h, far_low, seams
    )

    low, high = swap(near, next_chip), swap(x, next_core)
    side = beside(plan, side, alone)
    c_low, c_high = beside(plan, c0, next_chip), beside(plan, c1, next_core)
    g, far = call(bind(inner, plan), (whole, half), products, flops=2_000_000_000)(
        matrices, m, force, x, side
    )
    far_low = swap(far, next_chip)
    back, n0, h0, x1, rates = call(
        bind(middle, plan), (f32(sectors, RATES, LANES), half, half, half, f32(RATES, slab)),
        products + (vmem(pad, 2 * slab), vmem(pad, LANES), vmem(pad, 2 * slab), vmem(pad, slab)), flops=4_000_000_000,
    )(
        matrices, m, force, x, g, low, high, side, c_low, c_high, low_first, high_first, side_first, seams, weight
    )
    returned = lax.all_to_all(back, "sector", 0, 0, tiled=True)
    sens = call(bind(collect_panels, plan), f32(fields, plan.width, insts), (vmem(insts * RATES, LANES),))(returned)
    out = call(bind(outer, plan), f32(plan.tf * cells, LANES))(down, rates, n0, h0, x1, far_low)
    sens = jnp.transpose(sens.reshape(fields, plan.panels, plan.rows, insts), (3, 0, 1, 2))
    return out.reshape(rhs.shape), sens


def solution(mesh):
    in_specs = (
        P(None, None, "sector", "span", None),
        P("sector", "span", None),
        P(None, "sector", "span", None),
        P("sector", "span", None),
        P(),
        P(),
        P("sector", "span", None),
        P(None, None, "sector", "span"),
        P(None, "sector", "span"),
        P(None, "sector", "span"),
    )
    out_specs = (P(None, None, "sector", "span", None), P(None, None, "sector", "span"))
    return jax.shard_map(
        functools.partial(on_device, mesh.shape["sector"], mesh.shape["span"]),
        mesh=mesh, in_specs=in_specs, out_specs=out_specs, check_vma=False,
    )
```

```python
import functools

import jax
import jax.numpy as jnp
import ml_dtypes
import numpy as np
from jax import lax
from jax.experimental import pallas as pl
from jax.experimental.pallas import tpu as pltpu
from jax.sharding import PartitionSpec as P

SWEEPS = 4
DEPTH = 2
LANES = 128
CHUNK = 256
WINDOW = 8
HIGHEST = lax.Precision.HIGHEST
DOWN_AZ, SPECTRAL, UP_SP, DOWN_SP, UP_AX, DOWN_AX, UP_AZ = range(7)
C_TIME, C_AZ, C_SP, C_UP, C_DOWN, C_MASK, C_OTHER, C_OWNER = range(8)
RATES = 8
AXES = ("sector", "span")


class Plan:
    def __init__(self, rhs, stator_adj, sectors, spans):
        self.insts, self.fields, self.ct, self.rows, self.nax = rhs.shape
        self.panels = stator_adj.shape[2]
        self.sectors, self.spans = sectors, spans
        self.tf = self.insts * self.fields
        self.pad = -(-self.tf // 16) * 16
        self.cells = self.ct * self.rows
        self.slab = self.rows * LANES
        self.width = self.panels * self.rows
        self.shift = [
            ((t * sectors) // (self.insts - 1) - t // (self.insts - 1)) % sectors for t in range(self.insts)
        ]
        assert self.ct == 2 and self.nax == LANES and SWEEPS % DEPTH == 0 and spans > 1
        assert len(set(self.shift)) == self.insts and self.cells * WINDOW == LANES and self.rows >= SWEEPS
        assert self.slab % CHUNK == 0 and 3 * self.pad <= 256 and 2 * self.ct * self.width == LANES
        assert sectors % 2 == 0
        self.ends = 1 if spans == 2 else 2
        self.blocks = [-1, 0, 1]
        self.halves = [0, 1] if spans == 2 else [-1, 0, 1]
        self.tiles = [(k, x) for k in self.blocks for x in self.halves]
        self.slots = [
            [t for t in range(self.insts) if any((k + self.shift[t]) % sectors == o for k in self.blocks)]
            for o in range(sectors)
        ]
        assert max(map(len, self.slots)) * self.width <= LANES

    def spectral(self):
        t = np.arange(self.insts)
        off = t[:, None] - t[None, :]
        sines = np.where(off == 0, 1.0, np.sin(np.pi * off / self.insts))
        table = np.where(off == 0, 0.0, 0.5 * (1.0 - 2.0 * (off % 2)) / sines).astype(np.float32)
        full = np.zeros((self.pad, self.pad), np.float32)
        full[: self.tf, : self.tf] = np.kron(table.T, np.eye(self.fields, dtype=np.float32))
        hi = full.astype(ml_dtypes.bfloat16)
        lo = (full - hi.astype(np.float32)).astype(ml_dtypes.bfloat16)
        return np.concatenate([hi, lo, hi], axis=1)

    def field_rows(self):
        out = np.zeros((self.pad, self.fields), np.float32)
        out[np.arange(self.tf), np.arange(self.tf) % self.fields] = 1.0
        return out

    def field_lanes(self):
        return np.tile(self.field_rows().T, (1, 3))

    def block_diagonal(self):
        block = np.full(self.pad, -1)
        block[: self.tf] = np.arange(self.tf) // self.fields
        same = (block[:, None] == block[None, :]) & (block[:, None] >= 0)
        return np.tile(same.astype(np.float32), (1, 3))


    def inst_rows(self):
        row, inst = table_index(self.pad, 16)
        return ((row >= inst * self.fields) & (row < (inst + 1) * self.fields)).astype(jnp.float32)

    def cell_of(self, lane):
        return lax.div(lane, self.width) * self.rows + lax.rem(lane, self.rows)

    def window_lanes(self):
        lane, to = table_index(LANES, LANES)
        return (lane < self.ct * self.width) & (to == self.cell_of(lane) * WINDOW)

    def window_spread(self):
        to, lane = table_index(LANES, LANES)
        return (lane < self.ct * self.width) & (to == self.cell_of(lane) * WINDOW)

    def weight_lanes(self):
        cell, lane = table_index(LANES, LANES)
        half = self.ct * self.width
        wanted = jnp.where(lane < half, self.cell_of(lane), self.cells + self.cell_of(lane - half))
        return cell == wanted

    def panel_lanes(self):
        lane = lane_index(1)
        panel = lax.rem(lax.div(lane, self.rows), self.panels)
        return jnp.where(lane < self.ct * self.width, panel, -9).astype(jnp.float32)


def table_index(rows, columns):
    return [lax.broadcasted_iota(jnp.int32, (rows, columns), axis) for axis in (0, 1)]


def call(kernel, out, scratch=(), flops=2_000_000, nbytes=1_000_000):
    return pl.pallas_call(
        kernel,
        out_shape=out,
        scratch_shapes=list(scratch),
        compiler_params=pltpu.CompilerParams(vmem_limit_bytes=20 * 1024 * 1024),
        cost_estimate=pl.CostEstimate(flops=flops, bytes_accessed=nbytes, transcendentals=0),
    )


def f32(*shape):
    return jax.ShapeDtypeStruct(shape, jnp.float32)


def vmem(*shape):
    return pltpu.VMEM(shape, jnp.float32)


def halves_of(x):
    hi = x.astype(jnp.bfloat16)
    return hi, (x - hi.astype(jnp.float32)).astype(jnp.bfloat16)


def dot3(w, x):
    hi, lo = halves_of(x)
    return jnp.dot(w, jnp.concatenate([hi, hi, lo], axis=0), preferred_element_type=jnp.float32)


def pick(x, table):
    table = table.astype(jnp.float32).astype(jnp.bfloat16)
    table = jnp.concatenate([table, table], axis=0)
    return jnp.dot(jnp.concatenate(halves_of(x), axis=1), table, preferred_element_type=jnp.float32)


def dot_full(a, b):
    return jnp.dot(a, b, precision=HIGHEST, preferred_element_type=jnp.float32)


def lane_index(rows):
    return lax.broadcasted_iota(jnp.int32, (rows, LANES), 1)


def rolled(x, by):
    by %= LANES
    return pltpu.roll(x, by, axis=1) if by else x


def at(r, count=1, start=0):
    return slice(start + r * LANES, start + (r + count) * LANES)


def parity():
    return lax.rem(lax.axis_index("sector"), 2)


def has_sides(plan):
    span = lax.axis_index("span")
    return jnp.where(span < plan.spans - 1, 1.0, 0.0), jnp.where(span > 0, 1.0, 0.0)


class Layer:
    def __init__(self, plan, ref, start=0, rates=None, seam=None, layer=0, scale=C_MASK):
        self.plan, self.ref, self.start, self.seam, self.layer, self.scale = plan, ref, start, seam, layer, scale
        self.rates = rates or (ref, start)

    def rate(self, which, r, count=1):
        ref, start = self.rates
        row = self.plan.pad + which
        return ref[row : row + 1, at(r, count, start)]

    def row(self, r):
        value = self.ref[: self.plan.pad, at(r, 1, self.start)]
        if self.seam is None:
            return value
        return value + placed(self.seam, self.layer * self.plan.rows + r) * self.rate(self.scale, r)

    def chunk(self, c):
        count = CHUNK // LANES
        if self.seam is None:
            return self.ref[: self.plan.pad, at(c * count, count, self.start)]
        return jnp.concatenate([self.row(c * count + part) for part in range(count)], axis=1)


def placed(tile, cell):
    return jnp.where(lane_index(tile.shape[0]) == 0, rolled(tile, -cell * WINDOW), 0.0)


class Products:
    def __init__(self, plan, w_ref, p_ref, first):
        self.plan, self.w, self.p, self.first = plan, w_ref, p_ref, first

    def fill(self, layer):
        for c in range(self.plan.slab // CHUNK):
            self.p[:, c * CHUNK : (c + 1) * CHUNK] = dot3(matrix(self.plan, self.w, self.first, 6), layer.chunk(c))
        self.layer = layer
        return self

    def get(self, block, r):
        row = (block - self.first) * self.plan.pad
        return self.p[row : row + self.plan.pad, at(r)]

    def own_terms(self, r):
        rate = self.layer.rate
        total = rate(C_TIME, r) * self.get(SPECTRAL, r)
        beside = []
        if r + 1 < self.plan.rows:
            beside.append(self.get(UP_SP, r + 1))
        if r > 0:
            beside.append(self.get(DOWN_SP, r - 1))
        total = total + rate(C_SP, r) * sum(beside[1:], beside[0])
        total = total + rate(C_UP, r) * rolled(self.get(UP_AX, r), -1)
        return total + rate(C_DOWN, r) * rolled(self.get(DOWN_AX, r), 1)


def matrix(plan, w_ref, block, count=1):
    return w_ref[block * plan.pad : (block + count) * plan.pad, :]


def two_layers(plan, refs, rates, seam=None):
    split = isinstance(refs, tuple)
    return [
        Layer(plan, refs[a] if split else refs, 0 if split else a * plan.slab, (rates[a], 0), seam, a)
        for a in range(plan.ct)
    ]


def inner_rows(plan, w_ref, p_refs, layers, force, g_ref):
    first = Products(plan, w_ref, p_refs[0], DOWN_AZ).fill(layers[0])
    second = Products(plan, w_ref, p_refs[1], SPECTRAL).fill(layers[1])
    for r in range(plan.rows):
        other = second.get(UP_AZ, r), first.get(DOWN_AZ, r)
        for a, products in enumerate((first, second)):
            total = products.own_terms(r) + layers[a].rate(C_AZ, r) * other[a]
            g_ref[:, at(r, 1, a * plan.slab)] = force[a].row(r) - total


def azimuthal(plan, w_ref, block, chunk_of, take):
    for c in range(plan.slab // CHUNK):
        terms = dot3(matrix(plan, w_ref, block), chunk_of(c))
        for part in range(CHUNK // LANES):
            take(c * (CHUNK // LANES) + part, terms[:, at(part)])


def middle_rows(plan, w_ref, p_refs, own, own_force, g_ref, near, near_force, side, corner, y_ref, h_ref, n_refs):
    pad, rows, ct = plan.pad, plan.rows, plan.ct
    outward, inward, last = (UP_SP, DOWN_SP), (DOWN_SP, UP_SP), (rows - 1, 0)
    edge_terms, edge_new, corner_terms = [], [], []
    for n in range(2):
        first, second, edge_force, edge_rate = side(n)
        corners = corner(n)
        every = dot3(w_ref[...], first)
        edge_terms.append(every[outward[n] * pad : (outward[n] + 1) * pad])
        corner_terms.append([dot3(matrix(plan, w_ref, outward[n]), c) for c in corners])
        beyond = dot3(matrix(plan, w_ref, outward[n]), second)
        within = dot3(matrix(plan, w_ref, inward[n]), jnp.concatenate([x.row(last[n]) for x in own], axis=1))
        from_low = dot3(matrix(plan, w_ref, DOWN_AZ), corners[0])
        from_high = dot3(matrix(plan, w_ref, UP_AZ), corners[1])
        new = []
        for a in range(ct):

            def part(block, b=a):
                return every[block * pad : (block + 1) * pad, at(b)]

            around = part(UP_AZ, 1) + from_low if a == 0 else from_high + part(DOWN_AZ, 0)
            total = edge_rate(C_TIME, a) * part(SPECTRAL) + edge_rate(C_AZ, a) * around
            total = total + edge_rate(C_SP, a) * (beyond[:, at(a)] + within[:, at(a)])
            total = total + edge_rate(C_UP, a) * rolled(part(UP_AX), -1)
            total = total + edge_rate(C_DOWN, a) * rolled(part(DOWN_AX), 1)
            new.append(edge_force[:, at(a)] - total)
        edge_new.append(dot3(matrix(plan, w_ref, outward[n]), jnp.concatenate(new, axis=1)))

    products = (
        Products(plan, w_ref, p_refs[0], DOWN_AZ).fill(near[0]), Products(plan, w_ref, p_refs[1], SPECTRAL).fill(near[1]),
    )
    for a, (to_own, to_near) in enumerate(((DOWN_AZ, UP_AZ), (UP_AZ, DOWN_AZ))):

        def take(r, terms):
            total = products[a].own_terms(r) + near[a].rate(C_AZ, r) * terms
            mine = own[a].rate(C_AZ, r) * products[a].get(to_own, r)
            for n in range(2):
                if r == last[n]:
                    total = total + near[a].rate(C_SP, r) * corner_terms[n][a]
                    mine = mine + own[a].rate(C_SP, r) * edge_terms[n][:, at(a)]
            n_refs[a][:, at(r)] = near_force[a].row(r) - total
            lanes = at(r, 1, a * plan.slab)
            y_ref[:, lanes] = g_ref[:, lanes] - mine

        azimuthal(plan, w_ref, to_near, own[a].chunk, take)

    after = [Layer(plan, y_ref, a * plan.slab, own[a].rates) for a in range(ct)]
    inner_rows(plan, w_ref, p_refs, after, own_force, h_ref)
    for a in range(ct):
        for n in range(2):
            lanes = at(last[n], 1, a * plan.slab)
            h_ref[:, lanes] -= own[a].rate(C_SP, last[n]) * edge_new[n][:, at(a)]


def outer_rows(plan, w_ref, own, near, far_chunks, n_refs, h_ref, put, layers=(0, 1)):
    count = CHUNK // LANES
    for a in layers:
        block = (DOWN_AZ, UP_AZ)[a]

        def near_chunk(c):
            terms = dot3(matrix(plan, w_ref, block), far_chunks[a](c))
            return n_refs[a][:, at(c * count, count)] - near[a].rate(C_AZ, c * count, count) * terms

        def take(r, terms):
            put(a, r, h_ref[:, at(r, 1, a * plan.slab)] - own[a].rate(C_AZ, r) * terms)

        azimuthal(plan, w_ref, block, near_chunk, take)


def sides_of(plan, side_ref, force_ref, seams_ref):
    pad, ct = plan.pad, plan.ct
    keeps = has_sides(plan)

    def read(n, ref, e, seam):
        i = n if plan.ends == 2 else 0
        value = ref[i, :pad, at(e * ct, ct)]
        if seam:
            r = e if n == 0 else plan.rows - 1 - e
            tile = seams_ref[1, 1 + i]
            scale = ref[i, pad + C_MASK : pad + C_MASK + 1, at(e * ct, ct)]
            value = value + jnp.concatenate([placed(tile, a * plan.rows + r) for a in range(ct)], axis=1) * scale
        return value * keeps[n]

    def side(n):
        i = n if plan.ends == 2 else 0
        same = side_ref is force_ref

        def rate(which, a):
            return force_ref[i, pad + which : pad + which + 1, at(a)] * keeps[n]

        force = read(n, force_ref, 0, True)
        first = force if same else read(n, side_ref, 0, False)
        return first, read(n, side_ref, 1, same), force, rate

    return side


def corners_of(plan, c_refs, seams_ref):
    keeps = has_sides(plan)

    def corner(n):
        i = n if plan.ends == 2 else 0
        out = []
        for a, c_ref in enumerate(c_refs):
            value = c_ref[i, : plan.pad]
            if seams_ref is not None:
                r = 0 if n == 0 else plan.rows - 1
                scale = c_ref[i, plan.pad + C_MASK : plan.pad + C_MASK + 1]
                value = value + placed(seams_ref[2 * a, 1 + i], a * plan.rows + r) * scale
            out.append(value * keeps[n])
        return out

    return corner


def prepare(plan, rhs_ref, coef_ref, both_ref, m0_ref, m1_ref, side_ref, c0_ref, c1_ref, rates_ref):
    pad, cells = plan.pad, plan.cells
    mask, diag, time, *face = [coef_ref[cells * i : cells * (i + 1), :] for i in range(6)]
    scale = mask / diag
    lane = lane_index(cells)
    axial = scale * face[2]
    rates = (
        scale * time, scale * face[0], scale * face[1],
        jnp.where(lane < LANES - 1, axial, 0.0), jnp.where(lane > 0, axial, 0.0), scale,
    )
    for i, rate in enumerate(rates):
        rates_ref[i] = rate
    tail = jnp.zeros((pad - plan.tf, LANES), jnp.float32)
    mirror = parity()
    m_refs = m0_ref, m1_ref

    def rate_of(i, a, r):
        there = jnp.where(mirror == 0, a, plan.ct - 1 - a) * plan.rows + r
        return rates_ref[i, pl.ds(there, 1), :]

    for a, m_ref in enumerate(m_refs):
        for r in range(plan.rows):
            there = jnp.where(mirror == 0, a, plan.ct - 1 - a) * plan.rows + r
            table = [rate_of(i, a, r) for i in range(6)]
            field = jnp.concatenate([rhs_ref[pl.ds(there, plan.tf, stride=cells), :], tail], axis=0)
            m_ref[:pad, at(r)] = field * table[C_MASK]
            m_ref[pad:, at(r)] = jnp.concatenate(
                table + [rate_of(C_MASK, 1 - a, r), jnp.zeros((1, LANES), jnp.float32)], axis=0
            )
    write_edges(plan, [m_ref[...] for m_ref in m_refs], side_ref, (c0_ref, c1_ref))
    wide = 2 * cells
    row = slice(pad + C_OWNER, pad + C_OWNER + 1)
    for t in range(plan.insts):
        both = both_ref[t : t + 1, :]
        lanes = slice(t * wide, (t + 1) * wide)
        for ref in m_refs:
            ref[row, lanes] = both
        group, part = divmod(t, LANES // wide)
        for n in range(plan.ends):
            side_ref[n, row, lanes] = both
            for ref in (c0_ref, c1_ref):
                ref[n, pad + group : pad + group + 1, part * wide : (part + 1) * wide] = both


def write_edges(plan, layers, side_ref, c_refs):
    first = lax.axis_index("span") == 0
    for a in range(plan.ct):
        for e in range(DEPTH):
            low, high = layers[a][:, at(e)], layers[a][:, at(plan.rows - 1 - e)]
            ends = [jnp.where(first, high, low)] if plan.ends == 1 else [low, high]
            for n, end in enumerate(ends):
                side_ref[n, :, at(e * plan.ct + a)] = end
                if e == 0:
                    c_refs[a][n] = end


def stack_matrices(plan, up_ref, down_ref, spectral_ref, rows_ref, lanes_ref, diagonal_ref, out_ref, down_out, up_out):
    pad = plan.pad
    lane = lax.broadcasted_iota(jnp.int32, (pad, 3 * pad), 1)
    second = (lane >= pad) & (lane < 2 * pad)
    out_ref[SPECTRAL * pad : (SPECTRAL + 1) * pad, :] = spectral_ref[...]
    even = parity() == 0
    for block, small in (
        (DOWN_AZ, jnp.where(even, down_ref[0], up_ref[0])), (UP_AZ, jnp.where(even, up_ref[0], down_ref[0])),
        (UP_SP, up_ref[1]), (DOWN_SP, down_ref[1]), (UP_AX, up_ref[2]), (DOWN_AX, down_ref[2]),
    ):
        full = dot_full(dot_full(rows_ref[...], small), lanes_ref[...]) * diagonal_ref[...]
        hi = full.astype(jnp.bfloat16).astype(jnp.float32)
        out_ref[block * pad : (block + 1) * pad, :] = jnp.where(second, full - hi, hi).astype(jnp.bfloat16)
    down_out[...] = matrix(plan, out_ref, DOWN_AZ)
    up_out[...] = matrix(plan, out_ref, UP_AZ)


def hold_far(plan, m0_ref, m1_ref, low_ref, high_ref, side_ref, c_low, c_high, far0_ref, far1_ref):
    come = 0.0 * (low_ref[0:1, 0:1] + high_ref[0:1, 0:1] + side_ref[0, 0:1, 0:1] + c_low[0, 0:1, 0:1] + c_high[0, 0:1, 0:1])
    far0_ref[...] = m0_ref[: plan.pad, :] + come
    far1_ref[...] = m1_ref[: plan.pad, :] + come


def send_panels(plan, stator_ref, out_ref, panels_ref):
    me = lax.axis_index("sector")
    for f in range(plan.fields):
        panels_ref[pl.ds(f, plan.insts, stride=RATES), : plan.width] = jnp.transpose(stator_ref[f])
    out_ref[...] = jnp.zeros_like(out_ref)
    for o, slots in enumerate(plan.slots):
        to = lax.rem(me + (plan.sectors - o), plan.sectors) * plan.spans
        for slot, t in enumerate(slots):
            lanes = slice(slot * plan.width, (slot + 1) * plan.width)
            panels = panels_ref[t * RATES : t * RATES + plan.fields, : plan.width]
            for x in range(plan.spans):
                out_ref[to + x, : plan.fields, lanes] = panels


def begin(
    plan, w_ref, m0_ref, m1_ref, got_ref, low_ref, high_ref, side_ref, c_low, c_high,
    seams_ref, weight_ref, x_ref, g_ref, panels_ref, terms_ref, rows_ref, p0_ref, p1_ref,
):
    pad, insts, fields = plan.pad, plan.insts, plan.fields
    me, span = lax.axis_index("sector"), lax.axis_index("span")
    even, is_first = parity() == 0, span == 0
    tiles = plan.tiles
    panels_ref[...] = jnp.zeros_like(panels_ref)
    for n, (k, x) in enumerate(tiles):
        at_span = x if plan.spans == 2 else jnp.clip(span + x, 0, plan.spans - 1)
        for t in range(insts):
            o = (k + plan.shift[t]) % plan.sectors
            source = lax.rem(me + o, plan.sectors) * plan.spans + at_span
            tile = rolled(got_ref[source], -plan.slots[o].index(t) * plan.width)
            panels_ref[t * fields : (t + 1) * fields, n * LANES : n * LANES + plan.width] = tile[:fields, : plan.width]

    wide = 2 * plan.cells
    row = slice(pad + C_OWNER, pad + C_OWNER + 1)
    zeros = jnp.zeros((16 - insts, LANES), jnp.float32)

    def table(read, packed):
        out = []
        for t in range(insts):
            group, part = divmod(t, LANES // wide)
            lanes = at(0 if packed else group)
            out.append(rolled(read(pad + group if packed else row.start, lanes), -part * wide))
        return jnp.concatenate(out + [zeros], axis=0)

    own = [table(lambda i, lanes: m0_ref[i : i + 1, lanes], False)]
    low = [table(lambda i, lanes: low_ref[i : i + 1, lanes], False)]
    high = [table(lambda i, lanes: high_ref[i : i + 1, lanes], False)]
    for n in range(plan.ends):
        own.append(table(lambda i, lanes: side_ref[n, i : i + 1, lanes], False))
        low.append(table(lambda i, lanes: c_low[n, i : i + 1, lanes], True))
        high.append(table(lambda i, lanes: c_high[n, i : i + 1, lanes], True))
    for n, (k, x) in enumerate(tiles):
        if k == 0:
            block = own
        else:
            block = [jnp.where(even, *pair) for pair in (zip(low, high) if k < 0 else zip(high, low))]
        if plan.spans == 2:
            value = jnp.where(is_first, block[x], block[1 - x])
        else:
            value = block[(0, 1, 2)[x]]
        rows_ref[:, at(n)] = value
    spread = dot_full(plan.inst_rows(), rows_ref[...])
    spread = pick(jnp.concatenate([spread[:, at(n)] for n in range(len(tiles))], axis=0), plan.weight_lanes())
    first, share, panel = spread, rolled(spread, plan.ct * plan.width), plan.panel_lanes()
    lower = (jnp.abs(first - panel) < 0.5).astype(jnp.float32)
    upper = (jnp.abs(first + 1.0 - panel) < 0.5).astype(jnp.float32)
    weights = share * lower + (1.0 - share) * upper
    for n in range(len(tiles)):
        panels = panels_ref[:, at(n)]
        terms_ref[n * pad : (n + 1) * pad, :] = panels + rolled(panels, plan.width)
    seams = pick(terms_ref[...] * weights, plan.window_lanes())

    def tile(values, k, x):
        n = tiles.index((k, x))
        return values[n * pad : (n + 1) * pad]

    def around(values, k):
        if plan.spans == 2:
            pair = tile(values, k, 0), tile(values, k, 1)
            return [jnp.where(is_first, pair[0], pair[1]), jnp.where(is_first, pair[1], pair[0])]
        return [tile(values, k, x) for x in (0, 1, -1)]

    def mirrored(value):
        return rolled(value, LANES // 2)

    here = around(seams, 0)
    behind, ahead = around(seams, -1), around(seams, 1)
    for i in range(1 + plan.ends):
        seams_ref[0, i] = jnp.where(even, mirrored(behind[i]), ahead[i])
        seams_ref[1, i] = jnp.where(even, here[i], mirrored(here[i]))
        seams_ref[2, i] = jnp.where(even, mirrored(ahead[i]), behind[i])
    weight_ref[...] = around(weights, 0)[0]

    rates = m0_ref, m1_ref
    for a, layer in enumerate(two_layers(plan, rates, rates, seams_ref[1, 0])):
        for r in range(plan.rows):
            x_ref[:, at(r, 1, a * plan.slab)] = layer.row(r)
    layers = two_layers(plan, x_ref, rates)
    inner_rows(plan, w_ref, (p0_ref, p1_ref), layers, layers, g_ref)


def middle_first(
    plan, w_ref, m0_ref, m1_ref, f_ref, g_ref, low_ref, high_ref, side_ref, c_low, c_high, seams_ref,
    h_ref, n0_ref, n1_ref, p0_ref, p1_ref, y_ref,
):
    own = two_layers(plan, f_ref, (m0_ref, m1_ref))
    near = Layer(plan, low_ref, 0, None, seams_ref[0, 0], 0), Layer(plan, high_ref, 0, None, seams_ref[2, 0], 1)
    middle_rows(
        plan, w_ref, (p0_ref, p1_ref), own, own, g_ref, near, near, sides_of(plan, side_ref, side_ref, seams_ref),
        corners_of(plan, (c_low, c_high), seams_ref), y_ref, h_ref, (n0_ref, n1_ref),
    )


def outer_first(
    plan, w_ref, m0_ref, m1_ref, low_first, high_first, n0_ref, n1_ref, h_ref, far_low, far_high, seams_ref,
    x0_ref, x1_ref, side_out, c0_ref, c1_ref,
):
    pad = plan.pad
    rates = m0_ref, m1_ref
    own = two_layers(plan, rates, rates)
    near = Layer(plan, low_first), Layer(plan, high_first)
    far = (
        Layer(plan, far_low, 0, (low_first, 0), seams_ref[0, 0], 1, C_OTHER),
        Layer(plan, far_high, 0, (high_first, 0), seams_ref[2, 0], 0, C_OTHER),
    )
    lane = lane_index(pad)
    x_refs = x0_ref, x1_ref
    for ref in x_refs:
        ref[:, plan.slab :] = jnp.zeros((pad, LANES), jnp.float32)

    def put(a, r, value):
        x_refs[a][:, at(r)] = value
        inlet = x_refs[1 - a].at[:, plan.slab :]
        inlet[...] = jnp.where(lane == r * WINDOW, rolled(value, r * WINDOW), inlet[...])

    outer_rows(plan, w_ref, own, near, [layer.chunk for layer in far], (n0_ref, n1_ref), h_ref, put)
    write_edges(plan, x_refs, side_out, (c0_ref, c1_ref))


def inner(plan, w_ref, m0_ref, m1_ref, f_ref, x0_ref, x1_ref, side_ref, g_ref, far0_ref, far1_ref, p0_ref, p1_ref):
    come = 0.0 * side_ref[0, 0:1, 0:1]
    far0_ref[...] = x0_ref[:, : plan.slab] + come
    far1_ref[...] = x1_ref[:, : plan.slab] + come
    rates = m0_ref, m1_ref
    inner_rows(
        plan, w_ref, (p0_ref, p1_ref), two_layers(plan, (x0_ref, x1_ref), rates), two_layers(plan, f_ref, rates), g_ref
    )


def middle(
    plan, w_ref, m0_ref, m1_ref, f_ref, x0_ref, x1_ref, g_ref, low_ref, high_ref, side_ref, c_low, c_high,
    low_first, high_first, side_first, seams_ref, weight_ref,
    send_ref, n0_ref, n1_ref, h_ref, rates_ref, p0_ref, p1_ref, y_ref, inlet_ref,
):
    pad = plan.pad
    rates = m0_ref, m1_ref
    own, force = two_layers(plan, (x0_ref, x1_ref), rates), two_layers(plan, f_ref, rates)
    near_force = (
        Layer(plan, low_first, 0, None, seams_ref[0, 0], 0), Layer(plan, high_first, 0, None, seams_ref[2, 0], 1),
    )
    near = Layer(plan, low_ref, 0, (low_first, 0)), Layer(plan, high_ref, 0, (high_first, 0))
    n_refs = n0_ref, n1_ref
    middle_rows(
        plan, w_ref, (p0_ref, p1_ref), own, force, g_ref, near, near_force,
        sides_of(plan, side_ref, side_first, seams_ref), corners_of(plan, (c_low, c_high), None), y_ref, h_ref, n_refs,
    )
    lane = lane_index(pad)
    inlet_ref[...] = jnp.zeros_like(inlet_ref)

    def put(a, r, value):
        cell = a * plan.rows + r
        inlet_ref[...] = jnp.where(lane == cell * WINDOW, rolled(value, cell * WINDOW), inlet_ref[...])

    def far_inlet(ref):
        def chunk(c):
            tile = ref[:, plan.slab :]
            count = CHUNK // LANES
            return jnp.concatenate([placed(tile, c * count + part) for part in range(count)], axis=1)

        return chunk

    outer_rows(plan, w_ref, own, near, (far_inlet(low_ref), far_inlet(high_ref)), n_refs, h_ref, put)
    inlet = inlet_ref[...]
    inlet = jnp.where(parity() == 0, inlet, rolled(inlet, LANES // 2))
    back = pick(inlet, plan.window_spread()) * weight_ref[...]
    back = back + rolled(back, -plan.width)
    me = lax.axis_index("sector")
    send_ref[...] = jnp.zeros_like(send_ref)
    for t in range(plan.insts):
        to = lax.rem(me + plan.shift[t], plan.sectors)
        send_ref[to, : plan.fields, : plan.width] = back[t * plan.fields : (t + 1) * plan.fields, : plan.width]
    for r in range(plan.rows):
        last = [layer.rate(C_AZ, r) for layer in near + tuple(own)]
        rates_ref[:, at(r)] = jnp.concatenate(last + [jnp.zeros((RATES - 4, LANES), jnp.float32)], axis=0)


def outer(plan, down_ref, up_ref, rates_ref, n0_ref, n1_ref, h_ref, low_ref, high_ref, out_ref):
    mirror = parity()
    for a, (w_ref, n_ref, far_ref) in enumerate(((down_ref, n0_ref, low_ref), (up_ref, n1_ref, high_ref))):

        def near_chunk(c):
            lanes = slice(c * CHUNK, (c + 1) * CHUNK)
            return n_ref[:, lanes] - rates_ref[a : a + 1, lanes] * dot3(w_ref[...], far_ref[:, lanes])

        def take(r, terms):
            value = h_ref[:, at(r, 1, a * plan.slab)] - rates_ref[2 + a : 3 + a, at(r)] * terms
            there = jnp.where(mirror == 0, a, plan.ct - 1 - a) * plan.rows + r
            out_ref[pl.ds(there, plan.tf, stride=plan.cells), :] = value[: plan.tf]

        azimuthal(plan, w_ref, 0, near_chunk, take)


def collect_panels(plan, got_ref, out_ref, panels_ref):
    me = lax.axis_index("sector")
    for t in range(plan.insts):
        source = lax.rem(me + (plan.sectors - plan.shift[t]), plan.sectors)
        panels_ref[t * RATES : (t + 1) * RATES, :] = got_ref[source]
    for f in range(plan.fields):
        tile = panels_ref[pl.ds(f, plan.insts, stride=RATES), : plan.width]
        out_ref[f] = jnp.transpose(tile)


def sibling(plan):
    return [s ^ 1 for s in range(plan.sectors)]


def outside(plan):
    return [(s - 1 if s % 2 == 0 else s + 1) % plan.sectors for s in range(plan.sectors)]


def swap(array, partner):
    return lax.ppermute(array, "sector", list(enumerate(partner)))


def beside(plan, array, partner):
    def pairs(step):
        out = []
        for s in range(plan.sectors):
            for x in range(plan.spans):
                to = 1 - x if plan.ends == 1 else x + step
                if 0 <= to < plan.spans:
                    out.append((s * plan.spans + x, partner[s] * plan.spans + to))
        return out

    if plan.ends == 1:
        return lax.ppermute(array, AXES, pairs(0))
    return jnp.concatenate([lax.ppermute(array[:1], AXES, pairs(-1)), lax.ppermute(array[1:], AXES, pairs(1))])


def on_device(
    sectors, spans,
    rhs, diag_coef, face_coef, time_coef, jac_up, jac_down, wall_mask, stator_adj, owner, first_panel_share,
):
    plan = Plan(rhs, stator_adj, sectors, spans)
    pad, cells, slab, insts, fields, ends = plan.pad, plan.cells, plan.slab, plan.insts, plan.fields, plan.ends
    bind = functools.partial
    whole, half = f32(pad, plan.ct * slab), f32(pad, slab)
    products = (vmem(6 * pad, slab),) * 2
    alone, next_chip, next_core = list(range(sectors)), outside(plan), sibling(plan)

    def edges(rows):
        return f32(ends, rows, DEPTH * plan.ct * LANES), f32(ends, rows, LANES), f32(ends, rows, LANES)

    stator = jnp.transpose(stator_adj, (1, 2, 3, 0)).reshape(fields, plan.width, insts)
    sent = call(bind(send_panels, plan), f32(sectors * spans, RATES, LANES), (vmem(insts * RATES, LANES),))(stator)
    got = lax.all_to_all(sent, AXES, 0, 0, tiled=True)
    m0, m1, side, c0, c1 = call(
        bind(prepare, plan), (f32(pad + RATES, slab),) * 2 + edges(pad + RATES), (vmem(6, cells, LANES),)
    )(
        rhs.reshape(plan.tf * cells, LANES),
        jnp.concatenate([
            wall_mask.astype(jnp.float32).reshape(cells, LANES), diag_coef.reshape(cells, LANES),
            time_coef.reshape(cells, LANES), face_coef.reshape(3 * cells, LANES),
        ]),
        jnp.concatenate([
            lax.rem(owner, plan.panels).astype(jnp.float32).reshape(insts, cells), first_panel_share.reshape(insts, cells),
        ], axis=1),
    )
    low_first, high_first = swap(m0, next_chip), swap(m1, next_core)
    side_first = beside(plan, side, alone)
    c_low, c_high = beside(plan, c0, next_chip), beside(plan, c1, next_core)
    far0, far1 = call(bind(hold_far, plan), (half, half))(m0, m1, low_first, high_first, side_first, c_low, c_high)
    far_low, far_high = swap(far1, next_chip), swap(far0, next_core)
    matrices, down, up = call(
        bind(stack_matrices, plan),
        [jax.ShapeDtypeStruct((count * pad, 3 * pad), jnp.bfloat16) for count in (7, 1, 1)],
    )(jac_up, jac_down, plan.spectral(), plan.field_rows(), plan.field_lanes(), plan.block_diagonal())
    tiles = len(plan.tiles)
    seams, weight, force, g = call(
        bind(begin, plan), (f32(3, 1 + ends, pad, LANES), f32(pad, LANES), whole, whole),
        (vmem(pad, tiles * LANES), vmem(tiles * pad, LANES), vmem(16, tiles * LANES)) + products,
    )(matrices, m0, m1, got, low_first, high_first, side_first, c_low, c_high)
    h, n0, n1 = call(bind(middle_first, plan), (whole, half, half), products + (vmem(pad, 2 * slab),))(
        matrices, m0, m1, force, g, low_first, high_first, side_first, c_low, c_high, seams
    )
    with_inlet = f32(pad, slab + LANES)
    x0, x1, side, c0, c1 = call(bind(outer_first, plan), (with_inlet, with_inlet) + edges(pad))(
        matrices, m0, m1, low_first, high_first, n0, n1, h, far_low, far_high, seams
    )

    low, high = swap(x0, next_chip), swap(x1, next_core)
    side = beside(plan, side, alone)
    c_low, c_high = beside(plan, c0, next_chip), beside(plan, c1, next_core)
    g, far0, far1 = call(bind(inner, plan), (whole, half, half), products, flops=2_000_000_000)(
        matrices, m0, m1, force, x0, x1, side
    )
    far_low, far_high = swap(far1, next_chip), swap(far0, next_core)
    back, n0, n1, h, rates = call(
        bind(middle, plan), (f32(sectors, RATES, LANES), half, half, whole, f32(RATES, slab)),
        products + (vmem(pad, 2 * slab), vmem(pad, LANES)), flops=4_000_000_000,
    )(
        matrices, m0, m1, force, x0, x1, g, low, high, side, c_low, c_high, low_first, high_first, side_first, seams,
        weight,
    )
    returned = lax.all_to_all(back, "sector", 0, 0, tiled=True)
    sens = call(bind(collect_panels, plan), f32(fields, plan.width, insts), (vmem(insts * RATES, LANES),))(returned)
    out = call(bind(outer, plan), f32(plan.tf * cells, LANES))(down, up, rates, n0, n1, h, far_low, far_high)
    sens = jnp.transpose(sens.reshape(fields, plan.panels, plan.rows, insts), (3, 0, 1, 2))
    return out.reshape(rhs.shape), sens


def solution(mesh):
    in_specs = (
        P(None, None, "sector", "span", None),
        P("sector", "span", None),
        P(None, "sector", "span", None),
        P("sector", "span", None),
        P(),
        P(),
        P("sector", "span", None),
        P(None, None, "sector", "span"),
        P(None, "sector", "span"),
        P(None, "sector", "span"),
    )
    out_specs = (P(None, None, "sector", "span", None), P(None, None, "sector", "span"))
    return jax.shard_map(
        functools.partial(on_device, mesh.shape["sector"], mesh.shape["span"]),
        mesh=mesh, in_specs=in_specs, out_specs=out_specs, check_vma=False,
    )
```

```python
import functools

import jax
import jax.numpy as jnp
import ml_dtypes
import numpy as np
from jax import lax
from jax.experimental import pallas as pl
from jax.experimental.pallas import tpu as pltpu
from jax.sharding import PartitionSpec as P

SWEEPS = 4
DEPTH = 2
LANES = 128
CHUNK = 256
WINDOW = 8
HIGHEST = lax.Precision.HIGHEST
DOWN_AZ, SPECTRAL, UP_SP, DOWN_SP, UP_AX, DOWN_AX, UP_AZ = range(7)
C_TIME, C_AZ, C_SP, C_UP, C_DOWN, C_MASK, C_OTHER, C_OWNER = range(8)
RATES = 8
AXES = ("sector", "span")


class Plan:
    def __init__(self, rhs, stator_adj, sectors, spans):
        self.insts, self.fields, self.ct, self.rows, self.nax = rhs.shape
        self.panels = stator_adj.shape[2]
        self.sectors, self.spans = sectors, spans
        self.tf = self.insts * self.fields
        self.pad = -(-self.tf // 16) * 16
        self.cells = self.ct * self.rows
        self.slab = self.rows * LANES
        self.width = self.panels * self.rows
        self.shift = [
            ((t * sectors) // (self.insts - 1) - t // (self.insts - 1)) % sectors for t in range(self.insts)
        ]
        assert self.ct == 2 and self.nax == LANES and SWEEPS % DEPTH == 0 and spans > 1
        assert len(set(self.shift)) == self.insts and self.cells * WINDOW == LANES and self.rows >= SWEEPS
        assert self.slab % CHUNK == 0 and 3 * self.pad <= 256 and 2 * self.ct * self.width == LANES
        assert sectors % 2 == 0
        self.ends = 1 if spans == 2 else 2
        self.blocks = [-1, 0, 1]
        self.halves = [0, 1] if spans == 2 else [-1, 0, 1]
        self.tiles = [(k, x) for k in self.blocks for x in self.halves]
        self.slots = [
            [t for t in range(self.insts) if any((k + self.shift[t]) % sectors == o for k in self.blocks)]
            for o in range(sectors)
        ]
        assert max(map(len, self.slots)) * self.width <= LANES

    def spectral(self):
        t = np.arange(self.insts)
        off = t[:, None] - t[None, :]
        sines = np.where(off == 0, 1.0, np.sin(np.pi * off / self.insts))
        table = np.where(off == 0, 0.0, 0.5 * (1.0 - 2.0 * (off % 2)) / sines).astype(np.float32)
        full = np.zeros((self.pad, self.pad), np.float32)
        full[: self.tf, : self.tf] = np.kron(table.T, np.eye(self.fields, dtype=np.float32))
        hi = full.astype(ml_dtypes.bfloat16)
        lo = (full - hi.astype(np.float32)).astype(ml_dtypes.bfloat16)
        return np.concatenate([hi, lo, hi], axis=1)

    def field_rows(self):
        out = np.zeros((self.pad, self.fields), np.float32)
        out[np.arange(self.tf), np.arange(self.tf) % self.fields] = 1.0
        return out

    def field_lanes(self):
        return np.tile(self.field_rows().T, (1, 3))

    def block_diagonal(self):
        block = np.full(self.pad, -1)
        block[: self.tf] = np.arange(self.tf) // self.fields
        same = (block[:, None] == block[None, :]) & (block[:, None] >= 0)
        return np.tile(same.astype(np.float32), (1, 3))


    def inst_rows(self):
        row, inst = table_index(self.pad, 16)
        return ((row >= inst * self.fields) & (row < (inst + 1) * self.fields)).astype(jnp.float32)

    def cell_of(self, lane):
        return lax.div(lane, self.width) * self.rows + lax.rem(lane, self.rows)

    def window_lanes(self):
        lane, to = table_index(LANES, LANES)
        return (lane < self.ct * self.width) & (to == self.cell_of(lane) * WINDOW)

    def window_spread(self):
        to, lane = table_index(LANES, LANES)
        return (lane < self.ct * self.width) & (to == self.cell_of(lane) * WINDOW)

    def weight_lanes(self):
        cell, lane = table_index(LANES, LANES)
        half = self.ct * self.width
        wanted = jnp.where(lane < half, self.cell_of(lane), self.cells + self.cell_of(lane - half))
        return cell == wanted

    def panel_lanes(self):
        lane = lane_index(1)
        panel = lax.rem(lax.div(lane, self.rows), self.panels)
        return jnp.where(lane < self.ct * self.width, panel, -9).astype(jnp.float32)


def table_index(rows, columns):
    return [lax.broadcasted_iota(jnp.int32, (rows, columns), axis) for axis in (0, 1)]


def call(kernel, out, scratch=(), flops=2_000_000, nbytes=1_000_000):
    return pl.pallas_call(
        kernel,
        out_shape=out,
        scratch_shapes=list(scratch),
        compiler_params=pltpu.CompilerParams(vmem_limit_bytes=20 * 1024 * 1024),
        cost_estimate=pl.CostEstimate(flops=flops, bytes_accessed=nbytes, transcendentals=0),
    )


def f32(*shape):
    return jax.ShapeDtypeStruct(shape, jnp.float32)


def vmem(*shape):
    return pltpu.VMEM(shape, jnp.float32)


def halves_of(x):
    hi = x.astype(jnp.bfloat16)
    return hi, (x - hi.astype(jnp.float32)).astype(jnp.bfloat16)


def dot3(w, x):
    hi, lo = halves_of(x)
    return jnp.dot(w, jnp.concatenate([hi, hi, lo], axis=0), preferred_element_type=jnp.float32)


def pick(x, table):
    table = table.astype(jnp.float32).astype(jnp.bfloat16)
    table = jnp.concatenate([table, table], axis=0)
    return jnp.dot(jnp.concatenate(halves_of(x), axis=1), table, preferred_element_type=jnp.float32)


def dot_full(a, b):
    return jnp.dot(a, b, precision=HIGHEST, preferred_element_type=jnp.float32)


def lane_index(rows):
    return lax.broadcasted_iota(jnp.int32, (rows, LANES), 1)


def rolled(x, by):
    by %= LANES
    return pltpu.roll(x, by, axis=1) if by else x


def at(r, count=1, start=0):
    return slice(start + r * LANES, start + (r + count) * LANES)


def parity():
    return lax.rem(lax.axis_index("sector"), 2)


def has_sides(plan):
    span = lax.axis_index("span")
    return jnp.where(span < plan.spans - 1, 1.0, 0.0), jnp.where(span > 0, 1.0, 0.0)


class Layer:
    def __init__(self, plan, ref, start=0, rates=None, seam=None, layer=0, scale=C_MASK):
        self.plan, self.ref, self.start, self.seam, self.layer, self.scale = plan, ref, start, seam, layer, scale
        self.rates = rates or (ref, start)

    def rate(self, which, r, count=1):
        ref, start = self.rates
        row = self.plan.pad + which
        return ref[row : row + 1, at(r, count, start)]

    def row(self, r):
        value = self.ref[: self.plan.pad, at(r, 1, self.start)]
        if self.seam is None:
            return value
        return value + placed(self.seam, self.layer * self.plan.rows + r) * self.rate(self.scale, r)

    def chunk(self, c):
        count = CHUNK // LANES
        if self.seam is None:
            return self.ref[: self.plan.pad, at(c * count, count, self.start)]
        return jnp.concatenate([self.row(c * count + part) for part in range(count)], axis=1)


def placed(tile, cell):
    return jnp.where(lane_index(tile.shape[0]) == 0, rolled(tile, -cell * WINDOW), 0.0)


class Products:
    def __init__(self, plan, w_ref, p_ref, first):
        self.plan, self.w, self.p, self.first = plan, w_ref, p_ref, first

    def fill(self, layer):
        for c in range(self.plan.slab // CHUNK):
            self.p[:, c * CHUNK : (c + 1) * CHUNK] = dot3(matrix(self.plan, self.w, self.first, 6), layer.chunk(c))
        self.layer = layer
        return self

    def get(self, block, r):
        row = (block - self.first) * self.plan.pad
        return self.p[row : row + self.plan.pad, at(r)]

    def own_terms(self, r):
        rate = self.layer.rate
        total = rate(C_TIME, r) * self.get(SPECTRAL, r)
        beside = []
        if r + 1 < self.plan.rows:
            beside.append(self.get(UP_SP, r + 1))
        if r > 0:
            beside.append(self.get(DOWN_SP, r - 1))
        total = total + rate(C_SP, r) * sum(beside[1:], beside[0])
        total = total + rate(C_UP, r) * rolled(self.get(UP_AX, r), -1)
        return total + rate(C_DOWN, r) * rolled(self.get(DOWN_AX, r), 1)


def matrix(plan, w_ref, block, count=1):
    return w_ref[block * plan.pad : (block + count) * plan.pad, :]


def two_layers(plan, refs, rates, seam=None):
    split = isinstance(refs, tuple)
    return [
        Layer(plan, refs[a] if split else refs, 0 if split else a * plan.slab, (rates[a], 0), seam, a)
        for a in range(plan.ct)
    ]


def inner_rows(plan, w_ref, p_refs, layers, force, g_ref):
    first = Products(plan, w_ref, p_refs[0], DOWN_AZ).fill(layers[0])
    second = Products(plan, w_ref, p_refs[1], SPECTRAL).fill(layers[1])
    for r in range(plan.rows):
        other = second.get(UP_AZ, r), first.get(DOWN_AZ, r)
        for a, products in enumerate((first, second)):
            total = products.own_terms(r) + layers[a].rate(C_AZ, r) * other[a]
            g_ref[:, at(r, 1, a * plan.slab)] = force[a].row(r) - total


def azimuthal(plan, w_ref, block, chunk_of, take):
    for c in range(plan.slab // CHUNK):
        terms = dot3(matrix(plan, w_ref, block), chunk_of(c))
        for part in range(CHUNK // LANES):
            take(c * (CHUNK // LANES) + part, terms[:, at(part)])


def middle_rows(plan, w_ref, p_refs, own, own_force, g_ref, near, near_force, side, corner, y_ref, h_ref, n_refs):
    pad, rows, ct = plan.pad, plan.rows, plan.ct
    outward, inward, last = (UP_SP, DOWN_SP), (DOWN_SP, UP_SP), (rows - 1, 0)
    edge_terms, edge_new, corner_terms = [], [], []
    for n in range(2):
        first, second, edge_force, edge_rate = side(n)
        corners = corner(n)
        every = dot3(w_ref[...], first)
        edge_terms.append(every[outward[n] * pad : (outward[n] + 1) * pad])
        corner_terms.append([dot3(matrix(plan, w_ref, outward[n]), c) for c in corners])
        beyond = dot3(matrix(plan, w_ref, outward[n]), second)
        within = dot3(matrix(plan, w_ref, inward[n]), jnp.concatenate([x.row(last[n]) for x in own], axis=1))
        from_low = dot3(matrix(plan, w_ref, DOWN_AZ), corners[0])
        from_high = dot3(matrix(plan, w_ref, UP_AZ), corners[1])
        new = []
        for a in range(ct):

            def part(block, b=a):
                return every[block * pad : (block + 1) * pad, at(b)]

            around = part(UP_AZ, 1) + from_low if a == 0 else from_high + part(DOWN_AZ, 0)
            total = edge_rate(C_TIME, a) * part(SPECTRAL) + edge_rate(C_AZ, a) * around
            total = total + edge_rate(C_SP, a) * (beyond[:, at(a)] + within[:, at(a)])
            total = total + edge_rate(C_UP, a) * rolled(part(UP_AX), -1)
            total = total + edge_rate(C_DOWN, a) * rolled(part(DOWN_AX), 1)
            new.append(edge_force[:, at(a)] - total)
        edge_new.append(dot3(matrix(plan, w_ref, outward[n]), jnp.concatenate(new, axis=1)))

    products = (
        Products(plan, w_ref, p_refs[0], DOWN_AZ).fill(near[0]), Products(plan, w_ref, p_refs[1], SPECTRAL).fill(near[1]),
    )
    for a, (to_own, to_near) in enumerate(((DOWN_AZ, UP_AZ), (UP_AZ, DOWN_AZ))):

        def take(r, terms):
            total = products[a].own_terms(r) + near[a].rate(C_AZ, r) * terms
            mine = own[a].rate(C_AZ, r) * products[a].get(to_own, r)
            for n in range(2):
                if r == last[n]:
                    total = total + near[a].rate(C_SP, r) * corner_terms[n][a]
                    mine = mine + own[a].rate(C_SP, r) * edge_terms[n][:, at(a)]
            n_refs[a][:, at(r)] = near_force[a].row(r) - total
            lanes = at(r, 1, a * plan.slab)
            y_ref[:, lanes] = g_ref[:, lanes] - mine

        azimuthal(plan, w_ref, to_near, own[a].chunk, take)

    after = [Layer(plan, y_ref, a * plan.slab, own[a].rates) for a in range(ct)]
    inner_rows(plan, w_ref, p_refs, after, own_force, h_ref)
    for a in range(ct):
        for n in range(2):
            lanes = at(last[n], 1, a * plan.slab)
            h_ref[:, lanes] -= own[a].rate(C_SP, last[n]) * edge_new[n][:, at(a)]


def outer_rows(plan, w_ref, own, near, far_chunks, n_refs, h_ref, put, layers=(0, 1)):
    count = CHUNK // LANES
    for a in layers:
        block = (DOWN_AZ, UP_AZ)[a]

        def near_chunk(c):
            terms = dot3(matrix(plan, w_ref, block), far_chunks[a](c))
            return n_refs[a][:, at(c * count, count)] - near[a].rate(C_AZ, c * count, count) * terms

        def take(r, terms):
            put(a, r, h_ref[:, at(r, 1, a * plan.slab)] - own[a].rate(C_AZ, r) * terms)

        azimuthal(plan, w_ref, block, near_chunk, take)


def sides_of(plan, side_ref, force_ref, seams_ref):
    pad, ct = plan.pad, plan.ct
    keeps = has_sides(plan)

    def read(n, ref, e, seam):
        i = n if plan.ends == 2 else 0
        value = ref[i, :pad, at(e * ct, ct)]
        if seam:
            r = e if n == 0 else plan.rows - 1 - e
            tile = seams_ref[1, 1 + i]
            scale = ref[i, pad + C_MASK : pad + C_MASK + 1, at(e * ct, ct)]
            value = value + jnp.concatenate([placed(tile, a * plan.rows + r) for a in range(ct)], axis=1) * scale
        return value * keeps[n]

    def side(n):
        i = n if plan.ends == 2 else 0
        same = side_ref is force_ref

        def rate(which, a):
            return force_ref[i, pad + which : pad + which + 1, at(a)] * keeps[n]

        force = read(n, force_ref, 0, True)
        first = force if same else read(n, side_ref, 0, False)
        return first, read(n, side_ref, 1, same), force, rate

    return side


def corners_of(plan, c_refs, seams_ref):
    keeps = has_sides(plan)

    def corner(n):
        i = n if plan.ends == 2 else 0
        out = []
        for a, c_ref in enumerate(c_refs):
            value = c_ref[i, : plan.pad]
            if seams_ref is not None:
                r = 0 if n == 0 else plan.rows - 1
                scale = c_ref[i, plan.pad + C_MASK : plan.pad + C_MASK + 1]
                value = value + placed(seams_ref[2 * a, 1 + i], a * plan.rows + r) * scale
            out.append(value * keeps[n])
        return out

    return corner


def prepare(plan, rhs_ref, coef_ref, both_ref, m0_ref, m1_ref, side_ref, c0_ref, c1_ref, rates_ref):
    pad, cells = plan.pad, plan.cells
    mask, diag, time, *face = [coef_ref[cells * i : cells * (i + 1), :] for i in range(6)]
    scale = mask / diag
    lane = lane_index(cells)
    axial = scale * face[2]
    rates = (
        scale * time, scale * face[0], scale * face[1],
        jnp.where(lane < LANES - 1, axial, 0.0), jnp.where(lane > 0, axial, 0.0), scale,
    )
    for i, rate in enumerate(rates):
        rates_ref[i] = rate
    tail = jnp.zeros((pad - plan.tf, LANES), jnp.float32)
    mirror = parity()
    m_refs = m0_ref, m1_ref

    def rate_of(i, a, r):
        there = jnp.where(mirror == 0, a, plan.ct - 1 - a) * plan.rows + r
        return rates_ref[i, pl.ds(there, 1), :]

    for a, m_ref in enumerate(m_refs):
        for r in range(plan.rows):
            there = jnp.where(mirror == 0, a, plan.ct - 1 - a) * plan.rows + r
            table = [rate_of(i, a, r) for i in range(6)]
            field = jnp.concatenate([rhs_ref[pl.ds(there, plan.tf, stride=cells), :], tail], axis=0)
            m_ref[:pad, at(r)] = field * table[C_MASK]
            m_ref[pad:, at(r)] = jnp.concatenate(
                table + [rate_of(C_MASK, 1 - a, r), jnp.zeros((1, LANES), jnp.float32)], axis=0
            )
    write_edges(plan, [m_ref[...] for m_ref in m_refs], side_ref, (c0_ref, c1_ref))
    wide = 2 * cells
    row = slice(pad + C_OWNER, pad + C_OWNER + 1)
    for t in range(plan.insts):
        both = both_ref[t : t + 1, :]
        lanes = slice(t * wide, (t + 1) * wide)
        for ref in m_refs:
            ref[row, lanes] = both
        group, part = divmod(t, LANES // wide)
        for n in range(plan.ends):
            side_ref[n, row, lanes] = both
            for ref in (c0_ref, c1_ref):
                ref[n, pad + group : pad + group + 1, part * wide : (part + 1) * wide] = both


def write_edges(plan, layers, side_ref, c_refs):
    first = lax.axis_index("span") == 0
    for a in range(plan.ct):
        for e in range(DEPTH):
            low, high = layers[a][:, at(e)], layers[a][:, at(plan.rows - 1 - e)]
            ends = [jnp.where(first, high, low)] if plan.ends == 1 else [low, high]
            for n, end in enumerate(ends):
                side_ref[n, :, at(e * plan.ct + a)] = end
                if e == 0:
                    c_refs[a][n] = end


def stack_matrices(plan, up_ref, down_ref, spectral_ref, rows_ref, lanes_ref, diagonal_ref, out_ref, down_out, up_out):
    pad = plan.pad
    lane = lax.broadcasted_iota(jnp.int32, (pad, 3 * pad), 1)
    second = (lane >= pad) & (lane < 2 * pad)
    out_ref[SPECTRAL * pad : (SPECTRAL + 1) * pad, :] = spectral_ref[...]
    even = parity() == 0
    for block, small in (
        (DOWN_AZ, jnp.where(even, down_ref[0], up_ref[0])), (UP_AZ, jnp.where(even, up_ref[0], down_ref[0])),
        (UP_SP, up_ref[1]), (DOWN_SP, down_ref[1]), (UP_AX, up_ref[2]), (DOWN_AX, down_ref[2]),
    ):
        full = dot_full(dot_full(rows_ref[...], small), lanes_ref[...]) * diagonal_ref[...]
        hi = full.astype(jnp.bfloat16).astype(jnp.float32)
        out_ref[block * pad : (block + 1) * pad, :] = jnp.where(second, full - hi, hi).astype(jnp.bfloat16)
    down_out[...] = matrix(plan, out_ref, DOWN_AZ)
    up_out[...] = matrix(plan, out_ref, UP_AZ)


def hold_far(plan, m0_ref, m1_ref, low_ref, high_ref, side_ref, c_low, c_high, w_ref, far0_ref, far1_ref):
    come = 0.0 * (low_ref[0:1, 0:1] + high_ref[0:1, 0:1] + side_ref[0, 0:1, 0:1] + c_low[0, 0:1, 0:1] + c_high[0, 0:1, 0:1])
    come = come + 0.0 * w_ref[:16, :LANES].astype(jnp.float32)[0:1, 0:1]
    far0_ref[...] = m0_ref[: plan.pad, :] + come
    far1_ref[...] = m1_ref[: plan.pad, :] + come


def send_panels(plan, stator_ref, out_ref, panels_ref):
    me = lax.axis_index("sector")
    for f in range(plan.fields):
        panels_ref[pl.ds(f, plan.insts, stride=RATES), : plan.width] = jnp.transpose(stator_ref[f])
    out_ref[...] = jnp.zeros_like(out_ref)
    for o, slots in enumerate(plan.slots):
        to = lax.rem(me + (plan.sectors - o), plan.sectors) * plan.spans
        for slot, t in enumerate(slots):
            lanes = slice(slot * plan.width, (slot + 1) * plan.width)
            panels = panels_ref[t * RATES : t * RATES + plan.fields, : plan.width]
            for x in range(plan.spans):
                out_ref[to + x, : plan.fields, lanes] = panels


def begin(
    plan, w_ref, m0_ref, m1_ref, got_ref, low_ref, high_ref, side_ref, c_low, c_high,
    seams_ref, weight_ref, x_ref, g_ref, panels_ref, terms_ref, rows_ref, p0_ref, p1_ref,
):
    pad, insts, fields = plan.pad, plan.insts, plan.fields
    me, span = lax.axis_index("sector"), lax.axis_index("span")
    even, is_first = parity() == 0, span == 0
    tiles = plan.tiles
    panels_ref[...] = jnp.zeros_like(panels_ref)
    for n, (k, x) in enumerate(tiles):
        at_span = x if plan.spans == 2 else jnp.clip(span + x, 0, plan.spans - 1)
        for t in range(insts):
            o = (k + plan.shift[t]) % plan.sectors
            source = lax.rem(me + o, plan.sectors) * plan.spans + at_span
            tile = rolled(got_ref[source], -plan.slots[o].index(t) * plan.width)
            panels_ref[t * fields : (t + 1) * fields, n * LANES : n * LANES + plan.width] = tile[:fields, : plan.width]

    wide = 2 * plan.cells
    row = slice(pad + C_OWNER, pad + C_OWNER + 1)
    zeros = jnp.zeros((16 - insts, LANES), jnp.float32)

    def table(read, packed):
        out = []
        for t in range(insts):
            group, part = divmod(t, LANES // wide)
            lanes = at(0 if packed else group)
            out.append(rolled(read(pad + group if packed else row.start, lanes), -part * wide))
        return jnp.concatenate(out + [zeros], axis=0)

    own = [table(lambda i, lanes: m0_ref[i : i + 1, lanes], False)]
    low = [table(lambda i, lanes: low_ref[i : i + 1, lanes], False)]
    high = [table(lambda i, lanes: high_ref[i : i + 1, lanes], False)]
    for n in range(plan.ends):
        own.append(table(lambda i, lanes: side_ref[n, i : i + 1, lanes], False))
        low.append(table(lambda i, lanes: c_low[n, i : i + 1, lanes], True))
        high.append(table(lambda i, lanes: c_high[n, i : i + 1, lanes], True))
    for n, (k, x) in enumerate(tiles):
        if k == 0:
            block = own
        else:
            block = [jnp.where(even, *pair) for pair in (zip(low, high) if k < 0 else zip(high, low))]
        if plan.spans == 2:
            value = jnp.where(is_first, block[x], block[1 - x])
        else:
            value = block[(0, 1, 2)[x]]
        rows_ref[:, at(n)] = value
    spread = dot_full(plan.inst_rows(), rows_ref[...])
    spread = pick(jnp.concatenate([spread[:, at(n)] for n in range(len(tiles))], axis=0), plan.weight_lanes())
    first, share, panel = spread, rolled(spread, plan.ct * plan.width), plan.panel_lanes()
    lower = (jnp.abs(first - panel) < 0.5).astype(jnp.float32)
    upper = (jnp.abs(first + 1.0 - panel) < 0.5).astype(jnp.float32)
    weights = share * lower + (1.0 - share) * upper
    for n in range(len(tiles)):
        panels = panels_ref[:, at(n)]
        terms_ref[n * pad : (n + 1) * pad, :] = panels + rolled(panels, plan.width)
    seams = pick(terms_ref[...] * weights, plan.window_lanes())

    def tile(values, k, x):
        n = tiles.index((k, x))
        return values[n * pad : (n + 1) * pad]

    def around(values, k):
        if plan.spans == 2:
            pair = tile(values, k, 0), tile(values, k, 1)
            return [jnp.where(is_first, pair[0], pair[1]), jnp.where(is_first, pair[1], pair[0])]
        return [tile(values, k, x) for x in (0, 1, -1)]

    def mirrored(value):
        return rolled(value, LANES // 2)

    here = around(seams, 0)
    behind, ahead = around(seams, -1), around(seams, 1)
    for i in range(1 + plan.ends):
        seams_ref[0, i] = jnp.where(even, mirrored(behind[i]), ahead[i])
        seams_ref[1, i] = jnp.where(even, here[i], mirrored(here[i]))
        seams_ref[2, i] = jnp.where(even, mirrored(ahead[i]), behind[i])
    weight_ref[...] = around(weights, 0)[0]

    rates = m0_ref, m1_ref
    for a, layer in enumerate(two_layers(plan, rates, rates, seams_ref[1, 0])):
        for r in range(plan.rows):
            x_ref[:, at(r, 1, a * plan.slab)] = layer.row(r)
    layers = two_layers(plan, x_ref, rates)
    inner_rows(plan, w_ref, (p0_ref, p1_ref), layers, layers, g_ref)


def middle_first(
    plan, w_ref, m0_ref, m1_ref, f_ref, g_ref, low_ref, high_ref, side_ref, c_low, c_high, seams_ref,
    h_ref, n0_ref, n1_ref, p0_ref, p1_ref, y_ref,
):
    own = two_layers(plan, f_ref, (m0_ref, m1_ref))
    near = Layer(plan, low_ref, 0, None, seams_ref[0, 0], 0), Layer(plan, high_ref, 0, None, seams_ref[2, 0], 1)
    middle_rows(
        plan, w_ref, (p0_ref, p1_ref), own, own, g_ref, near, near, sides_of(plan, side_ref, side_ref, seams_ref),
        corners_of(plan, (c_low, c_high), seams_ref), y_ref, h_ref, (n0_ref, n1_ref),
    )


def outer_first(
    plan, w_ref, m0_ref, m1_ref, low_first, high_first, n0_ref, n1_ref, h_ref, far_low, far_high, seams_ref,
    x0_ref, x1_ref, side_out, c0_ref, c1_ref,
):
    pad = plan.pad
    rates = m0_ref, m1_ref
    own = two_layers(plan, rates, rates)
    near = Layer(plan, low_first), Layer(plan, high_first)
    far = (
        Layer(plan, far_low, 0, (low_first, 0), seams_ref[0, 0], 1, C_OTHER),
        Layer(plan, far_high, 0, (high_first, 0), seams_ref[2, 0], 0, C_OTHER),
    )
    lane = lane_index(pad)
    x_refs = x0_ref, x1_ref
    for ref in x_refs:
        ref[:, plan.slab :] = jnp.zeros((pad, LANES), jnp.float32)

    def put(a, r, value):
        x_refs[a][:, at(r)] = value
        inlet = x_refs[1 - a].at[:, plan.slab :]
        inlet[...] = jnp.where(lane == r * WINDOW, rolled(value, r * WINDOW), inlet[...])

    outer_rows(plan, w_ref, own, near, [layer.chunk for layer in far], (n0_ref, n1_ref), h_ref, put)
    write_edges(plan, x_refs, side_out, (c0_ref, c1_ref))


def inner(plan, w_ref, m0_ref, m1_ref, f_ref, x0_ref, x1_ref, side_ref, g_ref, far0_ref, far1_ref, p0_ref, p1_ref):
    come = 0.0 * side_ref[0, 0:1, 0:1]
    far0_ref[...] = x0_ref[:, : plan.slab] + come
    far1_ref[...] = x1_ref[:, : plan.slab] + come
    rates = m0_ref, m1_ref
    inner_rows(
        plan, w_ref, (p0_ref, p1_ref), two_layers(plan, (x0_ref, x1_ref), rates), two_layers(plan, f_ref, rates), g_ref
    )


def middle(
    plan, w_ref, m0_ref, m1_ref, f_ref, x0_ref, x1_ref, g_ref, low_ref, high_ref, side_ref, c_low, c_high,
    low_first, high_first, side_first, seams_ref, weight_ref,
    send_ref, n0_ref, n1_ref, h_ref, rates_ref, p0_ref, p1_ref, y_ref, inlet_ref,
):
    pad = plan.pad
    rates = m0_ref, m1_ref
    own, force = two_layers(plan, (x0_ref, x1_ref), rates), two_layers(plan, f_ref, rates)
    near_force = (
        Layer(plan, low_first, 0, None, seams_ref[0, 0], 0), Layer(plan, high_first, 0, None, seams_ref[2, 0], 1),
    )
    near = Layer(plan, low_ref, 0, (low_first, 0)), Layer(plan, high_ref, 0, (high_first, 0))
    n_refs = n0_ref, n1_ref
    middle_rows(
        plan, w_ref, (p0_ref, p1_ref), own, force, g_ref, near, near_force,
        sides_of(plan, side_ref, side_first, seams_ref), corners_of(plan, (c_low, c_high), None), y_ref, h_ref, n_refs,
    )
    lane = lane_index(pad)
    inlet_ref[...] = jnp.zeros_like(inlet_ref)

    def put(a, r, value):
        cell = a * plan.rows + r
        inlet_ref[...] = jnp.where(lane == cell * WINDOW, rolled(value, cell * WINDOW), inlet_ref[...])

    def far_inlet(ref):
        def chunk(c):
            tile = ref[:, plan.slab :]
            count = CHUNK // LANES
            return jnp.concatenate([placed(tile, c * count + part) for part in range(count)], axis=1)

        return chunk

    outer_rows(plan, w_ref, own, near, (far_inlet(low_ref), far_inlet(high_ref)), n_refs, h_ref, put)
    inlet = inlet_ref[...]
    inlet = jnp.where(parity() == 0, inlet, rolled(inlet, LANES // 2))
    back = pick(inlet, plan.window_spread()) * weight_ref[...]
    back = back + rolled(back, -plan.width)
    me = lax.axis_index("sector")
    send_ref[...] = jnp.zeros_like(send_ref)
    for t in range(plan.insts):
        to = lax.rem(me + plan.shift[t], plan.sectors)
        send_ref[to, : plan.fields, : plan.width] = back[t * plan.fields : (t + 1) * plan.fields, : plan.width]
    for r in range(plan.rows):
        last = [layer.rate(C_AZ, r) for layer in near + tuple(own)]
        rates_ref[:, at(r)] = jnp.concatenate(last + [jnp.zeros((RATES - 4, LANES), jnp.float32)], axis=0)


def outer(plan, down_ref, up_ref, rates_ref, n0_ref, n1_ref, h_ref, low_ref, high_ref, out_ref):
    mirror = parity()
    for a, (w_ref, n_ref, far_ref) in enumerate(((down_ref, n0_ref, low_ref), (up_ref, n1_ref, high_ref))):

        def near_chunk(c):
            lanes = slice(c * CHUNK, (c + 1) * CHUNK)
            return n_ref[:, lanes] - rates_ref[a : a + 1, lanes] * dot3(w_ref[...], far_ref[:, lanes])

        def take(r, terms):
            value = h_ref[:, at(r, 1, a * plan.slab)] - rates_ref[2 + a : 3 + a, at(r)] * terms
            there = jnp.where(mirror == 0, a, plan.ct - 1 - a) * plan.rows + r
            out_ref[pl.ds(there, plan.tf, stride=plan.cells), :] = value[: plan.tf]

        azimuthal(plan, w_ref, 0, near_chunk, take)


def collect_panels(plan, got_ref, out_ref, panels_ref):
    me = lax.axis_index("sector")
    for t in range(plan.insts):
        source = lax.rem(me + (plan.sectors - plan.shift[t]), plan.sectors)
        panels_ref[t * RATES : (t + 1) * RATES, :] = got_ref[source]
    for f in range(plan.fields):
        tile = panels_ref[pl.ds(f, plan.insts, stride=RATES), : plan.width]
        out_ref[f] = jnp.transpose(tile)


def sibling(plan):
    return [s ^ 1 for s in range(plan.sectors)]


def outside(plan):
    return [(s - 1 if s % 2 == 0 else s + 1) % plan.sectors for s in range(plan.sectors)]


def swap(array, partner):
    return lax.ppermute(array, "sector", list(enumerate(partner)))


def beside(plan, array, partner):
    def pairs(step):
        out = []
        for s in range(plan.sectors):
            for x in range(plan.spans):
                to = 1 - x if plan.ends == 1 else x + step
                if 0 <= to < plan.spans:
                    out.append((s * plan.spans + x, partner[s] * plan.spans + to))
        return out

    if plan.ends == 1:
        return lax.ppermute(array, AXES, pairs(0))
    return jnp.concatenate([lax.ppermute(array[:1], AXES, pairs(-1)), lax.ppermute(array[1:], AXES, pairs(1))])


def on_device(
    sectors, spans,
    rhs, diag_coef, face_coef, time_coef, jac_up, jac_down, wall_mask, stator_adj, owner, first_panel_share,
):
    plan = Plan(rhs, stator_adj, sectors, spans)
    pad, cells, slab, insts, fields, ends = plan.pad, plan.cells, plan.slab, plan.insts, plan.fields, plan.ends
    bind = functools.partial
    whole, half = f32(pad, plan.ct * slab), f32(pad, slab)
    products = (vmem(6 * pad, slab),) * 2
    alone, next_chip, next_core = list(range(sectors)), outside(plan), sibling(plan)

    def edges(rows):
        return f32(ends, rows, DEPTH * plan.ct * LANES), f32(ends, rows, LANES), f32(ends, rows, LANES)

    stator = jnp.transpose(stator_adj, (1, 2, 3, 0)).reshape(fields, plan.width, insts)
    sent = call(bind(send_panels, plan), f32(sectors * spans, RATES, LANES), (vmem(insts * RATES, LANES),))(stator)
    got = lax.all_to_all(sent, AXES, 0, 0, tiled=True)
    m0, m1, side, c0, c1 = call(
        bind(prepare, plan), (f32(pad + RATES, slab),) * 2 + edges(pad + RATES), (vmem(6, cells, LANES),)
    )(
        rhs.reshape(plan.tf * cells, LANES),
        jnp.concatenate([
            wall_mask.astype(jnp.float32).reshape(cells, LANES), diag_coef.reshape(cells, LANES),
            time_coef.reshape(cells, LANES), face_coef.reshape(3 * cells, LANES),
        ]),
        jnp.concatenate([
            lax.rem(owner, plan.panels).astype(jnp.float32).reshape(insts, cells), first_panel_share.reshape(insts, cells),
        ], axis=1),
    )
    low_first, high_first = swap(m0, next_chip), swap(m1, next_core)
    side_first = beside(plan, side, alone)
    c_low, c_high = beside(plan, c0, next_chip), beside(plan, c1, next_core)
    matrices, down, up = call(
        bind(stack_matrices, plan),
        [jax.ShapeDtypeStruct((count * pad, 3 * pad), jnp.bfloat16) for count in (7, 1, 1)],
    )(jac_up, jac_down, plan.spectral(), plan.field_rows(), plan.field_lanes(), plan.block_diagonal())
    far0, far1 = call(bind(hold_far, plan), (half, half))(m0, m1, low_first, high_first, side_first, c_low, c_high, down)
    far_low, far_high = swap(far1, next_chip), swap(far0, next_core)
    tiles = len(plan.tiles)
    seams, weight, force, g = call(
        bind(begin, plan), (f32(3, 1 + ends, pad, LANES), f32(pad, LANES), whole, whole),
        (vmem(pad, tiles * LANES), vmem(tiles * pad, LANES), vmem(16, tiles * LANES)) + products,
    )(matrices, m0, m1, got, low_first, high_first, side_first, c_low, c_high)
    h, n0, n1 = call(bind(middle_first, plan), (whole, half, half), products + (vmem(pad, 2 * slab),))(
        matrices, m0, m1, force, g, low_first, high_first, side_first, c_low, c_high, seams
    )
    with_inlet = f32(pad, slab + LANES)
    x0, x1, side, c0, c1 = call(bind(outer_first, plan), (with_inlet, with_inlet) + edges(pad))(
        matrices, m0, m1, low_first, high_first, n0, n1, h, far_low, far_high, seams
    )

    low, high = swap(x0, next_chip), swap(x1, next_core)
    side = beside(plan, side, alone)
    c_low, c_high = beside(plan, c0, next_chip), beside(plan, c1, next_core)
    g, far0, far1 = call(bind(inner, plan), (whole, half, half), products, flops=2_000_000_000)(
        matrices, m0, m1, force, x0, x1, side
    )
    far_low, far_high = swap(far1, next_chip), swap(far0, next_core)
    back, n0, n1, h, rates = call(
        bind(middle, plan), (f32(sectors, RATES, LANES), half, half, whole, f32(RATES, slab)),
        products + (vmem(pad, 2 * slab), vmem(pad, LANES)), flops=4_000_000_000,
    )(
        matrices, m0, m1, force, x0, x1, g, low, high, side, c_low, c_high, low_first, high_first, side_first, seams,
        weight,
    )
    returned = lax.all_to_all(back, "sector", 0, 0, tiled=True)
    sens = call(bind(collect_panels, plan), f32(fields, plan.width, insts), (vmem(insts * RATES, LANES),))(returned)
    out = call(bind(outer, plan), f32(plan.tf * cells, LANES))(down, up, rates, n0, n1, h, far_low, far_high)
    sens = jnp.transpose(sens.reshape(fields, plan.panels, plan.rows, insts), (3, 0, 1, 2))
    return out.reshape(rhs.shape), sens


def solution(mesh):
    in_specs = (
        P(None, None, "sector", "span", None),
        P("sector", "span", None),
        P(None, "sector", "span", None),
        P("sector", "span", None),
        P(),
        P(),
        P("sector", "span", None),
        P(None, None, "sector", "span"),
        P(None, "sector", "span"),
        P(None, "sector", "span"),
    )
    out_specs = (P(None, None, "sector", "span", None), P(None, None, "sector", "span"))
    return jax.shard_map(
        functools.partial(on_device, mesh.shape["sector"], mesh.shape["span"]),
        mesh=mesh, in_specs=in_specs, out_specs=out_specs, check_vma=False,
    )
```

```python
import functools

import jax
import jax.numpy as jnp
import ml_dtypes
import numpy as np
from jax import lax
from jax.experimental import pallas as pl
from jax.experimental.pallas import tpu as pltpu
from jax.sharding import PartitionSpec as P

SWEEPS = 4
DEPTH = 2
LANES = 128
CHUNK = 256
WINDOW = 8
HIGHEST = lax.Precision.HIGHEST
DOWN_AZ, SPECTRAL, UP_SP, DOWN_SP, UP_AX, DOWN_AX, UP_AZ = range(7)
C_TIME, C_AZ, C_SP, C_UP, C_DOWN, C_MASK, C_OWNER = range(7)
RATES = 8
AXES = ("sector", "span")


class Plan:
    def __init__(self, rhs, stator_adj, sectors, spans):
        self.insts, self.fields, self.ct, self.rows, self.nax = rhs.shape
        self.panels = stator_adj.shape[2]
        self.sectors, self.spans = sectors, spans
        self.tf = self.insts * self.fields
        self.pad = -(-self.tf // 16) * 16
        self.cells = self.ct * self.rows
        self.slab = self.rows * LANES
        self.width = self.panels * self.rows
        self.shift = [
            ((t * sectors) // (self.insts - 1) - t // (self.insts - 1)) % sectors for t in range(self.insts)
        ]
        assert self.ct == 2 and self.nax == LANES and SWEEPS % DEPTH == 0 and spans > 1
        assert len(set(self.shift)) == self.insts and self.cells * WINDOW == LANES and self.rows >= SWEEPS
        assert self.slab % CHUNK == 0 and 3 * self.pad <= 256 and 2 * self.ct * self.width == LANES
        assert sectors % 2 == 0
        self.ends = 1 if spans == 2 else 2
        self.blocks = [-1, 0, 1]
        self.halves = [0, 1] if spans == 2 else [-1, 0, 1]
        self.tiles = [(k, x) for k in self.blocks for x in self.halves]
        self.slots = [
            [t for t in range(self.insts) if any((k + self.shift[t]) % sectors == o for k in self.blocks)]
            for o in range(sectors)
        ]
        assert max(map(len, self.slots)) * self.width <= LANES

    def spectral(self):
        t = np.arange(self.insts)
        off = t[:, None] - t[None, :]
        sines = np.where(off == 0, 1.0, np.sin(np.pi * off / self.insts))
        table = np.where(off == 0, 0.0, 0.5 * (1.0 - 2.0 * (off % 2)) / sines).astype(np.float32)
        full = np.zeros((self.pad, self.pad), np.float32)
        full[: self.tf, : self.tf] = np.kron(table.T, np.eye(self.fields, dtype=np.float32))
        hi = full.astype(ml_dtypes.bfloat16)
        lo = (full - hi.astype(np.float32)).astype(ml_dtypes.bfloat16)
        return np.concatenate([hi, lo, hi], axis=1)

    def field_rows(self):
        out = np.zeros((self.pad, self.fields), np.float32)
        out[np.arange(self.tf), np.arange(self.tf) % self.fields] = 1.0
        return out

    def field_lanes(self):
        return np.tile(self.field_rows().T, (1, 3))

    def block_diagonal(self):
        block = np.full(self.pad, -1)
        block[: self.tf] = np.arange(self.tf) // self.fields
        same = (block[:, None] == block[None, :]) & (block[:, None] >= 0)
        return np.tile(same.astype(np.float32), (1, 3))


    def inst_rows(self):
        row, inst = table_index(self.pad, 16)
        return ((row >= inst * self.fields) & (row < (inst + 1) * self.fields)).astype(jnp.float32)

    def cell_of(self, lane):
        return lax.div(lane, self.width) * self.rows + lax.rem(lane, self.rows)

    def window_lanes(self):
        lane, to = table_index(LANES, LANES)
        return (lane < self.ct * self.width) & (to == self.cell_of(lane) * WINDOW)

    def window_spread(self):
        to, lane = table_index(LANES, LANES)
        return (lane < self.ct * self.width) & (to == self.cell_of(lane) * WINDOW)

    def weight_lanes(self):
        cell, lane = table_index(LANES, LANES)
        half = self.ct * self.width
        wanted = jnp.where(lane < half, self.cell_of(lane), self.cells + self.cell_of(lane - half))
        return cell == wanted

    def panel_lanes(self):
        lane = lane_index(1)
        panel = lax.rem(lax.div(lane, self.rows), self.panels)
        return jnp.where(lane < self.ct * self.width, panel, -9).astype(jnp.float32)


def table_index(rows, columns):
    return [lax.broadcasted_iota(jnp.int32, (rows, columns), axis) for axis in (0, 1)]


def call(kernel, out, scratch=(), flops=2_000_000, nbytes=1_000_000):
    return pl.pallas_call(
        kernel,
        out_shape=out,
        scratch_shapes=list(scratch),
        compiler_params=pltpu.CompilerParams(vmem_limit_bytes=20 * 1024 * 1024),
        cost_estimate=pl.CostEstimate(flops=flops, bytes_accessed=nbytes, transcendentals=0),
    )


def f32(*shape):
    return jax.ShapeDtypeStruct(shape, jnp.float32)


def vmem(*shape):
    return pltpu.VMEM(shape, jnp.float32)


def halves_of(x):
    hi = x.astype(jnp.bfloat16)
    return hi, (x - hi.astype(jnp.float32)).astype(jnp.bfloat16)


def dot3(w, x):
    hi, lo = halves_of(x)
    return jnp.dot(w, jnp.concatenate([hi, hi, lo], axis=0), preferred_element_type=jnp.float32)


def pick(x, table):
    table = table.astype(jnp.float32).astype(jnp.bfloat16)
    table = jnp.concatenate([table, table], axis=0)
    return jnp.dot(jnp.concatenate(halves_of(x), axis=1), table, preferred_element_type=jnp.float32)


def dot_full(a, b):
    return jnp.dot(a, b, precision=HIGHEST, preferred_element_type=jnp.float32)


def lane_index(rows):
    return lax.broadcasted_iota(jnp.int32, (rows, LANES), 1)


def rolled(x, by):
    by %= LANES
    return pltpu.roll(x, by, axis=1) if by else x


def at(r, count=1, start=0):
    return slice(start + r * LANES, start + (r + count) * LANES)


def parity():
    return lax.rem(lax.axis_index("sector"), 2)


def has_sides(plan):
    span = lax.axis_index("span")
    return jnp.where(span < plan.spans - 1, 1.0, 0.0), jnp.where(span > 0, 1.0, 0.0)


class Layer:
    def __init__(self, plan, ref, start=0, rates=None, seam=None, layer=0):
        self.plan, self.ref, self.start, self.seam, self.layer = plan, ref, start, seam, layer
        self.rates = rates or (ref, start)

    def rate(self, which, r, count=1):
        ref, start = self.rates
        row = self.plan.pad + which
        return ref[row : row + 1, at(r, count, start)]

    def row(self, r):
        value = self.ref[: self.plan.pad, at(r, 1, self.start)]
        if self.seam is None:
            return value
        return value + placed(self.seam, self.layer * self.plan.rows + r) * self.rate(C_MASK, r)

    def chunk(self, c):
        count = CHUNK // LANES
        if self.seam is None:
            return self.ref[: self.plan.pad, at(c * count, count, self.start)]
        return jnp.concatenate([self.row(c * count + part) for part in range(count)], axis=1)


def placed(tile, cell):
    return jnp.where(lane_index(tile.shape[0]) == 0, rolled(tile, -cell * WINDOW), 0.0)


class Products:
    def __init__(self, plan, w_ref, p_ref, first):
        self.plan, self.w, self.p, self.first = plan, w_ref, p_ref, first

    def fill(self, layer):
        for c in range(self.plan.slab // CHUNK):
            self.p[:, c * CHUNK : (c + 1) * CHUNK] = dot3(matrix(self.plan, self.w, self.first, 6), layer.chunk(c))
        self.layer = layer
        return self

    def get(self, block, r):
        row = (block - self.first) * self.plan.pad
        return self.p[row : row + self.plan.pad, at(r)]

    def own_terms(self, r):
        rate = self.layer.rate
        total = rate(C_TIME, r) * self.get(SPECTRAL, r)
        beside = []
        if r + 1 < self.plan.rows:
            beside.append(self.get(UP_SP, r + 1))
        if r > 0:
            beside.append(self.get(DOWN_SP, r - 1))
        total = total + rate(C_SP, r) * sum(beside[1:], beside[0])
        total = total + rate(C_UP, r) * rolled(self.get(UP_AX, r), -1)
        return total + rate(C_DOWN, r) * rolled(self.get(DOWN_AX, r), 1)


def matrix(plan, w_ref, block, count=1):
    return w_ref[block * plan.pad : (block + count) * plan.pad, :]


def two_layers(plan, ref, rates=None, seam=None):
    return [
        Layer(plan, ref, a * plan.slab, (rates, a * plan.slab) if rates is not None else None, seam, a)
        for a in range(plan.ct)
    ]


def inner_rows(plan, w_ref, p_refs, layers, force, g_ref):
    first = Products(plan, w_ref, p_refs[0], DOWN_AZ).fill(layers[0])
    second = Products(plan, w_ref, p_refs[1], SPECTRAL).fill(layers[1])
    for r in range(plan.rows):
        other = second.get(UP_AZ, r), first.get(DOWN_AZ, r)
        for a, products in enumerate((first, second)):
            total = products.own_terms(r) + layers[a].rate(C_AZ, r) * other[a]
            g_ref[:, at(r, 1, a * plan.slab)] = force[a].row(r) - total


def azimuthal(plan, w_ref, block, chunk_of, take):
    for c in range(plan.slab // CHUNK):
        terms = dot3(matrix(plan, w_ref, block), chunk_of(c))
        for part in range(CHUNK // LANES):
            take(c * (CHUNK // LANES) + part, terms[:, at(part)])


def middle_rows(plan, w_ref, p_refs, own, own_force, g_ref, near, near_force, side, corner, y_ref, h_ref, n_refs):
    pad, rows, ct = plan.pad, plan.rows, plan.ct
    outward, inward, last = (UP_SP, DOWN_SP), (DOWN_SP, UP_SP), (rows - 1, 0)
    edge_terms, edge_new, corner_terms = [], [], []
    for n in range(2):
        first, second, edge_force, edge_rate = side(n)
        corners = corner(n)
        every = dot3(w_ref[...], first)
        edge_terms.append(every[outward[n] * pad : (outward[n] + 1) * pad])
        corner_terms.append([dot3(matrix(plan, w_ref, outward[n]), c) for c in corners])
        beyond = dot3(matrix(plan, w_ref, outward[n]), second)
        within = dot3(matrix(plan, w_ref, inward[n]), jnp.concatenate([x.row(last[n]) for x in own], axis=1))
        from_low = dot3(matrix(plan, w_ref, DOWN_AZ), corners[0])
        from_high = dot3(matrix(plan, w_ref, UP_AZ), corners[1])
        new = []
        for a in range(ct):

            def part(block, b=a):
                return every[block * pad : (block + 1) * pad, at(b)]

            around = part(UP_AZ, 1) + from_low if a == 0 else from_high + part(DOWN_AZ, 0)
            total = edge_rate(C_TIME, a) * part(SPECTRAL) + edge_rate(C_AZ, a) * around
            total = total + edge_rate(C_SP, a) * (beyond[:, at(a)] + within[:, at(a)])
            total = total + edge_rate(C_UP, a) * rolled(part(UP_AX), -1)
            total = total + edge_rate(C_DOWN, a) * rolled(part(DOWN_AX), 1)
            new.append(edge_force[:, at(a)] - total)
        edge_new.append(dot3(matrix(plan, w_ref, outward[n]), jnp.concatenate(new, axis=1)))

    products = (
        Products(plan, w_ref, p_refs[0], DOWN_AZ).fill(near[0]), Products(plan, w_ref, p_refs[1], SPECTRAL).fill(near[1]),
    )
    for a, (to_own, to_near) in enumerate(((DOWN_AZ, UP_AZ), (UP_AZ, DOWN_AZ))):

        def take(r, terms):
            total = products[a].own_terms(r) + near[a].rate(C_AZ, r) * terms
            mine = own[a].rate(C_AZ, r) * products[a].get(to_own, r)
            for n in range(2):
                if r == last[n]:
                    total = total + near[a].rate(C_SP, r) * corner_terms[n][a]
                    mine = mine + own[a].rate(C_SP, r) * edge_terms[n][:, at(a)]
            n_refs[a][:, at(r)] = near_force[a].row(r) - total
            lanes = at(r, 1, a * plan.slab)
            y_ref[:, lanes] = g_ref[:, lanes] - mine

        azimuthal(plan, w_ref, to_near, own[a].chunk, take)

    after = [Layer(plan, y_ref, a * plan.slab, own[a].rates) for a in range(ct)]
    inner_rows(plan, w_ref, p_refs, after, own_force, h_ref)
    for a in range(ct):
        for n in range(2):
            lanes = at(last[n], 1, a * plan.slab)
            h_ref[:, lanes] -= own[a].rate(C_SP, last[n]) * edge_new[n][:, at(a)]


def outer_rows(plan, w_ref, own, near, far_chunks, n_refs, h_ref, put, layers=(0, 1)):
    count = CHUNK // LANES
    for a in layers:
        block = (DOWN_AZ, UP_AZ)[a]

        def near_chunk(c):
            terms = dot3(matrix(plan, w_ref, block), far_chunks[a](c))
            return n_refs[a][:, at(c * count, count)] - near[a].rate(C_AZ, c * count, count) * terms

        def take(r, terms):
            put(a, r, h_ref[:, at(r, 1, a * plan.slab)] - own[a].rate(C_AZ, r) * terms)

        azimuthal(plan, w_ref, block, near_chunk, take)


def sides_of(plan, side_ref, force_ref, seams_ref):
    pad, ct = plan.pad, plan.ct
    keeps = has_sides(plan)

    def read(n, ref, e, seam):
        i = n if plan.ends == 2 else 0
        value = ref[i, :pad, at(e * ct, ct)]
        if seam:
            r = e if n == 0 else plan.rows - 1 - e
            tile = seams_ref[1, 1 + i]
            scale = ref[i, pad + C_MASK : pad + C_MASK + 1, at(e * ct, ct)]
            value = value + jnp.concatenate([placed(tile, a * plan.rows + r) for a in range(ct)], axis=1) * scale
        return value * keeps[n]

    def side(n):
        i = n if plan.ends == 2 else 0
        same = side_ref is force_ref

        def rate(which, a):
            return force_ref[i, pad + which : pad + which + 1, at(a)] * keeps[n]

        force = read(n, force_ref, 0, True)
        first = force if same else read(n, side_ref, 0, False)
        return first, read(n, side_ref, 1, same), force, rate

    return side


def corners_of(plan, c_refs, seams_ref):
    keeps = has_sides(plan)

    def corner(n):
        i = n if plan.ends == 2 else 0
        out = []
        for a, c_ref in enumerate(c_refs):
            value = c_ref[i, : plan.pad]
            if seams_ref is not None:
                r = 0 if n == 0 else plan.rows - 1
                scale = c_ref[i, plan.pad + C_MASK : plan.pad + C_MASK + 1]
                value = value + placed(seams_ref[2 * a, 1 + i], a * plan.rows + r) * scale
            out.append(value * keeps[n])
        return out

    return corner


def prepare(plan, rhs_ref, coef_ref, both_ref, m_ref, side_ref, c0_ref, c1_ref, rates_ref):
    pad, cells = plan.pad, plan.cells
    mask, diag, time, *face = [coef_ref[cells * i : cells * (i + 1), :] for i in range(6)]
    scale = mask / diag
    lane = lane_index(cells)
    axial = scale * face[2]
    rates = (
        scale * time, scale * face[0], scale * face[1],
        jnp.where(lane < LANES - 1, axial, 0.0), jnp.where(lane > 0, axial, 0.0), scale,
    )
    for i, rate in enumerate(rates):
        rates_ref[i] = rate
    tail = jnp.zeros((pad - plan.tf, LANES), jnp.float32)
    rest = jnp.zeros((RATES - 6, LANES), jnp.float32)
    mirror = parity()
    for cell in range(cells):
        a, r = divmod(cell, plan.rows)
        there = jnp.where(mirror == 0, a, plan.ct - 1 - a) * plan.rows + r
        table = [rates_ref[i, pl.ds(there, 1), :] for i in range(6)]
        field = jnp.concatenate([rhs_ref[pl.ds(there, plan.tf, stride=cells), :], tail], axis=0)
        m_ref[:pad, at(cell)] = field * table[C_MASK]
        m_ref[pad:, at(cell)] = jnp.concatenate(table + [rest], axis=0)
    write_edges(plan, m_ref, side_ref, (c0_ref, c1_ref))
    wide = 2 * cells
    row = slice(pad + C_OWNER, pad + C_OWNER + 1)
    for t in range(plan.insts):
        both = both_ref[t : t + 1, :]
        lanes = slice(t * wide, (t + 1) * wide)
        m_ref[row, lanes] = both
        group, part = divmod(t, LANES // wide)
        for n in range(plan.ends):
            side_ref[n, row, lanes] = both
            for ref in (c0_ref, c1_ref):
                ref[n, pad + group : pad + group + 1, part * wide : (part + 1) * wide] = both


def write_edges(plan, x_ref, side_ref, c_refs):
    first = lax.axis_index("span") == 0
    for a in range(plan.ct):
        for e in range(DEPTH):
            low, high = x_ref[:, at(a * plan.rows + e)], x_ref[:, at((a + 1) * plan.rows - 1 - e)]
            ends = [jnp.where(first, high, low)] if plan.ends == 1 else [low, high]
            for n, end in enumerate(ends):
                side_ref[n, :, at(e * plan.ct + a)] = end
                if e == 0:
                    c_refs[a][n] = end


def stack_matrices(plan, up_ref, down_ref, spectral_ref, rows_ref, lanes_ref, diagonal_ref, out_ref, down_out):
    pad = plan.pad
    lane = lax.broadcasted_iota(jnp.int32, (pad, 3 * pad), 1)
    second = (lane >= pad) & (lane < 2 * pad)
    out_ref[SPECTRAL * pad : (SPECTRAL + 1) * pad, :] = spectral_ref[...]
    even = parity() == 0
    for block, small in (
        (DOWN_AZ, jnp.where(even, down_ref[0], up_ref[0])), (UP_AZ, jnp.where(even, up_ref[0], down_ref[0])),
        (UP_SP, up_ref[1]), (DOWN_SP, down_ref[1]), (UP_AX, up_ref[2]), (DOWN_AX, down_ref[2]),
    ):
        full = dot_full(dot_full(rows_ref[...], small), lanes_ref[...]) * diagonal_ref[...]
        hi = full.astype(jnp.bfloat16).astype(jnp.float32)
        out_ref[block * pad : (block + 1) * pad, :] = jnp.where(second, full - hi, hi).astype(jnp.bfloat16)
    down_out[...] = matrix(plan, out_ref, DOWN_AZ)


def send_panels(plan, stator_ref, out_ref, panels_ref):
    me = lax.axis_index("sector")
    for f in range(plan.fields):
        panels_ref[pl.ds(f, plan.insts, stride=RATES), : plan.width] = jnp.transpose(stator_ref[f])
    out_ref[...] = jnp.zeros_like(out_ref)
    for o, slots in enumerate(plan.slots):
        to = lax.rem(me + (plan.sectors - o), plan.sectors) * plan.spans
        for slot, t in enumerate(slots):
            lanes = slice(slot * plan.width, (slot + 1) * plan.width)
            panels = panels_ref[t * RATES : t * RATES + plan.fields, : plan.width]
            for x in range(plan.spans):
                out_ref[to + x, : plan.fields, lanes] = panels


def begin(
    plan, w_ref, m_ref, got_ref, low_ref, high_ref, side_ref, c_low, c_high,
    seams_ref, weight_ref, x_ref, g_ref, panels_ref, terms_ref, rows_ref, p0_ref, p1_ref,
):
    pad, insts, fields = plan.pad, plan.insts, plan.fields
    me, span = lax.axis_index("sector"), lax.axis_index("span")
    even, is_first = parity() == 0, span == 0
    tiles = plan.tiles
    panels_ref[...] = jnp.zeros_like(panels_ref)
    for n, (k, x) in enumerate(tiles):
        at_span = x if plan.spans == 2 else jnp.clip(span + x, 0, plan.spans - 1)
        for t in range(insts):
            o = (k + plan.shift[t]) % plan.sectors
            source = lax.rem(me + o, plan.sectors) * plan.spans + at_span
            tile = rolled(got_ref[source], -plan.slots[o].index(t) * plan.width)
            panels_ref[t * fields : (t + 1) * fields, n * LANES : n * LANES + plan.width] = tile[:fields, : plan.width]

    wide = 2 * plan.cells
    row = slice(pad + C_OWNER, pad + C_OWNER + 1)
    zeros = jnp.zeros((16 - insts, LANES), jnp.float32)

    def table(read, packed):
        out = []
        for t in range(insts):
            group, part = divmod(t, LANES // wide)
            lanes = at(0 if packed else group)
            out.append(rolled(read(pad + group if packed else row.start, lanes), -part * wide))
        return jnp.concatenate(out + [zeros], axis=0)

    own = [table(lambda i, lanes: m_ref[i : i + 1, lanes], False)]
    low = [table(lambda i, lanes: low_ref[i : i + 1, lanes], False)]
    high = [table(lambda i, lanes: high_ref[i : i + 1, lanes], False)]
    for n in range(plan.ends):
        own.append(table(lambda i, lanes: side_ref[n, i : i + 1, lanes], False))
        low.append(table(lambda i, lanes: c_low[n, i : i + 1, lanes], True))
        high.append(table(lambda i, lanes: c_high[n, i : i + 1, lanes], True))
    for n, (k, x) in enumerate(tiles):
        if k == 0:
            block = own
        else:
            block = [jnp.where(even, *pair) for pair in (zip(low, high) if k < 0 else zip(high, low))]
        if plan.spans == 2:
            value = jnp.where(is_first, block[x], block[1 - x])
        else:
            value = block[(0, 1, 2)[x]]
        rows_ref[:, at(n)] = value
    spread = dot_full(plan.inst_rows(), rows_ref[...])
    spread = pick(jnp.concatenate([spread[:, at(n)] for n in range(len(tiles))], axis=0), plan.weight_lanes())
    first, share, panel = spread, rolled(spread, plan.ct * plan.width), plan.panel_lanes()
    lower = (jnp.abs(first - panel) < 0.5).astype(jnp.float32)
    upper = (jnp.abs(first + 1.0 - panel) < 0.5).astype(jnp.float32)
    weights = share * lower + (1.0 - share) * upper
    for n in range(len(tiles)):
        panels = panels_ref[:, at(n)]
        terms_ref[n * pad : (n + 1) * pad, :] = panels + rolled(panels, plan.width)
    seams = pick(terms_ref[...] * weights, plan.window_lanes())

    def tile(values, k, x):
        n = tiles.index((k, x))
        return values[n * pad : (n + 1) * pad]

    def around(values, k):
        if plan.spans == 2:
            pair = tile(values, k, 0), tile(values, k, 1)
            return [jnp.where(is_first, pair[0], pair[1]), jnp.where(is_first, pair[1], pair[0])]
        return [tile(values, k, x) for x in (0, 1, -1)]

    def mirrored(value):
        return rolled(value, LANES // 2)

    here = around(seams, 0)
    behind, ahead = around(seams, -1), around(seams, 1)
    for i in range(1 + plan.ends):
        seams_ref[0, i] = jnp.where(even, mirrored(behind[i]), ahead[i])
        seams_ref[1, i] = jnp.where(even, here[i], mirrored(here[i]))
        seams_ref[2, i] = jnp.where(even, mirrored(ahead[i]), behind[i])
    weight_ref[...] = around(weights, 0)[0]

    for layer in two_layers(plan, m_ref, seam=seams_ref[1, 0]):
        for r in range(plan.rows):
            x_ref[:, at(r, 1, layer.start)] = layer.row(r)
    layers = two_layers(plan, x_ref, m_ref)
    inner_rows(plan, w_ref, (p0_ref, p1_ref), layers, layers, g_ref)


def first_half(
    plan, w_ref, m_ref, f_ref, g_ref, low_ref, high_ref, side_ref, c_low, c_high, seams_ref,
    x_ref, near_ref, side_out, c0_ref, c1_ref, p0_ref, p1_ref, y_ref, h_ref, n0_ref, n1_ref, inlet_ref,
):
    own = two_layers(plan, f_ref, m_ref)
    low = two_layers(plan, low_ref, seam=seams_ref[0, 0])
    high = two_layers(plan, high_ref, seam=seams_ref[2, 0])
    near = low[0], high[1]
    n_refs = n0_ref, n1_ref
    middle_rows(
        plan, w_ref, (p0_ref, p1_ref), own, own, g_ref, near, near, sides_of(plan, side_ref, side_ref, seams_ref),
        corners_of(plan, (c_low, c_high), seams_ref), y_ref, h_ref, n_refs,
    )
    lane = lane_index(plan.pad)
    inlet_ref[...] = jnp.zeros_like(inlet_ref)

    def put(a, r, value):
        x_ref[:, at(r, 1, a * plan.slab)] = value
        if a == 0:
            near_ref[:, at(r)] = value
        else:
            inlet_ref[: plan.pad, :] = jnp.where(lane == r, rolled(value, r), inlet_ref[: plan.pad, :])

    outer_rows(plan, w_ref, own, near, (low[1].chunk, high[0].chunk), n_refs, h_ref, put)
    turned = jnp.transpose(inlet_ref[...])
    for r in range(plan.rows):
        near_ref[plan.tf : plan.tf + 1, at(r)] = turned[r : r + 1, :]
    write_edges(plan, x_ref, side_out, (c0_ref, c1_ref))


def inner(plan, w_ref, m_ref, f_ref, x_ref, side_ref, g_ref, far_ref, p0_ref, p1_ref):
    far_ref[...] = x_ref[:, plan.slab :] + 0.0 * side_ref[0, 0:1, 0:1]
    inner_rows(plan, w_ref, (p0_ref, p1_ref), two_layers(plan, x_ref, m_ref), two_layers(plan, f_ref, m_ref), g_ref)


def middle(
    plan, w_ref, m_ref, f_ref, x_ref, g_ref, low_ref, high_ref, side_ref, c_low, c_high,
    low_first, high_first, side_first, seams_ref, weight_ref,
    send_ref, n0_ref, h0_ref, x1_ref, rates_ref, p0_ref, p1_ref, y_ref, inlet_ref, h_ref, n1_ref, turn_ref,
):
    pad = plan.pad
    own, force = two_layers(plan, x_ref, m_ref), two_layers(plan, f_ref, m_ref)
    low_force = Layer(plan, low_first, 0, None, seams_ref[0, 0], 0)
    high_force = Layer(plan, high_first, plan.slab, None, seams_ref[2, 0], 1)
    near = Layer(plan, low_ref, 0, low_force.rates), Layer(plan, high_ref, plan.slab, high_force.rates)
    n_refs = n0_ref, n1_ref
    middle_rows(
        plan, w_ref, (p0_ref, p1_ref), own, force, g_ref, near, (low_force, high_force),
        sides_of(plan, side_ref, side_first, seams_ref), corners_of(plan, (c_low, c_high), None), y_ref, h_ref, n_refs,
    )
    lane = lane_index(pad)
    inlet_ref[...] = jnp.zeros_like(inlet_ref)

    def put(a, r, value):
        cell = a * plan.rows + r
        inlet_ref[...] = jnp.where(lane == cell * WINDOW, rolled(value, cell * WINDOW), inlet_ref[...])
        if a == 1:
            x1_ref[:, at(r)] = value

    turn_ref[...] = jnp.zeros_like(turn_ref)
    for r in range(plan.rows):
        turn_ref[r : r + 1, :] = low_ref[plan.tf : plan.tf + 1, at(r)]
    far_tile = jnp.transpose(turn_ref[...])[:pad]

    def far_inlet(c):
        count = CHUNK // LANES
        parts = [rolled(far_tile, -(c * count + part)) for part in range(count)]
        return jnp.concatenate([jnp.where(lane == 0, part, 0.0) for part in parts], axis=1)

    outer_rows(plan, w_ref, own, near, (far_inlet, Layer(plan, high_ref).chunk), n_refs, h_ref, put)
    inlet = inlet_ref[...]
    inlet = jnp.where(parity() == 0, inlet, rolled(inlet, LANES // 2))
    back = pick(inlet, plan.window_spread()) * weight_ref[...]
    back = back + rolled(back, -plan.width)
    me = lax.axis_index("sector")
    send_ref[...] = jnp.zeros_like(send_ref)
    for t in range(plan.insts):
        to = lax.rem(me + plan.shift[t], plan.sectors)
        send_ref[to, : plan.fields, : plan.width] = back[t * plan.fields : (t + 1) * plan.fields, : plan.width]
    h0_ref[...] = h_ref[:, : plan.slab]
    for r in range(plan.rows):
        rest = jnp.zeros((RATES - 2, LANES), jnp.float32)
        rates_ref[:, at(r)] = jnp.concatenate([near[0].rate(C_AZ, r), own[0].rate(C_AZ, r), rest], axis=0)


def outer(plan, w_ref, rates_ref, n0_ref, h0_ref, x1_ref, far_ref, out_ref):
    mirror = parity()

    def put(a, r, value):
        there = jnp.where(mirror == 0, a, plan.ct - 1 - a) * plan.rows + r
        out_ref[pl.ds(there, plan.tf, stride=plan.cells), :] = value[: plan.tf]

    for r in range(plan.rows):
        put(1, r, x1_ref[:, at(r)])

    def near_chunk(c):
        lanes = slice(c * CHUNK, (c + 1) * CHUNK)
        return n0_ref[:, lanes] - rates_ref[0:1, lanes] * dot3(w_ref[...], far_ref[:, lanes])

    azimuthal(plan, w_ref, 0, near_chunk, lambda r, terms: put(0, r, h0_ref[:, at(r)] - rates_ref[1:2, at(r)] * terms))


def collect_panels(plan, got_ref, out_ref, panels_ref):
    me = lax.axis_index("sector")
    for t in range(plan.insts):
        source = lax.rem(me + (plan.sectors - plan.shift[t]), plan.sectors)
        panels_ref[t * RATES : (t + 1) * RATES, :] = got_ref[source]
    for f in range(plan.fields):
        tile = panels_ref[pl.ds(f, plan.insts, stride=RATES), : plan.width]
        out_ref[f] = jnp.transpose(tile)


def sibling(plan):
    return [s ^ 1 for s in range(plan.sectors)]


def outside(plan):
    return [(s - 1 if s % 2 == 0 else s + 1) % plan.sectors for s in range(plan.sectors)]


def swap(array, partner):
    return lax.ppermute(array, "sector", list(enumerate(partner)))


def beside(plan, array, partner):
    def pairs(step):
        out = []
        for s in range(plan.sectors):
            for x in range(plan.spans):
                to = 1 - x if plan.ends == 1 else x + step
                if 0 <= to < plan.spans:
                    out.append((s * plan.spans + x, partner[s] * plan.spans + to))
        return out

    if plan.ends == 1:
        return lax.ppermute(array, AXES, pairs(0))
    return jnp.concatenate([lax.ppermute(array[:1], AXES, pairs(-1)), lax.ppermute(array[1:], AXES, pairs(1))])


def on_device(
    sectors, spans,
    rhs, diag_coef, face_coef, time_coef, jac_up, jac_down, wall_mask, stator_adj, owner, first_panel_share,
):
    plan = Plan(rhs, stator_adj, sectors, spans)
    pad, cells, slab, insts, fields, ends = plan.pad, plan.cells, plan.slab, plan.insts, plan.fields, plan.ends
    bind = functools.partial
    whole, half = f32(pad, plan.ct * slab), f32(pad, slab)
    products = (vmem(6 * pad, slab),) * 2
    alone, next_chip, next_core = list(range(sectors)), outside(plan), sibling(plan)

    def edges(rows):
        return f32(ends, rows, DEPTH * plan.ct * LANES), f32(ends, rows, LANES), f32(ends, rows, LANES)

    stator = jnp.transpose(stator_adj, (1, 2, 3, 0)).reshape(fields, plan.width, insts)
    sent = call(bind(send_panels, plan), f32(sectors * spans, RATES, LANES), (vmem(insts * RATES, LANES),))(stator)
    got = lax.all_to_all(sent, AXES, 0, 0, tiled=True)
    m, side, c0, c1 = call(
        bind(prepare, plan), (f32(pad + RATES, plan.ct * slab),) + edges(pad + RATES), (vmem(6, cells, LANES),)
    )(
        rhs.reshape(plan.tf * cells, LANES),
        jnp.concatenate([
            wall_mask.astype(jnp.float32).reshape(cells, LANES), diag_coef.reshape(cells, LANES),
            time_coef.reshape(cells, LANES), face_coef.reshape(3 * cells, LANES),
        ]),
        jnp.concatenate([
            lax.rem(owner, plan.panels).astype(jnp.float32).reshape(insts, cells), first_panel_share.reshape(insts, cells),
        ], axis=1),
    )
    low_first, high_first = swap(m, next_chip), swap(m, next_core)
    side_first = beside(plan, side, alone)
    c_low, c_high = beside(plan, c0, next_chip), beside(plan, c1, next_core)
    matrices, down = call(
        bind(stack_matrices, plan),
        [jax.ShapeDtypeStruct((count * pad, 3 * pad), jnp.bfloat16) for count in (7, 1)],
    )(jac_up, jac_down, plan.spectral(), plan.field_rows(), plan.field_lanes(), plan.block_diagonal())
    tiles = len(plan.tiles)
    seams, weight, force, g = call(
        bind(begin, plan), (f32(3, 1 + ends, pad, LANES), f32(pad, LANES), whole, whole),
        (vmem(pad, tiles * LANES), vmem(tiles * pad, LANES), vmem(16, tiles * LANES)) + products,
        flops=2_000_000_000,
    )(matrices, m, got, low_first, high_first, side_first, c_low, c_high)
    x, near, side, c0, c1 = call(
        bind(first_half, plan), (whole, half) + edges(pad),
        products + (vmem(pad, 2 * slab), vmem(pad, 2 * slab), vmem(pad, slab), vmem(pad, slab), vmem(LANES, LANES)),
        flops=4_000_000_000,
    )(matrices, m, force, g, low_first, high_first, side_first, c_low, c_high, seams)

    low, high = swap(near, next_chip), swap(x, next_core)
    side = beside(plan, side, alone)
    c_low, c_high = beside(plan, c0, next_chip), beside(plan, c1, next_core)
    g, far = call(bind(inner, plan), (whole, half), products, flops=2_000_000_000)(
        matrices, m, force, x, side
    )
    far_low = swap(far, next_chip)
    back, n0, h0, x1, rates = call(
        bind(middle, plan), (f32(sectors, RATES, LANES), half, half, half, f32(RATES, slab)),
        products + (vmem(pad, 2 * slab), vmem(pad, LANES), vmem(pad, 2 * slab), vmem(pad, slab), vmem(LANES, LANES)),
        flops=4_000_000_000,
    )(
        matrices, m, force, x, g, low, high, side, c_low, c_high, low_first, high_first, side_first, seams, weight
    )
    returned = lax.all_to_all(back, "sector", 0, 0, tiled=True)
    sens = call(bind(collect_panels, plan), f32(fields, plan.width, insts), (vmem(insts * RATES, LANES),))(returned)
    out = call(bind(outer, plan), f32(plan.tf * cells, LANES))(down, rates, n0, h0, x1, far_low)
    sens = jnp.transpose(sens.reshape(fields, plan.panels, plan.rows, insts), (3, 0, 1, 2))
    return out.reshape(rhs.shape), sens


def solution(mesh):
    in_specs = (
        P(None, None, "sector", "span", None),
        P("sector", "span", None),
        P(None, "sector", "span", None),
        P("sector", "span", None),
        P(),
        P(),
        P("sector", "span", None),
        P(None, None, "sector", "span"),
        P(None, "sector", "span"),
        P(None, "sector", "span"),
    )
    out_specs = (P(None, None, "sector", "span", None), P(None, None, "sector", "span"))
    return jax.shard_map(
        functools.partial(on_device, mesh.shape["sector"], mesh.shape["span"]),
        mesh=mesh, in_specs=in_specs, out_specs=out_specs, check_vma=False,
    )
```

```python
import functools

import jax
import jax.numpy as jnp
import ml_dtypes
import numpy as np
from jax import lax
from jax.experimental import pallas as pl
from jax.experimental.pallas import tpu as pltpu
from jax.sharding import PartitionSpec as P

SWEEPS = 4
DEPTH = 2
LANES = 128
CHUNK = 256
WINDOW = 8
HIGHEST = lax.Precision.HIGHEST
DOWN_AZ, SPECTRAL, UP_SP, DOWN_SP, UP_AX, DOWN_AX, UP_AZ = range(7)
C_TIME, C_AZ, C_SP, C_UP, C_DOWN, C_MASK, C_OWNER = range(7)
RATES = 8
AXES = ("sector", "span")


class Plan:
    def __init__(self, rhs, stator_adj, sectors, spans):
        self.insts, self.fields, self.ct, self.rows, self.nax = rhs.shape
        self.panels = stator_adj.shape[2]
        self.sectors, self.spans = sectors, spans
        self.tf = self.insts * self.fields
        self.pad = -(-self.tf // 16) * 16
        self.cells = self.ct * self.rows
        self.slab = self.rows * LANES
        self.width = self.panels * self.rows
        self.shift = [
            ((t * sectors) // (self.insts - 1) - t // (self.insts - 1)) % sectors for t in range(self.insts)
        ]
        assert self.ct == 2 and self.nax == LANES and SWEEPS % DEPTH == 0 and spans > 1
        assert len(set(self.shift)) == self.insts and self.cells * WINDOW == LANES and self.rows >= SWEEPS
        assert self.slab % CHUNK == 0 and 3 * self.pad <= 256 and 2 * self.ct * self.width == LANES
        assert sectors % 2 == 0
        self.ends = 1 if spans == 2 else 2
        self.blocks = [-1, 0, 1]
        self.halves = [0, 1] if spans == 2 else [-1, 0, 1]
        self.tiles = [(k, x) for k in self.blocks for x in self.halves]
        self.slots = [
            [t for t in range(self.insts) if any((k + self.shift[t]) % sectors == o for k in self.blocks)]
            for o in range(sectors)
        ]
        assert max(map(len, self.slots)) * self.width <= LANES

    def spectral(self):
        t = np.arange(self.insts)
        off = t[:, None] - t[None, :]
        sines = np.where(off == 0, 1.0, np.sin(np.pi * off / self.insts))
        table = np.where(off == 0, 0.0, 0.5 * (1.0 - 2.0 * (off % 2)) / sines).astype(np.float32)
        full = np.zeros((self.pad, self.pad), np.float32)
        full[: self.tf, : self.tf] = np.kron(table.T, np.eye(self.fields, dtype=np.float32))
        hi = full.astype(ml_dtypes.bfloat16)
        lo = (full - hi.astype(np.float32)).astype(ml_dtypes.bfloat16)
        return np.concatenate([hi, lo, hi], axis=1)

    def field_rows(self):
        out = np.zeros((self.pad, self.fields), np.float32)
        out[np.arange(self.tf), np.arange(self.tf) % self.fields] = 1.0
        return out

    def field_lanes(self):
        return np.tile(self.field_rows().T, (1, 3))

    def block_diagonal(self):
        block = np.full(self.pad, -1)
        block[: self.tf] = np.arange(self.tf) // self.fields
        same = (block[:, None] == block[None, :]) & (block[:, None] >= 0)
        return np.tile(same.astype(np.float32), (1, 3))


    def inst_rows(self):
        row, inst = table_index(self.pad, 16)
        return ((row >= inst * self.fields) & (row < (inst + 1) * self.fields)).astype(jnp.float32)

    def cell_of(self, lane):
        return lax.div(lane, self.width) * self.rows + lax.rem(lane, self.rows)

    def window_lanes(self):
        lane, to = table_index(LANES, LANES)
        return (lane < self.ct * self.width) & (to == self.cell_of(lane) * WINDOW)

    def window_spread(self):
        to, lane = table_index(LANES, LANES)
        return (lane < self.ct * self.width) & (to == self.cell_of(lane) * WINDOW)

    def weight_lanes(self):
        cell, lane = table_index(LANES, LANES)
        half = self.ct * self.width
        wanted = jnp.where(lane < half, self.cell_of(lane), self.cells + self.cell_of(lane - half))
        return cell == wanted

    def panel_lanes(self):
        lane = lane_index(1)
        panel = lax.rem(lax.div(lane, self.rows), self.panels)
        return jnp.where(lane < self.ct * self.width, panel, -9).astype(jnp.float32)


def table_index(rows, columns):
    return [lax.broadcasted_iota(jnp.int32, (rows, columns), axis) for axis in (0, 1)]


def call(kernel, out, scratch=(), flops=2_000_000, nbytes=1_000_000):
    return pl.pallas_call(
        kernel,
        out_shape=out,
        scratch_shapes=list(scratch),
        compiler_params=pltpu.CompilerParams(vmem_limit_bytes=20 * 1024 * 1024),
        cost_estimate=pl.CostEstimate(flops=flops, bytes_accessed=nbytes, transcendentals=0),
    )


def f32(*shape):
    return jax.ShapeDtypeStruct(shape, jnp.float32)


def vmem(*shape):
    return pltpu.VMEM(shape, jnp.float32)


def halves_of(x):
    hi = x.astype(jnp.bfloat16)
    return hi, (x - hi.astype(jnp.float32)).astype(jnp.bfloat16)


def dot3(w, x):
    hi, lo = halves_of(x)
    return jnp.dot(w, jnp.concatenate([hi, hi, lo], axis=0), preferred_element_type=jnp.float32)


def pick(x, table):
    table = table.astype(jnp.float32).astype(jnp.bfloat16)
    table = jnp.concatenate([table, table], axis=0)
    return jnp.dot(jnp.concatenate(halves_of(x), axis=1), table, preferred_element_type=jnp.float32)


def dot_full(a, b):
    return jnp.dot(a, b, precision=HIGHEST, preferred_element_type=jnp.float32)


def lane_index(rows):
    return lax.broadcasted_iota(jnp.int32, (rows, LANES), 1)


def rolled(x, by):
    by %= LANES
    return pltpu.roll(x, by, axis=1) if by else x


def at(r, count=1, start=0):
    return slice(start + r * LANES, start + (r + count) * LANES)


def parity():
    return lax.rem(lax.axis_index("sector"), 2)


def has_sides(plan):
    span = lax.axis_index("span")
    return jnp.where(span < plan.spans - 1, 1.0, 0.0), jnp.where(span > 0, 1.0, 0.0)


class Layer:
    def __init__(self, plan, ref, start=0, rates=None, seam=None, layer=0):
        self.plan, self.ref, self.start, self.seam, self.layer = plan, ref, start, seam, layer
        self.rates = rates or (ref, start)

    def rate(self, which, r, count=1):
        ref, start = self.rates
        row = self.plan.pad + which
        return ref[row : row + 1, at(r, count, start)]

    def row(self, r):
        value = self.ref[: self.plan.pad, at(r, 1, self.start)]
        if self.seam is None:
            return value
        return value + placed(self.seam, self.layer * self.plan.rows + r) * self.rate(C_MASK, r)

    def chunk(self, c):
        count = CHUNK // LANES
        if self.seam is None:
            return self.ref[: self.plan.pad, at(c * count, count, self.start)]
        return jnp.concatenate([self.row(c * count + part) for part in range(count)], axis=1)


def placed(tile, cell):
    return jnp.where(lane_index(tile.shape[0]) == 0, rolled(tile, -cell * WINDOW), 0.0)


class Products:
    def __init__(self, plan, w_ref, p_ref, first):
        self.plan, self.w, self.p, self.first = plan, w_ref, p_ref, first

    def fill(self, layer):
        for c in range(self.plan.slab // CHUNK):
            self.p[:, c * CHUNK : (c + 1) * CHUNK] = dot3(matrix(self.plan, self.w, self.first, 6), layer.chunk(c))
        self.layer = layer
        return self

    def get(self, block, r):
        row = (block - self.first) * self.plan.pad
        return self.p[row : row + self.plan.pad, at(r)]

    def own_terms(self, r):
        rate = self.layer.rate
        total = rate(C_TIME, r) * self.get(SPECTRAL, r)
        beside = []
        if r + 1 < self.plan.rows:
            beside.append(self.get(UP_SP, r + 1))
        if r > 0:
            beside.append(self.get(DOWN_SP, r - 1))
        total = total + rate(C_SP, r) * sum(beside[1:], beside[0])
        total = total + rate(C_UP, r) * rolled(self.get(UP_AX, r), -1)
        return total + rate(C_DOWN, r) * rolled(self.get(DOWN_AX, r), 1)


def matrix(plan, w_ref, block, count=1):
    return w_ref[block * plan.pad : (block + count) * plan.pad, :]


def two_layers(plan, ref, rates=None, seam=None):
    return [
        Layer(plan, ref, a * plan.slab, (rates, a * plan.slab) if rates is not None else None, seam, a)
        for a in range(plan.ct)
    ]


def inner_rows(plan, w_ref, p_refs, layers, force, g_ref):
    first = Products(plan, w_ref, p_refs[0], DOWN_AZ).fill(layers[0])
    second = Products(plan, w_ref, p_refs[1], SPECTRAL).fill(layers[1])
    for r in range(plan.rows):
        other = second.get(UP_AZ, r), first.get(DOWN_AZ, r)
        for a, products in enumerate((first, second)):
            total = products.own_terms(r) + layers[a].rate(C_AZ, r) * other[a]
            if isinstance(g_ref, tuple):
                g_ref[a][:, at(r)] = force[a].row(r) - total
            else:
                g_ref[:, at(r, 1, a * plan.slab)] = force[a].row(r) - total


def azimuthal(plan, w_ref, block, chunk_of, take):
    for c in range(plan.slab // CHUNK):
        terms = dot3(matrix(plan, w_ref, block), chunk_of(c))
        for part in range(CHUNK // LANES):
            take(c * (CHUNK // LANES) + part, terms[:, at(part)])


def middle_rows(plan, w_ref, p_refs, own, own_force, g_ref, near, near_force, side, corner, y_ref, h_refs, n_refs):
    pad, rows, ct = plan.pad, plan.rows, plan.ct
    outward, inward, last = (UP_SP, DOWN_SP), (DOWN_SP, UP_SP), (rows - 1, 0)
    edge_terms, edge_new, corner_terms = [], [], []
    for n in range(2):
        first, second, edge_force, edge_rate = side(n)
        corners = corner(n)
        every = dot3(w_ref[...], first)
        edge_terms.append(every[outward[n] * pad : (outward[n] + 1) * pad])
        corner_terms.append([dot3(matrix(plan, w_ref, outward[n]), c) for c in corners])
        beyond = dot3(matrix(plan, w_ref, outward[n]), second)
        within = dot3(matrix(plan, w_ref, inward[n]), jnp.concatenate([x.row(last[n]) for x in own], axis=1))
        from_low = dot3(matrix(plan, w_ref, DOWN_AZ), corners[0])
        from_high = dot3(matrix(plan, w_ref, UP_AZ), corners[1])
        new = []
        for a in range(ct):

            def part(block, b=a):
                return every[block * pad : (block + 1) * pad, at(b)]

            around = part(UP_AZ, 1) + from_low if a == 0 else from_high + part(DOWN_AZ, 0)
            total = edge_rate(C_TIME, a) * part(SPECTRAL) + edge_rate(C_AZ, a) * around
            total = total + edge_rate(C_SP, a) * (beyond[:, at(a)] + within[:, at(a)])
            total = total + edge_rate(C_UP, a) * rolled(part(UP_AX), -1)
            total = total + edge_rate(C_DOWN, a) * rolled(part(DOWN_AX), 1)
            new.append(edge_force[:, at(a)] - total)
        edge_new.append(dot3(matrix(plan, w_ref, outward[n]), jnp.concatenate(new, axis=1)))

    products = (
        Products(plan, w_ref, p_refs[0], DOWN_AZ).fill(near[0]), Products(plan, w_ref, p_refs[1], SPECTRAL).fill(near[1]),
    )
    for a, (to_own, to_near) in enumerate(((DOWN_AZ, UP_AZ), (UP_AZ, DOWN_AZ))):

        def take(r, terms):
            total = products[a].own_terms(r) + near[a].rate(C_AZ, r) * terms
            mine = own[a].rate(C_AZ, r) * products[a].get(to_own, r)
            for n in range(2):
                if r == last[n]:
                    total = total + near[a].rate(C_SP, r) * corner_terms[n][a]
                    mine = mine + own[a].rate(C_SP, r) * edge_terms[n][:, at(a)]
            n_refs[a][:, at(r)] = near_force[a].row(r) - total
            lanes = at(r, 1, a * plan.slab)
            y_ref[:, lanes] = g_ref[:, lanes] - mine

        azimuthal(plan, w_ref, to_near, own[a].chunk, take)

    after = [Layer(plan, y_ref, a * plan.slab, own[a].rates) for a in range(ct)]
    inner_rows(plan, w_ref, p_refs, after, own_force, h_refs)
    for a in range(ct):
        for n in range(2):
            h_refs[a][:, at(last[n])] -= own[a].rate(C_SP, last[n]) * edge_new[n][:, at(a)]


def outer_rows(plan, w_ref, own, near, far_chunks, n_refs, h_refs, put, layers=(0, 1)):
    count = CHUNK // LANES
    for a in layers:
        block = (DOWN_AZ, UP_AZ)[a]

        def near_chunk(c):
            terms = dot3(matrix(plan, w_ref, block), far_chunks[a](c))
            return n_refs[a][:, at(c * count, count)] - near[a].rate(C_AZ, c * count, count) * terms

        def take(r, terms):
            put(a, r, h_refs[a][:, at(r)] - own[a].rate(C_AZ, r) * terms)

        azimuthal(plan, w_ref, block, near_chunk, take)


def sides_of(plan, side_ref, force_ref, seams_ref):
    pad, ct = plan.pad, plan.ct
    keeps = has_sides(plan)

    def read(n, ref, e, seam):
        i = n if plan.ends == 2 else 0
        value = ref[i, :pad, at(e * ct, ct)]
        if seam:
            r = e if n == 0 else plan.rows - 1 - e
            tile = seams_ref[1, 1 + i]
            scale = ref[i, pad + C_MASK : pad + C_MASK + 1, at(e * ct, ct)]
            value = value + jnp.concatenate([placed(tile, a * plan.rows + r) for a in range(ct)], axis=1) * scale
        return value * keeps[n]

    def side(n):
        i = n if plan.ends == 2 else 0
        same = side_ref is force_ref

        def rate(which, a):
            return force_ref[i, pad + which : pad + which + 1, at(a)] * keeps[n]

        force = read(n, force_ref, 0, True)
        first = force if same else read(n, side_ref, 0, False)
        return first, read(n, side_ref, 1, same), force, rate

    return side


def corners_of(plan, c_refs, seams_ref):
    keeps = has_sides(plan)

    def corner(n):
        i = n if plan.ends == 2 else 0
        out = []
        for a, c_ref in enumerate(c_refs):
            value = c_ref[i, : plan.pad]
            if seams_ref is not None:
                r = 0 if n == 0 else plan.rows - 1
                scale = c_ref[i, plan.pad + C_MASK : plan.pad + C_MASK + 1]
                value = value + placed(seams_ref[2 * a, 1 + i], a * plan.rows + r) * scale
            out.append(value * keeps[n])
        return out

    return corner


def prepare(plan, rhs_ref, coef_ref, both_ref, m_ref, side_ref, c0_ref, c1_ref, rates_ref):
    pad, cells = plan.pad, plan.cells
    mask, diag, time, *face = [coef_ref[cells * i : cells * (i + 1), :] for i in range(6)]
    scale = mask / diag
    lane = lane_index(cells)
    axial = scale * face[2]
    rates = (
        scale * time, scale * face[0], scale * face[1],
        jnp.where(lane < LANES - 1, axial, 0.0), jnp.where(lane > 0, axial, 0.0), scale,
    )
    for i, rate in enumerate(rates):
        rates_ref[i] = rate
    tail = jnp.zeros((pad - plan.tf, LANES), jnp.float32)
    rest = jnp.zeros((RATES - 6, LANES), jnp.float32)
    mirror = parity()
    for cell in range(cells):
        a, r = divmod(cell, plan.rows)
        there = jnp.where(mirror == 0, a, plan.ct - 1 - a) * plan.rows + r
        table = [rates_ref[i, pl.ds(there, 1), :] for i in range(6)]
        field = jnp.concatenate([rhs_ref[pl.ds(there, plan.tf, stride=cells), :], tail], axis=0)
        m_ref[:pad, at(cell)] = field * table[C_MASK]
        m_ref[pad:, at(cell)] = jnp.concatenate(table + [rest], axis=0)
    write_edges(plan, m_ref, side_ref, (c0_ref, c1_ref))
    wide = 2 * cells
    row = slice(pad + C_OWNER, pad + C_OWNER + 1)
    for t in range(plan.insts):
        both = both_ref[t : t + 1, :]
        lanes = slice(t * wide, (t + 1) * wide)
        m_ref[row, lanes] = both
        group, part = divmod(t, LANES // wide)
        for n in range(plan.ends):
            side_ref[n, row, lanes] = both
            for ref in (c0_ref, c1_ref):
                ref[n, pad + group : pad + group + 1, part * wide : (part + 1) * wide] = both


def write_edges(plan, x_ref, side_ref, c_refs):
    first = lax.axis_index("span") == 0
    for a in range(plan.ct):
        for e in range(DEPTH):
            low, high = x_ref[:, at(a * plan.rows + e)], x_ref[:, at((a + 1) * plan.rows - 1 - e)]
            ends = [jnp.where(first, high, low)] if plan.ends == 1 else [low, high]
            for n, end in enumerate(ends):
                side_ref[n, :, at(e * plan.ct + a)] = end
                if e == 0:
                    c_refs[a][n] = end


def stack_matrices(plan, up_ref, down_ref, spectral_ref, rows_ref, lanes_ref, diagonal_ref, out_ref, down_out):
    pad = plan.pad
    lane = lax.broadcasted_iota(jnp.int32, (pad, 3 * pad), 1)
    second = (lane >= pad) & (lane < 2 * pad)
    out_ref[SPECTRAL * pad : (SPECTRAL + 1) * pad, :] = spectral_ref[...]
    even = parity() == 0
    for block, small in (
        (DOWN_AZ, jnp.where(even, down_ref[0], up_ref[0])), (UP_AZ, jnp.where(even, up_ref[0], down_ref[0])),
        (UP_SP, up_ref[1]), (DOWN_SP, down_ref[1]), (UP_AX, up_ref[2]), (DOWN_AX, down_ref[2]),
    ):
        full = dot_full(dot_full(rows_ref[...], small), lanes_ref[...]) * diagonal_ref[...]
        hi = full.astype(jnp.bfloat16).astype(jnp.float32)
        out_ref[block * pad : (block + 1) * pad, :] = jnp.where(second, full - hi, hi).astype(jnp.bfloat16)
    down_out[...] = matrix(plan, out_ref, DOWN_AZ)


def send_panels(plan, stator_ref, out_ref, panels_ref):
    me = lax.axis_index("sector")
    for f in range(plan.fields):
        panels_ref[pl.ds(f, plan.insts, stride=RATES), : plan.width] = jnp.transpose(stator_ref[f])
    out_ref[...] = jnp.zeros_like(out_ref)
    for o, slots in enumerate(plan.slots):
        to = lax.rem(me + (plan.sectors - o), plan.sectors) * plan.spans
        for slot, t in enumerate(slots):
            lanes = slice(slot * plan.width, (slot + 1) * plan.width)
            panels = panels_ref[t * RATES : t * RATES + plan.fields, : plan.width]
            for x in range(plan.spans):
                out_ref[to + x, : plan.fields, lanes] = panels


def begin(
    plan, w_ref, m_ref, got_ref, low_ref, high_ref, side_ref, c_low, c_high,
    seams_ref, weight_ref, x_ref, g_ref, panels_ref, terms_ref, rows_ref, p0_ref, p1_ref,
):
    pad, insts, fields = plan.pad, plan.insts, plan.fields
    me, span = lax.axis_index("sector"), lax.axis_index("span")
    even, is_first = parity() == 0, span == 0
    tiles = plan.tiles
    panels_ref[...] = jnp.zeros_like(panels_ref)
    for n, (k, x) in enumerate(tiles):
        at_span = x if plan.spans == 2 else jnp.clip(span + x, 0, plan.spans - 1)
        for t in range(insts):
            o = (k + plan.shift[t]) % plan.sectors
            source = lax.rem(me + o, plan.sectors) * plan.spans + at_span
            tile = rolled(got_ref[source], -plan.slots[o].index(t) * plan.width)
            panels_ref[t * fields : (t + 1) * fields, n * LANES : n * LANES + plan.width] = tile[:fields, : plan.width]

    wide = 2 * plan.cells
    row = slice(pad + C_OWNER, pad + C_OWNER + 1)
    zeros = jnp.zeros((16 - insts, LANES), jnp.float32)

    def table(read, packed):
        out = []
        for t in range(insts):
            group, part = divmod(t, LANES // wide)
            lanes = at(0 if packed else group)
            out.append(rolled(read(pad + group if packed else row.start, lanes), -part * wide))
        return jnp.concatenate(out + [zeros], axis=0)

    own = [table(lambda i, lanes: m_ref[i : i + 1, lanes], False)]
    low = [table(lambda i, lanes: low_ref[i : i + 1, lanes], False)]
    high = [table(lambda i, lanes: high_ref[i : i + 1, lanes], False)]
    for n in range(plan.ends):
        own.append(table(lambda i, lanes: side_ref[n, i : i + 1, lanes], False))
        low.append(table(lambda i, lanes: c_low[n, i : i + 1, lanes], True))
        high.append(table(lambda i, lanes: c_high[n, i : i + 1, lanes], True))
    for n, (k, x) in enumerate(tiles):
        if k == 0:
            block = own
        else:
            block = [jnp.where(even, *pair) for pair in (zip(low, high) if k < 0 else zip(high, low))]
        if plan.spans == 2:
            value = jnp.where(is_first, block[x], block[1 - x])
        else:
            value = block[(0, 1, 2)[x]]
        rows_ref[:, at(n)] = value
    spread = dot_full(plan.inst_rows(), rows_ref[...])
    spread = pick(jnp.concatenate([spread[:, at(n)] for n in range(len(tiles))], axis=0), plan.weight_lanes())
    first, share, panel = spread, rolled(spread, plan.ct * plan.width), plan.panel_lanes()
    lower = (jnp.abs(first - panel) < 0.5).astype(jnp.float32)
    upper = (jnp.abs(first + 1.0 - panel) < 0.5).astype(jnp.float32)
    weights = share * lower + (1.0 - share) * upper
    for n in range(len(tiles)):
        panels = panels_ref[:, at(n)]
        terms_ref[n * pad : (n + 1) * pad, :] = panels + rolled(panels, plan.width)
    seams = pick(terms_ref[...] * weights, plan.window_lanes())

    def tile(values, k, x):
        n = tiles.index((k, x))
        return values[n * pad : (n + 1) * pad]

    def around(values, k):
        if plan.spans == 2:
            pair = tile(values, k, 0), tile(values, k, 1)
            return [jnp.where(is_first, pair[0], pair[1]), jnp.where(is_first, pair[1], pair[0])]
        return [tile(values, k, x) for x in (0, 1, -1)]

    def mirrored(value):
        return rolled(value, LANES // 2)

    here = around(seams, 0)
    behind, ahead = around(seams, -1), around(seams, 1)
    for i in range(1 + plan.ends):
        seams_ref[0, i] = jnp.where(even, mirrored(behind[i]), ahead[i])
        seams_ref[1, i] = jnp.where(even, here[i], mirrored(here[i]))
        seams_ref[2, i] = jnp.where(even, mirrored(ahead[i]), behind[i])
    weight_ref[...] = around(weights, 0)[0]

    for layer in two_layers(plan, m_ref, seam=seams_ref[1, 0]):
        for r in range(plan.rows):
            x_ref[:, at(r, 1, layer.start)] = layer.row(r)
    layers = two_layers(plan, x_ref, m_ref)
    inner_rows(plan, w_ref, (p0_ref, p1_ref), layers, layers, g_ref)


def first_half(
    plan, w_ref, m_ref, f_ref, g_ref, low_ref, high_ref, side_ref, c_low, c_high, seams_ref,
    x_ref, near_ref, side_out, c0_ref, c1_ref, p0_ref, p1_ref, y_ref, h0_ref, h1_ref, n0_ref, n1_ref, inlet_ref,
):
    own = two_layers(plan, f_ref, m_ref)
    low = two_layers(plan, low_ref, seam=seams_ref[0, 0])
    high = two_layers(plan, high_ref, seam=seams_ref[2, 0])
    near = low[0], high[1]
    n_refs = n0_ref, n1_ref
    middle_rows(
        plan, w_ref, (p0_ref, p1_ref), own, own, g_ref, near, near, sides_of(plan, side_ref, side_ref, seams_ref),
        corners_of(plan, (c_low, c_high), seams_ref), y_ref, (h0_ref, h1_ref), n_refs,
    )
    lane = lane_index(plan.pad)
    inlet_ref[...] = jnp.zeros_like(inlet_ref)

    def put(a, r, value):
        x_ref[:, at(r, 1, a * plan.slab)] = value
        if a == 0:
            near_ref[:, at(r)] = value
        else:
            inlet_ref[: plan.pad, :] = jnp.where(lane == r, rolled(value, r), inlet_ref[: plan.pad, :])

    outer_rows(plan, w_ref, own, near, (low[1].chunk, high[0].chunk), n_refs, (h0_ref, h1_ref), put)
    turned = jnp.transpose(inlet_ref[...])
    for r in range(plan.rows):
        near_ref[plan.tf : plan.tf + 1, at(r)] = turned[r : r + 1, :]
    write_edges(plan, x_ref, side_out, (c0_ref, c1_ref))


def hold_far(plan, x_ref, side_ref, c_low, c_high, far_ref):
    come = side_ref[0, 0:1, 0:1] + c_low[0, 0:1, 0:1] + c_high[0, 0:1, 0:1]
    far_ref[...] = x_ref[:, plan.slab :] + 0.0 * come


def inner(plan, w_ref, m_ref, f_ref, x_ref, g_ref, p0_ref, p1_ref):
    inner_rows(plan, w_ref, (p0_ref, p1_ref), two_layers(plan, x_ref, m_ref), two_layers(plan, f_ref, m_ref), g_ref)


def middle(
    plan, w_ref, m_ref, f_ref, x_ref, g_ref, low_ref, high_ref, side_ref, c_low, c_high,
    low_first, high_first, side_first, seams_ref, weight_ref,
    send_ref, n0_ref, h0_ref, x1_ref, rates_ref, p0_ref, p1_ref, y_ref, h1_ref, n1_ref, turn_ref,
):
    pad = plan.pad
    own, force = two_layers(plan, x_ref, m_ref), two_layers(plan, f_ref, m_ref)
    low_force = Layer(plan, low_first, 0, None, seams_ref[0, 0], 0)
    high_force = Layer(plan, high_first, plan.slab, None, seams_ref[2, 0], 1)
    near = Layer(plan, low_ref, 0, low_force.rates), Layer(plan, high_ref, plan.slab, high_force.rates)
    n_refs = n0_ref, n1_ref
    middle_rows(
        plan, w_ref, (p0_ref, p1_ref), own, force, g_ref, near, (low_force, high_force),
        sides_of(plan, side_ref, side_first, seams_ref), corners_of(plan, (c_low, c_high), None), y_ref,
        (h0_ref, h1_ref), n_refs,
    )

    def put(a, r, value):
        x1_ref[:, at(r)] = value

    outer_rows(plan, w_ref, own, near, (None, Layer(plan, high_ref).chunk), n_refs, (h0_ref, h1_ref), put, (1,))
    for r in range(plan.rows):
        last = [near[0].rate(C_AZ, r), own[0].rate(C_AZ, r), jnp.zeros((RATES - 2, LANES), jnp.float32)]
        rates_ref[:, at(r)] = jnp.concatenate(last, axis=0)

    turn_ref[...] = jnp.zeros_like(turn_ref)
    for r in range(plan.rows):
        turn_ref[r : r + 1, :] = low_ref[plan.tf : plan.tf + 1, at(r)]
    far = jnp.transpose(turn_ref[...])[:pad]

    def packed(read, count, first=0, step=1):
        lane = lane_index(count)
        out = jnp.zeros((count, LANES), jnp.float32)
        for r in range(plan.rows):
            to = first + r * step
            out = jnp.where(lane == to, rolled(read(r), to), out)
        return out

    rates = packed(lambda r: rates_ref[:, at(r)], RATES)
    inlet = packed(lambda r: n0_ref[:, at(r)], pad) - rates[0:1] * dot3(matrix(plan, w_ref, DOWN_AZ), far)
    inlet = packed(lambda r: h0_ref[:, at(r)], pad) - rates[1:2] * dot3(matrix(plan, w_ref, DOWN_AZ), inlet)
    lane = lane_index(pad)
    spread = packed(lambda r: x1_ref[:, at(r)], pad, plan.rows * WINDOW, WINDOW)
    for r in range(plan.rows):
        spread = jnp.where(lane == r * WINDOW, rolled(inlet, r * (WINDOW - 1)), spread)
    inlet = jnp.where(parity() == 0, spread, rolled(spread, LANES // 2))
    back = pick(inlet, plan.window_spread()) * weight_ref[...]
    back = back + rolled(back, -plan.width)
    me = lax.axis_index("sector")
    send_ref[...] = jnp.zeros_like(send_ref)
    for t in range(plan.insts):
        to = lax.rem(me + plan.shift[t], plan.sectors)
        send_ref[to, : plan.fields, : plan.width] = back[t * plan.fields : (t + 1) * plan.fields, : plan.width]


def outer(plan, w_ref, rates_ref, n0_ref, h0_ref, x1_ref, far_ref, out_ref):
    mirror = parity()

    def put(a, r, value):
        there = jnp.where(mirror == 0, a, plan.ct - 1 - a) * plan.rows + r
        out_ref[pl.ds(there, plan.tf, stride=plan.cells), :] = value[: plan.tf]

    for r in range(plan.rows):
        put(1, r, x1_ref[:, at(r)])

    def near_chunk(c):
        lanes = slice(c * CHUNK, (c + 1) * CHUNK)
        return n0_ref[:, lanes] - rates_ref[0:1, lanes] * dot3(w_ref[...], far_ref[:, lanes])

    azimuthal(plan, w_ref, 0, near_chunk, lambda r, terms: put(0, r, h0_ref[:, at(r)] - rates_ref[1:2, at(r)] * terms))


def collect_panels(plan, got_ref, out_ref, panels_ref):
    me = lax.axis_index("sector")
    for t in range(plan.insts):
        source = lax.rem(me + (plan.sectors - plan.shift[t]), plan.sectors)
        panels_ref[t * RATES : (t + 1) * RATES, :] = got_ref[source]
    for f in range(plan.fields):
        tile = panels_ref[pl.ds(f, plan.insts, stride=RATES), : plan.width]
        out_ref[f] = jnp.transpose(tile)


def sibling(plan):
    return [s ^ 1 for s in range(plan.sectors)]


def outside(plan):
    return [(s - 1 if s % 2 == 0 else s + 1) % plan.sectors for s in range(plan.sectors)]


def swap(array, partner):
    return lax.ppermute(array, "sector", list(enumerate(partner)))


def beside(plan, array, partner):
    def pairs(step):
        out = []
        for s in range(plan.sectors):
            for x in range(plan.spans):
                to = 1 - x if plan.ends == 1 else x + step
                if 0 <= to < plan.spans:
                    out.append((s * plan.spans + x, partner[s] * plan.spans + to))
        return out

    if plan.ends == 1:
        return lax.ppermute(array, AXES, pairs(0))
    return jnp.concatenate([lax.ppermute(array[:1], AXES, pairs(-1)), lax.ppermute(array[1:], AXES, pairs(1))])


def on_device(
    sectors, spans,
    rhs, diag_coef, face_coef, time_coef, jac_up, jac_down, wall_mask, stator_adj, owner, first_panel_share,
):
    plan = Plan(rhs, stator_adj, sectors, spans)
    pad, cells, slab, insts, fields, ends = plan.pad, plan.cells, plan.slab, plan.insts, plan.fields, plan.ends
    bind = functools.partial
    whole, half = f32(pad, plan.ct * slab), f32(pad, slab)
    products = (vmem(6 * pad, slab),) * 2
    alone, next_chip, next_core = list(range(sectors)), outside(plan), sibling(plan)

    def edges(rows):
        return f32(ends, rows, DEPTH * plan.ct * LANES), f32(ends, rows, LANES), f32(ends, rows, LANES)

    stator = jnp.transpose(stator_adj, (1, 2, 3, 0)).reshape(fields, plan.width, insts)
    sent = call(bind(send_panels, plan), f32(sectors * spans, RATES, LANES), (vmem(insts * RATES, LANES),))(stator)
    got = lax.all_to_all(sent, AXES, 0, 0, tiled=True)
    m, side, c0, c1 = call(
        bind(prepare, plan), (f32(pad + RATES, plan.ct * slab),) + edges(pad + RATES), (vmem(6, cells, LANES),)
    )(
        rhs.reshape(plan.tf * cells, LANES),
        jnp.concatenate([
            wall_mask.astype(jnp.float32).reshape(cells, LANES), diag_coef.reshape(cells, LANES),
            time_coef.reshape(cells, LANES), face_coef.reshape(3 * cells, LANES),
        ]),
        jnp.concatenate([
            lax.rem(owner, plan.panels).astype(jnp.float32).reshape(insts, cells), first_panel_share.reshape(insts, cells),
        ], axis=1),
    )
    low_first, high_first = swap(m, next_chip), swap(m, next_core)
    side_first = beside(plan, side, alone)
    c_low, c_high = beside(plan, c0, next_chip), beside(plan, c1, next_core)
    matrices, down = call(
        bind(stack_matrices, plan),
        [jax.ShapeDtypeStruct((count * pad, 3 * pad), jnp.bfloat16) for count in (7, 1)],
    )(jac_up, jac_down, plan.spectral(), plan.field_rows(), plan.field_lanes(), plan.block_diagonal())
    tiles = len(plan.tiles)
    seams, weight, force, g = call(
        bind(begin, plan), (f32(3, 1 + ends, pad, LANES), f32(pad, LANES), whole, whole),
        (vmem(pad, tiles * LANES), vmem(tiles * pad, LANES), vmem(16, tiles * LANES)) + products,
        flops=2_000_000_000,
    )(matrices, m, got, low_first, high_first, side_first, c_low, c_high)
    x, near, side, c0, c1 = call(
        bind(first_half, plan), (whole, half) + edges(pad),
        products + (vmem(pad, 2 * slab),) + (vmem(pad, slab),) * 4 + (vmem(LANES, LANES),),
        flops=4_000_000_000,
    )(matrices, m, force, g, low_first, high_first, side_first, c_low, c_high, seams)

    low, high = swap(near, next_chip), swap(x, next_core)
    side = beside(plan, side, alone)
    c_low, c_high = beside(plan, c0, next_chip), beside(plan, c1, next_core)
    (g,) = call(bind(inner, plan), (whole,), products, flops=2_000_000_000)(matrices, m, force, x)
    far = call(bind(hold_far, plan), half)(x, side, c_low, c_high)
    far_low = swap(far, next_chip)
    back, n0, h0, x1, rates = call(
        bind(middle, plan), (f32(sectors, RATES, LANES), half, half, half, f32(RATES, slab)),
        products + (vmem(pad, 2 * slab), vmem(pad, slab), vmem(pad, slab), vmem(LANES, LANES)),
        flops=4_000_000_000,
    )(
        matrices, m, force, x, g, low, high, side, c_low, c_high, low_first, high_first, side_first, seams, weight
    )
    returned = lax.all_to_all(back, "sector", 0, 0, tiled=True)
    sens = call(bind(collect_panels, plan), f32(fields, plan.width, insts), (vmem(insts * RATES, LANES),))(returned)
    out = call(bind(outer, plan), f32(plan.tf * cells, LANES))(down, rates, n0, h0, x1, far_low)
    sens = jnp.transpose(sens.reshape(fields, plan.panels, plan.rows, insts), (3, 0, 1, 2))
    return out.reshape(rhs.shape), sens


def solution(mesh):
    in_specs = (
        P(None, None, "sector", "span", None),
        P("sector", "span", None),
        P(None, "sector", "span", None),
        P("sector", "span", None),
        P(),
        P(),
        P("sector", "span", None),
        P(None, None, "sector", "span"),
        P(None, "sector", "span"),
        P(None, "sector", "span"),
    )
    out_specs = (P(None, None, "sector", "span", None), P(None, None, "sector", "span"))
    return jax.shard_map(
        functools.partial(on_device, mesh.shape["sector"], mesh.shape["span"]),
        mesh=mesh, in_specs=in_specs, out_specs=out_specs, check_vma=False,
    )
```

```python
import functools

import jax
import jax.numpy as jnp
import ml_dtypes
import numpy as np
from jax import lax
from jax.experimental import pallas as pl
from jax.experimental.pallas import tpu as pltpu
from jax.sharding import PartitionSpec as P

SWEEPS = 4
DEPTH = 2
LANES = 128
CHUNK = 256
WINDOW = 8
HIGHEST = lax.Precision.HIGHEST
DOWN_AZ, SPECTRAL, UP_SP, DOWN_SP, UP_AX, DOWN_AX, UP_AZ = range(7)
C_TIME, C_AZ, C_SP, C_UP, C_DOWN, C_MASK = range(6)
RATES = 8
AXES = ("sector", "span")


class Plan:
    def __init__(self, rhs, stator_adj, sectors, spans):
        self.insts, self.fields, self.ct, self.rows, self.nax = rhs.shape
        self.panels = stator_adj.shape[2]
        self.sectors, self.spans = sectors, spans
        self.tf = self.insts * self.fields
        self.pad = -(-self.tf // 16) * 16
        self.cells = self.ct * self.rows
        self.slab = self.rows * LANES
        self.width = self.panels * self.rows
        self.shift = [
            ((t * sectors) // (self.insts - 1) - t // (self.insts - 1)) % sectors for t in range(self.insts)
        ]
        assert self.ct == 2 and self.nax == LANES and SWEEPS % DEPTH == 0 and spans > 1
        assert len(set(self.shift)) == self.insts and self.cells * WINDOW == LANES and self.rows >= SWEEPS
        assert self.slab % CHUNK == 0 and 3 * self.pad <= 256 and 2 * self.ct * self.width == LANES
        assert sectors % 2 == 0
        self.ends = 1 if spans == 2 else 2
        self.blocks = [-1, 0, 1]
        self.halves = [0, 1] if spans == 2 else [-1, 0, 1]
        self.tiles = [(k, x) for k in self.blocks for x in self.halves]
        self.slots = [
            [t for t in range(self.insts) if any((k + self.shift[t]) % sectors == o for k in self.blocks)]
            for o in range(sectors)
        ]
        last = LANES - self.width
        self.weight_at = [(t, last) for t in range(self.fields)] + [
            (self.fields, i * self.width) for i in range(self.insts - self.fields)
        ]
        assert max(map(len, self.slots)) * self.width <= last and 2 * self.cells == self.width
        assert self.fields == RATES - 1 and (self.insts - self.fields) * self.width <= LANES

    def spectral(self):
        t = np.arange(self.insts)
        off = t[:, None] - t[None, :]
        sines = np.where(off == 0, 1.0, np.sin(np.pi * off / self.insts))
        table = np.where(off == 0, 0.0, 0.5 * (1.0 - 2.0 * (off % 2)) / sines).astype(np.float32)
        full = np.zeros((self.pad, self.pad), np.float32)
        full[: self.tf, : self.tf] = np.kron(table.T, np.eye(self.fields, dtype=np.float32))
        hi = full.astype(ml_dtypes.bfloat16)
        lo = (full - hi.astype(np.float32)).astype(ml_dtypes.bfloat16)
        return np.concatenate([hi, lo, hi], axis=1)

    def field_rows(self):
        out = np.zeros((self.pad, self.fields), np.float32)
        out[np.arange(self.tf), np.arange(self.tf) % self.fields] = 1.0
        return out

    def field_lanes(self):
        return np.tile(self.field_rows().T, (1, 3))

    def block_diagonal(self):
        block = np.full(self.pad, -1)
        block[: self.tf] = np.arange(self.tf) // self.fields
        same = (block[:, None] == block[None, :]) & (block[:, None] >= 0)
        return np.tile(same.astype(np.float32), (1, 3))


    def inst_rows(self):
        row, inst = table_index(self.pad, 16)
        return ((row >= inst * self.fields) & (row < (inst + 1) * self.fields)).astype(jnp.float32)

    def cell_of(self, lane):
        return lax.div(lane, self.width) * self.rows + lax.rem(lane, self.rows)

    def window_lanes(self):
        lane, to = table_index(LANES, LANES)
        return (lane < self.ct * self.width) & (to == self.cell_of(lane) * WINDOW)

    def window_spread(self):
        to, lane = table_index(LANES, LANES)
        return (lane < self.ct * self.width) & (to == self.cell_of(lane) * WINDOW)

    def weight_lanes(self):
        cell, lane = table_index(LANES, LANES)
        half = self.ct * self.width
        wanted = jnp.where(lane < half, self.cell_of(lane), self.cells + self.cell_of(lane - half))
        return cell == wanted

    def panel_lanes(self):
        lane = lane_index(1)
        panel = lax.rem(lax.div(lane, self.rows), self.panels)
        return jnp.where(lane < self.ct * self.width, panel, -9).astype(jnp.float32)


def table_index(rows, columns):
    return [lax.broadcasted_iota(jnp.int32, (rows, columns), axis) for axis in (0, 1)]


def call(kernel, out, scratch=(), flops=2_000_000, nbytes=1_000_000):
    return pl.pallas_call(
        kernel,
        out_shape=out,
        scratch_shapes=list(scratch),
        compiler_params=pltpu.CompilerParams(vmem_limit_bytes=20 * 1024 * 1024),
        cost_estimate=pl.CostEstimate(flops=flops, bytes_accessed=nbytes, transcendentals=0),
    )


def f32(*shape):
    return jax.ShapeDtypeStruct(shape, jnp.float32)


def vmem(*shape):
    return pltpu.VMEM(shape, jnp.float32)


def halves_of(x):
    hi = x.astype(jnp.bfloat16)
    return hi, (x - hi.astype(jnp.float32)).astype(jnp.bfloat16)


def dot3(w, x):
    hi, lo = halves_of(x)
    return jnp.dot(w, jnp.concatenate([hi, hi, lo], axis=0), preferred_element_type=jnp.float32)


def pick(x, table):
    table = table.astype(jnp.float32).astype(jnp.bfloat16)
    table = jnp.concatenate([table, table], axis=0)
    return jnp.dot(jnp.concatenate(halves_of(x), axis=1), table, preferred_element_type=jnp.float32)


def dot_full(a, b):
    return jnp.dot(a, b, precision=HIGHEST, preferred_element_type=jnp.float32)


def lane_index(rows):
    return lax.broadcasted_iota(jnp.int32, (rows, LANES), 1)


def rolled(x, by):
    by %= LANES
    return pltpu.roll(x, by, axis=1) if by else x


def at(r, count=1, start=0):
    return slice(start + r * LANES, start + (r + count) * LANES)


def parity():
    return lax.rem(lax.axis_index("sector"), 2)


def has_sides(plan):
    span = lax.axis_index("span")
    return jnp.where(span < plan.spans - 1, 1.0, 0.0), jnp.where(span > 0, 1.0, 0.0)


class Layer:
    def __init__(self, plan, ref, start=0, rates=None, seam=None, layer=0):
        self.plan, self.ref, self.start, self.seam, self.layer = plan, ref, start, seam, layer
        self.rates = rates or (ref, start)

    def rate(self, which, r, count=1):
        ref, start = self.rates
        row = self.plan.pad + which
        return ref[row : row + 1, at(r, count, start)]

    def row(self, r):
        value = self.ref[: self.plan.pad, at(r, 1, self.start)]
        if self.seam is None:
            return value
        return value + placed(self.seam, self.layer * self.plan.rows + r) * self.rate(C_MASK, r)

    def chunk(self, c):
        count = CHUNK // LANES
        if self.seam is None:
            return self.ref[: self.plan.pad, at(c * count, count, self.start)]
        return jnp.concatenate([self.row(c * count + part) for part in range(count)], axis=1)


def placed(tile, cell):
    return jnp.where(lane_index(tile.shape[0]) == 0, rolled(tile, -cell * WINDOW), 0.0)


class Products:
    def __init__(self, plan, w_ref, p_ref, first):
        self.plan, self.w, self.p, self.first = plan, w_ref, p_ref, first

    def fill(self, layer):
        for c in range(self.plan.slab // CHUNK):
            self.p[:, c * CHUNK : (c + 1) * CHUNK] = dot3(matrix(self.plan, self.w, self.first, 6), layer.chunk(c))
        self.layer = layer
        return self

    def get(self, block, r):
        row = (block - self.first) * self.plan.pad
        return self.p[row : row + self.plan.pad, at(r)]

    def own_terms(self, r):
        rate = self.layer.rate
        total = rate(C_TIME, r) * self.get(SPECTRAL, r)
        beside = []
        if r + 1 < self.plan.rows:
            beside.append(self.get(UP_SP, r + 1))
        if r > 0:
            beside.append(self.get(DOWN_SP, r - 1))
        total = total + rate(C_SP, r) * sum(beside[1:], beside[0])
        total = total + rate(C_UP, r) * rolled(self.get(UP_AX, r), -1)
        return total + rate(C_DOWN, r) * rolled(self.get(DOWN_AX, r), 1)


def matrix(plan, w_ref, block, count=1):
    return w_ref[block * plan.pad : (block + count) * plan.pad, :]


def two_layers(plan, ref, rates=None, seam=None):
    return [
        Layer(plan, ref, a * plan.slab, (rates, a * plan.slab) if rates is not None else None, seam, a)
        for a in range(plan.ct)
    ]


def inner_rows(plan, w_ref, p_refs, layers, force, g_ref):
    first = Products(plan, w_ref, p_refs[0], DOWN_AZ).fill(layers[0])
    second = Products(plan, w_ref, p_refs[1], SPECTRAL).fill(layers[1])
    for r in range(plan.rows):
        other = second.get(UP_AZ, r), first.get(DOWN_AZ, r)
        for a, products in enumerate((first, second)):
            total = products.own_terms(r) + layers[a].rate(C_AZ, r) * other[a]
            if isinstance(g_ref, tuple):
                g_ref[a][:, at(r)] = force[a].row(r) - total
            else:
                g_ref[:, at(r, 1, a * plan.slab)] = force[a].row(r) - total


def azimuthal(plan, w_ref, block, chunk_of, take):
    for c in range(plan.slab // CHUNK):
        terms = dot3(matrix(plan, w_ref, block), chunk_of(c))
        for part in range(CHUNK // LANES):
            take(c * (CHUNK // LANES) + part, terms[:, at(part)])


def middle_rows(plan, w_ref, p_refs, own, own_force, g_ref, near, near_force, side, corner, y_ref, h_refs, n_refs):
    pad, rows, ct = plan.pad, plan.rows, plan.ct
    outward, inward, last = (UP_SP, DOWN_SP), (DOWN_SP, UP_SP), (rows - 1, 0)
    edge_terms, edge_new, corner_terms = [], [], []
    for n in range(2):
        first, second, edge_force, edge_rate = side(n)
        corners = corner(n)
        every = dot3(w_ref[...], first)
        edge_terms.append(every[outward[n] * pad : (outward[n] + 1) * pad])
        corner_terms.append([dot3(matrix(plan, w_ref, outward[n]), c) for c in corners])
        beyond = dot3(matrix(plan, w_ref, outward[n]), second)
        within = dot3(matrix(plan, w_ref, inward[n]), jnp.concatenate([x.row(last[n]) for x in own], axis=1))
        from_low = dot3(matrix(plan, w_ref, DOWN_AZ), corners[0])
        from_high = dot3(matrix(plan, w_ref, UP_AZ), corners[1])
        new = []
        for a in range(ct):

            def part(block, b=a):
                return every[block * pad : (block + 1) * pad, at(b)]

            around = part(UP_AZ, 1) + from_low if a == 0 else from_high + part(DOWN_AZ, 0)
            total = edge_rate(C_TIME, a) * part(SPECTRAL) + edge_rate(C_AZ, a) * around
            total = total + edge_rate(C_SP, a) * (beyond[:, at(a)] + within[:, at(a)])
            total = total + edge_rate(C_UP, a) * rolled(part(UP_AX), -1)
            total = total + edge_rate(C_DOWN, a) * rolled(part(DOWN_AX), 1)
            new.append(edge_force[:, at(a)] - total)
        edge_new.append(dot3(matrix(plan, w_ref, outward[n]), jnp.concatenate(new, axis=1)))

    products = (
        Products(plan, w_ref, p_refs[0], DOWN_AZ).fill(near[0]), Products(plan, w_ref, p_refs[1], SPECTRAL).fill(near[1]),
    )
    for a, (to_own, to_near) in enumerate(((DOWN_AZ, UP_AZ), (UP_AZ, DOWN_AZ))):

        def take(r, terms):
            total = products[a].own_terms(r) + near[a].rate(C_AZ, r) * terms
            mine = own[a].rate(C_AZ, r) * products[a].get(to_own, r)
            for n in range(2):
                if r == last[n]:
                    total = total + near[a].rate(C_SP, r) * corner_terms[n][a]
                    mine = mine + own[a].rate(C_SP, r) * edge_terms[n][:, at(a)]
            n_refs[a][:, at(r)] = near_force[a].row(r) - total
            lanes = at(r, 1, a * plan.slab)
            y_ref[:, lanes] = g_ref[:, lanes] - mine

        azimuthal(plan, w_ref, to_near, own[a].chunk, take)

    after = [Layer(plan, y_ref, a * plan.slab, own[a].rates) for a in range(ct)]
    inner_rows(plan, w_ref, p_refs, after, own_force, h_refs)
    for a in range(ct):
        for n in range(2):
            h_refs[a][:, at(last[n])] -= own[a].rate(C_SP, last[n]) * edge_new[n][:, at(a)]


def outer_rows(plan, w_ref, own, near, far_chunks, n_refs, h_refs, put, layers=(0, 1)):
    count = CHUNK // LANES
    for a in layers:
        block = (DOWN_AZ, UP_AZ)[a]

        def near_chunk(c):
            terms = dot3(matrix(plan, w_ref, block), far_chunks[a](c))
            return n_refs[a][:, at(c * count, count)] - near[a].rate(C_AZ, c * count, count) * terms

        def take(r, terms):
            put(a, r, h_refs[a][:, at(r)] - own[a].rate(C_AZ, r) * terms)

        azimuthal(plan, w_ref, block, near_chunk, take)


def sides_of(plan, side_ref, force_ref, seams_ref):
    pad, ct = plan.pad, plan.ct
    keeps = has_sides(plan)

    def read(n, ref, e, seam):
        i = n if plan.ends == 2 else 0
        value = ref[i, :pad, at(e * ct, ct)]
        if seam:
            r = e if n == 0 else plan.rows - 1 - e
            tile = seams_ref[1, 1 + i]
            scale = ref[i, pad + C_MASK : pad + C_MASK + 1, at(e * ct, ct)]
            value = value + jnp.concatenate([placed(tile, a * plan.rows + r) for a in range(ct)], axis=1) * scale
        return value * keeps[n]

    def side(n):
        i = n if plan.ends == 2 else 0
        same = side_ref is force_ref

        def rate(which, a):
            return force_ref[i, pad + which : pad + which + 1, at(a)] * keeps[n]

        force = read(n, force_ref, 0, True)
        first = force if same else read(n, side_ref, 0, False)
        return first, read(n, side_ref, 1, same), force, rate

    return side


def corners_of(plan, c_refs, seams_ref):
    keeps = has_sides(plan)

    def corner(n):
        i = n if plan.ends == 2 else 0
        out = []
        for a, c_ref in enumerate(c_refs):
            value = c_ref[i, : plan.pad]
            if seams_ref is not None:
                r = 0 if n == 0 else plan.rows - 1
                scale = c_ref[i, plan.pad + C_MASK : plan.pad + C_MASK + 1]
                value = value + placed(seams_ref[2 * a, 1 + i], a * plan.rows + r) * scale
            out.append(value * keeps[n])
        return out

    return corner


def prepare(plan, rhs_ref, coef_ref, m_ref, side_ref, c0_ref, c1_ref, rates_ref):
    pad, cells = plan.pad, plan.cells
    mask, diag, time, *face = [coef_ref[cells * i : cells * (i + 1), :] for i in range(6)]
    scale = mask / diag
    lane = lane_index(cells)
    axial = scale * face[2]
    rates = (
        scale * time, scale * face[0], scale * face[1],
        jnp.where(lane < LANES - 1, axial, 0.0), jnp.where(lane > 0, axial, 0.0), scale,
    )
    for i, rate in enumerate(rates):
        rates_ref[i] = rate
    tail = jnp.zeros((pad - plan.tf, LANES), jnp.float32)
    rest = jnp.zeros((RATES - 6, LANES), jnp.float32)
    mirror = parity()
    for cell in range(cells):
        a, r = divmod(cell, plan.rows)
        there = jnp.where(mirror == 0, a, plan.ct - 1 - a) * plan.rows + r
        table = [rates_ref[i, pl.ds(there, 1), :] for i in range(6)]
        field = jnp.concatenate([rhs_ref[pl.ds(there, plan.tf, stride=cells), :], tail], axis=0)
        m_ref[:pad, at(cell)] = field * table[C_MASK]
        m_ref[pad:, at(cell)] = jnp.concatenate(table + [rest], axis=0)
    write_edges(plan, m_ref, side_ref, (c0_ref, c1_ref))


def write_edges(plan, x_ref, side_ref, c_refs):
    first = lax.axis_index("span") == 0
    for a in range(plan.ct):
        for e in range(DEPTH):
            low, high = x_ref[:, at(a * plan.rows + e)], x_ref[:, at((a + 1) * plan.rows - 1 - e)]
            ends = [jnp.where(first, high, low)] if plan.ends == 1 else [low, high]
            for n, end in enumerate(ends):
                side_ref[n, :, at(e * plan.ct + a)] = end
                if e == 0:
                    c_refs[a][n] = end


def stack_matrices(plan, up_ref, down_ref, spectral_ref, rows_ref, lanes_ref, diagonal_ref, out_ref, down_out):
    pad = plan.pad
    lane = lax.broadcasted_iota(jnp.int32, (pad, 3 * pad), 1)
    second = (lane >= pad) & (lane < 2 * pad)
    out_ref[SPECTRAL * pad : (SPECTRAL + 1) * pad, :] = spectral_ref[...]
    even = parity() == 0
    for block, small in (
        (DOWN_AZ, jnp.where(even, down_ref[0], up_ref[0])), (UP_AZ, jnp.where(even, up_ref[0], down_ref[0])),
        (UP_SP, up_ref[1]), (DOWN_SP, down_ref[1]), (UP_AX, up_ref[2]), (DOWN_AX, down_ref[2]),
    ):
        full = dot_full(dot_full(rows_ref[...], small), lanes_ref[...]) * diagonal_ref[...]
        hi = full.astype(jnp.bfloat16).astype(jnp.float32)
        out_ref[block * pad : (block + 1) * pad, :] = jnp.where(second, full - hi, hi).astype(jnp.bfloat16)
    down_out[...] = matrix(plan, out_ref, DOWN_AZ)


def send_panels(plan, stator_ref, both_ref, out_ref, panels_ref):
    me = lax.axis_index("sector")
    for f in range(plan.fields):
        panels_ref[pl.ds(f, plan.insts, stride=RATES), : plan.width] = jnp.transpose(stator_ref[f])
    out_ref[...] = jnp.zeros_like(out_ref)
    for t, (row, start) in enumerate(plan.weight_at):
        both = jnp.broadcast_to(both_ref[t : t + 1, :][None], (out_ref.shape[0], 1, plan.width))
        out_ref[:, row : row + 1, start : start + plan.width] = both
    for o, slots in enumerate(plan.slots):
        to = lax.rem(me + (plan.sectors - o), plan.sectors) * plan.spans
        for slot, t in enumerate(slots):
            lanes = slice(slot * plan.width, (slot + 1) * plan.width)
            panels = panels_ref[t * RATES : t * RATES + plan.fields, : plan.width]
            for x in range(plan.spans):
                out_ref[to + x, : plan.fields, lanes] = panels


def begin(
    plan, w_ref, m_ref, got_ref,
    seams_ref, weight_ref, x_ref, g_ref, panels_ref, terms_ref, rows_ref, p0_ref, p1_ref,
):
    pad, insts, fields = plan.pad, plan.insts, plan.fields
    me, span = lax.axis_index("sector"), lax.axis_index("span")
    even, is_first = parity() == 0, span == 0
    tiles = plan.tiles
    panels_ref[...] = jnp.zeros_like(panels_ref)
    rows_ref[...] = jnp.zeros_like(rows_ref)
    for n, (k, x) in enumerate(tiles):
        at_span = x if plan.spans == 2 else jnp.clip(span + x, 0, plan.spans - 1)
        for t in range(insts):
            o = (k + plan.shift[t]) % plan.sectors
            source = lax.rem(me + o, plan.sectors) * plan.spans + at_span
            tile = rolled(got_ref[source], -plan.slots[o].index(t) * plan.width)
            panels_ref[t * fields : (t + 1) * fields, n * LANES : n * LANES + plan.width] = tile[:fields, : plan.width]
        tile = got_ref[lax.rem(me + k + plan.sectors, plan.sectors) * plan.spans + at_span]
        lanes = slice(n * LANES, n * LANES + plan.width)
        rows_ref[:fields, lanes] = rolled(tile, -plan.weight_at[0][1])[:fields, : plan.width]
        for t in range(fields, insts):
            row, start = plan.weight_at[t]
            rows_ref[t : t + 1, lanes] = rolled(tile, -start)[row : row + 1, : plan.width]
    spread = dot_full(plan.inst_rows(), rows_ref[...])
    spread = pick(jnp.concatenate([spread[:, at(n)] for n in range(len(tiles))], axis=0), plan.weight_lanes())
    first, share, panel = spread, rolled(spread, plan.ct * plan.width), plan.panel_lanes()
    lower = (jnp.abs(first - panel) < 0.5).astype(jnp.float32)
    upper = (jnp.abs(first + 1.0 - panel) < 0.5).astype(jnp.float32)
    weights = share * lower + (1.0 - share) * upper
    for n in range(len(tiles)):
        panels = panels_ref[:, at(n)]
        terms_ref[n * pad : (n + 1) * pad, :] = panels + rolled(panels, plan.width)
    seams = pick(terms_ref[...] * weights, plan.window_lanes())

    def tile(values, k, x):
        n = tiles.index((k, x))
        return values[n * pad : (n + 1) * pad]

    def around(values, k):
        if plan.spans == 2:
            pair = tile(values, k, 0), tile(values, k, 1)
            return [jnp.where(is_first, pair[0], pair[1]), jnp.where(is_first, pair[1], pair[0])]
        return [tile(values, k, x) for x in (0, 1, -1)]

    def mirrored(value):
        return rolled(value, LANES // 2)

    here = around(seams, 0)
    behind, ahead = around(seams, -1), around(seams, 1)
    for i in range(1 + plan.ends):
        seams_ref[0, i] = jnp.where(even, mirrored(behind[i]), ahead[i])
        seams_ref[1, i] = jnp.where(even, here[i], mirrored(here[i]))
        seams_ref[2, i] = jnp.where(even, mirrored(ahead[i]), behind[i])
    weight_ref[...] = around(weights, 0)[0]

    for layer in two_layers(plan, m_ref, seam=seams_ref[1, 0]):
        for r in range(plan.rows):
            x_ref[:, at(r, 1, layer.start)] = layer.row(r)
    layers = two_layers(plan, x_ref, m_ref)
    inner_rows(plan, w_ref, (p0_ref, p1_ref), layers, layers, g_ref)


def first_half(
    plan, w_ref, m_ref, f_ref, g_ref, low_ref, high_ref, side_ref, c_low, c_high, seams_ref,
    x_ref, near_ref, side_out, c0_ref, c1_ref, p0_ref, p1_ref, y_ref, h0_ref, h1_ref, n0_ref, n1_ref, inlet_ref,
):
    own = two_layers(plan, f_ref, m_ref)
    low = two_layers(plan, low_ref, seam=seams_ref[0, 0])
    high = two_layers(plan, high_ref, seam=seams_ref[2, 0])
    near = low[0], high[1]
    n_refs = n0_ref, n1_ref
    middle_rows(
        plan, w_ref, (p0_ref, p1_ref), own, own, g_ref, near, near, sides_of(plan, side_ref, side_ref, seams_ref),
        corners_of(plan, (c_low, c_high), seams_ref), y_ref, (h0_ref, h1_ref), n_refs,
    )
    lane = lane_index(plan.pad)
    inlet_ref[...] = jnp.zeros_like(inlet_ref)

    def put(a, r, value):
        x_ref[:, at(r, 1, a * plan.slab)] = value
        if a == 0:
            near_ref[:, at(r)] = value
        else:
            inlet_ref[: plan.pad, :] = jnp.where(lane == r, rolled(value, r), inlet_ref[: plan.pad, :])

    outer_rows(plan, w_ref, own, near, (low[1].chunk, high[0].chunk), n_refs, (h0_ref, h1_ref), put)
    turned = jnp.transpose(inlet_ref[...])
    for r in range(plan.rows):
        near_ref[plan.tf : plan.tf + 1, at(r)] = turned[r : r + 1, :]
    write_edges(plan, x_ref, side_out, (c0_ref, c1_ref))


def hold_far(plan, x_ref, side_ref, c_high, far_ref):
    come = side_ref[0, 0:1, 0:1] + c_high[0, 0:1, 0:1]
    far_ref[...] = x_ref[:, plan.slab :] + 0.0 * come


def inner(plan, w_ref, m_ref, f_ref, x_ref, g_ref, p0_ref, p1_ref):
    inner_rows(plan, w_ref, (p0_ref, p1_ref), two_layers(plan, x_ref, m_ref), two_layers(plan, f_ref, m_ref), g_ref)


def middle(
    plan, w_ref, m_ref, f_ref, x_ref, g_ref, low_ref, high_ref, side_ref, c_low, c_high,
    low_first, high_first, side_first, seams_ref, weight_ref,
    send_ref, n0_ref, h0_ref, x1_ref, rates_ref, p0_ref, p1_ref, y_ref, h1_ref, n1_ref, turn_ref,
):
    pad = plan.pad
    own, force = two_layers(plan, x_ref, m_ref), two_layers(plan, f_ref, m_ref)
    low_force = Layer(plan, low_first, 0, None, seams_ref[0, 0], 0)
    high_force = Layer(plan, high_first, plan.slab, None, seams_ref[2, 0], 1)
    near = Layer(plan, low_ref, 0, low_force.rates), Layer(plan, high_ref, plan.slab, high_force.rates)
    n_refs = n0_ref, n1_ref
    middle_rows(
        plan, w_ref, (p0_ref, p1_ref), own, force, g_ref, near, (low_force, high_force),
        sides_of(plan, side_ref, side_first, seams_ref), corners_of(plan, (c_low, c_high), None), y_ref,
        (h0_ref, h1_ref), n_refs,
    )

    def put(a, r, value):
        x1_ref[:, at(r)] = value

    outer_rows(plan, w_ref, own, near, (None, Layer(plan, high_ref).chunk), n_refs, (h0_ref, h1_ref), put, (1,))
    for r in range(plan.rows):
        last = [near[0].rate(C_AZ, r), own[0].rate(C_AZ, r), jnp.zeros((RATES - 2, LANES), jnp.float32)]
        rates_ref[:, at(r)] = jnp.concatenate(last, axis=0)

    turn_ref[...] = jnp.zeros_like(turn_ref)
    for r in range(plan.rows):
        turn_ref[r : r + 1, :] = low_ref[plan.tf : plan.tf + 1, at(r)]
    far = jnp.transpose(turn_ref[...])[:pad]

    def packed(read, count, first=0, step=1):
        lane = lane_index(count)
        out = jnp.zeros((count, LANES), jnp.float32)
        for r in range(plan.rows):
            to = first + r * step
            out = jnp.where(lane == to, rolled(read(r), to), out)
        return out

    rates = packed(lambda r: rates_ref[:, at(r)], RATES)
    inlet = packed(lambda r: n0_ref[:, at(r)], pad) - rates[0:1] * dot3(matrix(plan, w_ref, DOWN_AZ), far)
    inlet = packed(lambda r: h0_ref[:, at(r)], pad) - rates[1:2] * dot3(matrix(plan, w_ref, DOWN_AZ), inlet)
    lane = lane_index(pad)
    spread = packed(lambda r: x1_ref[:, at(r)], pad, plan.rows * WINDOW, WINDOW)
    for r in range(plan.rows):
        spread = jnp.where(lane == r * WINDOW, rolled(inlet, r * (WINDOW - 1)), spread)
    inlet = jnp.where(parity() == 0, spread, rolled(spread, LANES // 2))
    back = pick(inlet, plan.window_spread()) * weight_ref[...]
    back = back + rolled(back, -plan.width)
    me = lax.axis_index("sector")
    send_ref[...] = jnp.zeros_like(send_ref)
    for t in range(plan.insts):
        to = lax.rem(me + plan.shift[t], plan.sectors)
        send_ref[to, : plan.fields, : plan.width] = back[t * plan.fields : (t + 1) * plan.fields, : plan.width]


def outer(plan, w_ref, rates_ref, n0_ref, h0_ref, x1_ref, far_ref, out_ref):
    mirror = parity()

    def put(a, r, value):
        there = jnp.where(mirror == 0, a, plan.ct - 1 - a) * plan.rows + r
        out_ref[pl.ds(there, plan.tf, stride=plan.cells), :] = value[: plan.tf]

    for r in range(plan.rows):
        put(1, r, x1_ref[:, at(r)])

    def near_chunk(c):
        lanes = slice(c * CHUNK, (c + 1) * CHUNK)
        return n0_ref[:, lanes] - rates_ref[0:1, lanes] * dot3(w_ref[...], far_ref[:, lanes])

    azimuthal(plan, w_ref, 0, near_chunk, lambda r, terms: put(0, r, h0_ref[:, at(r)] - rates_ref[1:2, at(r)] * terms))


def collect_panels(plan, got_ref, out_ref, panels_ref):
    me = lax.axis_index("sector")
    for t in range(plan.insts):
        source = lax.rem(me + (plan.sectors - plan.shift[t]), plan.sectors)
        panels_ref[t * RATES : (t + 1) * RATES, :] = got_ref[source]
    for f in range(plan.fields):
        tile = panels_ref[pl.ds(f, plan.insts, stride=RATES), : plan.width]
        out_ref[f] = jnp.transpose(tile)


def sibling(plan):
    return [s ^ 1 for s in range(plan.sectors)]


def outside(plan):
    return [(s - 1 if s % 2 == 0 else s + 1) % plan.sectors for s in range(plan.sectors)]


def swap(array, partner):
    return lax.ppermute(array, "sector", list(enumerate(partner)))


def beside(plan, array, partner):
    def pairs(step):
        out = []
        for s in range(plan.sectors):
            for x in range(plan.spans):
                to = 1 - x if plan.ends == 1 else x + step
                if 0 <= to < plan.spans:
                    out.append((s * plan.spans + x, partner[s] * plan.spans + to))
        return out

    if plan.ends == 1:
        return lax.ppermute(array, AXES, pairs(0))
    return jnp.concatenate([lax.ppermute(array[:1], AXES, pairs(-1)), lax.ppermute(array[1:], AXES, pairs(1))])


def on_device(
    sectors, spans,
    rhs, diag_coef, face_coef, time_coef, jac_up, jac_down, wall_mask, stator_adj, owner, first_panel_share,
):
    plan = Plan(rhs, stator_adj, sectors, spans)
    pad, cells, slab, insts, fields, ends = plan.pad, plan.cells, plan.slab, plan.insts, plan.fields, plan.ends
    bind = functools.partial
    whole, half = f32(pad, plan.ct * slab), f32(pad, slab)
    products = (vmem(6 * pad, slab),) * 2
    alone, next_chip, next_core = list(range(sectors)), outside(plan), sibling(plan)

    def edges(rows):
        return f32(ends, rows, DEPTH * plan.ct * LANES), f32(ends, rows, LANES), f32(ends, rows, LANES)

    stator = jnp.transpose(stator_adj, (1, 2, 3, 0)).reshape(fields, plan.width, insts)
    sent = call(bind(send_panels, plan), f32(sectors * spans, RATES, LANES), (vmem(insts * RATES, LANES),))(
        stator,
        jnp.concatenate([
            lax.rem(owner, plan.panels).astype(jnp.float32).reshape(insts, cells), first_panel_share.reshape(insts, cells),
        ], axis=1),
    )
    got = lax.all_to_all(sent, AXES, 0, 0, tiled=True)
    m, side, c0, c1 = call(
        bind(prepare, plan), (f32(pad + RATES, plan.ct * slab),) + edges(pad + RATES), (vmem(6, cells, LANES),)
    )(
        rhs.reshape(plan.tf * cells, LANES),
        jnp.concatenate([
            wall_mask.astype(jnp.float32).reshape(cells, LANES), diag_coef.reshape(cells, LANES),
            time_coef.reshape(cells, LANES), face_coef.reshape(3 * cells, LANES),
        ]),
    )
    low_first, high_first = swap(m, next_chip), swap(m, next_core)
    side_first = beside(plan, side, alone)
    c_low, c_high = beside(plan, c0, next_chip), beside(plan, c1, next_core)
    matrices, down = call(
        bind(stack_matrices, plan),
        [jax.ShapeDtypeStruct((count * pad, 3 * pad), jnp.bfloat16) for count in (7, 1)],
    )(jac_up, jac_down, plan.spectral(), plan.field_rows(), plan.field_lanes(), plan.block_diagonal())
    tiles = len(plan.tiles)
    seams, weight, force, g = call(
        bind(begin, plan), (f32(3, 1 + ends, pad, LANES), f32(pad, LANES), whole, whole),
        (vmem(pad, tiles * LANES), vmem(tiles * pad, LANES), vmem(16, tiles * LANES)) + products,
        flops=2_000_000_000,
    )(matrices, m, got)
    x, near, side, c0, c1 = call(
        bind(first_half, plan), (whole, half) + edges(pad),
        products + (vmem(pad, 2 * slab),) + (vmem(pad, slab),) * 4 + (vmem(LANES, LANES),),
        flops=4_000_000_000,
    )(matrices, m, force, g, low_first, high_first, side_first, c_low, c_high, seams)

    low, high = swap(near, next_chip), swap(x, next_core)
    side = beside(plan, side, alone)
    c_low, c_high = beside(plan, c0, next_chip), beside(plan, c1, next_core)
    (g,) = call(bind(inner, plan), (whole,), products, flops=2_000_000_000)(matrices, m, force, x)
    far = call(bind(hold_far, plan), half)(x, side, c_high)
    far_low = swap(far, next_chip)
    back, n0, h0, x1, rates = call(
        bind(middle, plan), (f32(sectors, RATES, LANES), half, half, half, f32(RATES, slab)),
        products + (vmem(pad, 2 * slab), vmem(pad, slab), vmem(pad, slab), vmem(LANES, LANES)),
        flops=4_000_000_000,
    )(
        matrices, m, force, x, g, low, high, side, c_low, c_high, low_first, high_first, side_first, seams, weight
    )
    returned = lax.all_to_all(back, "sector", 0, 0, tiled=True)
    sens = call(bind(collect_panels, plan), f32(fields, plan.width, insts), (vmem(insts * RATES, LANES),))(returned)
    out = call(bind(outer, plan), f32(plan.tf * cells, LANES))(down, rates, n0, h0, x1, far_low)
    sens = jnp.transpose(sens.reshape(fields, plan.panels, plan.rows, insts), (3, 0, 1, 2))
    return out.reshape(rhs.shape), sens


def solution(mesh):
    in_specs = (
        P(None, None, "sector", "span", None),
        P("sector", "span", None),
        P(None, "sector", "span", None),
        P("sector", "span", None),
        P(),
        P(),
        P("sector", "span", None),
        P(None, None, "sector", "span"),
        P(None, "sector", "span"),
        P(None, "sector", "span"),
    )
    out_specs = (P(None, None, "sector", "span", None), P(None, None, "sector", "span"))
    return jax.shard_map(
        functools.partial(on_device, mesh.shape["sector"], mesh.shape["span"]),
        mesh=mesh, in_specs=in_specs, out_specs=out_specs, check_vma=False,
    )
```

```python
import functools

import jax
import jax.numpy as jnp
import ml_dtypes
import numpy as np
from jax import lax
from jax.experimental import pallas as pl
from jax.experimental.pallas import tpu as pltpu
from jax.sharding import PartitionSpec as P

SWEEPS = 4
DEPTH = 2
LANES = 128
CHUNK = 256
WINDOW = 8
HIGHEST = lax.Precision.HIGHEST
DOWN_AZ, SPECTRAL, UP_SP, DOWN_SP, UP_AX, DOWN_AX, UP_AZ = range(7)
C_TIME, C_AZ, C_SP, C_UP, C_DOWN, C_MASK = range(6)
RATES = 8
AXES = ("sector", "span")


class Plan:
    def __init__(self, rhs, stator_adj, sectors, spans):
        self.insts, self.fields, self.ct, self.rows, self.nax = rhs.shape
        self.panels = stator_adj.shape[2]
        self.sectors, self.spans = sectors, spans
        self.tf = self.insts * self.fields
        self.pad = -(-self.tf // 16) * 16
        self.cells = self.ct * self.rows
        self.slab = self.rows * LANES
        self.width = self.panels * self.rows
        self.shift = [
            ((t * sectors) // (self.insts - 1) - t // (self.insts - 1)) % sectors for t in range(self.insts)
        ]
        assert self.ct == 2 and self.nax == LANES and SWEEPS % DEPTH == 0 and spans > 1
        assert len(set(self.shift)) == self.insts and self.cells * WINDOW == LANES and self.rows >= SWEEPS
        assert self.slab % CHUNK == 0 and 3 * self.pad <= 256 and 2 * self.ct * self.width == LANES
        assert sectors % 2 == 0 and self.pad - self.tf == 3
        self.ends = 1 if spans == 2 else 2
        self.blocks = [-1, 0, 1]
        self.halves = [0, 1] if spans == 2 else [-1, 0, 1]
        self.tiles = [(k, x) for k in self.blocks for x in self.halves]
        self.slots = [
            [t for t in range(self.insts) if any((k + self.shift[t]) % sectors == o for k in self.blocks)]
            for o in range(sectors)
        ]
        last = LANES - self.width
        self.weight_at = [(t, last) for t in range(self.fields)] + [
            (self.fields, i * self.width) for i in range(self.insts - self.fields)
        ]
        assert max(map(len, self.slots)) * self.width <= last and 2 * self.cells == self.width
        assert self.fields == RATES - 1 and (self.insts - self.fields) * self.width <= LANES

    def spectral(self):
        t = np.arange(self.insts)
        off = t[:, None] - t[None, :]
        sines = np.where(off == 0, 1.0, np.sin(np.pi * off / self.insts))
        table = np.where(off == 0, 0.0, 0.5 * (1.0 - 2.0 * (off % 2)) / sines).astype(np.float32)
        full = np.zeros((self.pad, self.pad), np.float32)
        full[: self.tf, : self.tf] = np.kron(table.T, np.eye(self.fields, dtype=np.float32))
        hi = full.astype(ml_dtypes.bfloat16)
        lo = (full - hi.astype(np.float32)).astype(ml_dtypes.bfloat16)
        return np.concatenate([hi, lo, hi], axis=1)

    def field_rows(self):
        out = np.zeros((self.pad, self.fields), np.float32)
        out[np.arange(self.tf), np.arange(self.tf) % self.fields] = 1.0
        return out

    def field_lanes(self):
        return np.tile(self.field_rows().T, (1, 3))

    def block_diagonal(self):
        block = np.full(self.pad, -1)
        block[: self.tf] = np.arange(self.tf) // self.fields
        same = (block[:, None] == block[None, :]) & (block[:, None] >= 0)
        return np.tile(same.astype(np.float32), (1, 3))


    def inst_rows(self):
        row, inst = table_index(self.pad, 16)
        return ((row >= inst * self.fields) & (row < (inst + 1) * self.fields)).astype(jnp.float32)

    def cell_of(self, lane):
        return lax.div(lane, self.width) * self.rows + lax.rem(lane, self.rows)

    def window_lanes(self):
        lane, to = table_index(LANES, LANES)
        return (lane < self.ct * self.width) & (to == self.cell_of(lane) * WINDOW)

    def window_spread(self):
        to, lane = table_index(LANES, LANES)
        return (lane < self.ct * self.width) & (to == self.cell_of(lane) * WINDOW)

    def weight_lanes(self):
        cell, lane = table_index(LANES, LANES)
        half = self.ct * self.width
        wanted = jnp.where(lane < half, self.cell_of(lane), self.cells + self.cell_of(lane - half))
        return cell == wanted

    def panel_lanes(self):
        lane = lane_index(1)
        panel = lax.rem(lax.div(lane, self.rows), self.panels)
        return jnp.where(lane < self.ct * self.width, panel, -9).astype(jnp.float32)


def table_index(rows, columns):
    return [lax.broadcasted_iota(jnp.int32, (rows, columns), axis) for axis in (0, 1)]


def call(kernel, out, scratch=(), flops=2_000_000, nbytes=1_000_000):
    return pl.pallas_call(
        kernel,
        out_shape=out,
        scratch_shapes=list(scratch),
        compiler_params=pltpu.CompilerParams(vmem_limit_bytes=20 * 1024 * 1024),
        cost_estimate=pl.CostEstimate(flops=flops, bytes_accessed=nbytes, transcendentals=0),
    )


def f32(*shape):
    return jax.ShapeDtypeStruct(shape, jnp.float32)


def vmem(*shape):
    return pltpu.VMEM(shape, jnp.float32)


def halves_of(x):
    hi = x.astype(jnp.bfloat16)
    return hi, (x - hi.astype(jnp.float32)).astype(jnp.bfloat16)


def dot3(w, x):
    hi, lo = halves_of(x)
    return jnp.dot(w, jnp.concatenate([hi, hi, lo], axis=0), preferred_element_type=jnp.float32)


def pick(x, table):
    table = table.astype(jnp.float32).astype(jnp.bfloat16)
    table = jnp.concatenate([table, table], axis=0)
    return jnp.dot(jnp.concatenate(halves_of(x), axis=1), table, preferred_element_type=jnp.float32)


def dot_full(a, b):
    return jnp.dot(a, b, precision=HIGHEST, preferred_element_type=jnp.float32)


def lane_index(rows):
    return lax.broadcasted_iota(jnp.int32, (rows, LANES), 1)


def rolled(x, by):
    by %= LANES
    return pltpu.roll(x, by, axis=1) if by else x


def at(r, count=1, start=0):
    return slice(start + r * LANES, start + (r + count) * LANES)


def parity():
    return lax.rem(lax.axis_index("sector"), 2)


def has_sides(plan):
    span = lax.axis_index("span")
    return jnp.where(span < plan.spans - 1, 1.0, 0.0), jnp.where(span > 0, 1.0, 0.0)


class Layer:
    def __init__(self, plan, ref, start=0, rates=None, seam=None, layer=0):
        self.plan, self.ref, self.start, self.seam, self.layer = plan, ref, start, seam, layer
        self.rates = rates or (ref, start)

    def rate(self, which, r, count=1):
        if isinstance(self.rates, Layer):
            return self.rates.rate(which, r, count)
        ref, start = self.rates
        row = self.plan.pad + which
        return ref[row : row + 1, at(r, count, start)]

    def row(self, r):
        value = self.ref[: self.plan.pad, at(r, 1, self.start)]
        if self.seam is None:
            return value
        return value + placed(self.seam, self.layer * self.plan.rows + r) * self.rate(C_MASK, r)

    def chunk(self, c):
        count = CHUNK // LANES
        if self.seam is None:
            return self.ref[: self.plan.pad, at(c * count, count, self.start)]
        return jnp.concatenate([self.row(c * count + part) for part in range(count)], axis=1)


class Packed(Layer):
    def rate(self, which, r, count=1):
        where = {C_AZ: (0, 0), C_SP: (1, 0), C_UP: (2, 0), C_DOWN: (2, 0), C_TIME: (0, 1), C_MASK: (1, 1)}
        row, layer = where[which] if self.layer == 0 else (2, 1)
        row += self.plan.tf
        value = self.ref[row : row + 1, at(r, count, layer * self.plan.slab)]
        if which in (C_UP, C_DOWN):
            end = LANES - 1 if which == C_UP else 0
            value = jnp.where(lane_index(1) == end, 0.0, value)
        return value


def placed(tile, cell):
    return jnp.where(lane_index(tile.shape[0]) == 0, rolled(tile, -cell * WINDOW), 0.0)


class Products:
    def __init__(self, plan, w_ref, p_ref, first):
        self.plan, self.w, self.p, self.first = plan, w_ref, p_ref, first

    def fill(self, layer):
        for c in range(self.plan.slab // CHUNK):
            self.p[:, c * CHUNK : (c + 1) * CHUNK] = dot3(matrix(self.plan, self.w, self.first, 6), layer.chunk(c))
        self.layer = layer
        return self

    def get(self, block, r):
        row = (block - self.first) * self.plan.pad
        return self.p[row : row + self.plan.pad, at(r)]

    def own_terms(self, r):
        rate = self.layer.rate
        total = rate(C_TIME, r) * self.get(SPECTRAL, r)
        beside = []
        if r + 1 < self.plan.rows:
            beside.append(self.get(UP_SP, r + 1))
        if r > 0:
            beside.append(self.get(DOWN_SP, r - 1))
        total = total + rate(C_SP, r) * sum(beside[1:], beside[0])
        total = total + rate(C_UP, r) * rolled(self.get(UP_AX, r), -1)
        return total + rate(C_DOWN, r) * rolled(self.get(DOWN_AX, r), 1)


def matrix(plan, w_ref, block, count=1):
    return w_ref[block * plan.pad : (block + count) * plan.pad, :]


def two_layers(plan, ref, rates=None, seam=None):
    return [
        Layer(plan, ref, a * plan.slab, (rates, a * plan.slab) if rates is not None else None, seam, a)
        for a in range(plan.ct)
    ]


def inner_rows(plan, w_ref, p_refs, layers, force, g_ref):
    first = Products(plan, w_ref, p_refs[0], DOWN_AZ).fill(layers[0])
    second = Products(plan, w_ref, p_refs[1], SPECTRAL).fill(layers[1])
    for r in range(plan.rows):
        other = second.get(UP_AZ, r), first.get(DOWN_AZ, r)
        for a, products in enumerate((first, second)):
            total = products.own_terms(r) + layers[a].rate(C_AZ, r) * other[a]
            if isinstance(g_ref, tuple):
                g_ref[a][:, at(r)] = force[a].row(r) - total
            else:
                g_ref[:, at(r, 1, a * plan.slab)] = force[a].row(r) - total


def azimuthal(plan, w_ref, block, chunk_of, take):
    for c in range(plan.slab // CHUNK):
        terms = dot3(matrix(plan, w_ref, block), chunk_of(c))
        for part in range(CHUNK // LANES):
            take(c * (CHUNK // LANES) + part, terms[:, at(part)])


def middle_rows(plan, w_ref, p_refs, own, own_force, g_ref, near, near_force, side, corner, y_ref, h_refs, n_refs):
    pad, rows, ct = plan.pad, plan.rows, plan.ct
    outward, inward, last = (UP_SP, DOWN_SP), (DOWN_SP, UP_SP), (rows - 1, 0)
    edge_terms, edge_new, corner_terms = [], [], []
    for n in range(2):
        first, second, edge_force, edge_rate = side(n)
        corners = corner(n)
        every = dot3(w_ref[...], first)
        edge_terms.append(every[outward[n] * pad : (outward[n] + 1) * pad])
        corner_terms.append([dot3(matrix(plan, w_ref, outward[n]), c) for c in corners])
        beyond = dot3(matrix(plan, w_ref, outward[n]), second)
        within = dot3(matrix(plan, w_ref, inward[n]), jnp.concatenate([x.row(last[n]) for x in own], axis=1))
        from_low = dot3(matrix(plan, w_ref, DOWN_AZ), corners[0])
        from_high = dot3(matrix(plan, w_ref, UP_AZ), corners[1])
        new = []
        for a in range(ct):

            def part(block, b=a):
                return every[block * pad : (block + 1) * pad, at(b)]

            around = part(UP_AZ, 1) + from_low if a == 0 else from_high + part(DOWN_AZ, 0)
            total = edge_rate(C_TIME, a) * part(SPECTRAL) + edge_rate(C_AZ, a) * around
            total = total + edge_rate(C_SP, a) * (beyond[:, at(a)] + within[:, at(a)])
            total = total + edge_rate(C_UP, a) * rolled(part(UP_AX), -1)
            total = total + edge_rate(C_DOWN, a) * rolled(part(DOWN_AX), 1)
            new.append(edge_force[:, at(a)] - total)
        edge_new.append(dot3(matrix(plan, w_ref, outward[n]), jnp.concatenate(new, axis=1)))

    products = (
        Products(plan, w_ref, p_refs[0], DOWN_AZ).fill(near[0]), Products(plan, w_ref, p_refs[1], SPECTRAL).fill(near[1]),
    )
    for a, (to_own, to_near) in enumerate(((DOWN_AZ, UP_AZ), (UP_AZ, DOWN_AZ))):

        def take(r, terms):
            total = products[a].own_terms(r) + near[a].rate(C_AZ, r) * terms
            mine = own[a].rate(C_AZ, r) * products[a].get(to_own, r)
            for n in range(2):
                if r == last[n]:
                    total = total + near[a].rate(C_SP, r) * corner_terms[n][a]
                    mine = mine + own[a].rate(C_SP, r) * edge_terms[n][:, at(a)]
            n_refs[a][:, at(r)] = near_force[a].row(r) - total
            lanes = at(r, 1, a * plan.slab)
            y_ref[:, lanes] = g_ref[:, lanes] - mine

        azimuthal(plan, w_ref, to_near, own[a].chunk, take)

    after = [Layer(plan, y_ref, a * plan.slab, own[a].rates) for a in range(ct)]
    inner_rows(plan, w_ref, p_refs, after, own_force, h_refs)
    for a in range(ct):
        for n in range(2):
            h_refs[a][:, at(last[n])] -= own[a].rate(C_SP, last[n]) * edge_new[n][:, at(a)]


def outer_rows(plan, w_ref, own, near, far_chunks, n_refs, h_refs, put, layers=(0, 1)):
    count = CHUNK // LANES
    for a in layers:
        block = (DOWN_AZ, UP_AZ)[a]

        def near_chunk(c):
            terms = dot3(matrix(plan, w_ref, block), far_chunks[a](c))
            return n_refs[a][:, at(c * count, count)] - near[a].rate(C_AZ, c * count, count) * terms

        def take(r, terms):
            put(a, r, h_refs[a][:, at(r)] - own[a].rate(C_AZ, r) * terms)

        azimuthal(plan, w_ref, block, near_chunk, take)


def sides_of(plan, side_ref, force_ref, seams_ref):
    pad, ct = plan.pad, plan.ct
    keeps = has_sides(plan)

    def read(n, ref, e, seam):
        i = n if plan.ends == 2 else 0
        value = ref[i, :pad, at(e * ct, ct)]
        if seam:
            r = e if n == 0 else plan.rows - 1 - e
            tile = seams_ref[1, 1 + i]
            scale = ref[i, pad + C_MASK : pad + C_MASK + 1, at(e * ct, ct)]
            value = value + jnp.concatenate([placed(tile, a * plan.rows + r) for a in range(ct)], axis=1) * scale
        return value * keeps[n]

    def side(n):
        i = n if plan.ends == 2 else 0
        same = side_ref is force_ref

        def rate(which, a):
            return force_ref[i, pad + which : pad + which + 1, at(a)] * keeps[n]

        force = read(n, force_ref, 0, True)
        first = force if same else read(n, side_ref, 0, False)
        return first, read(n, side_ref, 1, same), force, rate

    return side


def corners_of(plan, c_refs, seams_ref):
    keeps = has_sides(plan)

    def corner(n):
        i = n if plan.ends == 2 else 0
        out = []
        for a, c_ref in enumerate(c_refs):
            value = c_ref[i, : plan.pad]
            if seams_ref is not None:
                r = 0 if n == 0 else plan.rows - 1
                scale = c_ref[i, plan.pad + C_MASK : plan.pad + C_MASK + 1]
                value = value + placed(seams_ref[2 * a, 1 + i], a * plan.rows + r) * scale
            out.append(value * keeps[n])
        return out

    return corner


def prepare(plan, rhs_ref, coef_ref, m_ref, out_ref, side_ref, c0_ref, c1_ref, rates_ref):
    pad, cells = plan.pad, plan.cells
    mask, diag, time, *face = [coef_ref[i] for i in range(6)]
    scale = mask / diag
    lane = lane_index(cells)
    axial = scale * face[2]
    rates = (
        scale * time, scale * face[0], scale * face[1],
        jnp.where(lane < LANES - 1, axial, 0.0), jnp.where(lane > 0, axial, 0.0), scale, axial,
    )
    for i, rate in enumerate(rates):
        rates_ref[i] = rate
    rest = jnp.zeros((RATES - 6, LANES), jnp.float32)
    mirror = parity()

    def rate(i, a, r):
        return rates_ref[i, pl.ds(jnp.where(mirror == 0, a, plan.ct - 1 - a) * plan.rows + r, 1), :]

    for cell in range(cells):
        a, r = divmod(cell, plan.rows)
        there = jnp.where(mirror == 0, a, plan.ct - 1 - a) * plan.rows + r
        table = [rate(i, a, r) for i in range(6)]
        if a == 0:
            spare = [table[C_AZ], table[C_SP], rate(6, 0, r)]
        else:
            spare = [rate(C_TIME, 0, r), rate(C_MASK, 0, r), table[C_MASK]]
        field = rhs_ref[pl.ds(there, plan.tf, stride=cells), :] * table[C_MASK]
        field = jnp.concatenate([field] + spare, axis=0)
        m_ref[:pad, at(cell)] = field
        out_ref[:, at(cell)] = field
        m_ref[pad:, at(cell)] = jnp.concatenate(table + [rest], axis=0)
    write_edges(plan, m_ref, side_ref, (c0_ref, c1_ref))


def write_edges(plan, x_ref, side_ref, c_refs):
    first = lax.axis_index("span") == 0
    for a in range(plan.ct):
        for e in range(DEPTH):
            low, high = x_ref[:, at(a * plan.rows + e)], x_ref[:, at((a + 1) * plan.rows - 1 - e)]
            ends = [jnp.where(first, high, low)] if plan.ends == 1 else [low, high]
            for n, end in enumerate(ends):
                side_ref[n, :, at(e * plan.ct + a)] = end
                if e == 0:
                    c_refs[a][n] = end


def stack_matrices(plan, up_ref, down_ref, spectral_ref, rows_ref, lanes_ref, diagonal_ref, out_ref, down_out):
    pad = plan.pad
    lane = lax.broadcasted_iota(jnp.int32, (pad, 3 * pad), 1)
    second = (lane >= pad) & (lane < 2 * pad)
    out_ref[SPECTRAL * pad : (SPECTRAL + 1) * pad, :] = spectral_ref[...]
    even = parity() == 0
    for block, small in (
        (DOWN_AZ, jnp.where(even, down_ref[0], up_ref[0])), (UP_AZ, jnp.where(even, up_ref[0], down_ref[0])),
        (UP_SP, up_ref[1]), (DOWN_SP, down_ref[1]), (UP_AX, up_ref[2]), (DOWN_AX, down_ref[2]),
    ):
        full = dot_full(dot_full(rows_ref[...], small), lanes_ref[...]) * diagonal_ref[...]
        hi = full.astype(jnp.bfloat16).astype(jnp.float32)
        out_ref[block * pad : (block + 1) * pad, :] = jnp.where(second, full - hi, hi).astype(jnp.bfloat16)
    down_out[...] = matrix(plan, out_ref, DOWN_AZ)


def send_panels(plan, stator_ref, both_ref, out_ref, panels_ref):
    me = lax.axis_index("sector")
    for f in range(plan.fields):
        panels_ref[pl.ds(f, plan.insts, stride=RATES), : plan.width] = jnp.transpose(stator_ref[f])
    out_ref[...] = jnp.zeros_like(out_ref)
    for t, (row, start) in enumerate(plan.weight_at):
        both = jnp.broadcast_to(both_ref[t : t + 1, :][None], (out_ref.shape[0], 1, plan.width))
        out_ref[:, row : row + 1, start : start + plan.width] = both
    for o, slots in enumerate(plan.slots):
        to = lax.rem(me + (plan.sectors - o), plan.sectors) * plan.spans
        for slot, t in enumerate(slots):
            lanes = slice(slot * plan.width, (slot + 1) * plan.width)
            panels = panels_ref[t * RATES : t * RATES + plan.fields, : plan.width]
            for x in range(plan.spans):
                out_ref[to + x, : plan.fields, lanes] = panels


def begin(
    plan, w_ref, m_ref, got_ref,
    seams_ref, weight_ref, x_ref, g_ref, panels_ref, terms_ref, rows_ref, p0_ref, p1_ref,
):
    pad, insts, fields = plan.pad, plan.insts, plan.fields
    me, span = lax.axis_index("sector"), lax.axis_index("span")
    even, is_first = parity() == 0, span == 0
    tiles = plan.tiles
    panels_ref[...] = jnp.zeros_like(panels_ref)
    rows_ref[...] = jnp.zeros_like(rows_ref)
    for n, (k, x) in enumerate(tiles):
        at_span = x if plan.spans == 2 else jnp.clip(span + x, 0, plan.spans - 1)
        for t in range(insts):
            o = (k + plan.shift[t]) % plan.sectors
            source = lax.rem(me + o, plan.sectors) * plan.spans + at_span
            tile = rolled(got_ref[source], -plan.slots[o].index(t) * plan.width)
            panels_ref[t * fields : (t + 1) * fields, n * LANES : n * LANES + plan.width] = tile[:fields, : plan.width]
        tile = got_ref[lax.rem(me + k + plan.sectors, plan.sectors) * plan.spans + at_span]
        lanes = slice(n * LANES, n * LANES + plan.width)
        rows_ref[:fields, lanes] = rolled(tile, -plan.weight_at[0][1])[:fields, : plan.width]
        for t in range(fields, insts):
            row, start = plan.weight_at[t]
            rows_ref[t : t + 1, lanes] = rolled(tile, -start)[row : row + 1, : plan.width]
    spread = dot_full(plan.inst_rows(), rows_ref[...])
    spread = pick(jnp.concatenate([spread[:, at(n)] for n in range(len(tiles))], axis=0), plan.weight_lanes())
    first, share, panel = spread, rolled(spread, plan.ct * plan.width), plan.panel_lanes()
    lower = (jnp.abs(first - panel) < 0.5).astype(jnp.float32)
    upper = (jnp.abs(first + 1.0 - panel) < 0.5).astype(jnp.float32)
    weights = share * lower + (1.0 - share) * upper
    for n in range(len(tiles)):
        panels = panels_ref[:, at(n)]
        terms_ref[n * pad : (n + 1) * pad, :] = panels + rolled(panels, plan.width)
    seams = pick(terms_ref[...] * weights, plan.window_lanes())

    def tile(values, k, x):
        n = tiles.index((k, x))
        return values[n * pad : (n + 1) * pad]

    def around(values, k):
        if plan.spans == 2:
            pair = tile(values, k, 0), tile(values, k, 1)
            return [jnp.where(is_first, pair[0], pair[1]), jnp.where(is_first, pair[1], pair[0])]
        return [tile(values, k, x) for x in (0, 1, -1)]

    def mirrored(value):
        return rolled(value, LANES // 2)

    here = around(seams, 0)
    behind, ahead = around(seams, -1), around(seams, 1)
    for i in range(1 + plan.ends):
        seams_ref[0, i] = jnp.where(even, mirrored(behind[i]), ahead[i])
        seams_ref[1, i] = jnp.where(even, here[i], mirrored(here[i]))
        seams_ref[2, i] = jnp.where(even, mirrored(ahead[i]), behind[i])
    weight_ref[...] = around(weights, 0)[0]

    for layer in two_layers(plan, m_ref, seam=seams_ref[1, 0]):
        for r in range(plan.rows):
            x_ref[:, at(r, 1, layer.start)] = layer.row(r)
    layers = two_layers(plan, x_ref, m_ref)
    inner_rows(plan, w_ref, (p0_ref, p1_ref), layers, layers, g_ref)


def first_half(
    plan, w_ref, m_ref, f_ref, g_ref, low_ref, high_ref, side_ref, c_low, c_high, seams_ref,
    x_ref, near_ref, side_out, c0_ref, c1_ref, p0_ref, p1_ref, y_ref, h0_ref, h1_ref, n0_ref, n1_ref, inlet_ref,
):
    own = two_layers(plan, f_ref, m_ref)
    low = [Packed(plan, low_ref, a * plan.slab, None, seams_ref[0, 0], a) for a in range(plan.ct)]
    high = two_layers(plan, high_ref, seam=seams_ref[2, 0])
    near = low[0], high[1]
    n_refs = n0_ref, n1_ref
    middle_rows(
        plan, w_ref, (p0_ref, p1_ref), own, own, g_ref, near, near, sides_of(plan, side_ref, side_ref, seams_ref),
        corners_of(plan, (c_low, c_high), seams_ref), y_ref, (h0_ref, h1_ref), n_refs,
    )
    lane = lane_index(plan.pad)
    inlet_ref[...] = jnp.zeros_like(inlet_ref)

    def put(a, r, value):
        x_ref[:, at(r, 1, a * plan.slab)] = value
        if a == 0:
            near_ref[:, at(r)] = value
        else:
            inlet_ref[: plan.pad, :] = jnp.where(lane == r, rolled(value, r), inlet_ref[: plan.pad, :])

    outer_rows(plan, w_ref, own, near, (low[1].chunk, high[0].chunk), n_refs, (h0_ref, h1_ref), put)
    turned = jnp.transpose(inlet_ref[...])
    for r in range(plan.rows):
        near_ref[plan.tf : plan.tf + 1, at(r)] = turned[r : r + 1, :]
    write_edges(plan, x_ref, side_out, (c0_ref, c1_ref))


def hold_far(plan, x_ref, side_ref, c_high, far_ref):
    come = side_ref[0, 0:1, 0:1] + c_high[0, 0:1, 0:1]
    far_ref[...] = x_ref[:, plan.slab :] + 0.0 * come


def inner(plan, w_ref, m_ref, f_ref, x_ref, g_ref, p0_ref, p1_ref):
    inner_rows(plan, w_ref, (p0_ref, p1_ref), two_layers(plan, x_ref, m_ref), two_layers(plan, f_ref, m_ref), g_ref)


def middle(
    plan, w_ref, m_ref, f_ref, x_ref, g_ref, low_ref, high_ref, side_ref, c_low, c_high,
    low_first, high_first, side_first, seams_ref, weight_ref,
    send_ref, n0_ref, h0_ref, x1_ref, rates_ref, p0_ref, p1_ref, y_ref, h1_ref, n1_ref, turn_ref,
):
    pad = plan.pad
    own, force = two_layers(plan, x_ref, m_ref), two_layers(plan, f_ref, m_ref)
    low_force = Packed(plan, low_first, 0, None, seams_ref[0, 0], 0)
    high_force = Layer(plan, high_first, plan.slab, None, seams_ref[2, 0], 1)
    near = Layer(plan, low_ref, 0, low_force), Layer(plan, high_ref, plan.slab, high_force.rates)
    n_refs = n0_ref, n1_ref
    middle_rows(
        plan, w_ref, (p0_ref, p1_ref), own, force, g_ref, near, (low_force, high_force),
        sides_of(plan, side_ref, side_first, seams_ref), corners_of(plan, (c_low, c_high), None), y_ref,
        (h0_ref, h1_ref), n_refs,
    )

    def put(a, r, value):
        x1_ref[:, at(r)] = value

    outer_rows(plan, w_ref, own, near, (None, Layer(plan, high_ref).chunk), n_refs, (h0_ref, h1_ref), put, (1,))
    for r in range(plan.rows):
        last = [near[0].rate(C_AZ, r), own[0].rate(C_AZ, r), jnp.zeros((RATES - 2, LANES), jnp.float32)]
        rates_ref[:, at(r)] = jnp.concatenate(last, axis=0)

    turn_ref[...] = jnp.zeros_like(turn_ref)
    for r in range(plan.rows):
        turn_ref[r : r + 1, :] = low_ref[plan.tf : plan.tf + 1, at(r)]
    far = jnp.transpose(turn_ref[...])[:pad]

    def packed(read, count, first=0, step=1):
        lane = lane_index(count)
        out = jnp.zeros((count, LANES), jnp.float32)
        for r in range(plan.rows):
            to = first + r * step
            out = jnp.where(lane == to, rolled(read(r), to), out)
        return out

    rates = packed(lambda r: rates_ref[:, at(r)], RATES)
    inlet = packed(lambda r: n0_ref[:, at(r)], pad) - rates[0:1] * dot3(matrix(plan, w_ref, DOWN_AZ), far)
    inlet = packed(lambda r: h0_ref[:, at(r)], pad) - rates[1:2] * dot3(matrix(plan, w_ref, DOWN_AZ), inlet)
    lane = lane_index(pad)
    spread = packed(lambda r: x1_ref[:, at(r)], pad, plan.rows * WINDOW, WINDOW)
    for r in range(plan.rows):
        spread = jnp.where(lane == r * WINDOW, rolled(inlet, r * (WINDOW - 1)), spread)
    inlet = jnp.where(parity() == 0, spread, rolled(spread, LANES // 2))
    back = pick(inlet, plan.window_spread()) * weight_ref[...]
    back = back + rolled(back, -plan.width)
    me = lax.axis_index("sector")
    send_ref[...] = jnp.zeros_like(send_ref)
    for t in range(plan.insts):
        to = lax.rem(me + plan.shift[t], plan.sectors)
        send_ref[to, : plan.fields, : plan.width] = back[t * plan.fields : (t + 1) * plan.fields, : plan.width]


def outer(plan, w_ref, rates_ref, n0_ref, h0_ref, x1_ref, far_ref, out_ref):
    mirror = parity()

    def put(a, r, value):
        there = jnp.where(mirror == 0, a, plan.ct - 1 - a) * plan.rows + r
        out_ref[pl.ds(there, plan.tf, stride=plan.cells), :] = value[: plan.tf]

    for r in range(plan.rows):
        put(1, r, x1_ref[:, at(r)])

    def near_chunk(c):
        lanes = slice(c * CHUNK, (c + 1) * CHUNK)
        return n0_ref[:, lanes] - rates_ref[0:1, lanes] * dot3(w_ref[...], far_ref[:, lanes])

    azimuthal(plan, w_ref, 0, near_chunk, lambda r, terms: put(0, r, h0_ref[:, at(r)] - rates_ref[1:2, at(r)] * terms))


def collect_panels(plan, got_ref, out_ref, panels_ref):
    me = lax.axis_index("sector")
    for t in range(plan.insts):
        source = lax.rem(me + (plan.sectors - plan.shift[t]), plan.sectors)
        panels_ref[t * RATES : (t + 1) * RATES, :] = got_ref[source]
    for f in range(plan.fields):
        tile = panels_ref[pl.ds(f, plan.insts, stride=RATES), : plan.width]
        out_ref[f] = jnp.transpose(tile)


def sibling(plan):
    return [s ^ 1 for s in range(plan.sectors)]


def outside(plan):
    return [(s - 1 if s % 2 == 0 else s + 1) % plan.sectors for s in range(plan.sectors)]


def swap(array, partner):
    return lax.ppermute(array, "sector", list(enumerate(partner)))


def beside(plan, array, partner):
    def pairs(step):
        out = []
        for s in range(plan.sectors):
            for x in range(plan.spans):
                to = 1 - x if plan.ends == 1 else x + step
                if 0 <= to < plan.spans:
                    out.append((s * plan.spans + x, partner[s] * plan.spans + to))
        return out

    if plan.ends == 1:
        return lax.ppermute(array, AXES, pairs(0))
    return jnp.concatenate([lax.ppermute(array[:1], AXES, pairs(-1)), lax.ppermute(array[1:], AXES, pairs(1))])


def on_device(
    sectors, spans,
    rhs, diag_coef, face_coef, time_coef, jac_up, jac_down, wall_mask, stator_adj, owner, first_panel_share,
):
    plan = Plan(rhs, stator_adj, sectors, spans)
    pad, cells, slab, insts, fields, ends = plan.pad, plan.cells, plan.slab, plan.insts, plan.fields, plan.ends
    bind = functools.partial
    whole, half = f32(pad, plan.ct * slab), f32(pad, slab)
    products = (vmem(6 * pad, slab),) * 2
    alone, next_chip, next_core = list(range(sectors)), outside(plan), sibling(plan)

    def edges(rows):
        return f32(ends, rows, DEPTH * plan.ct * LANES), f32(ends, rows, LANES), f32(ends, rows, LANES)

    stator = jnp.transpose(stator_adj, (1, 2, 3, 0)).reshape(fields, plan.width, insts)
    sent = call(bind(send_panels, plan), f32(sectors * spans, RATES, LANES), (vmem(insts * RATES, LANES),))(
        stator,
        jnp.concatenate([
            lax.rem(owner, plan.panels).astype(jnp.float32).reshape(insts, cells), first_panel_share.reshape(insts, cells),
        ], axis=1),
    )
    got = lax.all_to_all(sent, AXES, 0, 0, tiled=True)
    which = lax.broadcasted_iota(jnp.int32, (6, cells, LANES), 0)
    coefs = jnp.pad(face_coef.reshape(3, cells, LANES), ((3, 0), (0, 0), (0, 0)))
    for i, value in enumerate((wall_mask.astype(jnp.float32), diag_coef, time_coef)):
        coefs = jnp.where(which == i, value.reshape(1, cells, LANES), coefs)
    m, to_next, side, c0, c1 = call(
        bind(prepare, plan), (f32(pad + RATES, plan.ct * slab), whole) + edges(pad + RATES), (vmem(7, cells, LANES),)
    )(rhs.reshape(plan.tf * cells, LANES), coefs)
    low_first, high_first = swap(to_next, next_chip), swap(m, next_core)
    side_first = beside(plan, side, alone)
    c_low, c_high = beside(plan, c0, next_chip), beside(plan, c1, next_core)
    matrices, down = call(
        bind(stack_matrices, plan),
        [jax.ShapeDtypeStruct((count * pad, 3 * pad), jnp.bfloat16) for count in (7, 1)],
    )(jac_up, jac_down, plan.spectral(), plan.field_rows(), plan.field_lanes(), plan.block_diagonal())
    tiles = len(plan.tiles)
    seams, weight, force, g = call(
        bind(begin, plan), (f32(3, 1 + ends, pad, LANES), f32(pad, LANES), whole, whole),
        (vmem(pad, tiles * LANES), vmem(tiles * pad, LANES), vmem(16, tiles * LANES)) + products,
        flops=2_000_000_000,
    )(matrices, m, got)
    x, near, side, c0, c1 = call(
        bind(first_half, plan), (whole, half) + edges(pad),
        products + (vmem(pad, 2 * slab),) + (vmem(pad, slab),) * 4 + (vmem(LANES, LANES),),
        flops=4_000_000_000,
    )(matrices, m, force, g, low_first, high_first, side_first, c_low, c_high, seams)

    low, high = swap(near, next_chip), swap(x, next_core)
    side = beside(plan, side, alone)
    c_low, c_high = beside(plan, c0, next_chip), beside(plan, c1, next_core)
    (g,) = call(bind(inner, plan), (whole,), products, flops=2_000_000_000)(matrices, m, force, x)
    far = call(bind(hold_far, plan), half)(x, side, c_high)
    far_low = swap(far, next_chip)
    back, n0, h0, x1, rates = call(
        bind(middle, plan), (f32(sectors, RATES, LANES), half, half, half, f32(RATES, slab)),
        products + (vmem(pad, 2 * slab), vmem(pad, slab), vmem(pad, slab), vmem(LANES, LANES)),
        flops=4_000_000_000,
    )(
        matrices, m, force, x, g, low, high, side, c_low, c_high, low_first, high_first, side_first, seams, weight
    )
    returned = lax.all_to_all(back, "sector", 0, 0, tiled=True)
    sens = call(bind(collect_panels, plan), f32(fields, plan.width, insts), (vmem(insts * RATES, LANES),))(returned)
    out = call(bind(outer, plan), f32(plan.tf * cells, LANES))(down, rates, n0, h0, x1, far_low)
    sens = jnp.transpose(sens.reshape(fields, plan.panels, plan.rows, insts), (3, 0, 1, 2))
    return out.reshape(rhs.shape), sens


def solution(mesh):
    in_specs = (
        P(None, None, "sector", "span", None),
        P("sector", "span", None),
        P(None, "sector", "span", None),
        P("sector", "span", None),
        P(),
        P(),
        P("sector", "span", None),
        P(None, None, "sector", "span"),
        P(None, "sector", "span"),
        P(None, "sector", "span"),
    )
    out_specs = (P(None, None, "sector", "span", None), P(None, None, "sector", "span"))
    return jax.shard_map(
        functools.partial(on_device, mesh.shape["sector"], mesh.shape["span"]),
        mesh=mesh, in_specs=in_specs, out_specs=out_specs, check_vma=False,
    )
```

```python
import functools

import jax
import jax.numpy as jnp
import ml_dtypes
import numpy as np
from jax import lax
from jax.experimental import pallas as pl
from jax.experimental.pallas import tpu as pltpu
from jax.sharding import PartitionSpec as P

SWEEPS = 4
GROUP = 4
DEPTH = 2
LANES = 128
CHUNK = 256
WINDOW = 8
HIGHEST = lax.Precision.HIGHEST
DOWN_AZ, SPECTRAL, UP_SP, DOWN_SP, UP_AX, DOWN_AX, UP_AZ = range(7)
C_TIME, C_AZ, C_SP, C_UP, C_DOWN, C_MASK = range(6)
RATES = 8
AXES = ("sector", "span")


class Plan:
    def __init__(self, rhs, stator_adj, sectors, spans):
        self.insts, self.fields, self.ct, self.rows, self.nax = rhs.shape
        self.panels = stator_adj.shape[2]
        self.sectors, self.spans = sectors, spans
        self.tf = self.insts * self.fields
        self.pad = -(-self.tf // 16) * 16
        self.cells = self.ct * self.rows
        self.slab = self.rows * LANES
        self.width = self.panels * self.rows
        self.shift = [
            ((t * sectors) // (self.insts - 1) - t // (self.insts - 1)) % sectors for t in range(self.insts)
        ]
        assert self.ct == 2 and self.nax == LANES and SWEEPS % DEPTH == 0 and spans > 1
        assert len(set(self.shift)) == self.insts and self.cells * WINDOW == LANES and self.rows >= SWEEPS
        assert self.slab % CHUNK == 0 and 3 * self.pad <= 256 and 2 * self.ct * self.width == LANES
        assert sectors % 2 == 0
        self.groups = sectors // GROUP
        assert sectors % GROUP == 0 and self.groups & (self.groups - 1) == 0
        self.ends = 1 if spans == 2 else 2
        self.blocks = [-1, 0, 1]
        self.halves = [0, 1] if spans == 2 else [-1, 0, 1]
        self.tiles = [(k, x) for k in self.blocks for x in self.halves]
        self.slots = [
            [t for t in range(self.insts) if any((k + self.shift[t]) % sectors == o for k in self.blocks)]
            for o in range(sectors)
        ]
        last = LANES - self.width
        self.weight_at = [(t, last) for t in range(self.fields)] + [
            (self.fields, i * self.width) for i in range(self.insts - self.fields)
        ]
        assert max(map(len, self.slots)) * self.width <= last and 2 * self.cells == self.width
        assert self.fields == RATES - 1 and (self.insts - self.fields) * self.width <= LANES

    def spectral(self):
        t = np.arange(self.insts)
        off = t[:, None] - t[None, :]
        sines = np.where(off == 0, 1.0, np.sin(np.pi * off / self.insts))
        table = np.where(off == 0, 0.0, 0.5 * (1.0 - 2.0 * (off % 2)) / sines).astype(np.float32)
        full = np.zeros((self.pad, self.pad), np.float32)
        full[: self.tf, : self.tf] = np.kron(table.T, np.eye(self.fields, dtype=np.float32))
        hi = full.astype(ml_dtypes.bfloat16)
        lo = (full - hi.astype(np.float32)).astype(ml_dtypes.bfloat16)
        return np.concatenate([hi, lo, hi], axis=1)

    def field_rows(self):
        out = np.zeros((self.pad, self.fields), np.float32)
        out[np.arange(self.tf), np.arange(self.tf) % self.fields] = 1.0
        return out

    def field_lanes(self):
        return np.tile(self.field_rows().T, (1, 3))

    def block_diagonal(self):
        block = np.full(self.pad, -1)
        block[: self.tf] = np.arange(self.tf) // self.fields
        same = (block[:, None] == block[None, :]) & (block[:, None] >= 0)
        return np.tile(same.astype(np.float32), (1, 3))


    def inst_rows(self):
        row, inst = table_index(self.pad, 16)
        return ((row >= inst * self.fields) & (row < (inst + 1) * self.fields)).astype(jnp.float32)

    def cell_of(self, lane):
        return lax.div(lane, self.width) * self.rows + lax.rem(lane, self.rows)

    def window_lanes(self):
        lane, to = table_index(LANES, LANES)
        return (lane < self.ct * self.width) & (to == self.cell_of(lane) * WINDOW)

    def window_spread(self):
        to, lane = table_index(LANES, LANES)
        return (lane < self.ct * self.width) & (to == self.cell_of(lane) * WINDOW)

    def weight_lanes(self):
        cell, lane = table_index(LANES, LANES)
        half = self.ct * self.width
        wanted = jnp.where(lane < half, self.cell_of(lane), self.cells + self.cell_of(lane - half))
        return cell == wanted

    def panel_lanes(self):
        lane = lane_index(1)
        panel = lax.rem(lax.div(lane, self.rows), self.panels)
        return jnp.where(lane < self.ct * self.width, panel, -9).astype(jnp.float32)


def table_index(rows, columns):
    return [lax.broadcasted_iota(jnp.int32, (rows, columns), axis) for axis in (0, 1)]


def call(kernel, out, scratch=(), flops=2_000_000, nbytes=1_000_000):
    return pl.pallas_call(
        kernel,
        out_shape=out,
        scratch_shapes=list(scratch),
        compiler_params=pltpu.CompilerParams(vmem_limit_bytes=20 * 1024 * 1024),
        cost_estimate=pl.CostEstimate(flops=flops, bytes_accessed=nbytes, transcendentals=0),
    )


def f32(*shape):
    return jax.ShapeDtypeStruct(shape, jnp.float32)


def vmem(*shape):
    return pltpu.VMEM(shape, jnp.float32)


def halves_of(x):
    hi = x.astype(jnp.bfloat16)
    return hi, (x - hi.astype(jnp.float32)).astype(jnp.bfloat16)


def dot3(w, x):
    hi, lo = halves_of(x)
    return jnp.dot(w, jnp.concatenate([hi, hi, lo], axis=0), preferred_element_type=jnp.float32)


def pick(x, table):
    table = table.astype(jnp.float32).astype(jnp.bfloat16)
    table = jnp.concatenate([table, table], axis=0)
    return jnp.dot(jnp.concatenate(halves_of(x), axis=1), table, preferred_element_type=jnp.float32)


def dot_full(a, b):
    return jnp.dot(a, b, precision=HIGHEST, preferred_element_type=jnp.float32)


def lane_index(rows):
    return lax.broadcasted_iota(jnp.int32, (rows, LANES), 1)


def rolled(x, by):
    by %= LANES
    return pltpu.roll(x, by, axis=1) if by else x


def at(r, count=1, start=0):
    return slice(start + r * LANES, start + (r + count) * LANES)


def parity():
    return lax.rem(lax.axis_index("sector"), 2)


def has_sides(plan):
    span = lax.axis_index("span")
    return jnp.where(span < plan.spans - 1, 1.0, 0.0), jnp.where(span > 0, 1.0, 0.0)


class Layer:
    def __init__(self, plan, ref, start=0, rates=None, seam=None, layer=0):
        self.plan, self.ref, self.start, self.seam, self.layer = plan, ref, start, seam, layer
        self.rates = rates or (ref, start)

    def rate(self, which, r, count=1):
        ref, start = self.rates
        row = self.plan.pad + which
        return ref[row : row + 1, at(r, count, start)]

    def row(self, r):
        value = self.ref[: self.plan.pad, at(r, 1, self.start)]
        if self.seam is None:
            return value
        return value + placed(self.seam, self.layer * self.plan.rows + r) * self.rate(C_MASK, r)

    def chunk(self, c):
        count = CHUNK // LANES
        if self.seam is None:
            return self.ref[: self.plan.pad, at(c * count, count, self.start)]
        return jnp.concatenate([self.row(c * count + part) for part in range(count)], axis=1)


def placed(tile, cell):
    return jnp.where(lane_index(tile.shape[0]) == 0, rolled(tile, -cell * WINDOW), 0.0)


class Products:
    def __init__(self, plan, w_ref, p_ref, first):
        self.plan, self.w, self.p, self.first = plan, w_ref, p_ref, first

    def fill(self, layer):
        for c in range(self.plan.slab // CHUNK):
            self.p[:, c * CHUNK : (c + 1) * CHUNK] = dot3(matrix(self.plan, self.w, self.first, 6), layer.chunk(c))
        self.layer = layer
        return self

    def get(self, block, r):
        row = (block - self.first) * self.plan.pad
        return self.p[row : row + self.plan.pad, at(r)]

    def own_terms(self, r):
        rate = self.layer.rate
        total = rate(C_TIME, r) * self.get(SPECTRAL, r)
        beside = []
        if r + 1 < self.plan.rows:
            beside.append(self.get(UP_SP, r + 1))
        if r > 0:
            beside.append(self.get(DOWN_SP, r - 1))
        total = total + rate(C_SP, r) * sum(beside[1:], beside[0])
        total = total + rate(C_UP, r) * rolled(self.get(UP_AX, r), -1)
        return total + rate(C_DOWN, r) * rolled(self.get(DOWN_AX, r), 1)


def matrix(plan, w_ref, block, count=1):
    return w_ref[block * plan.pad : (block + count) * plan.pad, :]


def two_layers(plan, ref, rates=None, seam=None):
    return [
        Layer(plan, ref, a * plan.slab, (rates, a * plan.slab) if rates is not None else None, seam, a)
        for a in range(plan.ct)
    ]


def inner_rows(plan, w_ref, p_refs, layers, force, g_ref):
    first = Products(plan, w_ref, p_refs[0], DOWN_AZ).fill(layers[0])
    second = Products(plan, w_ref, p_refs[1], SPECTRAL).fill(layers[1])
    for r in range(plan.rows):
        other = second.get(UP_AZ, r), first.get(DOWN_AZ, r)
        for a, products in enumerate((first, second)):
            total = products.own_terms(r) + layers[a].rate(C_AZ, r) * other[a]
            if isinstance(g_ref, tuple):
                g_ref[a][:, at(r)] = force[a].row(r) - total
            else:
                g_ref[:, at(r, 1, a * plan.slab)] = force[a].row(r) - total


def azimuthal(plan, w_ref, block, chunk_of, take):
    for c in range(plan.slab // CHUNK):
        terms = dot3(matrix(plan, w_ref, block), chunk_of(c))
        for part in range(CHUNK // LANES):
            take(c * (CHUNK // LANES) + part, terms[:, at(part)])


def middle_rows(plan, w_ref, p_refs, own, own_force, g_ref, near, near_force, side, corner, y_ref, h_refs, n_refs):
    pad, rows, ct = plan.pad, plan.rows, plan.ct
    outward, inward, last = (UP_SP, DOWN_SP), (DOWN_SP, UP_SP), (rows - 1, 0)
    edge_terms, edge_new, corner_terms = [], [], []
    for n in range(2):
        first, second, edge_force, edge_rate = side(n)
        corners = corner(n)
        every = dot3(w_ref[...], first)
        edge_terms.append(every[outward[n] * pad : (outward[n] + 1) * pad])
        corner_terms.append([dot3(matrix(plan, w_ref, outward[n]), c) for c in corners])
        beyond = dot3(matrix(plan, w_ref, outward[n]), second)
        within = dot3(matrix(plan, w_ref, inward[n]), jnp.concatenate([x.row(last[n]) for x in own], axis=1))
        from_low = dot3(matrix(plan, w_ref, DOWN_AZ), corners[0])
        from_high = dot3(matrix(plan, w_ref, UP_AZ), corners[1])
        new = []
        for a in range(ct):

            def part(block, b=a):
                return every[block * pad : (block + 1) * pad, at(b)]

            around = part(UP_AZ, 1) + from_low if a == 0 else from_high + part(DOWN_AZ, 0)
            total = edge_rate(C_TIME, a) * part(SPECTRAL) + edge_rate(C_AZ, a) * around
            total = total + edge_rate(C_SP, a) * (beyond[:, at(a)] + within[:, at(a)])
            total = total + edge_rate(C_UP, a) * rolled(part(UP_AX), -1)
            total = total + edge_rate(C_DOWN, a) * rolled(part(DOWN_AX), 1)
            new.append(edge_force[:, at(a)] - total)
        edge_new.append(dot3(matrix(plan, w_ref, outward[n]), jnp.concatenate(new, axis=1)))

    products = (
        Products(plan, w_ref, p_refs[0], DOWN_AZ).fill(near[0]), Products(plan, w_ref, p_refs[1], SPECTRAL).fill(near[1]),
    )
    for a, (to_own, to_near) in enumerate(((DOWN_AZ, UP_AZ), (UP_AZ, DOWN_AZ))):

        def take(r, terms):
            total = products[a].own_terms(r) + near[a].rate(C_AZ, r) * terms
            mine = own[a].rate(C_AZ, r) * products[a].get(to_own, r)
            for n in range(2):
                if r == last[n]:
                    total = total + near[a].rate(C_SP, r) * corner_terms[n][a]
                    mine = mine + own[a].rate(C_SP, r) * edge_terms[n][:, at(a)]
            n_refs[a][:, at(r)] = near_force[a].row(r) - total
            lanes = at(r, 1, a * plan.slab)
            y_ref[:, lanes] = g_ref[:, lanes] - mine

        azimuthal(plan, w_ref, to_near, own[a].chunk, take)

    after = [Layer(plan, y_ref, a * plan.slab, own[a].rates) for a in range(ct)]
    inner_rows(plan, w_ref, p_refs, after, own_force, h_refs)
    for a in range(ct):
        for n in range(2):
            h_refs[a][:, at(last[n])] -= own[a].rate(C_SP, last[n]) * edge_new[n][:, at(a)]


def outer_rows(plan, w_ref, own, near, far_chunks, n_refs, h_refs, put, layers=(0, 1)):
    count = CHUNK // LANES
    for a in layers:
        block = (DOWN_AZ, UP_AZ)[a]

        def near_chunk(c):
            terms = dot3(matrix(plan, w_ref, block), far_chunks[a](c))
            return n_refs[a][:, at(c * count, count)] - near[a].rate(C_AZ, c * count, count) * terms

        def take(r, terms):
            put(a, r, h_refs[a][:, at(r)] - own[a].rate(C_AZ, r) * terms)

        azimuthal(plan, w_ref, block, near_chunk, take)


def sides_of(plan, side_ref, force_ref, seams_ref):
    pad, ct = plan.pad, plan.ct
    keeps = has_sides(plan)

    def read(n, ref, e, seam):
        i = n if plan.ends == 2 else 0
        value = ref[i, :pad, at(e * ct, ct)]
        if seam:
            r = e if n == 0 else plan.rows - 1 - e
            tile = seams_ref[1, 1 + i]
            scale = ref[i, pad + C_MASK : pad + C_MASK + 1, at(e * ct, ct)]
            value = value + jnp.concatenate([placed(tile, a * plan.rows + r) for a in range(ct)], axis=1) * scale
        return value * keeps[n]

    def side(n):
        i = n if plan.ends == 2 else 0
        same = side_ref is force_ref

        def rate(which, a):
            return force_ref[i, pad + which : pad + which + 1, at(a)] * keeps[n]

        force = read(n, force_ref, 0, True)
        first = force if same else read(n, side_ref, 0, False)
        return first, read(n, side_ref, 1, same), force, rate

    return side


def corners_of(plan, c_refs, seams_ref):
    keeps = has_sides(plan)

    def corner(n):
        i = n if plan.ends == 2 else 0
        out = []
        for a, c_ref in enumerate(c_refs):
            value = c_ref[i, : plan.pad]
            if seams_ref is not None:
                r = 0 if n == 0 else plan.rows - 1
                scale = c_ref[i, plan.pad + C_MASK : plan.pad + C_MASK + 1]
                value = value + placed(seams_ref[2 * a, 1 + i], a * plan.rows + r) * scale
            out.append(value * keeps[n])
        return out

    return corner


def prepare(plan, rhs_ref, coef_ref, m_ref, side_ref, c0_ref, c1_ref, rates_ref):
    pad, cells = plan.pad, plan.cells
    mask, diag, time, *face = [coef_ref[cells * i : cells * (i + 1), :] for i in range(6)]
    scale = mask / diag
    lane = lane_index(cells)
    axial = scale * face[2]
    rates = (
        scale * time, scale * face[0], scale * face[1],
        jnp.where(lane < LANES - 1, axial, 0.0), jnp.where(lane > 0, axial, 0.0), scale,
    )
    for i, rate in enumerate(rates):
        rates_ref[i] = rate
    tail = jnp.zeros((pad - plan.tf, LANES), jnp.float32)
    rest = jnp.zeros((RATES - 6, LANES), jnp.float32)
    mirror = parity()
    for cell in range(cells):
        a, r = divmod(cell, plan.rows)
        there = jnp.where(mirror == 0, a, plan.ct - 1 - a) * plan.rows + r
        table = [rates_ref[i, pl.ds(there, 1), :] for i in range(6)]
        field = jnp.concatenate([rhs_ref[pl.ds(there, plan.tf, stride=cells), :], tail], axis=0)
        m_ref[:pad, at(cell)] = field * table[C_MASK]
        m_ref[pad:, at(cell)] = jnp.concatenate(table + [rest], axis=0)
    write_edges(plan, m_ref, side_ref, (c0_ref, c1_ref))


def write_edges(plan, x_ref, side_ref, c_refs):
    first = lax.axis_index("span") == 0
    for a in range(plan.ct):
        for e in range(DEPTH):
            low, high = x_ref[:, at(a * plan.rows + e)], x_ref[:, at((a + 1) * plan.rows - 1 - e)]
            ends = [jnp.where(first, high, low)] if plan.ends == 1 else [low, high]
            for n, end in enumerate(ends):
                side_ref[n, :, at(e * plan.ct + a)] = end
                if e == 0:
                    c_refs[a][n] = end


def stack_matrices(plan, up_ref, down_ref, spectral_ref, rows_ref, lanes_ref, diagonal_ref, out_ref, down_out):
    pad = plan.pad
    lane = lax.broadcasted_iota(jnp.int32, (pad, 3 * pad), 1)
    second = (lane >= pad) & (lane < 2 * pad)
    out_ref[SPECTRAL * pad : (SPECTRAL + 1) * pad, :] = spectral_ref[...]
    even = parity() == 0
    for block, small in (
        (DOWN_AZ, jnp.where(even, down_ref[0], up_ref[0])), (UP_AZ, jnp.where(even, up_ref[0], down_ref[0])),
        (UP_SP, up_ref[1]), (DOWN_SP, down_ref[1]), (UP_AX, up_ref[2]), (DOWN_AX, down_ref[2]),
    ):
        full = dot_full(dot_full(rows_ref[...], small), lanes_ref[...]) * diagonal_ref[...]
        hi = full.astype(jnp.bfloat16).astype(jnp.float32)
        out_ref[block * pad : (block + 1) * pad, :] = jnp.where(second, full - hi, hi).astype(jnp.bfloat16)
    down_out[...] = matrix(plan, out_ref, DOWN_AZ)


def send_panels(plan, stator_ref, both_ref, out_ref, panels_ref):
    me = lax.axis_index("sector")
    for f in range(plan.fields):
        panels_ref[pl.ds(f, plan.insts, stride=RATES), : plan.width] = jnp.transpose(stator_ref[f])
    out_ref[...] = jnp.zeros_like(out_ref)
    for t, (row, start) in enumerate(plan.weight_at):
        both = jnp.broadcast_to(both_ref[t : t + 1, :][None], (out_ref.shape[0], 1, plan.width))
        out_ref[:, row : row + 1, start : start + plan.width] = both
    for o, slots in enumerate(plan.slots):
        to = lax.rem(me + (plan.sectors - o), plan.sectors) * plan.spans
        for slot, t in enumerate(slots):
            lanes = slice(slot * plan.width, (slot + 1) * plan.width)
            panels = panels_ref[t * RATES : t * RATES + plan.fields, : plan.width]
            for x in range(plan.spans):
                out_ref[to + x, : plan.fields, lanes] = panels


def begin(
    plan, w_ref, m_ref, got_ref,
    seams_ref, weight_ref, x_ref, g_ref, panels_ref, terms_ref, rows_ref, p0_ref, p1_ref,
):
    pad, insts, fields = plan.pad, plan.insts, plan.fields
    me, span = lax.axis_index("sector"), lax.axis_index("span")
    even, is_first = parity() == 0, span == 0
    tiles = plan.tiles
    panels_ref[...] = jnp.zeros_like(panels_ref)
    rows_ref[...] = jnp.zeros_like(rows_ref)
    for n, (k, x) in enumerate(tiles):
        at_span = x if plan.spans == 2 else jnp.clip(span + x, 0, plan.spans - 1)
        for t in range(insts):
            o = (k + plan.shift[t]) % plan.sectors
            source = lax.rem(me + o, plan.sectors) * plan.spans + at_span
            tile = rolled(got_ref[source], -plan.slots[o].index(t) * plan.width)
            panels_ref[t * fields : (t + 1) * fields, n * LANES : n * LANES + plan.width] = tile[:fields, : plan.width]
        tile = got_ref[lax.rem(me + k + plan.sectors, plan.sectors) * plan.spans + at_span]
        lanes = slice(n * LANES, n * LANES + plan.width)
        rows_ref[:fields, lanes] = rolled(tile, -plan.weight_at[0][1])[:fields, : plan.width]
        for t in range(fields, insts):
            row, start = plan.weight_at[t]
            rows_ref[t : t + 1, lanes] = rolled(tile, -start)[row : row + 1, : plan.width]
    spread = dot_full(plan.inst_rows(), rows_ref[...])
    spread = pick(jnp.concatenate([spread[:, at(n)] for n in range(len(tiles))], axis=0), plan.weight_lanes())
    first, share, panel = spread, rolled(spread, plan.ct * plan.width), plan.panel_lanes()
    lower = (jnp.abs(first - panel) < 0.5).astype(jnp.float32)
    upper = (jnp.abs(first + 1.0 - panel) < 0.5).astype(jnp.float32)
    weights = share * lower + (1.0 - share) * upper
    for n in range(len(tiles)):
        panels = panels_ref[:, at(n)]
        terms_ref[n * pad : (n + 1) * pad, :] = panels + rolled(panels, plan.width)
    seams = pick(terms_ref[...] * weights, plan.window_lanes())

    def tile(values, k, x):
        n = tiles.index((k, x))
        return values[n * pad : (n + 1) * pad]

    def around(values, k):
        if plan.spans == 2:
            pair = tile(values, k, 0), tile(values, k, 1)
            return [jnp.where(is_first, pair[0], pair[1]), jnp.where(is_first, pair[1], pair[0])]
        return [tile(values, k, x) for x in (0, 1, -1)]

    def mirrored(value):
        return rolled(value, LANES // 2)

    here = around(seams, 0)
    behind, ahead = around(seams, -1), around(seams, 1)
    for i in range(1 + plan.ends):
        seams_ref[0, i] = jnp.where(even, mirrored(behind[i]), ahead[i])
        seams_ref[1, i] = jnp.where(even, here[i], mirrored(here[i]))
        seams_ref[2, i] = jnp.where(even, mirrored(ahead[i]), behind[i])
    weight_ref[...] = around(weights, 0)[0]

    for layer in two_layers(plan, m_ref, seam=seams_ref[1, 0]):
        for r in range(plan.rows):
            x_ref[:, at(r, 1, layer.start)] = layer.row(r)
    layers = two_layers(plan, x_ref, m_ref)
    inner_rows(plan, w_ref, (p0_ref, p1_ref), layers, layers, g_ref)


def first_half(
    plan, w_ref, m_ref, f_ref, g_ref, low_ref, high_ref, side_ref, c_low, c_high, seams_ref,
    x_ref, near_ref, side_out, c0_ref, c1_ref, p0_ref, p1_ref, y_ref, h0_ref, h1_ref, n0_ref, n1_ref, inlet_ref,
):
    own = two_layers(plan, f_ref, m_ref)
    low = two_layers(plan, low_ref, seam=seams_ref[0, 0])
    high = two_layers(plan, high_ref, seam=seams_ref[2, 0])
    near = low[0], high[1]
    n_refs = n0_ref, n1_ref
    middle_rows(
        plan, w_ref, (p0_ref, p1_ref), own, own, g_ref, near, near, sides_of(plan, side_ref, side_ref, seams_ref),
        corners_of(plan, (c_low, c_high), seams_ref), y_ref, (h0_ref, h1_ref), n_refs,
    )
    lane = lane_index(plan.pad)
    inlet_ref[...] = jnp.zeros_like(inlet_ref)

    def put(a, r, value):
        x_ref[:, at(r, 1, a * plan.slab)] = value
        if a == 0:
            near_ref[:, at(r)] = value
        else:
            inlet_ref[: plan.pad, :] = jnp.where(lane == r, rolled(value, r), inlet_ref[: plan.pad, :])

    outer_rows(plan, w_ref, own, near, (low[1].chunk, high[0].chunk), n_refs, (h0_ref, h1_ref), put)
    turned = jnp.transpose(inlet_ref[...])
    for r in range(plan.rows):
        near_ref[plan.tf : plan.tf + 1, at(r)] = turned[r : r + 1, :]
    write_edges(plan, x_ref, side_out, (c0_ref, c1_ref))


def hold_far(plan, x_ref, side_ref, c_high, far_ref):
    come = side_ref[0, 0:1, 0:1] + c_high[0, 0:1, 0:1]
    far_ref[...] = x_ref[:, plan.slab :] + 0.0 * come


def inner(plan, w_ref, m_ref, f_ref, x_ref, g_ref, p0_ref, p1_ref):
    inner_rows(plan, w_ref, (p0_ref, p1_ref), two_layers(plan, x_ref, m_ref), two_layers(plan, f_ref, m_ref), g_ref)


def middle(
    plan, w_ref, m_ref, f_ref, x_ref, g_ref, low_ref, high_ref, side_ref, c_low, c_high,
    low_first, high_first, side_first, seams_ref, weight_ref,
    *refs,
):
    pad = plan.pad
    send_refs = refs[: plan.groups]
    n0_ref, h0_ref, x1_ref, rates_ref, p0_ref, p1_ref, y_ref, h1_ref, n1_ref, turn_ref, send_ref = refs[plan.groups :]
    own, force = two_layers(plan, x_ref, m_ref), two_layers(plan, f_ref, m_ref)
    low_force = Layer(plan, low_first, 0, None, seams_ref[0, 0], 0)
    high_force = Layer(plan, high_first, plan.slab, None, seams_ref[2, 0], 1)
    near = Layer(plan, low_ref, 0, low_force.rates), Layer(plan, high_ref, plan.slab, high_force.rates)
    n_refs = n0_ref, n1_ref
    middle_rows(
        plan, w_ref, (p0_ref, p1_ref), own, force, g_ref, near, (low_force, high_force),
        sides_of(plan, side_ref, side_first, seams_ref), corners_of(plan, (c_low, c_high), None), y_ref,
        (h0_ref, h1_ref), n_refs,
    )

    def put(a, r, value):
        x1_ref[:, at(r)] = value

    outer_rows(plan, w_ref, own, near, (None, Layer(plan, high_ref).chunk), n_refs, (h0_ref, h1_ref), put, (1,))
    for r in range(plan.rows):
        last = [near[0].rate(C_AZ, r), own[0].rate(C_AZ, r), jnp.zeros((RATES - 2, LANES), jnp.float32)]
        rates_ref[:, at(r)] = jnp.concatenate(last, axis=0)

    turn_ref[...] = jnp.zeros_like(turn_ref)
    for r in range(plan.rows):
        turn_ref[r : r + 1, :] = low_ref[plan.tf : plan.tf + 1, at(r)]
    far = jnp.transpose(turn_ref[...])[:pad]

    def packed(read, count, first=0, step=1):
        lane = lane_index(count)
        out = jnp.zeros((count, LANES), jnp.float32)
        for r in range(plan.rows):
            to = first + r * step
            out = jnp.where(lane == to, rolled(read(r), to), out)
        return out

    rates = packed(lambda r: rates_ref[:, at(r)], RATES)
    inlet = packed(lambda r: n0_ref[:, at(r)], pad) - rates[0:1] * dot3(matrix(plan, w_ref, DOWN_AZ), far)
    inlet = packed(lambda r: h0_ref[:, at(r)], pad) - rates[1:2] * dot3(matrix(plan, w_ref, DOWN_AZ), inlet)
    lane = lane_index(pad)
    spread = packed(lambda r: x1_ref[:, at(r)], pad, plan.rows * WINDOW, WINDOW)
    for r in range(plan.rows):
        spread = jnp.where(lane == r * WINDOW, rolled(inlet, r * (WINDOW - 1)), spread)
    inlet = jnp.where(parity() == 0, spread, rolled(spread, LANES // 2))
    back = pick(inlet, plan.window_spread()) * weight_ref[...]
    back = back + rolled(back, -plan.width)
    me = lax.axis_index("sector")
    send_ref[...] = jnp.zeros_like(send_ref)
    for t in range(plan.insts):
        to = lax.rem(me + plan.shift[t], plan.sectors)
        place = (lax.div(to, GROUP) ^ lax.div(me, GROUP)) * GROUP + lax.rem(to, GROUP)
        send_ref[place, : plan.fields, : plan.width] = back[t * plan.fields : (t + 1) * plan.fields, : plan.width]
    for i, ref in enumerate(send_refs):
        ref[...] = send_ref[i * GROUP : (i + 1) * GROUP]


def outer(plan, w_ref, rates_ref, n0_ref, h0_ref, x1_ref, far_ref, out_ref):
    mirror = parity()

    def put(a, r, value):
        there = jnp.where(mirror == 0, a, plan.ct - 1 - a) * plan.rows + r
        out_ref[pl.ds(there, plan.tf, stride=plan.cells), :] = value[: plan.tf]

    for r in range(plan.rows):
        put(1, r, x1_ref[:, at(r)])

    def near_chunk(c):
        lanes = slice(c * CHUNK, (c + 1) * CHUNK)
        return n0_ref[:, lanes] - rates_ref[0:1, lanes] * dot3(w_ref[...], far_ref[:, lanes])

    azimuthal(plan, w_ref, 0, near_chunk, lambda r, terms: put(0, r, h0_ref[:, at(r)] - rates_ref[1:2, at(r)] * terms))


def turn_panels(plan, *refs):
    place = lax.rem(lax.axis_index("sector"), GROUP)
    for j, out_ref in enumerate(refs[plan.groups :]):
        for i, ref in enumerate(refs[: plan.groups]):
            out_ref[i] = ref[place ^ j]


def collect_panels(plan, *refs):
    out_ref, tiles_ref, panels_ref = refs[GROUP:]
    for j, ref in enumerate(refs[:GROUP]):
        tiles_ref[j * plan.groups : (j + 1) * plan.groups] = ref[...]
    me = lax.axis_index("sector")
    for t in range(plan.insts):
        source = lax.rem(me + (plan.sectors - plan.shift[t]), plan.sectors)
        j = lax.rem(source, GROUP) ^ lax.rem(me, GROUP)
        i = lax.div(source, GROUP) ^ lax.div(me, GROUP)
        panels_ref[t * RATES : (t + 1) * RATES, :] = tiles_ref[j * plan.groups + i]
    for f in range(plan.fields):
        tile = panels_ref[pl.ds(f, plan.insts, stride=RATES), : plan.width]
        out_ref[f] = jnp.transpose(tile)


def sibling(plan):
    return [s ^ 1 for s in range(plan.sectors)]


def outside(plan):
    return [(s - 1 if s % 2 == 0 else s + 1) % plan.sectors for s in range(plan.sectors)]


def swap(array, partner):
    return lax.ppermute(array, "sector", list(enumerate(partner)))


def beside(plan, array, partner):
    def pairs(step):
        out = []
        for s in range(plan.sectors):
            for x in range(plan.spans):
                to = 1 - x if plan.ends == 1 else x + step
                if 0 <= to < plan.spans:
                    out.append((s * plan.spans + x, partner[s] * plan.spans + to))
        return out

    if plan.ends == 1:
        return lax.ppermute(array, AXES, pairs(0))
    return jnp.concatenate([lax.ppermute(array[:1], AXES, pairs(-1)), lax.ppermute(array[1:], AXES, pairs(1))])


def on_device(
    sectors, spans,
    rhs, diag_coef, face_coef, time_coef, jac_up, jac_down, wall_mask, stator_adj, owner, first_panel_share,
):
    plan = Plan(rhs, stator_adj, sectors, spans)
    pad, cells, slab, insts, fields, ends = plan.pad, plan.cells, plan.slab, plan.insts, plan.fields, plan.ends
    bind = functools.partial
    whole, half = f32(pad, plan.ct * slab), f32(pad, slab)
    products = (vmem(6 * pad, slab),) * 2
    alone, next_chip, next_core = list(range(sectors)), outside(plan), sibling(plan)

    def edges(rows):
        return f32(ends, rows, DEPTH * plan.ct * LANES), f32(ends, rows, LANES), f32(ends, rows, LANES)

    stator = jnp.transpose(stator_adj, (1, 2, 3, 0)).reshape(fields, plan.width, insts)
    sent = call(bind(send_panels, plan), f32(sectors * spans, RATES, LANES), (vmem(insts * RATES, LANES),))(
        stator,
        jnp.concatenate([
            lax.rem(owner, plan.panels).astype(jnp.float32).reshape(insts, cells), first_panel_share.reshape(insts, cells),
        ], axis=1),
    )
    got = lax.all_to_all(sent, AXES, 0, 0, tiled=True)
    m, side, c0, c1 = call(
        bind(prepare, plan), (f32(pad + RATES, plan.ct * slab),) + edges(pad + RATES), (vmem(6, cells, LANES),)
    )(
        rhs.reshape(plan.tf * cells, LANES),
        jnp.concatenate([
            wall_mask.astype(jnp.float32).reshape(cells, LANES), diag_coef.reshape(cells, LANES),
            time_coef.reshape(cells, LANES), face_coef.reshape(3 * cells, LANES),
        ]),
    )
    low_first, high_first = swap(m, next_chip), swap(m, next_core)
    side_first = beside(plan, side, alone)
    c_low, c_high = beside(plan, c0, next_chip), beside(plan, c1, next_core)
    matrices, down = call(
        bind(stack_matrices, plan),
        [jax.ShapeDtypeStruct((count * pad, 3 * pad), jnp.bfloat16) for count in (7, 1)],
    )(jac_up, jac_down, plan.spectral(), plan.field_rows(), plan.field_lanes(), plan.block_diagonal())
    tiles = len(plan.tiles)
    seams, weight, force, g = call(
        bind(begin, plan), (f32(3, 1 + ends, pad, LANES), f32(pad, LANES), whole, whole),
        (vmem(pad, tiles * LANES), vmem(tiles * pad, LANES), vmem(16, tiles * LANES)) + products,
        flops=2_000_000_000,
    )(matrices, m, got)
    x, near, side, c0, c1 = call(
        bind(first_half, plan), (whole, half) + edges(pad),
        products + (vmem(pad, 2 * slab),) + (vmem(pad, slab),) * 4 + (vmem(LANES, LANES),),
        flops=4_000_000_000,
    )(matrices, m, force, g, low_first, high_first, side_first, c_low, c_high, seams)

    low, high = swap(near, next_chip), swap(x, next_core)
    side = beside(plan, side, alone)
    c_low, c_high = beside(plan, c0, next_chip), beside(plan, c1, next_core)
    (g,) = call(bind(inner, plan), (whole,), products, flops=2_000_000_000)(matrices, m, force, x)
    far = call(bind(hold_far, plan), half)(x, side, c_high)
    far_low = swap(far, next_chip)
    tiles = f32(GROUP, RATES, LANES)
    *back, n0, h0, x1, rates = call(
        bind(middle, plan), (tiles,) * plan.groups + (half, half, half, f32(RATES, slab)),
        products + (
            vmem(pad, 2 * slab), vmem(pad, slab), vmem(pad, slab), vmem(LANES, LANES), vmem(sectors, RATES, LANES),
        ),
        flops=4_000_000_000,
    )(
        matrices, m, force, x, g, low, high, side, c_low, c_high, low_first, high_first, side_first, seams, weight
    )
    for i in range(1, plan.groups):
        back[i] = swap(back[i], [(s // GROUP ^ i) * GROUP + s % GROUP for s in range(sectors)])
    back = list(call(bind(turn_panels, plan), (f32(plan.groups, RATES, LANES),) * GROUP)(*back))
    for j in range(1, GROUP):
        back[j] = swap(back[j], [s ^ j for s in range(sectors)])
    sens = call(
        bind(collect_panels, plan), f32(fields, plan.width, insts),
        (vmem(sectors, RATES, LANES), vmem(insts * RATES, LANES)),
    )(*back)
    out = call(bind(outer, plan), f32(plan.tf * cells, LANES))(down, rates, n0, h0, x1, far_low)
    sens = jnp.transpose(sens.reshape(fields, plan.panels, plan.rows, insts), (3, 0, 1, 2))
    return out.reshape(rhs.shape), sens


def solution(mesh):
    in_specs = (
        P(None, None, "sector", "span", None),
        P("sector", "span", None),
        P(None, "sector", "span", None),
        P("sector", "span", None),
        P(),
        P(),
        P("sector", "span", None),
        P(None, None, "sector", "span"),
        P(None, "sector", "span"),
        P(None, "sector", "span"),
    )
    out_specs = (P(None, None, "sector", "span", None), P(None, None, "sector", "span"))
    return jax.shard_map(
        functools.partial(on_device, mesh.shape["sector"], mesh.shape["span"]),
        mesh=mesh, in_specs=in_specs, out_specs=out_specs, check_vma=False,
    )
```

```python
import functools

import jax
import jax.numpy as jnp
import ml_dtypes
import numpy as np
from jax import lax
from jax.experimental import pallas as pl
from jax.experimental.pallas import tpu as pltpu
from jax.sharding import PartitionSpec as P

SWEEPS = 4
GROUP = 4
DEPTH = 2
LANES = 128
CHUNK = 256
WINDOW = 8
HIGHEST = lax.Precision.HIGHEST
DOWN_AZ, SPECTRAL, UP_SP, DOWN_SP, UP_AX, DOWN_AX, UP_AZ = range(7)
C_TIME, C_AZ, C_SP, C_UP, C_DOWN, C_MASK = range(6)
RATES = 8
AXES = ("sector", "span")


class Plan:
    def __init__(self, rhs, stator_adj, sectors, spans):
        self.insts, self.fields, self.ct, self.rows, self.nax = rhs.shape
        self.panels = stator_adj.shape[2]
        self.sectors, self.spans = sectors, spans
        self.tf = self.insts * self.fields
        self.pad = -(-self.tf // 16) * 16
        self.cells = self.ct * self.rows
        self.slab = self.rows * LANES
        self.width = self.panels * self.rows
        self.shift = [
            ((t * sectors) // (self.insts - 1) - t // (self.insts - 1)) % sectors for t in range(self.insts)
        ]
        assert self.ct == 2 and self.nax == LANES and SWEEPS % DEPTH == 0 and spans > 1
        assert len(set(self.shift)) == self.insts and self.cells * WINDOW == LANES and self.rows >= SWEEPS
        assert self.slab % CHUNK == 0 and 3 * self.pad <= 256 and 2 * self.ct * self.width == LANES
        assert sectors % 2 == 0
        self.groups = sectors // GROUP
        assert sectors % GROUP == 0 and self.groups & (self.groups - 1) == 0
        self.ends = 1 if spans == 2 else 2
        self.blocks = [-1, 0, 1]
        self.halves = [0, 1] if spans == 2 else [-1, 0, 1]
        self.tiles = [(k, x) for k in self.blocks for x in self.halves]
        self.slots = [
            [t for t in range(self.insts) if any((k + self.shift[t]) % sectors == o for k in self.blocks)]
            for o in range(sectors)
        ]
        last = LANES - self.width
        self.weight_at = [(t, last) for t in range(self.fields)] + [
            (self.fields, i * self.width) for i in range(self.insts - self.fields)
        ]
        assert max(map(len, self.slots)) * self.width <= last and 2 * self.cells == self.width
        assert self.fields == RATES - 1 and (self.insts - self.fields) * self.width <= LANES

    def spectral(self):
        t = np.arange(self.insts)
        off = t[:, None] - t[None, :]
        sines = np.where(off == 0, 1.0, np.sin(np.pi * off / self.insts))
        table = np.where(off == 0, 0.0, 0.5 * (1.0 - 2.0 * (off % 2)) / sines).astype(np.float32)
        full = np.zeros((self.pad, self.pad), np.float32)
        full[: self.tf, : self.tf] = np.kron(table.T, np.eye(self.fields, dtype=np.float32))
        hi = full.astype(ml_dtypes.bfloat16)
        lo = (full - hi.astype(np.float32)).astype(ml_dtypes.bfloat16)
        return np.concatenate([hi, lo, hi], axis=1)

    def field_rows(self):
        out = np.zeros((self.pad, self.fields), np.float32)
        out[np.arange(self.tf), np.arange(self.tf) % self.fields] = 1.0
        return out

    def field_lanes(self):
        return np.tile(self.field_rows().T, (1, 3))

    def block_diagonal(self):
        block = np.full(self.pad, -1)
        block[: self.tf] = np.arange(self.tf) // self.fields
        same = (block[:, None] == block[None, :]) & (block[:, None] >= 0)
        return np.tile(same.astype(np.float32), (1, 3))


    def inst_rows(self):
        row, inst = table_index(self.pad, 16)
        return ((row >= inst * self.fields) & (row < (inst + 1) * self.fields)).astype(jnp.float32)

    def cell_of(self, lane):
        return lax.div(lane, self.width) * self.rows + lax.rem(lane, self.rows)

    def window_lanes(self):
        lane, to = table_index(LANES, LANES)
        return (lane < self.ct * self.width) & (to == self.cell_of(lane) * WINDOW)

    def window_spread(self):
        to, lane = table_index(LANES, LANES)
        return (lane < self.ct * self.width) & (to == self.cell_of(lane) * WINDOW)

    def weight_lanes(self):
        cell, lane = table_index(LANES, LANES)
        half = self.ct * self.width
        wanted = jnp.where(lane < half, self.cell_of(lane), self.cells + self.cell_of(lane - half))
        return cell == wanted

    def panel_lanes(self):
        lane = lane_index(1)
        panel = lax.rem(lax.div(lane, self.rows), self.panels)
        return jnp.where(lane < self.ct * self.width, panel, -9).astype(jnp.float32)


def table_index(rows, columns):
    return [lax.broadcasted_iota(jnp.int32, (rows, columns), axis) for axis in (0, 1)]


def call(kernel, out, scratch=(), flops=2_000_000, nbytes=1_000_000):
    return pl.pallas_call(
        kernel,
        out_shape=out,
        scratch_shapes=list(scratch),
        compiler_params=pltpu.CompilerParams(vmem_limit_bytes=20 * 1024 * 1024),
        cost_estimate=pl.CostEstimate(flops=flops, bytes_accessed=nbytes, transcendentals=0),
    )


def f32(*shape):
    return jax.ShapeDtypeStruct(shape, jnp.float32)


def vmem(*shape):
    return pltpu.VMEM(shape, jnp.float32)


def halves_of(x):
    hi = x.astype(jnp.bfloat16)
    return hi, (x - hi.astype(jnp.float32)).astype(jnp.bfloat16)


def dot3(w, x):
    hi, lo = halves_of(x)
    return jnp.dot(w, jnp.concatenate([hi, hi, lo], axis=0), preferred_element_type=jnp.float32)


def pick(x, table):
    table = table.astype(jnp.float32).astype(jnp.bfloat16)
    table = jnp.concatenate([table, table], axis=0)
    return jnp.dot(jnp.concatenate(halves_of(x), axis=1), table, preferred_element_type=jnp.float32)


def dot_full(a, b):
    return jnp.dot(a, b, precision=HIGHEST, preferred_element_type=jnp.float32)


def lane_index(rows):
    return lax.broadcasted_iota(jnp.int32, (rows, LANES), 1)


def rolled(x, by):
    by %= LANES
    return pltpu.roll(x, by, axis=1) if by else x


def at(r, count=1, start=0):
    return slice(start + r * LANES, start + (r + count) * LANES)


def parity():
    return lax.rem(lax.axis_index("sector"), 2)


def has_sides(plan):
    span = lax.axis_index("span")
    return jnp.where(span < plan.spans - 1, 1.0, 0.0), jnp.where(span > 0, 1.0, 0.0)


class Layer:
    def __init__(self, plan, ref, start=0, rates=None, seam=None, layer=0):
        self.plan, self.ref, self.start, self.seam, self.layer = plan, ref, start, seam, layer
        self.rates = rates or (ref, start)

    def rate(self, which, r, count=1):
        ref, start = self.rates
        row = self.plan.pad + which
        return ref[row : row + 1, at(r, count, start)]

    def row(self, r):
        value = self.ref[: self.plan.pad, at(r, 1, self.start)]
        if self.seam is None:
            return value
        return value + placed(self.seam, self.layer * self.plan.rows + r) * self.rate(C_MASK, r)

    def chunk(self, c):
        count = CHUNK // LANES
        if self.seam is None:
            return self.ref[: self.plan.pad, at(c * count, count, self.start)]
        return jnp.concatenate([self.row(c * count + part) for part in range(count)], axis=1)


def placed(tile, cell):
    return jnp.where(lane_index(tile.shape[0]) == 0, rolled(tile, -cell * WINDOW), 0.0)


class Products:
    def __init__(self, plan, w_ref, p_ref, first):
        self.plan, self.w, self.p, self.first = plan, w_ref, p_ref, first

    def fill(self, layer):
        for c in range(self.plan.slab // CHUNK):
            self.p[:, c * CHUNK : (c + 1) * CHUNK] = dot3(matrix(self.plan, self.w, self.first, 6), layer.chunk(c))
        self.layer = layer
        return self

    def get(self, block, r):
        row = (block - self.first) * self.plan.pad
        return self.p[row : row + self.plan.pad, at(r)]

    def own_terms(self, r):
        rate = self.layer.rate
        total = rate(C_TIME, r) * self.get(SPECTRAL, r)
        beside = []
        if r + 1 < self.plan.rows:
            beside.append(self.get(UP_SP, r + 1))
        if r > 0:
            beside.append(self.get(DOWN_SP, r - 1))
        total = total + rate(C_SP, r) * sum(beside[1:], beside[0])
        total = total + rate(C_UP, r) * rolled(self.get(UP_AX, r), -1)
        return total + rate(C_DOWN, r) * rolled(self.get(DOWN_AX, r), 1)


def matrix(plan, w_ref, block, count=1):
    return w_ref[block * plan.pad : (block + count) * plan.pad, :]


def two_layers(plan, ref, rates=None, seam=None):
    return [
        Layer(plan, ref, a * plan.slab, (rates, a * plan.slab) if rates is not None else None, seam, a)
        for a in range(plan.ct)
    ]


def inner_rows(plan, w_ref, p_refs, layers, force, g_ref):
    first = Products(plan, w_ref, p_refs[0], DOWN_AZ).fill(layers[0])
    second = Products(plan, w_ref, p_refs[1], SPECTRAL).fill(layers[1])
    for r in range(plan.rows):
        other = second.get(UP_AZ, r), first.get(DOWN_AZ, r)
        for a, products in enumerate((first, second)):
            total = products.own_terms(r) + layers[a].rate(C_AZ, r) * other[a]
            if isinstance(g_ref, tuple):
                g_ref[a][:, at(r)] = force[a].row(r) - total
            else:
                g_ref[:, at(r, 1, a * plan.slab)] = force[a].row(r) - total


def azimuthal(plan, w_ref, block, chunk_of, take):
    for c in range(plan.slab // CHUNK):
        terms = dot3(matrix(plan, w_ref, block), chunk_of(c))
        for part in range(CHUNK // LANES):
            take(c * (CHUNK // LANES) + part, terms[:, at(part)])


def middle_rows(plan, w_ref, p_refs, own, own_force, g_ref, near, near_force, side, corner, y_ref, h_refs, n_refs):
    pad, rows, ct = plan.pad, plan.rows, plan.ct
    last = (rows - 1, 0)
    edge_terms, edge_new, corner_terms = [], [], []
    is_first = lax.axis_index("span") == 0

    def choose(n, above, below):
        return jnp.where(is_first, above, below) if plan.ends == 1 else (above, below)[n]

    for n in range(plan.ends):
        outward = choose(n, matrix(plan, w_ref, UP_SP), matrix(plan, w_ref, DOWN_SP))
        inward = choose(n, matrix(plan, w_ref, DOWN_SP), matrix(plan, w_ref, UP_SP))
        first, second, edge_force, edge_rate = side(n)
        corners = corner(n)
        every = dot3(w_ref[...], first)
        beyond = dot3(outward, second)
        within = [choose(n, x.row(last[0]), x.row(last[1])) for x in own]
        within = dot3(inward, jnp.concatenate(within, axis=1))
        from_low = dot3(matrix(plan, w_ref, DOWN_AZ), corners[0])
        from_high = dot3(matrix(plan, w_ref, UP_AZ), corners[1])
        new = []
        for a in range(ct):

            def part(block, b=a):
                return every[block * pad : (block + 1) * pad, at(b)]

            around = part(UP_AZ, 1) + from_low if a == 0 else from_high + part(DOWN_AZ, 0)
            total = edge_rate(C_TIME, a) * part(SPECTRAL) + edge_rate(C_AZ, a) * around
            total = total + edge_rate(C_SP, a) * (beyond[:, at(a)] + within[:, at(a)])
            total = total + edge_rate(C_UP, a) * rolled(part(UP_AX), -1)
            total = total + edge_rate(C_DOWN, a) * rolled(part(DOWN_AX), 1)
            new.append(edge_force[:, at(a)] - total)
        of_edge = choose(n, *(every[block * pad : (block + 1) * pad] for block in (UP_SP, DOWN_SP)))
        of_new = dot3(outward, jnp.concatenate(new, axis=1))
        of_corners = dot3(outward, jnp.concatenate(corners, axis=1))
        for keep in has_sides(plan) if plan.ends == 1 else (1.0,):
            edge_terms.append(of_edge * keep)
            edge_new.append(of_new * keep)
            corner_terms.append([of_corners[:, at(a)] * keep for a in range(ct)])

    products = (
        Products(plan, w_ref, p_refs[0], DOWN_AZ).fill(near[0]), Products(plan, w_ref, p_refs[1], SPECTRAL).fill(near[1]),
    )
    for a, (to_own, to_near) in enumerate(((DOWN_AZ, UP_AZ), (UP_AZ, DOWN_AZ))):

        def take(r, terms):
            total = products[a].own_terms(r) + near[a].rate(C_AZ, r) * terms
            mine = own[a].rate(C_AZ, r) * products[a].get(to_own, r)
            for n in range(2):
                if r == last[n]:
                    total = total + near[a].rate(C_SP, r) * corner_terms[n][a]
                    mine = mine + own[a].rate(C_SP, r) * edge_terms[n][:, at(a)]
            n_refs[a][:, at(r)] = near_force[a].row(r) - total
            lanes = at(r, 1, a * plan.slab)
            y_ref[:, lanes] = g_ref[:, lanes] - mine

        azimuthal(plan, w_ref, to_near, own[a].chunk, take)

    after = [Layer(plan, y_ref, a * plan.slab, own[a].rates) for a in range(ct)]
    inner_rows(plan, w_ref, p_refs, after, own_force, h_refs)
    for a in range(ct):
        for n in range(2):
            h_refs[a][:, at(last[n])] -= own[a].rate(C_SP, last[n]) * edge_new[n][:, at(a)]


def outer_rows(plan, w_ref, own, near, far_chunks, n_refs, h_refs, put, layers=(0, 1)):
    count = CHUNK // LANES
    for a in layers:
        block = (DOWN_AZ, UP_AZ)[a]

        def near_chunk(c):
            terms = dot3(matrix(plan, w_ref, block), far_chunks[a](c))
            return n_refs[a][:, at(c * count, count)] - near[a].rate(C_AZ, c * count, count) * terms

        def take(r, terms):
            put(a, r, h_refs[a][:, at(r)] - own[a].rate(C_AZ, r) * terms)

        azimuthal(plan, w_ref, block, near_chunk, take)


def sides_of(plan, side_ref, force_ref, seams_ref):
    pad, ct = plan.pad, plan.ct
    keeps = (1.0,) if plan.ends == 1 else has_sides(plan)
    is_first = lax.axis_index("span") == 0

    def inlet(n, e, a):
        above, below = a * plan.rows + e, a * plan.rows + plan.rows - 1 - e
        tile = seams_ref[1, 1 + n]
        if plan.ends == 1:
            return jnp.where(is_first, placed(tile, above), placed(tile, below))
        return placed(tile, (above, below)[n])

    def read(n, ref, e, seam):
        value = ref[n, :pad, at(e * ct, ct)]
        if seam:
            scale = ref[n, pad + C_MASK : pad + C_MASK + 1, at(e * ct, ct)]
            value = value + jnp.concatenate([inlet(n, e, a) for a in range(ct)], axis=1) * scale
        return value * keeps[n]

    def side(n):
        same = side_ref is force_ref

        def rate(which, a):
            return force_ref[n, pad + which : pad + which + 1, at(a)] * keeps[n]

        force = read(n, force_ref, 0, True)
        first = force if same else read(n, side_ref, 0, False)
        return first, read(n, side_ref, 1, same), force, rate

    return side


def corners_of(plan, c_refs, seams_ref):
    keeps = (1.0,) if plan.ends == 1 else has_sides(plan)
    is_first = lax.axis_index("span") == 0

    def corner(n):
        out = []
        for a, c_ref in enumerate(c_refs):
            value = c_ref[n, : plan.pad]
            if seams_ref is not None:
                tile = seams_ref[2 * a, 1 + n]
                above, below = (placed(tile, a * plan.rows + r) for r in (0, plan.rows - 1))
                inlet = jnp.where(is_first, above, below) if plan.ends == 1 else (above, below)[n]
                value = value + inlet * c_ref[n, plan.pad + C_MASK : plan.pad + C_MASK + 1]
            out.append(value * keeps[n])
        return out

    return corner


def prepare(plan, rhs_ref, coef_ref, m_ref, side_ref, c0_ref, c1_ref, rates_ref):
    pad, cells = plan.pad, plan.cells
    mask, diag, time, *face = [coef_ref[cells * i : cells * (i + 1), :] for i in range(6)]
    scale = mask / diag
    lane = lane_index(cells)
    axial = scale * face[2]
    rates = (
        scale * time, scale * face[0], scale * face[1],
        jnp.where(lane < LANES - 1, axial, 0.0), jnp.where(lane > 0, axial, 0.0), scale,
    )
    for i, rate in enumerate(rates):
        rates_ref[i] = rate
    tail = jnp.zeros((pad - plan.tf, LANES), jnp.float32)
    rest = jnp.zeros((RATES - 6, LANES), jnp.float32)
    mirror = parity()
    for cell in range(cells):
        a, r = divmod(cell, plan.rows)
        there = jnp.where(mirror == 0, a, plan.ct - 1 - a) * plan.rows + r
        table = [rates_ref[i, pl.ds(there, 1), :] for i in range(6)]
        field = jnp.concatenate([rhs_ref[pl.ds(there, plan.tf, stride=cells), :], tail], axis=0)
        m_ref[:pad, at(cell)] = field * table[C_MASK]
        m_ref[pad:, at(cell)] = jnp.concatenate(table + [rest], axis=0)
    write_edges(plan, m_ref, side_ref, (c0_ref, c1_ref))


def write_edges(plan, x_ref, side_ref, c_refs):
    first = lax.axis_index("span") == 0
    for a in range(plan.ct):
        for e in range(DEPTH):
            low, high = x_ref[:, at(a * plan.rows + e)], x_ref[:, at((a + 1) * plan.rows - 1 - e)]
            ends = [jnp.where(first, high, low)] if plan.ends == 1 else [low, high]
            for n, end in enumerate(ends):
                side_ref[n, :, at(e * plan.ct + a)] = end
                if e == 0:
                    c_refs[a][n] = end


def stack_matrices(plan, up_ref, down_ref, spectral_ref, rows_ref, lanes_ref, diagonal_ref, out_ref, down_out):
    pad = plan.pad
    lane = lax.broadcasted_iota(jnp.int32, (pad, 3 * pad), 1)
    second = (lane >= pad) & (lane < 2 * pad)
    out_ref[SPECTRAL * pad : (SPECTRAL + 1) * pad, :] = spectral_ref[...]
    even = parity() == 0
    for block, small in (
        (DOWN_AZ, jnp.where(even, down_ref[0], up_ref[0])), (UP_AZ, jnp.where(even, up_ref[0], down_ref[0])),
        (UP_SP, up_ref[1]), (DOWN_SP, down_ref[1]), (UP_AX, up_ref[2]), (DOWN_AX, down_ref[2]),
    ):
        full = dot_full(dot_full(rows_ref[...], small), lanes_ref[...]) * diagonal_ref[...]
        hi = full.astype(jnp.bfloat16).astype(jnp.float32)
        out_ref[block * pad : (block + 1) * pad, :] = jnp.where(second, full - hi, hi).astype(jnp.bfloat16)
    down_out[...] = matrix(plan, out_ref, DOWN_AZ)


def send_panels(plan, stator_ref, both_ref, out_ref, panels_ref):
    me = lax.axis_index("sector")
    for f in range(plan.fields):
        panels_ref[pl.ds(f, plan.insts, stride=RATES), : plan.width] = jnp.transpose(stator_ref[f])
    out_ref[...] = jnp.zeros_like(out_ref)
    for t, (row, start) in enumerate(plan.weight_at):
        both = jnp.broadcast_to(both_ref[t : t + 1, :][None], (out_ref.shape[0], 1, plan.width))
        out_ref[:, row : row + 1, start : start + plan.width] = both
    for o, slots in enumerate(plan.slots):
        to = lax.rem(me + (plan.sectors - o), plan.sectors) * plan.spans
        for slot, t in enumerate(slots):
            lanes = slice(slot * plan.width, (slot + 1) * plan.width)
            panels = panels_ref[t * RATES : t * RATES + plan.fields, : plan.width]
            for x in range(plan.spans):
                out_ref[to + x, : plan.fields, lanes] = panels


def begin(
    plan, w_ref, m_ref, got_ref,
    seams_ref, weight_ref, x_ref, g_ref, panels_ref, terms_ref, rows_ref, p0_ref, p1_ref,
):
    pad, insts, fields = plan.pad, plan.insts, plan.fields
    me, span = lax.axis_index("sector"), lax.axis_index("span")
    even, is_first = parity() == 0, span == 0
    tiles = plan.tiles
    panels_ref[...] = jnp.zeros_like(panels_ref)
    rows_ref[...] = jnp.zeros_like(rows_ref)
    for n, (k, x) in enumerate(tiles):
        at_span = x if plan.spans == 2 else jnp.clip(span + x, 0, plan.spans - 1)
        for t in range(insts):
            o = (k + plan.shift[t]) % plan.sectors
            source = lax.rem(me + o, plan.sectors) * plan.spans + at_span
            tile = rolled(got_ref[source], -plan.slots[o].index(t) * plan.width)
            panels_ref[t * fields : (t + 1) * fields, n * LANES : n * LANES + plan.width] = tile[:fields, : plan.width]
        tile = got_ref[lax.rem(me + k + plan.sectors, plan.sectors) * plan.spans + at_span]
        lanes = slice(n * LANES, n * LANES + plan.width)
        rows_ref[:fields, lanes] = rolled(tile, -plan.weight_at[0][1])[:fields, : plan.width]
        for t in range(fields, insts):
            row, start = plan.weight_at[t]
            rows_ref[t : t + 1, lanes] = rolled(tile, -start)[row : row + 1, : plan.width]
    spread = dot_full(plan.inst_rows(), rows_ref[...])
    spread = pick(jnp.concatenate([spread[:, at(n)] for n in range(len(tiles))], axis=0), plan.weight_lanes())
    first, share, panel = spread, rolled(spread, plan.ct * plan.width), plan.panel_lanes()
    lower = (jnp.abs(first - panel) < 0.5).astype(jnp.float32)
    upper = (jnp.abs(first + 1.0 - panel) < 0.5).astype(jnp.float32)
    weights = share * lower + (1.0 - share) * upper
    for n in range(len(tiles)):
        panels = panels_ref[:, at(n)]
        terms_ref[n * pad : (n + 1) * pad, :] = panels + rolled(panels, plan.width)
    seams = pick(terms_ref[...] * weights, plan.window_lanes())

    def tile(values, k, x):
        n = tiles.index((k, x))
        return values[n * pad : (n + 1) * pad]

    def around(values, k):
        if plan.spans == 2:
            pair = tile(values, k, 0), tile(values, k, 1)
            return [jnp.where(is_first, pair[0], pair[1]), jnp.where(is_first, pair[1], pair[0])]
        return [tile(values, k, x) for x in (0, 1, -1)]

    def mirrored(value):
        return rolled(value, LANES // 2)

    here = around(seams, 0)
    behind, ahead = around(seams, -1), around(seams, 1)
    for i in range(1 + plan.ends):
        seams_ref[0, i] = jnp.where(even, mirrored(behind[i]), ahead[i])
        seams_ref[1, i] = jnp.where(even, here[i], mirrored(here[i]))
        seams_ref[2, i] = jnp.where(even, mirrored(ahead[i]), behind[i])
    weight_ref[...] = around(weights, 0)[0]

    for layer in two_layers(plan, m_ref, seam=seams_ref[1, 0]):
        for r in range(plan.rows):
            x_ref[:, at(r, 1, layer.start)] = layer.row(r)
    layers = two_layers(plan, x_ref, m_ref)
    inner_rows(plan, w_ref, (p0_ref, p1_ref), layers, layers, g_ref)


def first_half(
    plan, w_ref, m_ref, f_ref, g_ref, low_ref, high_ref, side_ref, c_low, c_high, seams_ref,
    x_ref, near_ref, side_out, c0_ref, c1_ref, p0_ref, p1_ref, y_ref, h0_ref, h1_ref, n0_ref, n1_ref, inlet_ref,
):
    own = two_layers(plan, f_ref, m_ref)
    low = two_layers(plan, low_ref, seam=seams_ref[0, 0])
    high = two_layers(plan, high_ref, seam=seams_ref[2, 0])
    near = low[0], high[1]
    n_refs = n0_ref, n1_ref
    middle_rows(
        plan, w_ref, (p0_ref, p1_ref), own, own, g_ref, near, near, sides_of(plan, side_ref, side_ref, seams_ref),
        corners_of(plan, (c_low, c_high), seams_ref), y_ref, (h0_ref, h1_ref), n_refs,
    )
    lane = lane_index(plan.pad)
    inlet_ref[...] = jnp.zeros_like(inlet_ref)

    def put(a, r, value):
        x_ref[:, at(r, 1, a * plan.slab)] = value
        if a == 0:
            near_ref[:, at(r)] = value
        else:
            inlet_ref[: plan.pad, :] = jnp.where(lane == r, rolled(value, r), inlet_ref[: plan.pad, :])

    outer_rows(plan, w_ref, own, near, (low[1].chunk, high[0].chunk), n_refs, (h0_ref, h1_ref), put)
    turned = jnp.transpose(inlet_ref[...])
    for r in range(plan.rows):
        near_ref[plan.tf : plan.tf + 1, at(r)] = turned[r : r + 1, :]
    write_edges(plan, x_ref, side_out, (c0_ref, c1_ref))


def hold_far(plan, x_ref, side_ref, c_high, far_ref):
    come = side_ref[0, 0:1, 0:1] + c_high[0, 0:1, 0:1]
    far_ref[...] = x_ref[:, plan.slab :] + 0.0 * come


def inner(plan, w_ref, m_ref, f_ref, x_ref, g_ref, p0_ref, p1_ref):
    inner_rows(plan, w_ref, (p0_ref, p1_ref), two_layers(plan, x_ref, m_ref), two_layers(plan, f_ref, m_ref), g_ref)


def middle(
    plan, w_ref, m_ref, f_ref, x_ref, g_ref, low_ref, high_ref, side_ref, c_low, c_high,
    low_first, high_first, side_first, seams_ref, weight_ref,
    *refs,
):
    pad = plan.pad
    send_refs = refs[:GROUP]
    n0_ref, h0_ref, x1_ref, rates_ref, p0_ref, p1_ref, y_ref, h1_ref, n1_ref, turn_ref, send_ref = refs[GROUP:]
    own, force = two_layers(plan, x_ref, m_ref), two_layers(plan, f_ref, m_ref)
    low_force = Layer(plan, low_first, 0, None, seams_ref[0, 0], 0)
    high_force = Layer(plan, high_first, plan.slab, None, seams_ref[2, 0], 1)
    near = Layer(plan, low_ref, 0, low_force.rates), Layer(plan, high_ref, plan.slab, high_force.rates)
    n_refs = n0_ref, n1_ref
    middle_rows(
        plan, w_ref, (p0_ref, p1_ref), own, force, g_ref, near, (low_force, high_force),
        sides_of(plan, side_ref, side_first, seams_ref), corners_of(plan, (c_low, c_high), None), y_ref,
        (h0_ref, h1_ref), n_refs,
    )

    def put(a, r, value):
        x1_ref[:, at(r)] = value

    outer_rows(plan, w_ref, own, near, (None, Layer(plan, high_ref).chunk), n_refs, (h0_ref, h1_ref), put, (1,))
    for r in range(plan.rows):
        last = [near[0].rate(C_AZ, r), own[0].rate(C_AZ, r), jnp.zeros((RATES - 2, LANES), jnp.float32)]
        rates_ref[:, at(r)] = jnp.concatenate(last, axis=0)

    turn_ref[...] = jnp.zeros_like(turn_ref)
    for r in range(plan.rows):
        turn_ref[r : r + 1, :] = low_ref[plan.tf : plan.tf + 1, at(r)]
    far = jnp.transpose(turn_ref[...])[:pad]

    def packed(read, count, first=0, step=1):
        lane = lane_index(count)
        out = jnp.zeros((count, LANES), jnp.float32)
        for r in range(plan.rows):
            to = first + r * step
            out = jnp.where(lane == to, rolled(read(r), to), out)
        return out

    rates = packed(lambda r: rates_ref[:, at(r)], RATES)
    inlet = packed(lambda r: n0_ref[:, at(r)], pad) - rates[0:1] * dot3(matrix(plan, w_ref, DOWN_AZ), far)
    inlet = packed(lambda r: h0_ref[:, at(r)], pad) - rates[1:2] * dot3(matrix(plan, w_ref, DOWN_AZ), inlet)
    lane = lane_index(pad)
    spread = packed(lambda r: x1_ref[:, at(r)], pad, plan.rows * WINDOW, WINDOW)
    for r in range(plan.rows):
        spread = jnp.where(lane == r * WINDOW, rolled(inlet, r * (WINDOW - 1)), spread)
    inlet = jnp.where(parity() == 0, spread, rolled(spread, LANES // 2))
    back = pick(inlet, plan.window_spread()) * weight_ref[...]
    back = back + rolled(back, -plan.width)
    me = lax.axis_index("sector")
    send_ref[...] = jnp.zeros_like(send_ref)
    for t in range(plan.insts):
        to = lax.rem(me + plan.shift[t], plan.sectors)
        place = (lax.rem(to, GROUP) ^ lax.rem(me, GROUP)) * plan.groups + (lax.div(to, GROUP) ^ lax.div(me, GROUP))
        send_ref[place, : plan.fields, : plan.width] = back[t * plan.fields : (t + 1) * plan.fields, : plan.width]
    for i, ref in enumerate(send_refs):
        ref[...] = send_ref[i * plan.groups : (i + 1) * plan.groups]


def outer(plan, w_ref, rates_ref, n0_ref, h0_ref, x1_ref, far_ref, out_ref):
    mirror = parity()

    def put(a, r, value):
        there = jnp.where(mirror == 0, a, plan.ct - 1 - a) * plan.rows + r
        out_ref[pl.ds(there, plan.tf, stride=plan.cells), :] = value[: plan.tf]

    for r in range(plan.rows):
        put(1, r, x1_ref[:, at(r)])

    def near_chunk(c):
        lanes = slice(c * CHUNK, (c + 1) * CHUNK)
        return n0_ref[:, lanes] - rates_ref[0:1, lanes] * dot3(w_ref[...], far_ref[:, lanes])

    azimuthal(plan, w_ref, 0, near_chunk, lambda r, terms: put(0, r, h0_ref[:, at(r)] - rates_ref[1:2, at(r)] * terms))


def turn_panels(plan, *refs):
    for i, out_ref in enumerate(refs[GROUP:]):
        for j, ref in enumerate(refs[:GROUP]):
            out_ref[j] = ref[i]


def collect_panels(plan, *refs):
    out_ref, tiles_ref, panels_ref = refs[plan.groups :]
    for i, ref in enumerate(refs[: plan.groups]):
        tiles_ref[i * GROUP : (i + 1) * GROUP] = ref[...]
    me = lax.axis_index("sector")
    for t in range(plan.insts):
        source = lax.rem(me + (plan.sectors - plan.shift[t]), plan.sectors)
        j = lax.rem(source, GROUP) ^ lax.rem(me, GROUP)
        i = lax.div(source, GROUP) ^ lax.div(me, GROUP)
        panels_ref[t * RATES : (t + 1) * RATES, :] = tiles_ref[i * GROUP + j]
    for f in range(plan.fields):
        tile = panels_ref[pl.ds(f, plan.insts, stride=RATES), : plan.width]
        out_ref[f] = jnp.transpose(tile)


def sibling(plan):
    return [s ^ 1 for s in range(plan.sectors)]


def outside(plan):
    return [(s - 1 if s % 2 == 0 else s + 1) % plan.sectors for s in range(plan.sectors)]


def swap(array, partner):
    return lax.ppermute(array, "sector", list(enumerate(partner)))


def beside(plan, array, partner):
    def pairs(step):
        out = []
        for s in range(plan.sectors):
            for x in range(plan.spans):
                to = 1 - x if plan.ends == 1 else x + step
                if 0 <= to < plan.spans:
                    out.append((s * plan.spans + x, partner[s] * plan.spans + to))
        return out

    if plan.ends == 1:
        return lax.ppermute(array, AXES, pairs(0))
    return jnp.concatenate([lax.ppermute(array[:1], AXES, pairs(-1)), lax.ppermute(array[1:], AXES, pairs(1))])


def on_device(
    sectors, spans,
    rhs, diag_coef, face_coef, time_coef, jac_up, jac_down, wall_mask, stator_adj, owner, first_panel_share,
):
    plan = Plan(rhs, stator_adj, sectors, spans)
    pad, cells, slab, insts, fields, ends = plan.pad, plan.cells, plan.slab, plan.insts, plan.fields, plan.ends
    bind = functools.partial
    whole, half = f32(pad, plan.ct * slab), f32(pad, slab)
    products = (vmem(6 * pad, slab),) * 2
    alone, next_chip, next_core = list(range(sectors)), outside(plan), sibling(plan)

    def edges(rows):
        return f32(ends, rows, DEPTH * plan.ct * LANES), f32(ends, rows, LANES), f32(ends, rows, LANES)

    stator = jnp.transpose(stator_adj, (1, 2, 3, 0)).reshape(fields, plan.width, insts)
    sent = call(bind(send_panels, plan), f32(sectors * spans, RATES, LANES), (vmem(insts * RATES, LANES),))(
        stator,
        jnp.concatenate([
            lax.rem(owner, plan.panels).astype(jnp.float32).reshape(insts, cells), first_panel_share.reshape(insts, cells),
        ], axis=1),
    )
    got = lax.all_to_all(sent, AXES, 0, 0, tiled=True)
    m, side, c0, c1 = call(
        bind(prepare, plan), (f32(pad + RATES, plan.ct * slab),) + edges(pad + RATES), (vmem(6, cells, LANES),)
    )(
        rhs.reshape(plan.tf * cells, LANES),
        jnp.concatenate([
            wall_mask.astype(jnp.float32).reshape(cells, LANES), diag_coef.reshape(cells, LANES),
            time_coef.reshape(cells, LANES), face_coef.reshape(3 * cells, LANES),
        ]),
    )
    low_first, high_first = swap(m, next_chip), swap(m, next_core)
    side_first = beside(plan, side, alone)
    c_low, c_high = beside(plan, c0, next_chip), beside(plan, c1, next_core)
    matrices, down = call(
        bind(stack_matrices, plan),
        [jax.ShapeDtypeStruct((count * pad, 3 * pad), jnp.bfloat16) for count in (7, 1)],
    )(jac_up, jac_down, plan.spectral(), plan.field_rows(), plan.field_lanes(), plan.block_diagonal())
    tiles = len(plan.tiles)
    seams, weight, force, g = call(
        bind(begin, plan), (f32(3, 1 + ends, pad, LANES), f32(pad, LANES), whole, whole),
        (vmem(pad, tiles * LANES), vmem(tiles * pad, LANES), vmem(16, tiles * LANES)) + products,
        flops=2_000_000_000,
    )(matrices, m, got)
    x, near, side, c0, c1 = call(
        bind(first_half, plan), (whole, half) + edges(pad),
        products + (vmem(pad, 2 * slab),) + (vmem(pad, slab),) * 4 + (vmem(LANES, LANES),),
        flops=4_000_000_000,
    )(matrices, m, force, g, low_first, high_first, side_first, c_low, c_high, seams)

    low, high = swap(near, next_chip), swap(x, next_core)
    side = beside(plan, side, alone)
    c_low, c_high = beside(plan, c0, next_chip), beside(plan, c1, next_core)
    (g,) = call(bind(inner, plan), (whole,), products, flops=2_000_000_000)(matrices, m, force, x)
    far = call(bind(hold_far, plan), half)(x, side, c_high)
    far_low = swap(far, next_chip)
    tiles = f32(plan.groups, RATES, LANES)
    *back, n0, h0, x1, rates = call(
        bind(middle, plan), (tiles,) * GROUP + (half, half, half, f32(RATES, slab)),
        products + (
            vmem(pad, 2 * slab), vmem(pad, slab), vmem(pad, slab), vmem(LANES, LANES), vmem(sectors, RATES, LANES),
        ),
        flops=4_000_000_000,
    )(
        matrices, m, force, x, g, low, high, side, c_low, c_high, low_first, high_first, side_first, seams, weight
    )
    for j in range(1, GROUP):
        back[j] = swap(back[j], [s ^ j for s in range(sectors)])
    back = list(call(bind(turn_panels, plan), (f32(GROUP, RATES, LANES),) * plan.groups)(*back))
    for i in range(1, plan.groups):
        back[i] = swap(back[i], [(s // GROUP ^ i) * GROUP + s % GROUP for s in range(sectors)])
    sens = call(
        bind(collect_panels, plan), f32(fields, plan.width, insts),
        (vmem(sectors, RATES, LANES), vmem(insts * RATES, LANES)),
    )(*back)
    out = call(bind(outer, plan), f32(plan.tf * cells, LANES))(down, rates, n0, h0, x1, far_low)
    sens = jnp.transpose(sens.reshape(fields, plan.panels, plan.rows, insts), (3, 0, 1, 2))
    return out.reshape(rhs.shape), sens


def solution(mesh):
    in_specs = (
        P(None, None, "sector", "span", None),
        P("sector", "span", None),
        P(None, "sector", "span", None),
        P("sector", "span", None),
        P(),
        P(),
        P("sector", "span", None),
        P(None, None, "sector", "span"),
        P(None, "sector", "span"),
        P(None, "sector", "span"),
    )
    out_specs = (P(None, None, "sector", "span", None), P(None, None, "sector", "span"))
    return jax.shard_map(
        functools.partial(on_device, mesh.shape["sector"], mesh.shape["span"]),
        mesh=mesh, in_specs=in_specs, out_specs=out_specs, check_vma=False,
    )
```

```python
import functools

import jax
import jax.numpy as jnp
import ml_dtypes
import numpy as np
from jax import lax
from jax.experimental import pallas as pl
from jax.experimental.pallas import tpu as pltpu
from jax.sharding import PartitionSpec as P

SWEEPS = 4
DEPTH = 2
LANES = 128
CHUNK = 256
WINDOW = 8
HIGHEST = lax.Precision.HIGHEST
DOWN_AZ, SPECTRAL, UP_SP, DOWN_SP, UP_AX, DOWN_AX, UP_AZ = range(7)
C_TIME, C_AZ, C_SP, C_UP, C_DOWN, C_MASK = range(6)
RATES = 8
AXES = ("sector", "span")


class Plan:
    def __init__(self, rhs, stator_adj, sectors, spans):
        self.insts, self.fields, self.ct, self.rows, self.nax = rhs.shape
        self.panels = stator_adj.shape[2]
        self.sectors, self.spans = sectors, spans
        self.tf = self.insts * self.fields
        self.pad = -(-self.tf // 16) * 16
        self.cells = self.ct * self.rows
        self.slab = self.rows * LANES
        self.width = self.panels * self.rows
        self.shift = [
            ((t * sectors) // (self.insts - 1) - t // (self.insts - 1)) % sectors for t in range(self.insts)
        ]
        assert self.ct == 2 and self.nax == LANES and SWEEPS % DEPTH == 0 and spans > 1
        assert len(set(self.shift)) == self.insts and self.cells * WINDOW == LANES and self.rows >= SWEEPS
        assert self.slab % CHUNK == 0 and 3 * self.pad <= 256 and 2 * self.ct * self.width == LANES
        assert sectors % 2 == 0
        self.ends = 1 if spans == 2 else 2
        self.blocks = [-1, 0, 1]
        self.halves = [0, 1] if spans == 2 else [-1, 0, 1]
        self.tiles = [(k, x) for k in self.blocks for x in self.halves]
        self.slots = [
            [t for t in range(self.insts) if any((k + self.shift[t]) % sectors == o for k in self.blocks)]
            for o in range(sectors)
        ]
        last = LANES - self.width
        self.weight_at = [(t, last) for t in range(self.fields)] + [
            (self.fields, i * self.width) for i in range(self.insts - self.fields)
        ]
        assert max(map(len, self.slots)) * self.width <= last and 2 * self.cells == self.width
        assert self.fields == RATES - 1 and (self.insts - self.fields) * self.width <= LANES

    def spectral(self):
        t = np.arange(self.insts)
        off = t[:, None] - t[None, :]
        sines = np.where(off == 0, 1.0, np.sin(np.pi * off / self.insts))
        table = np.where(off == 0, 0.0, 0.5 * (1.0 - 2.0 * (off % 2)) / sines).astype(np.float32)
        full = np.zeros((self.pad, self.pad), np.float32)
        full[: self.tf, : self.tf] = np.kron(table.T, np.eye(self.fields, dtype=np.float32))
        hi = full.astype(ml_dtypes.bfloat16)
        lo = (full - hi.astype(np.float32)).astype(ml_dtypes.bfloat16)
        return np.concatenate([hi, lo, hi], axis=1)

    def field_rows(self):
        out = np.zeros((self.pad, self.fields), np.float32)
        out[np.arange(self.tf), np.arange(self.tf) % self.fields] = 1.0
        return out

    def field_lanes(self):
        return np.tile(self.field_rows().T, (1, 3))

    def block_diagonal(self):
        block = np.full(self.pad, -1)
        block[: self.tf] = np.arange(self.tf) // self.fields
        same = (block[:, None] == block[None, :]) & (block[:, None] >= 0)
        return np.tile(same.astype(np.float32), (1, 3))


    def inst_rows(self):
        row, inst = table_index(self.pad, 16)
        return ((row >= inst * self.fields) & (row < (inst + 1) * self.fields)).astype(jnp.float32)

    def cell_of(self, lane):
        return lax.div(lane, self.width) * self.rows + lax.rem(lane, self.rows)

    def window_lanes(self):
        lane, to = table_index(LANES, LANES)
        return (lane < self.ct * self.width) & (to == self.cell_of(lane) * WINDOW)

    def window_spread(self):
        to, lane = table_index(LANES, LANES)
        return (lane < self.ct * self.width) & (to == self.cell_of(lane) * WINDOW)

    def weight_lanes(self):
        cell, lane = table_index(LANES, LANES)
        half = self.ct * self.width
        wanted = jnp.where(lane < half, self.cell_of(lane), self.cells + self.cell_of(lane - half))
        return cell == wanted

    def panel_lanes(self):
        lane = lane_index(1)
        panel = lax.rem(lax.div(lane, self.rows), self.panels)
        return jnp.where(lane < self.ct * self.width, panel, -9).astype(jnp.float32)


def table_index(rows, columns):
    return [lax.broadcasted_iota(jnp.int32, (rows, columns), axis) for axis in (0, 1)]


def call(kernel, out, scratch=(), flops=2_000_000, nbytes=1_000_000):
    return pl.pallas_call(
        kernel,
        out_shape=out,
        scratch_shapes=list(scratch),
        compiler_params=pltpu.CompilerParams(vmem_limit_bytes=20 * 1024 * 1024),
        cost_estimate=pl.CostEstimate(flops=flops, bytes_accessed=nbytes, transcendentals=0),
    )


def f32(*shape):
    return jax.ShapeDtypeStruct(shape, jnp.float32)


def vmem(*shape):
    return pltpu.VMEM(shape, jnp.float32)


def halves_of(x):
    hi = x.astype(jnp.bfloat16)
    return hi, (x - hi.astype(jnp.float32)).astype(jnp.bfloat16)


def dot3(w, x):
    hi, lo = halves_of(x)
    return jnp.dot(w, jnp.concatenate([hi, hi, lo], axis=0), preferred_element_type=jnp.float32)


def pick(x, table):
    table = table.astype(jnp.float32).astype(jnp.bfloat16)
    table = jnp.concatenate([table, table], axis=0)
    return jnp.dot(jnp.concatenate(halves_of(x), axis=1), table, preferred_element_type=jnp.float32)


def dot_full(a, b):
    return jnp.dot(a, b, precision=HIGHEST, preferred_element_type=jnp.float32)


def lane_index(rows):
    return lax.broadcasted_iota(jnp.int32, (rows, LANES), 1)


def rolled(x, by):
    by %= LANES
    return pltpu.roll(x, by, axis=1) if by else x


def at(r, count=1, start=0):
    return slice(start + r * LANES, start + (r + count) * LANES)


def parity():
    return lax.rem(lax.axis_index("sector"), 2)


def has_sides(plan):
    span = lax.axis_index("span")
    return jnp.where(span < plan.spans - 1, 1.0, 0.0), jnp.where(span > 0, 1.0, 0.0)


class Layer:
    def __init__(self, plan, ref, start=0, rates=None, seam=None, layer=0):
        self.plan, self.ref, self.start, self.seam, self.layer = plan, ref, start, seam, layer
        self.rates = rates or (ref, start)

    def rate(self, which, r, count=1):
        ref, start = self.rates
        row = self.plan.pad + which
        return ref[row : row + 1, at(r, count, start)]

    def row(self, r):
        value = self.ref[: self.plan.pad, at(r, 1, self.start)]
        if self.seam is None:
            return value
        return value + placed(self.seam, self.layer * self.plan.rows + r) * self.rate(C_MASK, r)

    def chunk(self, c):
        count = CHUNK // LANES
        if self.seam is None:
            return self.ref[: self.plan.pad, at(c * count, count, self.start)]
        return jnp.concatenate([self.row(c * count + part) for part in range(count)], axis=1)


def placed(tile, cell):
    return jnp.where(lane_index(tile.shape[0]) == 0, rolled(tile, -cell * WINDOW), 0.0)


class Products:
    def __init__(self, plan, w_ref, p_ref, first):
        self.plan, self.w, self.p, self.first = plan, w_ref, p_ref, first

    def fill(self, layer):
        for c in range(self.plan.slab // CHUNK):
            self.p[:, c * CHUNK : (c + 1) * CHUNK] = dot3(matrix(self.plan, self.w, self.first, 6), layer.chunk(c))
        self.layer = layer
        return self

    def get(self, block, r):
        row = (block - self.first) * self.plan.pad
        return self.p[row : row + self.plan.pad, at(r)]

    def own_terms(self, r):
        rate = self.layer.rate
        total = rate(C_TIME, r) * self.get(SPECTRAL, r)
        beside = []
        if r + 1 < self.plan.rows:
            beside.append(self.get(UP_SP, r + 1))
        if r > 0:
            beside.append(self.get(DOWN_SP, r - 1))
        total = total + rate(C_SP, r) * sum(beside[1:], beside[0])
        total = total + rate(C_UP, r) * rolled(self.get(UP_AX, r), -1)
        return total + rate(C_DOWN, r) * rolled(self.get(DOWN_AX, r), 1)


def matrix(plan, w_ref, block, count=1):
    return w_ref[block * plan.pad : (block + count) * plan.pad, :]


def two_layers(plan, ref, rates=None, seam=None):
    return [
        Layer(plan, ref, a * plan.slab, (rates, a * plan.slab) if rates is not None else None, seam, a)
        for a in range(plan.ct)
    ]


def inner_rows(plan, w_ref, p_refs, layers, force, g_ref):
    first = Products(plan, w_ref, p_refs[0], DOWN_AZ).fill(layers[0])
    second = Products(plan, w_ref, p_refs[1], SPECTRAL).fill(layers[1])
    for r in range(plan.rows):
        other = second.get(UP_AZ, r), first.get(DOWN_AZ, r)
        for a, products in enumerate((first, second)):
            total = products.own_terms(r) + layers[a].rate(C_AZ, r) * other[a]
            if isinstance(g_ref, tuple):
                g_ref[a][:, at(r)] = force[a].row(r) - total
            else:
                g_ref[:, at(r, 1, a * plan.slab)] = force[a].row(r) - total


def azimuthal(plan, w_ref, block, chunk_of, take):
    for c in range(plan.slab // CHUNK):
        terms = dot3(matrix(plan, w_ref, block), chunk_of(c))
        for part in range(CHUNK // LANES):
            take(c * (CHUNK // LANES) + part, terms[:, at(part)])


def middle_rows(plan, w_ref, p_refs, own, own_force, g_ref, near, near_force, side, corner, y_ref, h_refs, n_refs):
    pad, rows, ct = plan.pad, plan.rows, plan.ct
    last = (rows - 1, 0)
    edge_terms, edge_new, corner_terms = [], [], []
    is_first = lax.axis_index("span") == 0

    def choose(n, above, below):
        return jnp.where(is_first, above, below) if plan.ends == 1 else (above, below)[n]

    for n in range(plan.ends):
        outward = choose(n, matrix(plan, w_ref, UP_SP), matrix(plan, w_ref, DOWN_SP))
        inward = choose(n, matrix(plan, w_ref, DOWN_SP), matrix(plan, w_ref, UP_SP))
        first, second, edge_force, edge_rate = side(n)
        corners = corner(n)
        every = dot3(w_ref[...], first)
        beyond = dot3(outward, second)
        within = [choose(n, x.row(last[0]), x.row(last[1])) for x in own]
        within = dot3(inward, jnp.concatenate(within, axis=1))
        from_low = dot3(matrix(plan, w_ref, DOWN_AZ), corners[0])
        from_high = dot3(matrix(plan, w_ref, UP_AZ), corners[1])
        new = []
        for a in range(ct):

            def part(block, b=a):
                return every[block * pad : (block + 1) * pad, at(b)]

            around = part(UP_AZ, 1) + from_low if a == 0 else from_high + part(DOWN_AZ, 0)
            total = edge_rate(C_TIME, a) * part(SPECTRAL) + edge_rate(C_AZ, a) * around
            total = total + edge_rate(C_SP, a) * (beyond[:, at(a)] + within[:, at(a)])
            total = total + edge_rate(C_UP, a) * rolled(part(UP_AX), -1)
            total = total + edge_rate(C_DOWN, a) * rolled(part(DOWN_AX), 1)
            new.append(edge_force[:, at(a)] - total)
        of_edge = choose(n, *(every[block * pad : (block + 1) * pad] for block in (UP_SP, DOWN_SP)))
        of_new = dot3(outward, jnp.concatenate(new, axis=1))
        of_corners = dot3(outward, jnp.concatenate(corners, axis=1))
        for keep in has_sides(plan) if plan.ends == 1 else (1.0,):
            edge_terms.append(of_edge * keep)
            edge_new.append(of_new * keep)
            corner_terms.append([of_corners[:, at(a)] * keep for a in range(ct)])

    products = (
        Products(plan, w_ref, p_refs[0], DOWN_AZ).fill(near[0]), Products(plan, w_ref, p_refs[1], SPECTRAL).fill(near[1]),
    )
    for a, (to_own, to_near) in enumerate(((DOWN_AZ, UP_AZ), (UP_AZ, DOWN_AZ))):

        def take(r, terms):
            total = products[a].own_terms(r) + near[a].rate(C_AZ, r) * terms
            mine = own[a].rate(C_AZ, r) * products[a].get(to_own, r)
            for n in range(2):
                if r == last[n]:
                    total = total + near[a].rate(C_SP, r) * corner_terms[n][a]
                    mine = mine + own[a].rate(C_SP, r) * edge_terms[n][:, at(a)]
            n_refs[a][:, at(r)] = near_force[a].row(r) - total
            lanes = at(r, 1, a * plan.slab)
            y_ref[:, lanes] = g_ref[:, lanes] - mine

        azimuthal(plan, w_ref, to_near, own[a].chunk, take)

    after = [Layer(plan, y_ref, a * plan.slab, own[a].rates) for a in range(ct)]
    inner_rows(plan, w_ref, p_refs, after, own_force, h_refs)
    for a in range(ct):
        for n in range(2):
            h_refs[a][:, at(last[n])] -= own[a].rate(C_SP, last[n]) * edge_new[n][:, at(a)]


def outer_rows(plan, w_ref, own, near, far_chunks, n_refs, h_refs, put, layers=(0, 1)):
    count = CHUNK // LANES
    for a in layers:
        block = (DOWN_AZ, UP_AZ)[a]

        def near_chunk(c):
            terms = dot3(matrix(plan, w_ref, block), far_chunks[a](c))
            return n_refs[a][:, at(c * count, count)] - near[a].rate(C_AZ, c * count, count) * terms

        def take(r, terms):
            put(a, r, h_refs[a][:, at(r)] - own[a].rate(C_AZ, r) * terms)

        azimuthal(plan, w_ref, block, near_chunk, take)


def sides_of(plan, side_ref, force_ref, seams_ref):
    pad, ct = plan.pad, plan.ct
    keeps = (1.0,) if plan.ends == 1 else has_sides(plan)
    is_first = lax.axis_index("span") == 0

    def inlet(n, e, a):
        above, below = a * plan.rows + e, a * plan.rows + plan.rows - 1 - e
        tile = seams_ref[1, 1 + n]
        if plan.ends == 1:
            return jnp.where(is_first, placed(tile, above), placed(tile, below))
        return placed(tile, (above, below)[n])

    def read(n, ref, e, seam):
        value = ref[n, :pad, at(e * ct, ct)]
        if seam:
            scale = ref[n, pad + C_MASK : pad + C_MASK + 1, at(e * ct, ct)]
            value = value + jnp.concatenate([inlet(n, e, a) for a in range(ct)], axis=1) * scale
        return value * keeps[n]

    def side(n):
        same = side_ref is force_ref

        def rate(which, a):
            return force_ref[n, pad + which : pad + which + 1, at(a)] * keeps[n]

        force = read(n, force_ref, 0, True)
        first = force if same else read(n, side_ref, 0, False)
        return first, read(n, side_ref, 1, same), force, rate

    return side


def corners_of(plan, c_refs, seams_ref):
    keeps = (1.0,) if plan.ends == 1 else has_sides(plan)
    is_first = lax.axis_index("span") == 0

    def corner(n):
        out = []
        for a, c_ref in enumerate(c_refs):
            value = c_ref[n, : plan.pad]
            if seams_ref is not None:
                tile = seams_ref[2 * a, 1 + n]
                above, below = (placed(tile, a * plan.rows + r) for r in (0, plan.rows - 1))
                inlet = jnp.where(is_first, above, below) if plan.ends == 1 else (above, below)[n]
                value = value + inlet * c_ref[n, plan.pad + C_MASK : plan.pad + C_MASK + 1]
            out.append(value * keeps[n])
        return out

    return corner


def prepare(plan, rhs_ref, coef_ref, m_ref, side_ref, c0_ref, c1_ref, rates_ref):
    pad, cells = plan.pad, plan.cells
    mask, diag, time, *face = [coef_ref[cells * i : cells * (i + 1), :] for i in range(6)]
    scale = mask / diag
    lane = lane_index(cells)
    axial = scale * face[2]
    rates = (
        scale * time, scale * face[0], scale * face[1],
        jnp.where(lane < LANES - 1, axial, 0.0), jnp.where(lane > 0, axial, 0.0), scale,
    )
    for i, rate in enumerate(rates):
        rates_ref[i] = rate
    tail = jnp.zeros((pad - plan.tf, LANES), jnp.float32)
    rest = jnp.zeros((RATES - 6, LANES), jnp.float32)
    mirror = parity()
    for cell in range(cells):
        a, r = divmod(cell, plan.rows)
        there = jnp.where(mirror == 0, a, plan.ct - 1 - a) * plan.rows + r
        table = [rates_ref[i, pl.ds(there, 1), :] for i in range(6)]
        field = jnp.concatenate([rhs_ref[pl.ds(there, plan.tf, stride=cells), :], tail], axis=0)
        m_ref[:pad, at(cell)] = field * table[C_MASK]
        m_ref[pad:, at(cell)] = jnp.concatenate(table + [rest], axis=0)
    write_edges(plan, m_ref, side_ref, (c0_ref, c1_ref))


def write_edges(plan, x_ref, side_ref, c_refs):
    first = lax.axis_index("span") == 0
    for a in range(plan.ct):
        for e in range(DEPTH):
            low, high = x_ref[:, at(a * plan.rows + e)], x_ref[:, at((a + 1) * plan.rows - 1 - e)]
            ends = [jnp.where(first, high, low)] if plan.ends == 1 else [low, high]
            for n, end in enumerate(ends):
                side_ref[n, :, at(e * plan.ct + a)] = end
                if e == 0:
                    c_refs[a][n] = end


def stack_matrices(plan, up_ref, down_ref, spectral_ref, rows_ref, lanes_ref, diagonal_ref, out_ref, down_out):
    pad = plan.pad
    lane = lax.broadcasted_iota(jnp.int32, (pad, 3 * pad), 1)
    second = (lane >= pad) & (lane < 2 * pad)
    out_ref[SPECTRAL * pad : (SPECTRAL + 1) * pad, :] = spectral_ref[...]
    even = parity() == 0
    for block, small in (
        (DOWN_AZ, jnp.where(even, down_ref[0], up_ref[0])), (UP_AZ, jnp.where(even, up_ref[0], down_ref[0])),
        (UP_SP, up_ref[1]), (DOWN_SP, down_ref[1]), (UP_AX, up_ref[2]), (DOWN_AX, down_ref[2]),
    ):
        full = dot_full(dot_full(rows_ref[...], small), lanes_ref[...]) * diagonal_ref[...]
        hi = full.astype(jnp.bfloat16).astype(jnp.float32)
        out_ref[block * pad : (block + 1) * pad, :] = jnp.where(second, full - hi, hi).astype(jnp.bfloat16)
    down_out[...] = matrix(plan, out_ref, DOWN_AZ)


def send_panels(plan, stator_ref, both_ref, out_ref, panels_ref):
    me = lax.axis_index("sector")
    for f in range(plan.fields):
        panels_ref[pl.ds(f, plan.insts, stride=RATES), : plan.width] = jnp.transpose(stator_ref[f])
    out_ref[...] = jnp.zeros_like(out_ref)
    for t, (row, start) in enumerate(plan.weight_at):
        both = jnp.broadcast_to(both_ref[t : t + 1, :][None], (out_ref.shape[0], 1, plan.width))
        out_ref[:, row : row + 1, start : start + plan.width] = both
    for o, slots in enumerate(plan.slots):
        to = lax.rem(me + (plan.sectors - o), plan.sectors) * plan.spans
        for slot, t in enumerate(slots):
            lanes = slice(slot * plan.width, (slot + 1) * plan.width)
            panels = panels_ref[t * RATES : t * RATES + plan.fields, : plan.width]
            for x in range(plan.spans):
                out_ref[to + x, : plan.fields, lanes] = panels


def begin(
    plan, w_ref, m_ref, got_ref,
    seams_ref, weight_ref, x_ref, g_ref, panels_ref, terms_ref, rows_ref, p0_ref, p1_ref,
):
    pad, insts, fields = plan.pad, plan.insts, plan.fields
    me, span = lax.axis_index("sector"), lax.axis_index("span")
    even, is_first = parity() == 0, span == 0
    tiles = plan.tiles
    panels_ref[...] = jnp.zeros_like(panels_ref)
    rows_ref[...] = jnp.zeros_like(rows_ref)
    for n, (k, x) in enumerate(tiles):
        at_span = x if plan.spans == 2 else jnp.clip(span + x, 0, plan.spans - 1)
        for t in range(insts):
            o = (k + plan.shift[t]) % plan.sectors
            source = lax.rem(me + o, plan.sectors) * plan.spans + at_span
            tile = rolled(got_ref[source], -plan.slots[o].index(t) * plan.width)
            panels_ref[t * fields : (t + 1) * fields, n * LANES : n * LANES + plan.width] = tile[:fields, : plan.width]
        tile = got_ref[lax.rem(me + k + plan.sectors, plan.sectors) * plan.spans + at_span]
        lanes = slice(n * LANES, n * LANES + plan.width)
        rows_ref[:fields, lanes] = rolled(tile, -plan.weight_at[0][1])[:fields, : plan.width]
        for t in range(fields, insts):
            row, start = plan.weight_at[t]
            rows_ref[t : t + 1, lanes] = rolled(tile, -start)[row : row + 1, : plan.width]
    spread = dot_full(plan.inst_rows(), rows_ref[...])
    spread = pick(jnp.concatenate([spread[:, at(n)] for n in range(len(tiles))], axis=0), plan.weight_lanes())
    first, share, panel = spread, rolled(spread, plan.ct * plan.width), plan.panel_lanes()
    lower = (jnp.abs(first - panel) < 0.5).astype(jnp.float32)
    upper = (jnp.abs(first + 1.0 - panel) < 0.5).astype(jnp.float32)
    weights = share * lower + (1.0 - share) * upper
    for n in range(len(tiles)):
        panels = panels_ref[:, at(n)]
        terms_ref[n * pad : (n + 1) * pad, :] = panels + rolled(panels, plan.width)
    seams = pick(terms_ref[...] * weights, plan.window_lanes())

    def tile(values, k, x):
        n = tiles.index((k, x))
        return values[n * pad : (n + 1) * pad]

    def around(values, k):
        if plan.spans == 2:
            pair = tile(values, k, 0), tile(values, k, 1)
            return [jnp.where(is_first, pair[0], pair[1]), jnp.where(is_first, pair[1], pair[0])]
        return [tile(values, k, x) for x in (0, 1, -1)]

    def mirrored(value):
        return rolled(value, LANES // 2)

    here = around(seams, 0)
    behind, ahead = around(seams, -1), around(seams, 1)
    for i in range(1 + plan.ends):
        seams_ref[0, i] = jnp.where(even, mirrored(behind[i]), ahead[i])
        seams_ref[1, i] = jnp.where(even, here[i], mirrored(here[i]))
        seams_ref[2, i] = jnp.where(even, mirrored(ahead[i]), behind[i])
    weight_ref[...] = around(weights, 0)[0]

    for layer in two_layers(plan, m_ref, seam=seams_ref[1, 0]):
        for r in range(plan.rows):
            x_ref[:, at(r, 1, layer.start)] = layer.row(r)
    layers = two_layers(plan, x_ref, m_ref)
    inner_rows(plan, w_ref, (p0_ref, p1_ref), layers, layers, g_ref)


def first_half(
    plan, w_ref, m_ref, f_ref, g_ref, low_ref, high_ref, side_ref, c_low, c_high, seams_ref,
    x_ref, near_ref, side_out, c0_ref, c1_ref, p0_ref, p1_ref, y_ref, h0_ref, h1_ref, n0_ref, n1_ref, inlet_ref,
):
    own = two_layers(plan, f_ref, m_ref)
    low = two_layers(plan, low_ref, seam=seams_ref[0, 0])
    high = two_layers(plan, high_ref, seam=seams_ref[2, 0])
    near = low[0], high[1]
    n_refs = n0_ref, n1_ref
    middle_rows(
        plan, w_ref, (p0_ref, p1_ref), own, own, g_ref, near, near, sides_of(plan, side_ref, side_ref, seams_ref),
        corners_of(plan, (c_low, c_high), seams_ref), y_ref, (h0_ref, h1_ref), n_refs,
    )
    lane = lane_index(plan.pad)
    inlet_ref[...] = jnp.zeros_like(inlet_ref)

    def put(a, r, value):
        x_ref[:, at(r, 1, a * plan.slab)] = value
        if a == 0:
            near_ref[:, at(r)] = value
        else:
            inlet_ref[: plan.pad, :] = jnp.where(lane == r, rolled(value, r), inlet_ref[: plan.pad, :])

    outer_rows(plan, w_ref, own, near, (low[1].chunk, high[0].chunk), n_refs, (h0_ref, h1_ref), put)
    turned = jnp.transpose(inlet_ref[...])
    for r in range(plan.rows):
        near_ref[plan.tf : plan.tf + 1, at(r)] = turned[r : r + 1, :]
    write_edges(plan, x_ref, side_out, (c0_ref, c1_ref))


def hold_far(plan, x_ref, side_ref, c_high, far_ref):
    come = side_ref[0, 0:1, 0:1] + c_high[0, 0:1, 0:1]
    far_ref[...] = x_ref[:, plan.slab :] + 0.0 * come


def inner(plan, w_ref, m_ref, f_ref, x_ref, g_ref, p0_ref, p1_ref):
    inner_rows(plan, w_ref, (p0_ref, p1_ref), two_layers(plan, x_ref, m_ref), two_layers(plan, f_ref, m_ref), g_ref)


def middle(
    plan, w_ref, m_ref, f_ref, x_ref, g_ref, low_ref, high_ref, side_ref, c_low, c_high,
    low_first, high_first, side_first, seams_ref, weight_ref,
    send_ref, n0_ref, h0_ref, x1_ref, rates_ref, p0_ref, p1_ref, y_ref, h1_ref, n1_ref, turn_ref,
):
    pad = plan.pad
    own, force = two_layers(plan, x_ref, m_ref), two_layers(plan, f_ref, m_ref)
    low_force = Layer(plan, low_first, 0, None, seams_ref[0, 0], 0)
    high_force = Layer(plan, high_first, plan.slab, None, seams_ref[2, 0], 1)
    near = Layer(plan, low_ref, 0, low_force.rates), Layer(plan, high_ref, plan.slab, high_force.rates)
    n_refs = n0_ref, n1_ref
    middle_rows(
        plan, w_ref, (p0_ref, p1_ref), own, force, g_ref, near, (low_force, high_force),
        sides_of(plan, side_ref, side_first, seams_ref), corners_of(plan, (c_low, c_high), None), y_ref,
        (h0_ref, h1_ref), n_refs,
    )

    def put(a, r, value):
        x1_ref[:, at(r)] = value

    outer_rows(plan, w_ref, own, near, (None, Layer(plan, high_ref).chunk), n_refs, (h0_ref, h1_ref), put, (1,))
    for r in range(plan.rows):
        last = [near[0].rate(C_AZ, r), own[0].rate(C_AZ, r), jnp.zeros((RATES - 2, LANES), jnp.float32)]
        rates_ref[:, at(r)] = jnp.concatenate(last, axis=0)

    turn_ref[...] = jnp.zeros_like(turn_ref)
    for r in range(plan.rows):
        turn_ref[r : r + 1, :] = low_ref[plan.tf : plan.tf + 1, at(r)]
    far = jnp.transpose(turn_ref[...])[:pad]

    def packed(read, count, first=0, step=1):
        lane = lane_index(count)
        out = jnp.zeros((count, LANES), jnp.float32)
        for r in range(plan.rows):
            to = first + r * step
            out = jnp.where(lane == to, rolled(read(r), to), out)
        return out

    rates = packed(lambda r: rates_ref[:, at(r)], RATES)
    inlet = packed(lambda r: n0_ref[:, at(r)], pad) - rates[0:1] * dot3(matrix(plan, w_ref, DOWN_AZ), far)
    inlet = packed(lambda r: h0_ref[:, at(r)], pad) - rates[1:2] * dot3(matrix(plan, w_ref, DOWN_AZ), inlet)
    lane = lane_index(pad)
    spread = packed(lambda r: x1_ref[:, at(r)], pad, plan.rows * WINDOW, WINDOW)
    for r in range(plan.rows):
        spread = jnp.where(lane == r * WINDOW, rolled(inlet, r * (WINDOW - 1)), spread)
    inlet = jnp.where(parity() == 0, spread, rolled(spread, LANES // 2))
    back = pick(inlet, plan.window_spread()) * weight_ref[...]
    back = back + rolled(back, -plan.width)
    me = lax.axis_index("sector")
    send_ref[...] = jnp.zeros_like(send_ref)
    for t in range(plan.insts):
        to = lax.rem(me + plan.shift[t], plan.sectors)
        send_ref[to, : plan.fields, : plan.width] = back[t * plan.fields : (t + 1) * plan.fields, : plan.width]


def outer(plan, w_ref, rates_ref, n0_ref, h0_ref, x1_ref, far_ref, out_ref):
    mirror = parity()

    def put(a, r, value):
        there = jnp.where(mirror == 0, a, plan.ct - 1 - a) * plan.rows + r
        out_ref[pl.ds(there, plan.tf, stride=plan.cells), :] = value[: plan.tf]

    for r in range(plan.rows):
        put(1, r, x1_ref[:, at(r)])

    def near_chunk(c):
        lanes = slice(c * CHUNK, (c + 1) * CHUNK)
        return n0_ref[:, lanes] - rates_ref[0:1, lanes] * dot3(w_ref[...], far_ref[:, lanes])

    azimuthal(plan, w_ref, 0, near_chunk, lambda r, terms: put(0, r, h0_ref[:, at(r)] - rates_ref[1:2, at(r)] * terms))


def collect_panels(plan, got_ref, out_ref, panels_ref):
    me = lax.axis_index("sector")
    for t in range(plan.insts):
        source = lax.rem(me + (plan.sectors - plan.shift[t]), plan.sectors)
        panels_ref[t * RATES : (t + 1) * RATES, :] = got_ref[source]
    for f in range(plan.fields):
        tile = panels_ref[pl.ds(f, plan.insts, stride=RATES), : plan.width]
        out_ref[f] = jnp.transpose(tile)


def sibling(plan):
    return [s ^ 1 for s in range(plan.sectors)]


def outside(plan):
    return [(s - 1 if s % 2 == 0 else s + 1) % plan.sectors for s in range(plan.sectors)]


def swap(array, partner):
    return lax.ppermute(array, "sector", list(enumerate(partner)))


def beside(plan, array, partner):
    def pairs(step):
        out = []
        for s in range(plan.sectors):
            for x in range(plan.spans):
                to = 1 - x if plan.ends == 1 else x + step
                if 0 <= to < plan.spans:
                    out.append((s * plan.spans + x, partner[s] * plan.spans + to))
        return out

    if plan.ends == 1:
        return lax.ppermute(array, AXES, pairs(0))
    return jnp.concatenate([lax.ppermute(array[:1], AXES, pairs(-1)), lax.ppermute(array[1:], AXES, pairs(1))])


def on_device(
    sectors, spans,
    rhs, diag_coef, face_coef, time_coef, jac_up, jac_down, wall_mask, stator_adj, owner, first_panel_share,
):
    plan = Plan(rhs, stator_adj, sectors, spans)
    pad, cells, slab, insts, fields, ends = plan.pad, plan.cells, plan.slab, plan.insts, plan.fields, plan.ends
    bind = functools.partial
    whole, half = f32(pad, plan.ct * slab), f32(pad, slab)
    products = (vmem(6 * pad, slab),) * 2
    alone, next_chip, next_core = list(range(sectors)), outside(plan), sibling(plan)

    def edges(rows):
        return f32(ends, rows, DEPTH * plan.ct * LANES), f32(ends, rows, LANES), f32(ends, rows, LANES)

    stator = jnp.transpose(stator_adj, (1, 2, 3, 0)).reshape(fields, plan.width, insts)
    sent = call(bind(send_panels, plan), f32(sectors * spans, RATES, LANES), (vmem(insts * RATES, LANES),))(
        stator,
        jnp.concatenate([
            lax.rem(owner, plan.panels).astype(jnp.float32).reshape(insts, cells), first_panel_share.reshape(insts, cells),
        ], axis=1),
    )
    got = lax.all_to_all(sent, AXES, 0, 0, tiled=True)
    m, side, c0, c1 = call(
        bind(prepare, plan), (f32(pad + RATES, plan.ct * slab),) + edges(pad + RATES), (vmem(6, cells, LANES),)
    )(
        rhs.reshape(plan.tf * cells, LANES),
        jnp.concatenate([
            wall_mask.astype(jnp.float32).reshape(cells, LANES), diag_coef.reshape(cells, LANES),
            time_coef.reshape(cells, LANES), face_coef.reshape(3 * cells, LANES),
        ]),
    )
    low_first, high_first = swap(m, next_chip), swap(m, next_core)
    side_first = beside(plan, side, alone)
    c_low, c_high = beside(plan, c0, next_chip), beside(plan, c1, next_core)
    matrices, down = call(
        bind(stack_matrices, plan),
        [jax.ShapeDtypeStruct((count * pad, 3 * pad), jnp.bfloat16) for count in (7, 1)],
    )(jac_up, jac_down, plan.spectral(), plan.field_rows(), plan.field_lanes(), plan.block_diagonal())
    tiles = len(plan.tiles)
    seams, weight, force, g = call(
        bind(begin, plan), (f32(3, 1 + ends, pad, LANES), f32(pad, LANES), whole, whole),
        (vmem(pad, tiles * LANES), vmem(tiles * pad, LANES), vmem(16, tiles * LANES)) + products,
        flops=2_000_000_000,
    )(matrices, m, got)
    x, near, side, c0, c1 = call(
        bind(first_half, plan), (whole, half) + edges(pad),
        products + (vmem(pad, 2 * slab),) + (vmem(pad, slab),) * 4 + (vmem(LANES, LANES),),
        flops=4_000_000_000,
    )(matrices, m, force, g, low_first, high_first, side_first, c_low, c_high, seams)

    low, high = swap(near, next_chip), swap(x, next_core)
    side = beside(plan, side, alone)
    c_low, c_high = beside(plan, c0, next_chip), beside(plan, c1, next_core)
    (g,) = call(bind(inner, plan), (whole,), products, flops=2_000_000_000)(matrices, m, force, x)
    far = call(bind(hold_far, plan), half)(x, side, c_high)
    far_low = swap(far, next_chip)
    back, n0, h0, x1, rates = call(
        bind(middle, plan), (f32(sectors, RATES, LANES), half, half, half, f32(RATES, slab)),
        products + (vmem(pad, 2 * slab), vmem(pad, slab), vmem(pad, slab), vmem(LANES, LANES)),
        flops=4_000_000_000,
    )(
        matrices, m, force, x, g, low, high, side, c_low, c_high, low_first, high_first, side_first, seams, weight
    )
    returned = lax.all_to_all(back, "sector", 0, 0, tiled=True)
    sens = call(bind(collect_panels, plan), f32(fields, plan.width, insts), (vmem(insts * RATES, LANES),))(returned)
    out = call(bind(outer, plan), f32(plan.tf * cells, LANES))(down, rates, n0, h0, x1, far_low)
    sens = jnp.transpose(sens.reshape(fields, plan.panels, plan.rows, insts), (3, 0, 1, 2))
    return out.reshape(rhs.shape), sens


def solution(mesh):
    in_specs = (
        P(None, None, "sector", "span", None),
        P("sector", "span", None),
        P(None, "sector", "span", None),
        P("sector", "span", None),
        P(),
        P(),
        P("sector", "span", None),
        P(None, None, "sector", "span"),
        P(None, "sector", "span"),
        P(None, "sector", "span"),
    )
    out_specs = (P(None, None, "sector", "span", None), P(None, None, "sector", "span"))
    return jax.shard_map(
        functools.partial(on_device, mesh.shape["sector"], mesh.shape["span"]),
        mesh=mesh, in_specs=in_specs, out_specs=out_specs, check_vma=False,
    )
```

```python
import functools

import jax
import jax.numpy as jnp
import ml_dtypes
import numpy as np
from jax import lax
from jax.experimental import pallas as pl
from jax.experimental.pallas import tpu as pltpu
from jax.sharding import PartitionSpec as P

SWEEPS = 4
DEPTH = 2
LANES = 128
CHUNK = 256
WINDOW = 8
HIGHEST = lax.Precision.HIGHEST
DOWN_AZ, SPECTRAL, UP_SP, DOWN_SP, UP_AX, DOWN_AX, UP_AZ = range(7)
C_TIME, C_AZ, C_SP, C_UP, C_DOWN, C_MASK, C_OTHER = range(7)
RATES = 8
AXES = ("sector", "span")


class Plan:
    def __init__(self, rhs, stator_adj, sectors, spans):
        self.insts, self.fields, self.ct, self.rows, self.nax = rhs.shape
        self.panels = stator_adj.shape[2]
        self.sectors, self.spans = sectors, spans
        self.tf = self.insts * self.fields
        self.pad = -(-self.tf // 16) * 16
        self.cells = self.ct * self.rows
        self.slab = self.rows * LANES
        self.width = self.panels * self.rows
        self.shift = [
            ((t * sectors) // (self.insts - 1) - t // (self.insts - 1)) % sectors for t in range(self.insts)
        ]
        assert self.ct == 2 and self.nax == LANES and SWEEPS % DEPTH == 0 and spans > 1
        assert len(set(self.shift)) == self.insts and self.cells * WINDOW == LANES and self.rows >= SWEEPS
        assert self.slab % CHUNK == 0 and 3 * self.pad <= 256 and 2 * self.ct * self.width == LANES
        assert sectors % 2 == 0
        self.ends = 1 if spans == 2 else 2
        self.blocks = [-1, 0, 1]
        self.halves = [0, 1] if spans == 2 else [-1, 0, 1]
        self.tiles = [(k, x) for k in self.blocks for x in self.halves]
        self.slots = [
            [t for t in range(self.insts) if any((k + self.shift[t]) % sectors == o for k in self.blocks)]
            for o in range(sectors)
        ]
        last = LANES - self.width
        self.weight_at = [(t, last) for t in range(self.fields)] + [
            (self.fields, i * self.width) for i in range(self.insts - self.fields)
        ]
        assert max(map(len, self.slots)) * self.width <= last and 2 * self.cells == self.width
        assert self.fields == RATES - 1 and (self.insts - self.fields) * self.width <= LANES

    def spectral(self):
        t = np.arange(self.insts)
        off = t[:, None] - t[None, :]
        sines = np.where(off == 0, 1.0, np.sin(np.pi * off / self.insts))
        table = np.where(off == 0, 0.0, 0.5 * (1.0 - 2.0 * (off % 2)) / sines).astype(np.float32)
        full = np.zeros((self.pad, self.pad), np.float32)
        full[: self.tf, : self.tf] = np.kron(table.T, np.eye(self.fields, dtype=np.float32))
        hi = full.astype(ml_dtypes.bfloat16)
        lo = (full - hi.astype(np.float32)).astype(ml_dtypes.bfloat16)
        return np.concatenate([hi, lo, hi], axis=1)

    def field_rows(self):
        out = np.zeros((self.pad, self.fields), np.float32)
        out[np.arange(self.tf), np.arange(self.tf) % self.fields] = 1.0
        return out

    def field_lanes(self):
        return np.tile(self.field_rows().T, (1, 3))

    def block_diagonal(self):
        block = np.full(self.pad, -1)
        block[: self.tf] = np.arange(self.tf) // self.fields
        same = (block[:, None] == block[None, :]) & (block[:, None] >= 0)
        return np.tile(same.astype(np.float32), (1, 3))


    def inst_rows(self):
        row, inst = table_index(self.pad, 16)
        return ((row >= inst * self.fields) & (row < (inst + 1) * self.fields)).astype(jnp.float32)

    def cell_of(self, lane):
        return lax.div(lane, self.width) * self.rows + lax.rem(lane, self.rows)

    def window_lanes(self):
        lane, to = table_index(LANES, LANES)
        return (lane < self.ct * self.width) & (to == self.cell_of(lane) * WINDOW)

    def window_spread(self):
        to, lane = table_index(LANES, LANES)
        return (lane < self.ct * self.width) & (to == self.cell_of(lane) * WINDOW)

    def weight_lanes(self):
        cell, lane = table_index(LANES, LANES)
        half = self.ct * self.width
        wanted = jnp.where(lane < half, self.cell_of(lane), self.cells + self.cell_of(lane - half))
        return cell == wanted

    def panel_lanes(self):
        lane = lane_index(1)
        panel = lax.rem(lax.div(lane, self.rows), self.panels)
        return jnp.where(lane < self.ct * self.width, panel, -9).astype(jnp.float32)


def table_index(rows, columns):
    return [lax.broadcasted_iota(jnp.int32, (rows, columns), axis) for axis in (0, 1)]


def call(kernel, out, scratch=(), flops=2_000_000, nbytes=1_000_000):
    return pl.pallas_call(
        kernel,
        out_shape=out,
        scratch_shapes=list(scratch),
        compiler_params=pltpu.CompilerParams(vmem_limit_bytes=20 * 1024 * 1024),
        cost_estimate=pl.CostEstimate(flops=flops, bytes_accessed=nbytes, transcendentals=0),
    )


def f32(*shape):
    return jax.ShapeDtypeStruct(shape, jnp.float32)


def vmem(*shape):
    return pltpu.VMEM(shape, jnp.float32)


def halves_of(x):
    hi = x.astype(jnp.bfloat16)
    return hi, (x - hi.astype(jnp.float32)).astype(jnp.bfloat16)


def dot3(w, x):
    hi, lo = halves_of(x)
    return jnp.dot(w, jnp.concatenate([hi, hi, lo], axis=0), preferred_element_type=jnp.float32)


def pick(x, table):
    table = table.astype(jnp.float32).astype(jnp.bfloat16)
    table = jnp.concatenate([table, table], axis=0)
    return jnp.dot(jnp.concatenate(halves_of(x), axis=1), table, preferred_element_type=jnp.float32)


def dot_full(a, b):
    return jnp.dot(a, b, precision=HIGHEST, preferred_element_type=jnp.float32)


def lane_index(rows):
    return lax.broadcasted_iota(jnp.int32, (rows, LANES), 1)


def rolled(x, by):
    by %= LANES
    return pltpu.roll(x, by, axis=1) if by else x


def at(r, count=1, start=0):
    return slice(start + r * LANES, start + (r + count) * LANES)


def parity():
    return lax.rem(lax.axis_index("sector"), 2)


def has_sides(plan):
    span = lax.axis_index("span")
    return jnp.where(span < plan.spans - 1, 1.0, 0.0), jnp.where(span > 0, 1.0, 0.0)


class Layer:
    def __init__(self, plan, ref, start=0, rates=None, seam=None, layer=0):
        self.plan, self.ref, self.start, self.seam, self.layer = plan, ref, start, seam, layer
        self.rates = rates or (ref, start)

    def rate(self, which, r, count=1):
        if isinstance(self.rates, Layer):
            return self.rates.rate(which, r, count)
        ref, start = self.rates
        row = self.plan.pad + which
        return ref[row : row + 1, at(r, count, start)]

    def row(self, r):
        value = self.ref[: self.plan.pad, at(r, 1, self.start)]
        if self.seam is None:
            return value
        return value + placed(self.seam, self.layer * self.plan.rows + r) * self.rate(C_MASK, r)

    def chunk(self, c):
        count = CHUNK // LANES
        if self.seam is None:
            return self.ref[: self.plan.pad, at(c * count, count, self.start)]
        return jnp.concatenate([self.row(c * count + part) for part in range(count)], axis=1)


class Native(Layer):
    def __init__(self, plan, ref, table, seam, layer, near):
        super().__init__(plan, ref, 0, None, seam, layer)
        self.table, self.near = table, near

    def rate(self, which, r, count=1):
        row = which if self.near else C_OTHER
        return self.table[row : row + 1, at(r, count)]

    def row(self, r):
        plan = self.plan
        there = jnp.where(parity() == 1, self.layer, plan.ct - 1 - self.layer) * plan.rows + r
        field = self.ref[pl.ds(there, plan.tf, stride=plan.cells), :]
        field = jnp.concatenate([field, jnp.zeros((plan.pad - plan.tf, LANES), jnp.float32)], axis=0)
        return (field + placed(self.seam, self.layer * plan.rows + r)) * self.rate(C_MASK, r)


def placed(tile, cell):
    return jnp.where(lane_index(tile.shape[0]) == 0, rolled(tile, -cell * WINDOW), 0.0)


class Products:
    def __init__(self, plan, w_ref, p_ref, first):
        self.plan, self.w, self.p, self.first = plan, w_ref, p_ref, first

    def fill(self, layer):
        for c in range(self.plan.slab // CHUNK):
            self.p[:, c * CHUNK : (c + 1) * CHUNK] = dot3(matrix(self.plan, self.w, self.first, 6), layer.chunk(c))
        self.layer = layer
        return self

    def get(self, block, r):
        row = (block - self.first) * self.plan.pad
        return self.p[row : row + self.plan.pad, at(r)]

    def own_terms(self, r):
        rate = self.layer.rate
        total = rate(C_TIME, r) * self.get(SPECTRAL, r)
        beside = []
        if r + 1 < self.plan.rows:
            beside.append(self.get(UP_SP, r + 1))
        if r > 0:
            beside.append(self.get(DOWN_SP, r - 1))
        total = total + rate(C_SP, r) * sum(beside[1:], beside[0])
        total = total + rate(C_UP, r) * rolled(self.get(UP_AX, r), -1)
        return total + rate(C_DOWN, r) * rolled(self.get(DOWN_AX, r), 1)


def matrix(plan, w_ref, block, count=1):
    return w_ref[block * plan.pad : (block + count) * plan.pad, :]


def two_layers(plan, ref, rates=None, seam=None):
    return [
        Layer(plan, ref, a * plan.slab, (rates, a * plan.slab) if rates is not None else None, seam, a)
        for a in range(plan.ct)
    ]


def inner_rows(plan, w_ref, p_refs, layers, force, g_ref):
    first = Products(plan, w_ref, p_refs[0], DOWN_AZ).fill(layers[0])
    second = Products(plan, w_ref, p_refs[1], SPECTRAL).fill(layers[1])
    for r in range(plan.rows):
        other = second.get(UP_AZ, r), first.get(DOWN_AZ, r)
        for a, products in enumerate((first, second)):
            total = products.own_terms(r) + layers[a].rate(C_AZ, r) * other[a]
            if isinstance(g_ref, tuple):
                g_ref[a][:, at(r)] = force[a].row(r) - total
            else:
                g_ref[:, at(r, 1, a * plan.slab)] = force[a].row(r) - total


def azimuthal(plan, w_ref, block, chunk_of, take):
    for c in range(plan.slab // CHUNK):
        terms = dot3(matrix(plan, w_ref, block), chunk_of(c))
        for part in range(CHUNK // LANES):
            take(c * (CHUNK // LANES) + part, terms[:, at(part)])


def middle_rows(plan, w_ref, p_refs, own, own_force, g_ref, near, near_force, side, corner, y_ref, h_refs, n_refs):
    pad, rows, ct = plan.pad, plan.rows, plan.ct
    last = (rows - 1, 0)
    edge_terms, edge_new, corner_terms = [], [], []
    is_first = lax.axis_index("span") == 0

    def choose(n, above, below):
        return jnp.where(is_first, above, below) if plan.ends == 1 else (above, below)[n]

    for n in range(plan.ends):
        outward = choose(n, matrix(plan, w_ref, UP_SP), matrix(plan, w_ref, DOWN_SP))
        inward = choose(n, matrix(plan, w_ref, DOWN_SP), matrix(plan, w_ref, UP_SP))
        first, second, edge_force, edge_rate = side(n)
        corners = corner(n)
        every = dot3(w_ref[...], first)
        beyond = dot3(outward, second)
        within = [choose(n, x.row(last[0]), x.row(last[1])) for x in own]
        within = dot3(inward, jnp.concatenate(within, axis=1))
        from_low = dot3(matrix(plan, w_ref, DOWN_AZ), corners[0])
        from_high = dot3(matrix(plan, w_ref, UP_AZ), corners[1])
        new = []
        for a in range(ct):

            def part(block, b=a):
                return every[block * pad : (block + 1) * pad, at(b)]

            around = part(UP_AZ, 1) + from_low if a == 0 else from_high + part(DOWN_AZ, 0)
            total = edge_rate(C_TIME, a) * part(SPECTRAL) + edge_rate(C_AZ, a) * around
            total = total + edge_rate(C_SP, a) * (beyond[:, at(a)] + within[:, at(a)])
            total = total + edge_rate(C_UP, a) * rolled(part(UP_AX), -1)
            total = total + edge_rate(C_DOWN, a) * rolled(part(DOWN_AX), 1)
            new.append(edge_force[:, at(a)] - total)
        of_edge = choose(n, *(every[block * pad : (block + 1) * pad] for block in (UP_SP, DOWN_SP)))
        of_new = dot3(outward, jnp.concatenate(new, axis=1))
        of_corners = dot3(outward, jnp.concatenate(corners, axis=1))
        for keep in has_sides(plan) if plan.ends == 1 else (1.0,):
            edge_terms.append(of_edge * keep)
            edge_new.append(of_new * keep)
            corner_terms.append([of_corners[:, at(a)] * keep for a in range(ct)])

    products = (
        Products(plan, w_ref, p_refs[0], DOWN_AZ).fill(near[0]), Products(plan, w_ref, p_refs[1], SPECTRAL).fill(near[1]),
    )
    for a, (to_own, to_near) in enumerate(((DOWN_AZ, UP_AZ), (UP_AZ, DOWN_AZ))):

        def take(r, terms):
            total = products[a].own_terms(r) + near[a].rate(C_AZ, r) * terms
            mine = own[a].rate(C_AZ, r) * products[a].get(to_own, r)
            for n in range(2):
                if r == last[n]:
                    total = total + near[a].rate(C_SP, r) * corner_terms[n][a]
                    mine = mine + own[a].rate(C_SP, r) * edge_terms[n][:, at(a)]
            n_refs[a][:, at(r)] = near_force[a].row(r) - total
            lanes = at(r, 1, a * plan.slab)
            y_ref[:, lanes] = g_ref[:, lanes] - mine

        azimuthal(plan, w_ref, to_near, own[a].chunk, take)

    after = [Layer(plan, y_ref, a * plan.slab, own[a].rates) for a in range(ct)]
    inner_rows(plan, w_ref, p_refs, after, own_force, h_refs)
    for a in range(ct):
        for n in range(2):
            h_refs[a][:, at(last[n])] -= own[a].rate(C_SP, last[n]) * edge_new[n][:, at(a)]


def outer_rows(plan, w_ref, own, near, far_chunks, n_refs, h_refs, put, layers=(0, 1)):
    count = CHUNK // LANES
    for a in layers:
        block = (DOWN_AZ, UP_AZ)[a]

        def near_chunk(c):
            terms = dot3(matrix(plan, w_ref, block), far_chunks[a](c))
            return n_refs[a][:, at(c * count, count)] - near[a].rate(C_AZ, c * count, count) * terms

        def take(r, terms):
            put(a, r, h_refs[a][:, at(r)] - own[a].rate(C_AZ, r) * terms)

        azimuthal(plan, w_ref, block, near_chunk, take)


def sides_of(plan, side_ref, force_ref, seams_ref):
    pad, ct = plan.pad, plan.ct
    keeps = (1.0,) if plan.ends == 1 else has_sides(plan)
    is_first = lax.axis_index("span") == 0

    def inlet(n, e, a):
        above, below = a * plan.rows + e, a * plan.rows + plan.rows - 1 - e
        tile = seams_ref[1, 1 + n]
        if plan.ends == 1:
            return jnp.where(is_first, placed(tile, above), placed(tile, below))
        return placed(tile, (above, below)[n])

    def read(n, ref, e, seam):
        value = ref[n, :pad, at(e * ct, ct)]
        if seam:
            scale = ref[n, pad + C_MASK : pad + C_MASK + 1, at(e * ct, ct)]
            value = value + jnp.concatenate([inlet(n, e, a) for a in range(ct)], axis=1) * scale
        return value * keeps[n]

    def side(n):
        same = side_ref is force_ref

        def rate(which, a):
            return force_ref[n, pad + which : pad + which + 1, at(a)] * keeps[n]

        force = read(n, force_ref, 0, True)
        first = force if same else read(n, side_ref, 0, False)
        return first, read(n, side_ref, 1, same), force, rate

    return side


def corners_of(plan, c_refs, seams_ref):
    keeps = (1.0,) if plan.ends == 1 else has_sides(plan)
    is_first = lax.axis_index("span") == 0

    def corner(n):
        out = []
        for a, c_ref in enumerate(c_refs):
            value = c_ref[n, : plan.pad]
            if seams_ref is not None:
                tile = seams_ref[2 * a, 1 + n]
                above, below = (placed(tile, a * plan.rows + r) for r in (0, plan.rows - 1))
                inlet = jnp.where(is_first, above, below) if plan.ends == 1 else (above, below)[n]
                value = value + inlet * c_ref[n, plan.pad + C_MASK : plan.pad + C_MASK + 1]
            out.append(value * keeps[n])
        return out

    return corner


def prepare(plan, rhs_ref, coef_ref, m_ref, table0_ref, table1_ref, side_ref, c0_ref, c1_ref, rates_ref):
    pad, cells = plan.pad, plan.cells
    mask, diag, time, *face = [coef_ref[cells * i : cells * (i + 1), :] for i in range(6)]
    scale = mask / diag
    lane = lane_index(cells)
    axial = scale * face[2]
    rates = (
        scale * time, scale * face[0], scale * face[1],
        jnp.where(lane < LANES - 1, axial, 0.0), jnp.where(lane > 0, axial, 0.0), scale,
    )
    for i, rate in enumerate(rates):
        rates_ref[i] = rate
    tail = jnp.zeros((pad - plan.tf, LANES), jnp.float32)
    rest = jnp.zeros((RATES - 6, LANES), jnp.float32)
    mirror = parity()
    for cell in range(cells):
        a, r = divmod(cell, plan.rows)
        there = jnp.where(mirror == 0, a, plan.ct - 1 - a) * plan.rows + r
        table = [rates_ref[i, pl.ds(there, 1), :] for i in range(6)]
        field = jnp.concatenate([rhs_ref[pl.ds(there, plan.tf, stride=cells), :], tail], axis=0)
        m_ref[:pad, at(cell)] = field * table[C_MASK]
        m_ref[pad:, at(cell)] = jnp.concatenate(table + [rest], axis=0)
        other = jnp.where(mirror == 0, plan.ct - 1 - a, a) * plan.rows + r
        table = table + [rates_ref[C_MASK, pl.ds(other, 1), :], rest[:1]]
        (table0_ref, table1_ref)[a][:, at(r)] = jnp.concatenate(table, axis=0)
    write_edges(plan, m_ref, side_ref, (c0_ref, c1_ref))


def write_edges(plan, x_ref, side_ref, c_refs):
    first = lax.axis_index("span") == 0
    for a in range(plan.ct):
        for e in range(DEPTH):
            low, high = x_ref[:, at(a * plan.rows + e)], x_ref[:, at((a + 1) * plan.rows - 1 - e)]
            ends = [jnp.where(first, high, low)] if plan.ends == 1 else [low, high]
            for n, end in enumerate(ends):
                side_ref[n, :, at(e * plan.ct + a)] = end
                if e == 0:
                    c_refs[a][n] = end


def stack_matrices(plan, up_ref, down_ref, spectral_ref, rows_ref, lanes_ref, diagonal_ref, out_ref, down_out):
    pad = plan.pad
    lane = lax.broadcasted_iota(jnp.int32, (pad, 3 * pad), 1)
    second = (lane >= pad) & (lane < 2 * pad)
    out_ref[SPECTRAL * pad : (SPECTRAL + 1) * pad, :] = spectral_ref[...]
    even = parity() == 0
    for block, small in (
        (DOWN_AZ, jnp.where(even, down_ref[0], up_ref[0])), (UP_AZ, jnp.where(even, up_ref[0], down_ref[0])),
        (UP_SP, up_ref[1]), (DOWN_SP, down_ref[1]), (UP_AX, up_ref[2]), (DOWN_AX, down_ref[2]),
    ):
        full = dot_full(dot_full(rows_ref[...], small), lanes_ref[...]) * diagonal_ref[...]
        hi = full.astype(jnp.bfloat16).astype(jnp.float32)
        out_ref[block * pad : (block + 1) * pad, :] = jnp.where(second, full - hi, hi).astype(jnp.bfloat16)
    down_out[...] = matrix(plan, out_ref, DOWN_AZ)


def send_panels(plan, stator_ref, both_ref, out_ref, panels_ref):
    me = lax.axis_index("sector")
    for f in range(plan.fields):
        panels_ref[pl.ds(f, plan.insts, stride=RATES), : plan.width] = jnp.transpose(stator_ref[f])
    out_ref[...] = jnp.zeros_like(out_ref)
    for t, (row, start) in enumerate(plan.weight_at):
        both = jnp.broadcast_to(both_ref[t : t + 1, :][None], (out_ref.shape[0], 1, plan.width))
        out_ref[:, row : row + 1, start : start + plan.width] = both
    for o, slots in enumerate(plan.slots):
        to = lax.rem(me + (plan.sectors - o), plan.sectors) * plan.spans
        for slot, t in enumerate(slots):
            lanes = slice(slot * plan.width, (slot + 1) * plan.width)
            panels = panels_ref[t * RATES : t * RATES + plan.fields, : plan.width]
            for x in range(plan.spans):
                out_ref[to + x, : plan.fields, lanes] = panels


def begin(
    plan, w_ref, m_ref, got_ref,
    seams_ref, weight_ref, x_ref, g_ref, panels_ref, terms_ref, rows_ref, p0_ref, p1_ref,
):
    pad, insts, fields = plan.pad, plan.insts, plan.fields
    me, span = lax.axis_index("sector"), lax.axis_index("span")
    even, is_first = parity() == 0, span == 0
    tiles = plan.tiles
    panels_ref[...] = jnp.zeros_like(panels_ref)
    rows_ref[...] = jnp.zeros_like(rows_ref)
    for n, (k, x) in enumerate(tiles):
        at_span = x if plan.spans == 2 else jnp.clip(span + x, 0, plan.spans - 1)
        for t in range(insts):
            o = (k + plan.shift[t]) % plan.sectors
            source = lax.rem(me + o, plan.sectors) * plan.spans + at_span
            tile = rolled(got_ref[source], -plan.slots[o].index(t) * plan.width)
            panels_ref[t * fields : (t + 1) * fields, n * LANES : n * LANES + plan.width] = tile[:fields, : plan.width]
        tile = got_ref[lax.rem(me + k + plan.sectors, plan.sectors) * plan.spans + at_span]
        lanes = slice(n * LANES, n * LANES + plan.width)
        rows_ref[:fields, lanes] = rolled(tile, -plan.weight_at[0][1])[:fields, : plan.width]
        for t in range(fields, insts):
            row, start = plan.weight_at[t]
            rows_ref[t : t + 1, lanes] = rolled(tile, -start)[row : row + 1, : plan.width]
    spread = dot_full(plan.inst_rows(), rows_ref[...])
    spread = pick(jnp.concatenate([spread[:, at(n)] for n in range(len(tiles))], axis=0), plan.weight_lanes())
    first, share, panel = spread, rolled(spread, plan.ct * plan.width), plan.panel_lanes()
    lower = (jnp.abs(first - panel) < 0.5).astype(jnp.float32)
    upper = (jnp.abs(first + 1.0 - panel) < 0.5).astype(jnp.float32)
    weights = share * lower + (1.0 - share) * upper
    for n in range(len(tiles)):
        panels = panels_ref[:, at(n)]
        terms_ref[n * pad : (n + 1) * pad, :] = panels + rolled(panels, plan.width)
    seams = pick(terms_ref[...] * weights, plan.window_lanes())

    def tile(values, k, x):
        n = tiles.index((k, x))
        return values[n * pad : (n + 1) * pad]

    def around(values, k):
        if plan.spans == 2:
            pair = tile(values, k, 0), tile(values, k, 1)
            return [jnp.where(is_first, pair[0], pair[1]), jnp.where(is_first, pair[1], pair[0])]
        return [tile(values, k, x) for x in (0, 1, -1)]

    def mirrored(value):
        return rolled(value, LANES // 2)

    here = around(seams, 0)
    behind, ahead = around(seams, -1), around(seams, 1)
    for i in range(1 + plan.ends):
        seams_ref[0, i] = jnp.where(even, mirrored(behind[i]), ahead[i])
        seams_ref[1, i] = jnp.where(even, here[i], mirrored(here[i]))
        seams_ref[2, i] = jnp.where(even, mirrored(ahead[i]), behind[i])
    weight_ref[...] = around(weights, 0)[0]

    for layer in two_layers(plan, m_ref, seam=seams_ref[1, 0]):
        for r in range(plan.rows):
            x_ref[:, at(r, 1, layer.start)] = layer.row(r)
    layers = two_layers(plan, x_ref, m_ref)
    inner_rows(plan, w_ref, (p0_ref, p1_ref), layers, layers, g_ref)


def first_half(
    plan, w_ref, m_ref, f_ref, g_ref, low_ref, high_ref, low_table, high_table, side_ref, c_low, c_high, seams_ref,
    x_ref, near_ref, side_out, c0_ref, c1_ref, p0_ref, p1_ref, y_ref, h0_ref, h1_ref, n0_ref, n1_ref, inlet_ref,
):
    own = two_layers(plan, f_ref, m_ref)
    low = [Native(plan, low_ref, low_table, seams_ref[0, 0], a, a == 0) for a in range(plan.ct)]
    high = [Native(plan, high_ref, high_table, seams_ref[2, 0], a, a == 1) for a in range(plan.ct)]
    near = low[0], high[1]
    n_refs = n0_ref, n1_ref
    middle_rows(
        plan, w_ref, (p0_ref, p1_ref), own, own, g_ref, near, near, sides_of(plan, side_ref, side_ref, seams_ref),
        corners_of(plan, (c_low, c_high), seams_ref), y_ref, (h0_ref, h1_ref), n_refs,
    )
    lane = lane_index(plan.pad)
    inlet_ref[...] = jnp.zeros_like(inlet_ref)

    def put(a, r, value):
        x_ref[:, at(r, 1, a * plan.slab)] = value
        if a == 0:
            near_ref[:, at(r)] = value
        else:
            inlet_ref[: plan.pad, :] = jnp.where(lane == r, rolled(value, r), inlet_ref[: plan.pad, :])

    outer_rows(plan, w_ref, own, near, (low[1].chunk, high[0].chunk), n_refs, (h0_ref, h1_ref), put)
    turned = jnp.transpose(inlet_ref[...])
    for r in range(plan.rows):
        near_ref[plan.tf : plan.tf + 1, at(r)] = turned[r : r + 1, :]
    write_edges(plan, x_ref, side_out, (c0_ref, c1_ref))


def hold_far(plan, x_ref, side_ref, c_high, far_ref):
    come = side_ref[0, 0:1, 0:1] + c_high[0, 0:1, 0:1]
    far_ref[...] = x_ref[:, plan.slab :] + 0.0 * come


def inner(plan, w_ref, m_ref, f_ref, x_ref, g_ref, p0_ref, p1_ref):
    inner_rows(plan, w_ref, (p0_ref, p1_ref), two_layers(plan, x_ref, m_ref), two_layers(plan, f_ref, m_ref), g_ref)


def middle(
    plan, w_ref, m_ref, f_ref, x_ref, g_ref, low_ref, high_ref, side_ref, c_low, c_high,
    low_first, high_first, low_table, high_table, side_first, seams_ref, weight_ref,
    send_ref, n0_ref, h0_ref, x1_ref, rates_ref, p0_ref, p1_ref, y_ref, h1_ref, n1_ref, turn_ref,
):
    pad = plan.pad
    own, force = two_layers(plan, x_ref, m_ref), two_layers(plan, f_ref, m_ref)
    low_force = Native(plan, low_first, low_table, seams_ref[0, 0], 0, True)
    high_force = Native(plan, high_first, high_table, seams_ref[2, 0], 1, True)
    near = Layer(plan, low_ref, 0, low_force), Layer(plan, high_ref, plan.slab, high_force)
    n_refs = n0_ref, n1_ref
    middle_rows(
        plan, w_ref, (p0_ref, p1_ref), own, force, g_ref, near, (low_force, high_force),
        sides_of(plan, side_ref, side_first, seams_ref), corners_of(plan, (c_low, c_high), None), y_ref,
        (h0_ref, h1_ref), n_refs,
    )

    def put(a, r, value):
        x1_ref[:, at(r)] = value

    outer_rows(plan, w_ref, own, near, (None, Layer(plan, high_ref).chunk), n_refs, (h0_ref, h1_ref), put, (1,))
    for r in range(plan.rows):
        last = [near[0].rate(C_AZ, r), own[0].rate(C_AZ, r), jnp.zeros((RATES - 2, LANES), jnp.float32)]
        rates_ref[:, at(r)] = jnp.concatenate(last, axis=0)

    turn_ref[...] = jnp.zeros_like(turn_ref)
    for r in range(plan.rows):
        turn_ref[r : r + 1, :] = low_ref[plan.tf : plan.tf + 1, at(r)]
    far = jnp.transpose(turn_ref[...])[:pad]

    def packed(read, count, first=0, step=1):
        lane = lane_index(count)
        out = jnp.zeros((count, LANES), jnp.float32)
        for r in range(plan.rows):
            to = first + r * step
            out = jnp.where(lane == to, rolled(read(r), to), out)
        return out

    rates = packed(lambda r: rates_ref[:, at(r)], RATES)
    inlet = packed(lambda r: n0_ref[:, at(r)], pad) - rates[0:1] * dot3(matrix(plan, w_ref, DOWN_AZ), far)
    inlet = packed(lambda r: h0_ref[:, at(r)], pad) - rates[1:2] * dot3(matrix(plan, w_ref, DOWN_AZ), inlet)
    lane = lane_index(pad)
    spread = packed(lambda r: x1_ref[:, at(r)], pad, plan.rows * WINDOW, WINDOW)
    for r in range(plan.rows):
        spread = jnp.where(lane == r * WINDOW, rolled(inlet, r * (WINDOW - 1)), spread)
    inlet = jnp.where(parity() == 0, spread, rolled(spread, LANES // 2))
    back = pick(inlet, plan.window_spread()) * weight_ref[...]
    back = back + rolled(back, -plan.width)
    me = lax.axis_index("sector")
    send_ref[...] = jnp.zeros_like(send_ref)
    for t in range(plan.insts):
        to = lax.rem(me + plan.shift[t], plan.sectors)
        send_ref[to, : plan.fields, : plan.width] = back[t * plan.fields : (t + 1) * plan.fields, : plan.width]


def outer(plan, w_ref, rates_ref, n0_ref, h0_ref, x1_ref, far_ref, out_ref):
    mirror = parity()

    def put(a, r, value):
        there = jnp.where(mirror == 0, a, plan.ct - 1 - a) * plan.rows + r
        out_ref[pl.ds(there, plan.tf, stride=plan.cells), :] = value[: plan.tf]

    for r in range(plan.rows):
        put(1, r, x1_ref[:, at(r)])

    def near_chunk(c):
        lanes = slice(c * CHUNK, (c + 1) * CHUNK)
        return n0_ref[:, lanes] - rates_ref[0:1, lanes] * dot3(w_ref[...], far_ref[:, lanes])

    azimuthal(plan, w_ref, 0, near_chunk, lambda r, terms: put(0, r, h0_ref[:, at(r)] - rates_ref[1:2, at(r)] * terms))


def collect_panels(plan, got_ref, out_ref, panels_ref):
    me = lax.axis_index("sector")
    for t in range(plan.insts):
        source = lax.rem(me + (plan.sectors - plan.shift[t]), plan.sectors)
        panels_ref[t * RATES : (t + 1) * RATES, :] = got_ref[source]
    for f in range(plan.fields):
        tile = panels_ref[pl.ds(f, plan.insts, stride=RATES), : plan.width]
        out_ref[f] = jnp.transpose(tile)


def sibling(plan):
    return [s ^ 1 for s in range(plan.sectors)]


def outside(plan):
    return [(s - 1 if s % 2 == 0 else s + 1) % plan.sectors for s in range(plan.sectors)]


def swap(array, partner):
    return lax.ppermute(array, "sector", list(enumerate(partner)))


def beside(plan, array, partner):
    def pairs(step):
        out = []
        for s in range(plan.sectors):
            for x in range(plan.spans):
                to = 1 - x if plan.ends == 1 else x + step
                if 0 <= to < plan.spans:
                    out.append((s * plan.spans + x, partner[s] * plan.spans + to))
        return out

    if plan.ends == 1:
        return lax.ppermute(array, AXES, pairs(0))
    return jnp.concatenate([lax.ppermute(array[:1], AXES, pairs(-1)), lax.ppermute(array[1:], AXES, pairs(1))])


def on_device(
    sectors, spans,
    rhs, diag_coef, face_coef, time_coef, jac_up, jac_down, wall_mask, stator_adj, owner, first_panel_share,
):
    plan = Plan(rhs, stator_adj, sectors, spans)
    pad, cells, slab, insts, fields, ends = plan.pad, plan.cells, plan.slab, plan.insts, plan.fields, plan.ends
    bind = functools.partial
    whole, half = f32(pad, plan.ct * slab), f32(pad, slab)
    products = (vmem(6 * pad, slab),) * 2
    alone, next_chip, next_core = list(range(sectors)), outside(plan), sibling(plan)

    def edges(rows):
        return f32(ends, rows, DEPTH * plan.ct * LANES), f32(ends, rows, LANES), f32(ends, rows, LANES)

    stator = jnp.transpose(stator_adj, (1, 2, 3, 0)).reshape(fields, plan.width, insts)
    sent = call(bind(send_panels, plan), f32(sectors * spans, RATES, LANES), (vmem(insts * RATES, LANES),))(
        stator,
        jnp.concatenate([
            lax.rem(owner, plan.panels).astype(jnp.float32).reshape(insts, cells), first_panel_share.reshape(insts, cells),
        ], axis=1),
    )
    got = lax.all_to_all(sent, AXES, 0, 0, tiled=True)
    native = rhs.reshape(plan.tf * cells, LANES)
    low_first, high_first = swap(native, next_chip), swap(native, next_core)
    m, table0, table1, side, c0, c1 = call(
        bind(prepare, plan),
        (f32(pad + RATES, plan.ct * slab), f32(RATES, slab), f32(RATES, slab)) + edges(pad + RATES),
        (vmem(6, cells, LANES),),
    )(
        native,
        jnp.concatenate([
            wall_mask.astype(jnp.float32).reshape(cells, LANES), diag_coef.reshape(cells, LANES),
            time_coef.reshape(cells, LANES), face_coef.reshape(3 * cells, LANES),
        ]),
    )
    low_table, high_table = swap(table0, next_chip), swap(table1, next_core)
    side_first = beside(plan, side, alone)
    c_low, c_high = beside(plan, c0, next_chip), beside(plan, c1, next_core)
    matrices, down = call(
        bind(stack_matrices, plan),
        [jax.ShapeDtypeStruct((count * pad, 3 * pad), jnp.bfloat16) for count in (7, 1)],
    )(jac_up, jac_down, plan.spectral(), plan.field_rows(), plan.field_lanes(), plan.block_diagonal())
    tiles = len(plan.tiles)
    seams, weight, force, g = call(
        bind(begin, plan), (f32(3, 1 + ends, pad, LANES), f32(pad, LANES), whole, whole),
        (vmem(pad, tiles * LANES), vmem(tiles * pad, LANES), vmem(16, tiles * LANES)) + products,
        flops=2_000_000_000,
    )(matrices, m, got)
    x, near, side, c0, c1 = call(
        bind(first_half, plan), (whole, half) + edges(pad),
        products + (vmem(pad, 2 * slab),) + (vmem(pad, slab),) * 4 + (vmem(LANES, LANES),),
        flops=4_000_000_000,
    )(matrices, m, force, g, low_first, high_first, low_table, high_table, side_first, c_low, c_high, seams)

    low, high = swap(near, next_chip), swap(x, next_core)
    side = beside(plan, side, alone)
    c_low, c_high = beside(plan, c0, next_chip), beside(plan, c1, next_core)
    (g,) = call(bind(inner, plan), (whole,), products, flops=2_000_000_000)(matrices, m, force, x)
    far = call(bind(hold_far, plan), half)(x, side, c_high)
    far_low = swap(far, next_chip)
    back, n0, h0, x1, rates = call(
        bind(middle, plan), (f32(sectors, RATES, LANES), half, half, half, f32(RATES, slab)),
        products + (vmem(pad, 2 * slab), vmem(pad, slab), vmem(pad, slab), vmem(LANES, LANES)),
        flops=4_000_000_000,
    )(
        matrices, m, force, x, g, low, high, side, c_low, c_high, low_first, high_first, low_table, high_table, side_first,
        seams, weight,
    )
    returned = lax.all_to_all(back, "sector", 0, 0, tiled=True)
    sens = call(bind(collect_panels, plan), f32(fields, plan.width, insts), (vmem(insts * RATES, LANES),))(returned)
    out = call(bind(outer, plan), f32(plan.tf * cells, LANES))(down, rates, n0, h0, x1, far_low)
    sens = jnp.transpose(sens.reshape(fields, plan.panels, plan.rows, insts), (3, 0, 1, 2))
    return out.reshape(rhs.shape), sens


def solution(mesh):
    in_specs = (
        P(None, None, "sector", "span", None),
        P("sector", "span", None),
        P(None, "sector", "span", None),
        P("sector", "span", None),
        P(),
        P(),
        P("sector", "span", None),
        P(None, None, "sector", "span"),
        P(None, "sector", "span"),
        P(None, "sector", "span"),
    )
    out_specs = (P(None, None, "sector", "span", None), P(None, None, "sector", "span"))
    return jax.shard_map(
        functools.partial(on_device, mesh.shape["sector"], mesh.shape["span"]),
        mesh=mesh, in_specs=in_specs, out_specs=out_specs, check_vma=False,
    )
```

```python
import functools

import jax
import jax.numpy as jnp
import ml_dtypes
import numpy as np
from jax import lax
from jax.experimental import pallas as pl
from jax.experimental.pallas import tpu as pltpu
from jax.sharding import PartitionSpec as P

SWEEPS = 4
DEPTH = 2
LANES = 128
CHUNK = 256
WINDOW = 8
HIGHEST = lax.Precision.HIGHEST
DOWN_AZ, SPECTRAL, UP_SP, DOWN_SP, UP_AX, DOWN_AX, UP_AZ = range(7)
C_TIME, C_AZ, C_SP, C_UP, C_DOWN, C_MASK, C_OTHER = range(7)
RATES = 8
AXES = ("sector", "span")


class Plan:
    def __init__(self, rhs, stator_adj, sectors, spans):
        self.insts, self.fields, self.ct, self.rows, self.nax = rhs.shape
        self.panels = stator_adj.shape[2]
        self.sectors, self.spans = sectors, spans
        self.tf = self.insts * self.fields
        self.pad = -(-self.tf // 16) * 16
        self.cells = self.ct * self.rows
        self.slab = self.rows * LANES
        self.width = self.panels * self.rows
        self.shift = [
            ((t * sectors) // (self.insts - 1) - t // (self.insts - 1)) % sectors for t in range(self.insts)
        ]
        assert self.ct == 2 and self.nax == LANES and SWEEPS % DEPTH == 0 and spans > 1
        assert len(set(self.shift)) == self.insts and self.cells * WINDOW == LANES and self.rows >= SWEEPS
        assert self.slab % CHUNK == 0 and 3 * self.pad <= 256 and 2 * self.ct * self.width == LANES
        assert sectors % 2 == 0
        self.ends = 1 if spans == 2 else 2
        self.blocks = [-1, 0, 1]
        self.halves = [0, 1] if spans == 2 else [-1, 0, 1]
        self.tiles = [(k, x) for k in self.blocks for x in self.halves]
        self.slots = [
            [t for t in range(self.insts) if any((k + self.shift[t]) % sectors == o for k in self.blocks)]
            for o in range(sectors)
        ]
        last = LANES - self.width
        self.weight_at = [(t, last) for t in range(self.fields)] + [
            (self.fields, i * self.width) for i in range(self.insts - self.fields)
        ]
        assert max(map(len, self.slots)) * self.width <= last and 2 * self.cells == self.width
        assert self.fields == RATES - 1 and (self.insts - self.fields) * self.width <= LANES

    def spectral(self):
        t = np.arange(self.insts)
        off = t[:, None] - t[None, :]
        sines = np.where(off == 0, 1.0, np.sin(np.pi * off / self.insts))
        table = np.where(off == 0, 0.0, 0.5 * (1.0 - 2.0 * (off % 2)) / sines).astype(np.float32)
        full = np.zeros((self.pad, self.pad), np.float32)
        full[: self.tf, : self.tf] = np.kron(table.T, np.eye(self.fields, dtype=np.float32))
        hi = full.astype(ml_dtypes.bfloat16)
        lo = (full - hi.astype(np.float32)).astype(ml_dtypes.bfloat16)
        return np.concatenate([hi, lo, hi], axis=1)

    def field_rows(self):
        out = np.zeros((self.pad, self.fields), np.float32)
        out[np.arange(self.tf), np.arange(self.tf) % self.fields] = 1.0
        return out

    def field_lanes(self):
        return np.tile(self.field_rows().T, (1, 3))

    def block_diagonal(self):
        block = np.full(self.pad, -1)
        block[: self.tf] = np.arange(self.tf) // self.fields
        same = (block[:, None] == block[None, :]) & (block[:, None] >= 0)
        return np.tile(same.astype(np.float32), (1, 3))


    def inst_rows(self):
        row, inst = table_index(self.pad, 16)
        return ((row >= inst * self.fields) & (row < (inst + 1) * self.fields)).astype(jnp.float32)

    def cell_of(self, lane):
        return lax.div(lane, self.width) * self.rows + lax.rem(lane, self.rows)

    def window_lanes(self):
        lane, to = table_index(LANES, LANES)
        return (lane < self.ct * self.width) & (to == self.cell_of(lane) * WINDOW)

    def window_spread(self):
        to, lane = table_index(LANES, LANES)
        return (lane < self.ct * self.width) & (to == self.cell_of(lane) * WINDOW)

    def weight_lanes(self):
        cell, lane = table_index(LANES, LANES)
        half = self.ct * self.width
        wanted = jnp.where(lane < half, self.cell_of(lane), self.cells + self.cell_of(lane - half))
        return cell == wanted

    def panel_lanes(self):
        lane = lane_index(1)
        panel = lax.rem(lax.div(lane, self.rows), self.panels)
        return jnp.where(lane < self.ct * self.width, panel, -9).astype(jnp.float32)


def table_index(rows, columns):
    return [lax.broadcasted_iota(jnp.int32, (rows, columns), axis) for axis in (0, 1)]


def call(kernel, out, scratch=(), flops=2_000_000, nbytes=1_000_000):
    return pl.pallas_call(
        kernel,
        out_shape=out,
        scratch_shapes=list(scratch),
        compiler_params=pltpu.CompilerParams(vmem_limit_bytes=20 * 1024 * 1024),
        cost_estimate=pl.CostEstimate(flops=flops, bytes_accessed=nbytes, transcendentals=0),
    )


def f32(*shape):
    return jax.ShapeDtypeStruct(shape, jnp.float32)


def vmem(*shape):
    return pltpu.VMEM(shape, jnp.float32)


def halves_of(x):
    hi = x.astype(jnp.bfloat16)
    return hi, (x - hi.astype(jnp.float32)).astype(jnp.bfloat16)


def dot3(w, x):
    hi, lo = halves_of(x)
    return jnp.dot(w, jnp.concatenate([hi, hi, lo], axis=0), preferred_element_type=jnp.float32)


def pick(x, table):
    table = table.astype(jnp.float32).astype(jnp.bfloat16)
    table = jnp.concatenate([table, table], axis=0)
    return jnp.dot(jnp.concatenate(halves_of(x), axis=1), table, preferred_element_type=jnp.float32)


def dot_full(a, b):
    return jnp.dot(a, b, precision=HIGHEST, preferred_element_type=jnp.float32)


def lane_index(rows):
    return lax.broadcasted_iota(jnp.int32, (rows, LANES), 1)


def rolled(x, by):
    by %= LANES
    return pltpu.roll(x, by, axis=1) if by else x


def at(r, count=1, start=0):
    return slice(start + r * LANES, start + (r + count) * LANES)


def parity():
    return lax.rem(lax.axis_index("sector"), 2)


def has_sides(plan):
    span = lax.axis_index("span")
    return jnp.where(span < plan.spans - 1, 1.0, 0.0), jnp.where(span > 0, 1.0, 0.0)


class Layer:
    def __init__(self, plan, ref, start=0, rates=None, seam=None, layer=0):
        self.plan, self.ref, self.start, self.seam, self.layer = plan, ref, start, seam, layer
        self.rates = rates or (ref, start)

    def rate(self, which, r, count=1):
        if isinstance(self.rates, Layer):
            return self.rates.rate(which, r, count)
        ref, start = self.rates
        row = self.plan.pad + which
        return ref[row : row + 1, at(r, count, start)]

    def row(self, r):
        value = self.ref[: self.plan.pad, at(r, 1, self.start)]
        if self.seam is None:
            return value
        return value + placed(self.seam, self.layer * self.plan.rows + r) * self.rate(C_MASK, r)

    def chunk(self, c):
        count = CHUNK // LANES
        if self.seam is None:
            return self.ref[: self.plan.pad, at(c * count, count, self.start)]
        return jnp.concatenate([self.row(c * count + part) for part in range(count)], axis=1)


class Native(Layer):
    def __init__(self, plan, ref, table, seam, layer, near):
        super().__init__(plan, ref, 0, None, seam, layer)
        self.table, self.near = table, near

    def rate(self, which, r, count=1):
        row = which if self.near else C_OTHER
        return self.table[row : row + 1, at(r, count)]

    def row(self, r):
        plan = self.plan
        there = jnp.where(parity() == 1, self.layer, plan.ct - 1 - self.layer) * plan.rows + r
        field = self.ref[pl.ds(there, plan.tf, stride=plan.cells), :]
        field = jnp.concatenate([field, jnp.zeros((plan.pad - plan.tf, LANES), jnp.float32)], axis=0)
        if self.seam is not None:
            field = field + placed(self.seam, self.layer * plan.rows + r)
        return field * self.rate(C_MASK, r)


def placed(tile, cell):
    return jnp.where(lane_index(tile.shape[0]) == 0, rolled(tile, -cell * WINDOW), 0.0)


class Products:
    def __init__(self, plan, w_ref, p_ref, first):
        self.plan, self.w, self.p, self.first = plan, w_ref, p_ref, first

    def fill(self, layer):
        for c in range(self.plan.slab // CHUNK):
            self.p[:, c * CHUNK : (c + 1) * CHUNK] = dot3(matrix(self.plan, self.w, self.first, 6), layer.chunk(c))
        self.layer = layer
        return self

    def get(self, block, r):
        row = (block - self.first) * self.plan.pad
        return self.p[row : row + self.plan.pad, at(r)]

    def own_terms(self, r):
        rate = self.layer.rate
        total = rate(C_TIME, r) * self.get(SPECTRAL, r)
        beside = []
        if r + 1 < self.plan.rows:
            beside.append(self.get(UP_SP, r + 1))
        if r > 0:
            beside.append(self.get(DOWN_SP, r - 1))
        total = total + rate(C_SP, r) * sum(beside[1:], beside[0])
        total = total + rate(C_UP, r) * rolled(self.get(UP_AX, r), -1)
        return total + rate(C_DOWN, r) * rolled(self.get(DOWN_AX, r), 1)


def matrix(plan, w_ref, block, count=1):
    return w_ref[block * plan.pad : (block + count) * plan.pad, :]


def two_layers(plan, ref, rates=None, seam=None):
    return [
        Layer(plan, ref, a * plan.slab, (rates, a * plan.slab) if rates is not None else None, seam, a)
        for a in range(plan.ct)
    ]


def inner_rows(plan, w_ref, p_refs, layers, force, g_ref):
    first = Products(plan, w_ref, p_refs[0], DOWN_AZ).fill(layers[0])
    second = Products(plan, w_ref, p_refs[1], SPECTRAL).fill(layers[1])
    for r in range(plan.rows):
        other = second.get(UP_AZ, r), first.get(DOWN_AZ, r)
        for a, products in enumerate((first, second)):
            total = products.own_terms(r) + layers[a].rate(C_AZ, r) * other[a]
            if isinstance(g_ref, tuple):
                g_ref[a][:, at(r)] = force[a].row(r) - total
            else:
                g_ref[:, at(r, 1, a * plan.slab)] = force[a].row(r) - total


def azimuthal(plan, w_ref, block, chunk_of, take):
    for c in range(plan.slab // CHUNK):
        terms = dot3(matrix(plan, w_ref, block), chunk_of(c))
        for part in range(CHUNK // LANES):
            take(c * (CHUNK // LANES) + part, terms[:, at(part)])


def middle_rows(plan, w_ref, p_refs, own, own_force, g_ref, near, near_force, side, corner, y_ref, h_refs, n_refs):
    pad, rows, ct = plan.pad, plan.rows, plan.ct
    last = (rows - 1, 0)
    edge_terms, edge_new, corner_terms = [], [], []
    is_first = lax.axis_index("span") == 0

    def choose(n, above, below):
        return jnp.where(is_first, above, below) if plan.ends == 1 else (above, below)[n]

    for n in range(plan.ends):
        outward = choose(n, matrix(plan, w_ref, UP_SP), matrix(plan, w_ref, DOWN_SP))
        inward = choose(n, matrix(plan, w_ref, DOWN_SP), matrix(plan, w_ref, UP_SP))
        first, second, edge_force, edge_rate = side(n)
        corners = corner(n)
        every = dot3(w_ref[...], first)
        beyond = dot3(outward, second)
        within = [choose(n, x.row(last[0]), x.row(last[1])) for x in own]
        within = dot3(inward, jnp.concatenate(within, axis=1))
        from_low = dot3(matrix(plan, w_ref, DOWN_AZ), corners[0])
        from_high = dot3(matrix(plan, w_ref, UP_AZ), corners[1])
        new = []
        for a in range(ct):

            def part(block, b=a):
                return every[block * pad : (block + 1) * pad, at(b)]

            around = part(UP_AZ, 1) + from_low if a == 0 else from_high + part(DOWN_AZ, 0)
            total = edge_rate(C_TIME, a) * part(SPECTRAL) + edge_rate(C_AZ, a) * around
            total = total + edge_rate(C_SP, a) * (beyond[:, at(a)] + within[:, at(a)])
            total = total + edge_rate(C_UP, a) * rolled(part(UP_AX), -1)
            total = total + edge_rate(C_DOWN, a) * rolled(part(DOWN_AX), 1)
            new.append(edge_force[:, at(a)] - total)
        of_edge = choose(n, *(every[block * pad : (block + 1) * pad] for block in (UP_SP, DOWN_SP)))
        of_new = dot3(outward, jnp.concatenate(new, axis=1))
        of_corners = dot3(outward, jnp.concatenate(corners, axis=1))
        for keep in has_sides(plan) if plan.ends == 1 else (1.0,):
            edge_terms.append(of_edge * keep)
            edge_new.append(of_new * keep)
            corner_terms.append([of_corners[:, at(a)] * keep for a in range(ct)])

    products = (
        Products(plan, w_ref, p_refs[0], DOWN_AZ).fill(near[0]), Products(plan, w_ref, p_refs[1], SPECTRAL).fill(near[1]),
    )
    for a, (to_own, to_near) in enumerate(((DOWN_AZ, UP_AZ), (UP_AZ, DOWN_AZ))):

        def take(r, terms):
            total = products[a].own_terms(r) + near[a].rate(C_AZ, r) * terms
            mine = own[a].rate(C_AZ, r) * products[a].get(to_own, r)
            for n in range(2):
                if r == last[n]:
                    total = total + near[a].rate(C_SP, r) * corner_terms[n][a]
                    mine = mine + own[a].rate(C_SP, r) * edge_terms[n][:, at(a)]
            n_refs[a][:, at(r)] = near_force[a].row(r) - total
            lanes = at(r, 1, a * plan.slab)
            y_ref[:, lanes] = g_ref[:, lanes] - mine

        azimuthal(plan, w_ref, to_near, own[a].chunk, take)

    after = [Layer(plan, y_ref, a * plan.slab, own[a].rates) for a in range(ct)]
    inner_rows(plan, w_ref, p_refs, after, own_force, h_refs)
    for a in range(ct):
        for n in range(2):
            h_refs[a][:, at(last[n])] -= own[a].rate(C_SP, last[n]) * edge_new[n][:, at(a)]


def outer_rows(plan, w_ref, own, near, far_chunks, n_refs, h_refs, put, layers=(0, 1)):
    count = CHUNK // LANES
    for a in layers:
        block = (DOWN_AZ, UP_AZ)[a]

        def near_chunk(c):
            terms = dot3(matrix(plan, w_ref, block), far_chunks[a](c))
            return n_refs[a][:, at(c * count, count)] - near[a].rate(C_AZ, c * count, count) * terms

        def take(r, terms):
            put(a, r, h_refs[a][:, at(r)] - own[a].rate(C_AZ, r) * terms)

        azimuthal(plan, w_ref, block, near_chunk, take)


def sides_of(plan, side_ref, force_ref, seams_ref):
    pad, ct = plan.pad, plan.ct
    keeps = (1.0,) if plan.ends == 1 else has_sides(plan)
    is_first = lax.axis_index("span") == 0

    def inlet(n, e, a):
        above, below = a * plan.rows + e, a * plan.rows + plan.rows - 1 - e
        tile = seams_ref[1, 1 + n]
        if plan.ends == 1:
            return jnp.where(is_first, placed(tile, above), placed(tile, below))
        return placed(tile, (above, below)[n])

    def read(n, ref, e, seam):
        value = ref[n, :pad, at(e * ct, ct)]
        if seam:
            scale = ref[n, pad + C_MASK : pad + C_MASK + 1, at(e * ct, ct)]
            value = value + jnp.concatenate([inlet(n, e, a) for a in range(ct)], axis=1) * scale
        return value * keeps[n]

    def side(n):
        same = side_ref is force_ref

        def rate(which, a):
            return force_ref[n, pad + which : pad + which + 1, at(a)] * keeps[n]

        force = read(n, force_ref, 0, True)
        first = force if same else read(n, side_ref, 0, False)
        return first, read(n, side_ref, 1, same), force, rate

    return side


def corners_of(plan, c_refs, seams_ref):
    keeps = (1.0,) if plan.ends == 1 else has_sides(plan)
    is_first = lax.axis_index("span") == 0

    def corner(n):
        out = []
        for a in range(plan.ct):
            if seams_ref is None:
                value = c_refs[a][n, : plan.pad]
            else:
                value = c_refs[n, : plan.pad, at(a)]
                tile = seams_ref[2 * a, 1 + n]
                above, below = (placed(tile, a * plan.rows + r) for r in (0, plan.rows - 1))
                inlet = jnp.where(is_first, above, below) if plan.ends == 1 else (above, below)[n]
                value = value + inlet * c_refs[n, plan.pad + C_MASK : plan.pad + C_MASK + 1, at(a)]
            out.append(value * keeps[n])
        return out

    return corner


def prepare(plan, rhs_ref, coef_ref, m_ref, table0_ref, table1_ref, side_ref, rates_ref):
    pad, cells = plan.pad, plan.cells
    mask, diag, time, *face = [coef_ref[cells * i : cells * (i + 1), :] for i in range(6)]
    scale = mask / diag
    lane = lane_index(cells)
    axial = scale * face[2]
    rates = (
        scale * time, scale * face[0], scale * face[1],
        jnp.where(lane < LANES - 1, axial, 0.0), jnp.where(lane > 0, axial, 0.0), scale,
    )
    for i, rate in enumerate(rates):
        rates_ref[i] = rate
    tail = jnp.zeros((pad - plan.tf, LANES), jnp.float32)
    rest = jnp.zeros((RATES - 6, LANES), jnp.float32)
    mirror = parity()
    for cell in range(cells):
        a, r = divmod(cell, plan.rows)
        there = jnp.where(mirror == 0, a, plan.ct - 1 - a) * plan.rows + r
        table = [rates_ref[i, pl.ds(there, 1), :] for i in range(6)]
        field = jnp.concatenate([rhs_ref[pl.ds(there, plan.tf, stride=cells), :], tail], axis=0)
        m_ref[:pad, at(cell)] = field * table[C_MASK]
        m_ref[pad:, at(cell)] = jnp.concatenate(table + [rest], axis=0)
        other = jnp.where(mirror == 0, plan.ct - 1 - a, a) * plan.rows + r
        table = table + [rates_ref[C_MASK, pl.ds(other, 1), :], rest[:1]]
        (table0_ref, table1_ref)[a][:, at(r)] = jnp.concatenate(table, axis=0)
    write_edges(plan, m_ref, side_ref, None)


def write_edges(plan, x_ref, side_ref, c_refs):
    first = lax.axis_index("span") == 0
    for a in range(plan.ct):
        for e in range(DEPTH):
            low, high = x_ref[:, at(a * plan.rows + e)], x_ref[:, at((a + 1) * plan.rows - 1 - e)]
            ends = [jnp.where(first, high, low)] if plan.ends == 1 else [low, high]
            for n, end in enumerate(ends):
                side_ref[n, :, at(e * plan.ct + a)] = end
                if e == 0 and c_refs:
                    c_refs[a][n] = end


def corner_rows(plan, low_ref, high_ref, low_table, high_table, c_ref):
    first = lax.axis_index("span") == 0
    near = Native(plan, low_ref, low_table, None, 0, True), Native(plan, high_ref, high_table, None, 1, True)
    for a, layer in enumerate(near):
        ends = []
        for r in (0, plan.rows - 1):
            rates = [layer.rate(C_MASK, r) if i == C_MASK else jnp.zeros((1, LANES), jnp.float32) for i in range(RATES)]
            ends.append(jnp.concatenate([layer.row(r)] + rates, axis=0))
        if plan.ends == 1:
            ends = [jnp.where(first, ends[1], ends[0])]
        for n, end in enumerate(ends):
            c_ref[n, :, at(a)] = end


def stack_matrices(plan, up_ref, down_ref, spectral_ref, rows_ref, lanes_ref, diagonal_ref, out_ref, down_out):
    pad = plan.pad
    lane = lax.broadcasted_iota(jnp.int32, (pad, 3 * pad), 1)
    second = (lane >= pad) & (lane < 2 * pad)
    out_ref[SPECTRAL * pad : (SPECTRAL + 1) * pad, :] = spectral_ref[...]
    even = parity() == 0
    for block, small in (
        (DOWN_AZ, jnp.where(even, down_ref[0], up_ref[0])), (UP_AZ, jnp.where(even, up_ref[0], down_ref[0])),
        (UP_SP, up_ref[1]), (DOWN_SP, down_ref[1]), (UP_AX, up_ref[2]), (DOWN_AX, down_ref[2]),
    ):
        full = dot_full(dot_full(rows_ref[...], small), lanes_ref[...]) * diagonal_ref[...]
        hi = full.astype(jnp.bfloat16).astype(jnp.float32)
        out_ref[block * pad : (block + 1) * pad, :] = jnp.where(second, full - hi, hi).astype(jnp.bfloat16)
    down_out[...] = matrix(plan, out_ref, DOWN_AZ)


def send_panels(plan, stator_ref, both_ref, out_ref, panels_ref):
    me = lax.axis_index("sector")
    for f in range(plan.fields):
        panels_ref[pl.ds(f, plan.insts, stride=RATES), : plan.width] = jnp.transpose(stator_ref[f])
    out_ref[...] = jnp.zeros_like(out_ref)
    for t, (row, start) in enumerate(plan.weight_at):
        both = jnp.broadcast_to(both_ref[t : t + 1, :][None], (out_ref.shape[0], 1, plan.width))
        out_ref[:, row : row + 1, start : start + plan.width] = both
    for o, slots in enumerate(plan.slots):
        to = lax.rem(me + (plan.sectors - o), plan.sectors) * plan.spans
        for slot, t in enumerate(slots):
            lanes = slice(slot * plan.width, (slot + 1) * plan.width)
            panels = panels_ref[t * RATES : t * RATES + plan.fields, : plan.width]
            for x in range(plan.spans):
                out_ref[to + x, : plan.fields, lanes] = panels


def begin(
    plan, w_ref, m_ref, got_ref,
    seams_ref, weight_ref, x_ref, g_ref, panels_ref, terms_ref, rows_ref, p0_ref, p1_ref,
):
    pad, insts, fields = plan.pad, plan.insts, plan.fields
    me, span = lax.axis_index("sector"), lax.axis_index("span")
    even, is_first = parity() == 0, span == 0
    tiles = plan.tiles
    panels_ref[...] = jnp.zeros_like(panels_ref)
    rows_ref[...] = jnp.zeros_like(rows_ref)
    for n, (k, x) in enumerate(tiles):
        at_span = x if plan.spans == 2 else jnp.clip(span + x, 0, plan.spans - 1)
        for t in range(insts):
            o = (k + plan.shift[t]) % plan.sectors
            source = lax.rem(me + o, plan.sectors) * plan.spans + at_span
            tile = rolled(got_ref[source], -plan.slots[o].index(t) * plan.width)
            panels_ref[t * fields : (t + 1) * fields, n * LANES : n * LANES + plan.width] = tile[:fields, : plan.width]
        tile = got_ref[lax.rem(me + k + plan.sectors, plan.sectors) * plan.spans + at_span]
        lanes = slice(n * LANES, n * LANES + plan.width)
        rows_ref[:fields, lanes] = rolled(tile, -plan.weight_at[0][1])[:fields, : plan.width]
        for t in range(fields, insts):
            row, start = plan.weight_at[t]
            rows_ref[t : t + 1, lanes] = rolled(tile, -start)[row : row + 1, : plan.width]
    spread = dot_full(plan.inst_rows(), rows_ref[...])
    spread = pick(jnp.concatenate([spread[:, at(n)] for n in range(len(tiles))], axis=0), plan.weight_lanes())
    first, share, panel = spread, rolled(spread, plan.ct * plan.width), plan.panel_lanes()
    lower = (jnp.abs(first - panel) < 0.5).astype(jnp.float32)
    upper = (jnp.abs(first + 1.0 - panel) < 0.5).astype(jnp.float32)
    weights = share * lower + (1.0 - share) * upper
    for n in range(len(tiles)):
        panels = panels_ref[:, at(n)]
        terms_ref[n * pad : (n + 1) * pad, :] = panels + rolled(panels, plan.width)
    seams = pick(terms_ref[...] * weights, plan.window_lanes())

    def tile(values, k, x):
        n = tiles.index((k, x))
        return values[n * pad : (n + 1) * pad]

    def around(values, k):
        if plan.spans == 2:
            pair = tile(values, k, 0), tile(values, k, 1)
            return [jnp.where(is_first, pair[0], pair[1]), jnp.where(is_first, pair[1], pair[0])]
        return [tile(values, k, x) for x in (0, 1, -1)]

    def mirrored(value):
        return rolled(value, LANES // 2)

    here = around(seams, 0)
    behind, ahead = around(seams, -1), around(seams, 1)
    for i in range(1 + plan.ends):
        seams_ref[0, i] = jnp.where(even, mirrored(behind[i]), ahead[i])
        seams_ref[1, i] = jnp.where(even, here[i], mirrored(here[i]))
        seams_ref[2, i] = jnp.where(even, mirrored(ahead[i]), behind[i])
    weight_ref[...] = around(weights, 0)[0]

    for layer in two_layers(plan, m_ref, seam=seams_ref[1, 0]):
        for r in range(plan.rows):
            x_ref[:, at(r, 1, layer.start)] = layer.row(r)
    layers = two_layers(plan, x_ref, m_ref)
    inner_rows(plan, w_ref, (p0_ref, p1_ref), layers, layers, g_ref)


def first_half(
    plan, w_ref, m_ref, f_ref, g_ref, low_ref, high_ref, low_table, high_table, side_ref, corner_ref, seams_ref,
    x_ref, near_ref, side_out, c0_ref, c1_ref, p0_ref, p1_ref, y_ref, h0_ref, h1_ref, n0_ref, n1_ref, inlet_ref,
):
    own = two_layers(plan, f_ref, m_ref)
    low = [Native(plan, low_ref, low_table, seams_ref[0, 0], a, a == 0) for a in range(plan.ct)]
    high = [Native(plan, high_ref, high_table, seams_ref[2, 0], a, a == 1) for a in range(plan.ct)]
    near = low[0], high[1]
    n_refs = n0_ref, n1_ref
    middle_rows(
        plan, w_ref, (p0_ref, p1_ref), own, own, g_ref, near, near, sides_of(plan, side_ref, side_ref, seams_ref),
        corners_of(plan, corner_ref, seams_ref), y_ref, (h0_ref, h1_ref), n_refs,
    )
    lane = lane_index(plan.pad)
    inlet_ref[...] = jnp.zeros_like(inlet_ref)

    def put(a, r, value):
        x_ref[:, at(r, 1, a * plan.slab)] = value
        if a == 0:
            near_ref[:, at(r)] = value
        else:
            inlet_ref[: plan.pad, :] = jnp.where(lane == r, rolled(value, r), inlet_ref[: plan.pad, :])

    outer_rows(plan, w_ref, own, near, (low[1].chunk, high[0].chunk), n_refs, (h0_ref, h1_ref), put)
    turned = jnp.transpose(inlet_ref[...])
    for r in range(plan.rows):
        near_ref[plan.tf : plan.tf + 1, at(r)] = turned[r : r + 1, :]
    write_edges(plan, x_ref, side_out, (c0_ref, c1_ref))


def hold_far(plan, x_ref, side_ref, c_high, far_ref):
    come = side_ref[0, 0:1, 0:1] + c_high[0, 0:1, 0:1]
    far_ref[...] = x_ref[:, plan.slab :] + 0.0 * come


def inner(plan, w_ref, m_ref, f_ref, x_ref, g_ref, p0_ref, p1_ref):
    inner_rows(plan, w_ref, (p0_ref, p1_ref), two_layers(plan, x_ref, m_ref), two_layers(plan, f_ref, m_ref), g_ref)


def middle(
    plan, w_ref, m_ref, f_ref, x_ref, g_ref, low_ref, high_ref, side_ref, c_low, c_high,
    low_first, high_first, low_table, high_table, side_first, seams_ref, weight_ref,
    send_ref, n0_ref, h0_ref, x1_ref, rates_ref, p0_ref, p1_ref, y_ref, h1_ref, n1_ref, turn_ref,
):
    pad = plan.pad
    own, force = two_layers(plan, x_ref, m_ref), two_layers(plan, f_ref, m_ref)
    low_force = Native(plan, low_first, low_table, seams_ref[0, 0], 0, True)
    high_force = Native(plan, high_first, high_table, seams_ref[2, 0], 1, True)
    near = Layer(plan, low_ref, 0, low_force), Layer(plan, high_ref, plan.slab, high_force)
    n_refs = n0_ref, n1_ref
    middle_rows(
        plan, w_ref, (p0_ref, p1_ref), own, force, g_ref, near, (low_force, high_force),
        sides_of(plan, side_ref, side_first, seams_ref), corners_of(plan, (c_low, c_high), None), y_ref,
        (h0_ref, h1_ref), n_refs,
    )

    def put(a, r, value):
        x1_ref[:, at(r)] = value

    outer_rows(plan, w_ref, own, near, (None, Layer(plan, high_ref).chunk), n_refs, (h0_ref, h1_ref), put, (1,))
    for r in range(plan.rows):
        last = [near[0].rate(C_AZ, r), own[0].rate(C_AZ, r), jnp.zeros((RATES - 2, LANES), jnp.float32)]
        rates_ref[:, at(r)] = jnp.concatenate(last, axis=0)

    turn_ref[...] = jnp.zeros_like(turn_ref)
    for r in range(plan.rows):
        turn_ref[r : r + 1, :] = low_ref[plan.tf : plan.tf + 1, at(r)]
    far = jnp.transpose(turn_ref[...])[:pad]

    def packed(read, count, first=0, step=1):
        lane = lane_index(count)
        out = jnp.zeros((count, LANES), jnp.float32)
        for r in range(plan.rows):
            to = first + r * step
            out = jnp.where(lane == to, rolled(read(r), to), out)
        return out

    rates = packed(lambda r: rates_ref[:, at(r)], RATES)
    inlet = packed(lambda r: n0_ref[:, at(r)], pad) - rates[0:1] * dot3(matrix(plan, w_ref, DOWN_AZ), far)
    inlet = packed(lambda r: h0_ref[:, at(r)], pad) - rates[1:2] * dot3(matrix(plan, w_ref, DOWN_AZ), inlet)
    lane = lane_index(pad)
    spread = packed(lambda r: x1_ref[:, at(r)], pad, plan.rows * WINDOW, WINDOW)
    for r in range(plan.rows):
        spread = jnp.where(lane == r * WINDOW, rolled(inlet, r * (WINDOW - 1)), spread)
    inlet = jnp.where(parity() == 0, spread, rolled(spread, LANES // 2))
    back = pick(inlet, plan.window_spread()) * weight_ref[...]
    back = back + rolled(back, -plan.width)
    me = lax.axis_index("sector")
    send_ref[...] = jnp.zeros_like(send_ref)
    for t in range(plan.insts):
        to = lax.rem(me + plan.shift[t], plan.sectors)
        send_ref[to, : plan.fields, : plan.width] = back[t * plan.fields : (t + 1) * plan.fields, : plan.width]


def outer(plan, w_ref, rates_ref, n0_ref, h0_ref, x1_ref, far_ref, out_ref):
    mirror = parity()

    def put(a, r, value):
        there = jnp.where(mirror == 0, a, plan.ct - 1 - a) * plan.rows + r
        out_ref[pl.ds(there, plan.tf, stride=plan.cells), :] = value[: plan.tf]

    for r in range(plan.rows):
        put(1, r, x1_ref[:, at(r)])

    def near_chunk(c):
        lanes = slice(c * CHUNK, (c + 1) * CHUNK)
        return n0_ref[:, lanes] - rates_ref[0:1, lanes] * dot3(w_ref[...], far_ref[:, lanes])

    azimuthal(plan, w_ref, 0, near_chunk, lambda r, terms: put(0, r, h0_ref[:, at(r)] - rates_ref[1:2, at(r)] * terms))


def collect_panels(plan, got_ref, out_ref, panels_ref):
    me = lax.axis_index("sector")
    for t in range(plan.insts):
        source = lax.rem(me + (plan.sectors - plan.shift[t]), plan.sectors)
        panels_ref[t * RATES : (t + 1) * RATES, :] = got_ref[source]
    for f in range(plan.fields):
        tile = panels_ref[pl.ds(f, plan.insts, stride=RATES), : plan.width]
        out_ref[f] = jnp.transpose(tile)


def sibling(plan):
    return [s ^ 1 for s in range(plan.sectors)]


def outside(plan):
    return [(s - 1 if s % 2 == 0 else s + 1) % plan.sectors for s in range(plan.sectors)]


def swap(array, partner):
    return lax.ppermute(array, "sector", list(enumerate(partner)))


def beside(plan, array, partner):
    def pairs(step):
        out = []
        for s in range(plan.sectors):
            for x in range(plan.spans):
                to = 1 - x if plan.ends == 1 else x + step
                if 0 <= to < plan.spans:
                    out.append((s * plan.spans + x, partner[s] * plan.spans + to))
        return out

    if plan.ends == 1:
        return lax.ppermute(array, AXES, pairs(0))
    return jnp.concatenate([lax.ppermute(array[:1], AXES, pairs(-1)), lax.ppermute(array[1:], AXES, pairs(1))])


def on_device(
    sectors, spans,
    rhs, diag_coef, face_coef, time_coef, jac_up, jac_down, wall_mask, stator_adj, owner, first_panel_share,
):
    plan = Plan(rhs, stator_adj, sectors, spans)
    pad, cells, slab, insts, fields, ends = plan.pad, plan.cells, plan.slab, plan.insts, plan.fields, plan.ends
    bind = functools.partial
    whole, half = f32(pad, plan.ct * slab), f32(pad, slab)
    products = (vmem(6 * pad, slab),) * 2
    alone, next_chip, next_core = list(range(sectors)), outside(plan), sibling(plan)

    def edges(rows):
        return f32(ends, rows, DEPTH * plan.ct * LANES), f32(ends, rows, LANES), f32(ends, rows, LANES)

    stator = jnp.transpose(stator_adj, (1, 2, 3, 0)).reshape(fields, plan.width, insts)
    sent = call(bind(send_panels, plan), f32(sectors * spans, RATES, LANES), (vmem(insts * RATES, LANES),))(
        stator,
        jnp.concatenate([
            lax.rem(owner, plan.panels).astype(jnp.float32).reshape(insts, cells), first_panel_share.reshape(insts, cells),
        ], axis=1),
    )
    got = lax.all_to_all(sent, AXES, 0, 0, tiled=True)
    native = rhs.reshape(plan.tf * cells, LANES)
    low_first, high_first = swap(native, next_chip), swap(native, next_core)
    m, table0, table1, side = call(
        bind(prepare, plan),
        (f32(pad + RATES, plan.ct * slab), f32(RATES, slab), f32(RATES, slab)) + edges(pad + RATES)[:1],
        (vmem(6, cells, LANES),),
    )(
        native,
        jnp.concatenate([
            wall_mask.astype(jnp.float32).reshape(cells, LANES), diag_coef.reshape(cells, LANES),
            time_coef.reshape(cells, LANES), face_coef.reshape(3 * cells, LANES),
        ]),
    )
    low_table, high_table = swap(table0, next_chip), swap(table1, next_core)
    side_first = beside(plan, side, alone)
    corner = call(bind(corner_rows, plan), f32(ends, pad + RATES, plan.ct * LANES))(
        low_first, high_first, low_table, high_table
    )
    corner = beside(plan, corner, alone)
    matrices, down = call(
        bind(stack_matrices, plan),
        [jax.ShapeDtypeStruct((count * pad, 3 * pad), jnp.bfloat16) for count in (7, 1)],
    )(jac_up, jac_down, plan.spectral(), plan.field_rows(), plan.field_lanes(), plan.block_diagonal())
    tiles = len(plan.tiles)
    seams, weight, force, g = call(
        bind(begin, plan), (f32(3, 1 + ends, pad, LANES), f32(pad, LANES), whole, whole),
        (vmem(pad, tiles * LANES), vmem(tiles * pad, LANES), vmem(16, tiles * LANES)) + products,
        flops=2_000_000_000,
    )(matrices, m, got)
    x, near, side, c0, c1 = call(
        bind(first_half, plan), (whole, half) + edges(pad),
        products + (vmem(pad, 2 * slab),) + (vmem(pad, slab),) * 4 + (vmem(LANES, LANES),),
        flops=4_000_000_000,
    )(matrices, m, force, g, low_first, high_first, low_table, high_table, side_first, corner, seams)

    low, high = swap(near, next_chip), swap(x, next_core)
    side = beside(plan, side, alone)
    c_low, c_high = beside(plan, c0, next_chip), beside(plan, c1, next_core)
    (g,) = call(bind(inner, plan), (whole,), products, flops=2_000_000_000)(matrices, m, force, x)
    far = call(bind(hold_far, plan), half)(x, side, c_high)
    far_low = swap(far, next_chip)
    back, n0, h0, x1, rates = call(
        bind(middle, plan), (f32(sectors, RATES, LANES), half, half, half, f32(RATES, slab)),
        products + (vmem(pad, 2 * slab), vmem(pad, slab), vmem(pad, slab), vmem(LANES, LANES)),
        flops=4_000_000_000,
    )(
        matrices, m, force, x, g, low, high, side, c_low, c_high, low_first, high_first, low_table, high_table, side_first,
        seams, weight,
    )
    returned = lax.all_to_all(back, "sector", 0, 0, tiled=True)
    sens = call(bind(collect_panels, plan), f32(fields, plan.width, insts), (vmem(insts * RATES, LANES),))(returned)
    out = call(bind(outer, plan), f32(plan.tf * cells, LANES))(down, rates, n0, h0, x1, far_low)
    sens = jnp.transpose(sens.reshape(fields, plan.panels, plan.rows, insts), (3, 0, 1, 2))
    return out.reshape(rhs.shape), sens


def solution(mesh):
    in_specs = (
        P(None, None, "sector", "span", None),
        P("sector", "span", None),
        P(None, "sector", "span", None),
        P("sector", "span", None),
        P(),
        P(),
        P("sector", "span", None),
        P(None, None, "sector", "span"),
        P(None, "sector", "span"),
        P(None, "sector", "span"),
    )
    out_specs = (P(None, None, "sector", "span", None), P(None, None, "sector", "span"))
    return jax.shard_map(
        functools.partial(on_device, mesh.shape["sector"], mesh.shape["span"]),
        mesh=mesh, in_specs=in_specs, out_specs=out_specs, check_vma=False,
    )
```

```python
import functools

import jax
import jax.numpy as jnp
import ml_dtypes
import numpy as np
from jax import lax
from jax.experimental import pallas as pl
from jax.experimental.pallas import tpu as pltpu
from jax.sharding import PartitionSpec as P

SWEEPS = 4
DEPTH = 2
LANES = 128
CHUNK = 256
WINDOW = 8
HIGHEST = lax.Precision.HIGHEST
DOWN_AZ, SPECTRAL, UP_SP, DOWN_SP, UP_AX, DOWN_AX, UP_AZ = range(7)
C_TIME, C_AZ, C_SP, C_UP, C_DOWN, C_MASK, C_OTHER = range(7)
RATES = 8
AXES = ("sector", "span")


class Plan:
    def __init__(self, rhs, stator_adj, sectors, spans):
        self.insts, self.fields, self.ct, self.rows, self.nax = rhs.shape
        self.panels = stator_adj.shape[2]
        self.sectors, self.spans = sectors, spans
        self.tf = self.insts * self.fields
        self.pad = -(-self.tf // 16) * 16
        self.cells = self.ct * self.rows
        self.slab = self.rows * LANES
        self.width = self.panels * self.rows
        self.shift = [
            ((t * sectors) // (self.insts - 1) - t // (self.insts - 1)) % sectors for t in range(self.insts)
        ]
        assert self.ct == 2 and self.nax == LANES and SWEEPS % DEPTH == 0 and spans > 1
        assert len(set(self.shift)) == self.insts and self.cells * WINDOW == LANES and self.rows >= SWEEPS
        assert self.slab % CHUNK == 0 and 3 * self.pad <= 256 and 2 * self.ct * self.width == LANES
        assert sectors % 2 == 0
        self.ends = 1 if spans == 2 else 2
        self.blocks = [-1, 0, 1]
        self.halves = [0, 1] if spans == 2 else [-1, 0, 1]
        self.tiles = [(k, x) for k in self.blocks for x in self.halves]
        self.slots = [
            [t for t in range(self.insts) if any((k + self.shift[t]) % sectors == o for k in self.blocks)]
            for o in range(sectors)
        ]
        last = LANES - self.width
        self.weight_at = [(t, last) for t in range(self.fields)] + [
            (self.fields, i * self.width) for i in range(self.insts - self.fields)
        ]
        assert max(map(len, self.slots)) * self.width <= last and 2 * self.cells == self.width
        assert self.fields == RATES - 1 and (self.insts - self.fields) * self.width <= LANES

    def spectral(self):
        t = np.arange(self.insts)
        off = t[:, None] - t[None, :]
        sines = np.where(off == 0, 1.0, np.sin(np.pi * off / self.insts))
        table = np.where(off == 0, 0.0, 0.5 * (1.0 - 2.0 * (off % 2)) / sines).astype(np.float32)
        full = np.zeros((self.pad, self.pad), np.float32)
        full[: self.tf, : self.tf] = np.kron(table.T, np.eye(self.fields, dtype=np.float32))
        hi = full.astype(ml_dtypes.bfloat16)
        lo = (full - hi.astype(np.float32)).astype(ml_dtypes.bfloat16)
        return np.concatenate([hi, lo, hi], axis=1)

    def field_rows(self):
        out = np.zeros((self.pad, self.fields), np.float32)
        out[np.arange(self.tf), np.arange(self.tf) % self.fields] = 1.0
        return out

    def field_lanes(self):
        return np.tile(self.field_rows().T, (1, 3))

    def block_diagonal(self):
        block = np.full(self.pad, -1)
        block[: self.tf] = np.arange(self.tf) // self.fields
        same = (block[:, None] == block[None, :]) & (block[:, None] >= 0)
        return np.tile(same.astype(np.float32), (1, 3))


    def inst_rows(self):
        row, inst = table_index(self.pad, 16)
        return ((row >= inst * self.fields) & (row < (inst + 1) * self.fields)).astype(jnp.float32)

    def cell_of(self, lane):
        return lax.div(lane, self.width) * self.rows + lax.rem(lane, self.rows)

    def window_lanes(self):
        lane, to = table_index(LANES, LANES)
        return (lane < self.ct * self.width) & (to == self.cell_of(lane) * WINDOW)

    def window_spread(self):
        to, lane = table_index(LANES, LANES)
        return (lane < self.ct * self.width) & (to == self.cell_of(lane) * WINDOW)

    def weight_lanes(self):
        cell, lane = table_index(LANES, LANES)
        half = self.ct * self.width
        wanted = jnp.where(lane < half, self.cell_of(lane), self.cells + self.cell_of(lane - half))
        return cell == wanted

    def panel_lanes(self):
        lane = lane_index(1)
        panel = lax.rem(lax.div(lane, self.rows), self.panels)
        return jnp.where(lane < self.ct * self.width, panel, -9).astype(jnp.float32)


def table_index(rows, columns):
    return [lax.broadcasted_iota(jnp.int32, (rows, columns), axis) for axis in (0, 1)]


def call(kernel, out, scratch=(), flops=2_000_000, nbytes=1_000_000):
    return pl.pallas_call(
        kernel,
        out_shape=out,
        scratch_shapes=list(scratch),
        compiler_params=pltpu.CompilerParams(vmem_limit_bytes=20 * 1024 * 1024),
        cost_estimate=pl.CostEstimate(flops=flops, bytes_accessed=nbytes, transcendentals=0),
    )


def f32(*shape):
    return jax.ShapeDtypeStruct(shape, jnp.float32)


def vmem(*shape):
    return pltpu.VMEM(shape, jnp.float32)


def halves_of(x):
    hi = x.astype(jnp.bfloat16)
    return hi, (x - hi.astype(jnp.float32)).astype(jnp.bfloat16)


def dot3(w, x):
    hi, lo = halves_of(x)
    return jnp.dot(w, jnp.concatenate([hi, hi, lo], axis=0), preferred_element_type=jnp.float32)


def pick(x, table):
    table = table.astype(jnp.float32).astype(jnp.bfloat16)
    table = jnp.concatenate([table, table], axis=0)
    return jnp.dot(jnp.concatenate(halves_of(x), axis=1), table, preferred_element_type=jnp.float32)


def dot_full(a, b):
    return jnp.dot(a, b, precision=HIGHEST, preferred_element_type=jnp.float32)


def lane_index(rows):
    return lax.broadcasted_iota(jnp.int32, (rows, LANES), 1)


def rolled(x, by):
    by %= LANES
    return pltpu.roll(x, by, axis=1) if by else x


def at(r, count=1, start=0):
    return slice(start + r * LANES, start + (r + count) * LANES)


def parity():
    return lax.rem(lax.axis_index("sector"), 2)


def has_sides(plan):
    span = lax.axis_index("span")
    return jnp.where(span < plan.spans - 1, 1.0, 0.0), jnp.where(span > 0, 1.0, 0.0)


class Layer:
    def __init__(self, plan, ref, start=0, rates=None, seam=None, layer=0):
        self.plan, self.ref, self.start, self.seam, self.layer = plan, ref, start, seam, layer
        self.rates = rates or (ref, start)

    def rate(self, which, r, count=1):
        if isinstance(self.rates, Layer):
            return self.rates.rate(which, r, count)
        ref, start = self.rates
        row = self.plan.pad + which
        return ref[row : row + 1, at(r, count, start)]

    def row(self, r):
        value = self.ref[: self.plan.pad, at(r, 1, self.start)]
        if self.seam is None:
            return value
        return value + placed(self.seam, self.layer * self.plan.rows + r) * self.rate(C_MASK, r)

    def chunk(self, c):
        count = CHUNK // LANES
        if self.seam is None:
            return self.ref[: self.plan.pad, at(c * count, count, self.start)]
        return jnp.concatenate([self.row(c * count + part) for part in range(count)], axis=1)


class Native(Layer):
    def __init__(self, plan, ref, table, seam, layer, near):
        super().__init__(plan, ref, 0, None, seam, layer)
        self.table, self.near = table, near

    def rate(self, which, r, count=1):
        row = which if self.near else C_OTHER
        return self.table[row : row + 1, at(r, count)]

    def row(self, r):
        plan = self.plan
        there = jnp.where(parity() == 1, self.layer, plan.ct - 1 - self.layer) * plan.rows + r
        field = self.ref[pl.ds(there, plan.tf, stride=plan.cells), :]
        field = jnp.concatenate([field, jnp.zeros((plan.pad - plan.tf, LANES), jnp.float32)], axis=0)
        if self.seam is not None:
            field = field + placed(self.seam, self.layer * plan.rows + r)
        return field * self.rate(C_MASK, r)


def placed(tile, cell):
    return jnp.where(lane_index(tile.shape[0]) == 0, rolled(tile, -cell * WINDOW), 0.0)


class Products:
    def __init__(self, plan, w_ref, p_ref, first):
        self.plan, self.w, self.p, self.first = plan, w_ref, p_ref, first

    def fill(self, layer):
        for c in range(self.plan.slab // CHUNK):
            self.p[:, c * CHUNK : (c + 1) * CHUNK] = dot3(matrix(self.plan, self.w, self.first, 6), layer.chunk(c))
        self.layer = layer
        return self

    def get(self, block, r):
        row = (block - self.first) * self.plan.pad
        return self.p[row : row + self.plan.pad, at(r)]

    def own_terms(self, r):
        rate = self.layer.rate
        total = rate(C_TIME, r) * self.get(SPECTRAL, r)
        beside = []
        if r + 1 < self.plan.rows:
            beside.append(self.get(UP_SP, r + 1))
        if r > 0:
            beside.append(self.get(DOWN_SP, r - 1))
        total = total + rate(C_SP, r) * sum(beside[1:], beside[0])
        total = total + rate(C_UP, r) * rolled(self.get(UP_AX, r), -1)
        return total + rate(C_DOWN, r) * rolled(self.get(DOWN_AX, r), 1)


def matrix(plan, w_ref, block, count=1):
    return w_ref[block * plan.pad : (block + count) * plan.pad, :]


def two_layers(plan, ref, rates=None, seam=None):
    return [
        Layer(plan, ref, a * plan.slab, (rates, a * plan.slab) if rates is not None else None, seam, a)
        for a in range(plan.ct)
    ]


def inner_rows(plan, w_ref, p_refs, layers, force, g_ref):
    first = Products(plan, w_ref, p_refs[0], DOWN_AZ).fill(layers[0])
    second = Products(plan, w_ref, p_refs[1], SPECTRAL).fill(layers[1])
    for r in range(plan.rows):
        other = second.get(UP_AZ, r), first.get(DOWN_AZ, r)
        for a, products in enumerate((first, second)):
            total = products.own_terms(r) + layers[a].rate(C_AZ, r) * other[a]
            if isinstance(g_ref, tuple):
                g_ref[a][:, at(r)] = force[a].row(r) - total
            else:
                g_ref[:, at(r, 1, a * plan.slab)] = force[a].row(r) - total


def azimuthal(plan, w_ref, block, chunk_of, take):
    for c in range(plan.slab // CHUNK):
        terms = dot3(matrix(plan, w_ref, block), chunk_of(c))
        for part in range(CHUNK // LANES):
            take(c * (CHUNK // LANES) + part, terms[:, at(part)])


def middle_rows(plan, w_ref, p_refs, own, own_force, g_ref, near, near_force, side, corner, y_ref, h_refs, n_refs):
    pad, rows, ct = plan.pad, plan.rows, plan.ct
    last = (rows - 1, 0)
    edge_terms, edge_new, corner_terms = [], [], []
    is_first = lax.axis_index("span") == 0

    def choose(n, above, below):
        return jnp.where(is_first, above, below) if plan.ends == 1 else (above, below)[n]

    for n in range(plan.ends):
        outward = choose(n, matrix(plan, w_ref, UP_SP), matrix(plan, w_ref, DOWN_SP))
        inward = choose(n, matrix(plan, w_ref, DOWN_SP), matrix(plan, w_ref, UP_SP))
        first, second, edge_force, edge_rate = side(n)
        corners = corner(n)
        every = dot3(w_ref[...], first)
        beyond = dot3(outward, second)
        within = [choose(n, x.row(last[0]), x.row(last[1])) for x in own]
        within = dot3(inward, jnp.concatenate(within, axis=1))
        from_low = dot3(matrix(plan, w_ref, DOWN_AZ), corners[0])
        from_high = dot3(matrix(plan, w_ref, UP_AZ), corners[1])
        new = []
        for a in range(ct):

            def part(block, b=a):
                return every[block * pad : (block + 1) * pad, at(b)]

            around = part(UP_AZ, 1) + from_low if a == 0 else from_high + part(DOWN_AZ, 0)
            total = edge_rate(C_TIME, a) * part(SPECTRAL) + edge_rate(C_AZ, a) * around
            total = total + edge_rate(C_SP, a) * (beyond[:, at(a)] + within[:, at(a)])
            total = total + edge_rate(C_UP, a) * rolled(part(UP_AX), -1)
            total = total + edge_rate(C_DOWN, a) * rolled(part(DOWN_AX), 1)
            new.append(edge_force[:, at(a)] - total)
        of_edge = choose(n, *(every[block * pad : (block + 1) * pad] for block in (UP_SP, DOWN_SP)))
        of_new = dot3(outward, jnp.concatenate(new, axis=1))
        of_corners = dot3(outward, jnp.concatenate(corners, axis=1))
        for keep in has_sides(plan) if plan.ends == 1 else (1.0,):
            edge_terms.append(of_edge * keep)
            edge_new.append(of_new * keep)
            corner_terms.append([of_corners[:, at(a)] * keep for a in range(ct)])

    products = (
        Products(plan, w_ref, p_refs[0], DOWN_AZ).fill(near[0]), Products(plan, w_ref, p_refs[1], SPECTRAL).fill(near[1]),
    )
    for a, (to_own, to_near) in enumerate(((DOWN_AZ, UP_AZ), (UP_AZ, DOWN_AZ))):

        def take(r, terms):
            total = products[a].own_terms(r) + near[a].rate(C_AZ, r) * terms
            mine = own[a].rate(C_AZ, r) * products[a].get(to_own, r)
            for n in range(2):
                if r == last[n]:
                    total = total + near[a].rate(C_SP, r) * corner_terms[n][a]
                    mine = mine + own[a].rate(C_SP, r) * edge_terms[n][:, at(a)]
            n_refs[a][:, at(r)] = near_force[a].row(r) - total
            lanes = at(r, 1, a * plan.slab)
            y_ref[:, lanes] = g_ref[:, lanes] - mine

        azimuthal(plan, w_ref, to_near, own[a].chunk, take)

    after = [Layer(plan, y_ref, a * plan.slab, own[a].rates) for a in range(ct)]
    inner_rows(plan, w_ref, p_refs, after, own_force, h_refs)
    for a in range(ct):
        for n in range(2):
            h_refs[a][:, at(last[n])] -= own[a].rate(C_SP, last[n]) * edge_new[n][:, at(a)]


def outer_rows(plan, w_ref, own, near, far_chunks, n_refs, h_refs, put, layers=(0, 1)):
    count = CHUNK // LANES
    for a in layers:
        block = (DOWN_AZ, UP_AZ)[a]

        def near_chunk(c):
            terms = dot3(matrix(plan, w_ref, block), far_chunks[a](c))
            return n_refs[a][:, at(c * count, count)] - near[a].rate(C_AZ, c * count, count) * terms

        def take(r, terms):
            put(a, r, h_refs[a][:, at(r)] - own[a].rate(C_AZ, r) * terms)

        azimuthal(plan, w_ref, block, near_chunk, take)


def sides_of(plan, side_ref, force_ref, seams_ref):
    pad, ct = plan.pad, plan.ct
    keeps = (1.0,) if plan.ends == 1 else has_sides(plan)
    is_first = lax.axis_index("span") == 0

    def inlet(n, e, a):
        above, below = a * plan.rows + e, a * plan.rows + plan.rows - 1 - e
        tile = seams_ref[1, 1 + n]
        if plan.ends == 1:
            return jnp.where(is_first, placed(tile, above), placed(tile, below))
        return placed(tile, (above, below)[n])

    def read(n, ref, e, seam):
        value = ref[n, :pad, at(e * ct, ct)]
        if seam:
            scale = ref[n, pad + C_MASK : pad + C_MASK + 1, at(e * ct, ct)]
            value = value + jnp.concatenate([inlet(n, e, a) for a in range(ct)], axis=1) * scale
        return value * keeps[n]

    def side(n):
        same = side_ref is force_ref

        def rate(which, a):
            return force_ref[n, pad + which : pad + which + 1, at(a)] * keeps[n]

        force = read(n, force_ref, 0, True)
        first = force if same else read(n, side_ref, 0, False)
        return first, read(n, side_ref, 1, same), force, rate

    return side


def corners_of(plan, c_refs, seams_ref):
    keeps = (1.0,) if plan.ends == 1 else has_sides(plan)
    is_first = lax.axis_index("span") == 0

    def corner(n):
        out = []
        for a in range(plan.ct):
            if seams_ref is None:
                value = c_refs[a][n, : plan.pad]
            else:
                value = c_refs[n, : plan.pad, at(a)]
                tile = seams_ref[2 * a, 1 + n]
                above, below = (placed(tile, a * plan.rows + r) for r in (0, plan.rows - 1))
                inlet = jnp.where(is_first, above, below) if plan.ends == 1 else (above, below)[n]
                value = value + inlet * c_refs[n, plan.pad + C_MASK : plan.pad + C_MASK + 1, at(a)]
            out.append(value * keeps[n])
        return out

    return corner


def prepare(plan, rhs_ref, coef_ref, m_ref, table0_ref, table1_ref, side_ref, rates_ref):
    pad, cells = plan.pad, plan.cells
    mask, diag, time, *face = [coef_ref[cells * i : cells * (i + 1), :] for i in range(6)]
    scale = mask / diag
    lane = lane_index(cells)
    axial = scale * face[2]
    rates = (
        scale * time, scale * face[0], scale * face[1],
        jnp.where(lane < LANES - 1, axial, 0.0), jnp.where(lane > 0, axial, 0.0), scale,
    )
    for i, rate in enumerate(rates):
        rates_ref[i] = rate
    tail = jnp.zeros((pad - plan.tf, LANES), jnp.float32)
    rest = jnp.zeros((RATES - 6, LANES), jnp.float32)
    mirror = parity()
    for cell in range(cells):
        a, r = divmod(cell, plan.rows)
        there = jnp.where(mirror == 0, a, plan.ct - 1 - a) * plan.rows + r
        table = [rates_ref[i, pl.ds(there, 1), :] for i in range(6)]
        field = jnp.concatenate([rhs_ref[pl.ds(there, plan.tf, stride=cells), :], tail], axis=0)
        m_ref[:pad, at(cell)] = field * table[C_MASK]
        m_ref[pad:, at(cell)] = jnp.concatenate(table + [rest], axis=0)
        other = jnp.where(mirror == 0, plan.ct - 1 - a, a) * plan.rows + r
        table = table + [rates_ref[C_MASK, pl.ds(other, 1), :], rest[:1]]
        (table0_ref, table1_ref)[a][:, at(r)] = jnp.concatenate(table, axis=0)
    write_edges(plan, m_ref, side_ref, None)


def write_edges(plan, x_ref, side_ref, c_refs):
    first = lax.axis_index("span") == 0
    for a in range(plan.ct):
        for e in range(DEPTH):
            low, high = x_ref[:, at(a * plan.rows + e)], x_ref[:, at((a + 1) * plan.rows - 1 - e)]
            ends = [jnp.where(first, high, low)] if plan.ends == 1 else [low, high]
            for n, end in enumerate(ends):
                side_ref[n, :, at(e * plan.ct + a)] = end
                if e == 0 and c_refs:
                    c_refs[a][n] = end


def corner_rows(plan, low_ref, high_ref, low_table, high_table, c_ref):
    first = lax.axis_index("span") == 0
    near = Native(plan, low_ref, low_table, None, 0, True), Native(plan, high_ref, high_table, None, 1, True)
    for a, layer in enumerate(near):
        ends = []
        for r in (0, plan.rows - 1):
            rates = [layer.rate(C_MASK, r) if i == C_MASK else jnp.zeros((1, LANES), jnp.float32) for i in range(RATES)]
            ends.append(jnp.concatenate([layer.row(r)] + rates, axis=0))
        if plan.ends == 1:
            ends = [jnp.where(first, ends[1], ends[0])]
        for n, end in enumerate(ends):
            c_ref[n, :, at(a)] = end


def stack_matrices(plan, up_ref, down_ref, spectral_ref, rows_ref, lanes_ref, diagonal_ref, out_ref, down_out):
    pad = plan.pad
    lane = lax.broadcasted_iota(jnp.int32, (pad, 3 * pad), 1)
    second = (lane >= pad) & (lane < 2 * pad)
    out_ref[SPECTRAL * pad : (SPECTRAL + 1) * pad, :] = spectral_ref[...]
    even = parity() == 0
    for block, small in (
        (DOWN_AZ, jnp.where(even, down_ref[0], up_ref[0])), (UP_AZ, jnp.where(even, up_ref[0], down_ref[0])),
        (UP_SP, up_ref[1]), (DOWN_SP, down_ref[1]), (UP_AX, up_ref[2]), (DOWN_AX, down_ref[2]),
    ):
        full = dot_full(dot_full(rows_ref[...], small), lanes_ref[...]) * diagonal_ref[...]
        hi = full.astype(jnp.bfloat16).astype(jnp.float32)
        out_ref[block * pad : (block + 1) * pad, :] = jnp.where(second, full - hi, hi).astype(jnp.bfloat16)
    down_out[...] = matrix(plan, out_ref, DOWN_AZ)


def send_panels(plan, stator_ref, both_ref, table_ref, out_ref, panels_ref):
    me = lax.axis_index("sector")
    for f in range(plan.fields):
        panels_ref[pl.ds(f, plan.insts, stride=RATES), : plan.width] = jnp.transpose(stator_ref[f])
    out_ref[...] = jnp.zeros_like(out_ref)
    for t, (row, start) in enumerate(plan.weight_at):
        both = both_ref[t : t + 1, :] + 0.0 * table_ref[0:1, 0:1]
        both = jnp.broadcast_to(both[None], (out_ref.shape[0], 1, plan.width))
        out_ref[:, row : row + 1, start : start + plan.width] = both
    for o, slots in enumerate(plan.slots):
        to = lax.rem(me + (plan.sectors - o), plan.sectors) * plan.spans
        for slot, t in enumerate(slots):
            lanes = slice(slot * plan.width, (slot + 1) * plan.width)
            panels = panels_ref[t * RATES : t * RATES + plan.fields, : plan.width]
            for x in range(plan.spans):
                out_ref[to + x, : plan.fields, lanes] = panels


def begin(
    plan, w_ref, m_ref, got_ref,
    seams_ref, weight_ref, x_ref, g_ref, panels_ref, terms_ref, rows_ref, p0_ref, p1_ref,
):
    pad, insts, fields = plan.pad, plan.insts, plan.fields
    me, span = lax.axis_index("sector"), lax.axis_index("span")
    even, is_first = parity() == 0, span == 0
    tiles = plan.tiles
    panels_ref[...] = jnp.zeros_like(panels_ref)
    rows_ref[...] = jnp.zeros_like(rows_ref)
    for n, (k, x) in enumerate(tiles):
        at_span = x if plan.spans == 2 else jnp.clip(span + x, 0, plan.spans - 1)
        for t in range(insts):
            o = (k + plan.shift[t]) % plan.sectors
            source = lax.rem(me + o, plan.sectors) * plan.spans + at_span
            tile = rolled(got_ref[source], -plan.slots[o].index(t) * plan.width)
            panels_ref[t * fields : (t + 1) * fields, n * LANES : n * LANES + plan.width] = tile[:fields, : plan.width]
        tile = got_ref[lax.rem(me + k + plan.sectors, plan.sectors) * plan.spans + at_span]
        lanes = slice(n * LANES, n * LANES + plan.width)
        rows_ref[:fields, lanes] = rolled(tile, -plan.weight_at[0][1])[:fields, : plan.width]
        for t in range(fields, insts):
            row, start = plan.weight_at[t]
            rows_ref[t : t + 1, lanes] = rolled(tile, -start)[row : row + 1, : plan.width]
    spread = dot_full(plan.inst_rows(), rows_ref[...])
    spread = pick(jnp.concatenate([spread[:, at(n)] for n in range(len(tiles))], axis=0), plan.weight_lanes())
    first, share, panel = spread, rolled(spread, plan.ct * plan.width), plan.panel_lanes()
    lower = (jnp.abs(first - panel) < 0.5).astype(jnp.float32)
    upper = (jnp.abs(first + 1.0 - panel) < 0.5).astype(jnp.float32)
    weights = share * lower + (1.0 - share) * upper
    for n in range(len(tiles)):
        panels = panels_ref[:, at(n)]
        terms_ref[n * pad : (n + 1) * pad, :] = panels + rolled(panels, plan.width)
    seams = pick(terms_ref[...] * weights, plan.window_lanes())

    def tile(values, k, x):
        n = tiles.index((k, x))
        return values[n * pad : (n + 1) * pad]

    def around(values, k):
        if plan.spans == 2:
            pair = tile(values, k, 0), tile(values, k, 1)
            return [jnp.where(is_first, pair[0], pair[1]), jnp.where(is_first, pair[1], pair[0])]
        return [tile(values, k, x) for x in (0, 1, -1)]

    def mirrored(value):
        return rolled(value, LANES // 2)

    here = around(seams, 0)
    behind, ahead = around(seams, -1), around(seams, 1)
    for i in range(1 + plan.ends):
        seams_ref[0, i] = jnp.where(even, mirrored(behind[i]), ahead[i])
        seams_ref[1, i] = jnp.where(even, here[i], mirrored(here[i]))
        seams_ref[2, i] = jnp.where(even, mirrored(ahead[i]), behind[i])
    weight_ref[...] = around(weights, 0)[0]

    for layer in two_layers(plan, m_ref, seam=seams_ref[1, 0]):
        for r in range(plan.rows):
            x_ref[:, at(r, 1, layer.start)] = layer.row(r)
    layers = two_layers(plan, x_ref, m_ref)
    inner_rows(plan, w_ref, (p0_ref, p1_ref), layers, layers, g_ref)


def first_half(
    plan, w_ref, m_ref, f_ref, g_ref, low_ref, high_ref, low_table, high_table, side_ref, corner_ref, seams_ref,
    x_ref, near_ref, side_out, c0_ref, c1_ref, p0_ref, p1_ref, y_ref, h0_ref, h1_ref, n0_ref, n1_ref, inlet_ref,
):
    own = two_layers(plan, f_ref, m_ref)
    low = [Native(plan, low_ref, low_table, seams_ref[0, 0], a, a == 0) for a in range(plan.ct)]
    high = [Native(plan, high_ref, high_table, seams_ref[2, 0], a, a == 1) for a in range(plan.ct)]
    near = low[0], high[1]
    n_refs = n0_ref, n1_ref
    middle_rows(
        plan, w_ref, (p0_ref, p1_ref), own, own, g_ref, near, near, sides_of(plan, side_ref, side_ref, seams_ref),
        corners_of(plan, corner_ref, seams_ref), y_ref, (h0_ref, h1_ref), n_refs,
    )
    lane = lane_index(plan.pad)
    inlet_ref[...] = jnp.zeros_like(inlet_ref)

    def put(a, r, value):
        x_ref[:, at(r, 1, a * plan.slab)] = value
        if a == 0:
            near_ref[:, at(r)] = value
        else:
            inlet_ref[: plan.pad, :] = jnp.where(lane == r, rolled(value, r), inlet_ref[: plan.pad, :])

    outer_rows(plan, w_ref, own, near, (low[1].chunk, high[0].chunk), n_refs, (h0_ref, h1_ref), put)
    turned = jnp.transpose(inlet_ref[...])
    for r in range(plan.rows):
        near_ref[plan.tf : plan.tf + 1, at(r)] = turned[r : r + 1, :]
    write_edges(plan, x_ref, side_out, (c0_ref, c1_ref))


def hold_far(plan, x_ref, side_ref, c_high, far_ref):
    come = side_ref[0, 0:1, 0:1] + c_high[0, 0:1, 0:1]
    far_ref[...] = x_ref[:, plan.slab :] + 0.0 * come


def inner(plan, w_ref, m_ref, f_ref, x_ref, g_ref, p0_ref, p1_ref):
    inner_rows(plan, w_ref, (p0_ref, p1_ref), two_layers(plan, x_ref, m_ref), two_layers(plan, f_ref, m_ref), g_ref)


def middle(
    plan, w_ref, m_ref, f_ref, x_ref, g_ref, low_ref, high_ref, side_ref, c_low, c_high,
    low_first, high_first, low_table, high_table, side_first, seams_ref, weight_ref,
    send_ref, n0_ref, h0_ref, x1_ref, rates_ref, p0_ref, p1_ref, y_ref, h1_ref, n1_ref, turn_ref,
):
    pad = plan.pad
    own, force = two_layers(plan, x_ref, m_ref), two_layers(plan, f_ref, m_ref)
    low_force = Native(plan, low_first, low_table, seams_ref[0, 0], 0, True)
    high_force = Native(plan, high_first, high_table, seams_ref[2, 0], 1, True)
    near = Layer(plan, low_ref, 0, low_force), Layer(plan, high_ref, plan.slab, high_force)
    n_refs = n0_ref, n1_ref
    middle_rows(
        plan, w_ref, (p0_ref, p1_ref), own, force, g_ref, near, (low_force, high_force),
        sides_of(plan, side_ref, side_first, seams_ref), corners_of(plan, (c_low, c_high), None), y_ref,
        (h0_ref, h1_ref), n_refs,
    )

    def put(a, r, value):
        x1_ref[:, at(r)] = value

    outer_rows(plan, w_ref, own, near, (None, Layer(plan, high_ref).chunk), n_refs, (h0_ref, h1_ref), put, (1,))
    for r in range(plan.rows):
        last = [near[0].rate(C_AZ, r), own[0].rate(C_AZ, r), jnp.zeros((RATES - 2, LANES), jnp.float32)]
        rates_ref[:, at(r)] = jnp.concatenate(last, axis=0)

    turn_ref[...] = jnp.zeros_like(turn_ref)
    for r in range(plan.rows):
        turn_ref[r : r + 1, :] = low_ref[plan.tf : plan.tf + 1, at(r)]
    far = jnp.transpose(turn_ref[...])[:pad]

    def packed(read, count, first=0, step=1):
        lane = lane_index(count)
        out = jnp.zeros((count, LANES), jnp.float32)
        for r in range(plan.rows):
            to = first + r * step
            out = jnp.where(lane == to, rolled(read(r), to), out)
        return out

    rates = packed(lambda r: rates_ref[:, at(r)], RATES)
    inlet = packed(lambda r: n0_ref[:, at(r)], pad) - rates[0:1] * dot3(matrix(plan, w_ref, DOWN_AZ), far)
    inlet = packed(lambda r: h0_ref[:, at(r)], pad) - rates[1:2] * dot3(matrix(plan, w_ref, DOWN_AZ), inlet)
    lane = lane_index(pad)
    spread = packed(lambda r: x1_ref[:, at(r)], pad, plan.rows * WINDOW, WINDOW)
    for r in range(plan.rows):
        spread = jnp.where(lane == r * WINDOW, rolled(inlet, r * (WINDOW - 1)), spread)
    inlet = jnp.where(parity() == 0, spread, rolled(spread, LANES // 2))
    back = pick(inlet, plan.window_spread()) * weight_ref[...]
    back = back + rolled(back, -plan.width)
    me = lax.axis_index("sector")
    send_ref[...] = jnp.zeros_like(send_ref)
    for t in range(plan.insts):
        to = lax.rem(me + plan.shift[t], plan.sectors)
        send_ref[to, : plan.fields, : plan.width] = back[t * plan.fields : (t + 1) * plan.fields, : plan.width]


def outer(plan, w_ref, rates_ref, n0_ref, h0_ref, x1_ref, far_ref, out_ref):
    mirror = parity()

    def put(a, r, value):
        there = jnp.where(mirror == 0, a, plan.ct - 1 - a) * plan.rows + r
        out_ref[pl.ds(there, plan.tf, stride=plan.cells), :] = value[: plan.tf]

    for r in range(plan.rows):
        put(1, r, x1_ref[:, at(r)])

    def near_chunk(c):
        lanes = slice(c * CHUNK, (c + 1) * CHUNK)
        return n0_ref[:, lanes] - rates_ref[0:1, lanes] * dot3(w_ref[...], far_ref[:, lanes])

    azimuthal(plan, w_ref, 0, near_chunk, lambda r, terms: put(0, r, h0_ref[:, at(r)] - rates_ref[1:2, at(r)] * terms))


def collect_panels(plan, got_ref, out_ref, panels_ref):
    me = lax.axis_index("sector")
    for t in range(plan.insts):
        source = lax.rem(me + (plan.sectors - plan.shift[t]), plan.sectors)
        panels_ref[t * RATES : (t + 1) * RATES, :] = got_ref[source]
    for f in range(plan.fields):
        tile = panels_ref[pl.ds(f, plan.insts, stride=RATES), : plan.width]
        out_ref[f] = jnp.transpose(tile)


def sibling(plan):
    return [s ^ 1 for s in range(plan.sectors)]


def outside(plan):
    return [(s - 1 if s % 2 == 0 else s + 1) % plan.sectors for s in range(plan.sectors)]


def swap(array, partner):
    return lax.ppermute(array, "sector", list(enumerate(partner)))


def beside(plan, array, partner):
    def pairs(step):
        out = []
        for s in range(plan.sectors):
            for x in range(plan.spans):
                to = 1 - x if plan.ends == 1 else x + step
                if 0 <= to < plan.spans:
                    out.append((s * plan.spans + x, partner[s] * plan.spans + to))
        return out

    if plan.ends == 1:
        return lax.ppermute(array, AXES, pairs(0))
    return jnp.concatenate([lax.ppermute(array[:1], AXES, pairs(-1)), lax.ppermute(array[1:], AXES, pairs(1))])


def on_device(
    sectors, spans,
    rhs, diag_coef, face_coef, time_coef, jac_up, jac_down, wall_mask, stator_adj, owner, first_panel_share,
):
    plan = Plan(rhs, stator_adj, sectors, spans)
    pad, cells, slab, insts, fields, ends = plan.pad, plan.cells, plan.slab, plan.insts, plan.fields, plan.ends
    bind = functools.partial
    whole, half = f32(pad, plan.ct * slab), f32(pad, slab)
    products = (vmem(6 * pad, slab),) * 2
    alone, next_chip, next_core = list(range(sectors)), outside(plan), sibling(plan)

    def edges(rows):
        return f32(ends, rows, DEPTH * plan.ct * LANES), f32(ends, rows, LANES), f32(ends, rows, LANES)

    native = rhs.reshape(plan.tf * cells, LANES)
    low_first, high_first = swap(native, next_chip), swap(native, next_core)
    m, table0, table1, side = call(
        bind(prepare, plan),
        (f32(pad + RATES, plan.ct * slab), f32(RATES, slab), f32(RATES, slab)) + edges(pad + RATES)[:1],
        (vmem(6, cells, LANES),),
    )(
        native,
        jnp.concatenate([
            wall_mask.astype(jnp.float32).reshape(cells, LANES), diag_coef.reshape(cells, LANES),
            time_coef.reshape(cells, LANES), face_coef.reshape(3 * cells, LANES),
        ]),
    )
    low_table, high_table = swap(table0, next_chip), swap(table1, next_core)
    stator = jnp.transpose(stator_adj, (1, 2, 3, 0)).reshape(fields, plan.width, insts)
    sent = call(bind(send_panels, plan), f32(sectors * spans, RATES, LANES), (vmem(insts * RATES, LANES),))(
        stator,
        jnp.concatenate([
            lax.rem(owner, plan.panels).astype(jnp.float32).reshape(insts, cells), first_panel_share.reshape(insts, cells),
        ], axis=1),
        table0,
    )
    got = lax.all_to_all(sent, AXES, 0, 0, tiled=True)
    side_first = beside(plan, side, alone)
    corner = call(bind(corner_rows, plan), f32(ends, pad + RATES, plan.ct * LANES))(
        low_first, high_first, low_table, high_table
    )
    corner = beside(plan, corner, alone)
    matrices, down = call(
        bind(stack_matrices, plan),
        [jax.ShapeDtypeStruct((count * pad, 3 * pad), jnp.bfloat16) for count in (7, 1)],
    )(jac_up, jac_down, plan.spectral(), plan.field_rows(), plan.field_lanes(), plan.block_diagonal())
    tiles = len(plan.tiles)
    seams, weight, force, g = call(
        bind(begin, plan), (f32(3, 1 + ends, pad, LANES), f32(pad, LANES), whole, whole),
        (vmem(pad, tiles * LANES), vmem(tiles * pad, LANES), vmem(16, tiles * LANES)) + products,
        flops=2_000_000_000,
    )(matrices, m, got)
    x, near, side, c0, c1 = call(
        bind(first_half, plan), (whole, half) + edges(pad),
        products + (vmem(pad, 2 * slab),) + (vmem(pad, slab),) * 4 + (vmem(LANES, LANES),),
        flops=4_000_000_000,
    )(matrices, m, force, g, low_first, high_first, low_table, high_table, side_first, corner, seams)

    low, high = swap(near, next_chip), swap(x, next_core)
    side = beside(plan, side, alone)
    c_low, c_high = beside(plan, c0, next_chip), beside(plan, c1, next_core)
    (g,) = call(bind(inner, plan), (whole,), products, flops=2_000_000_000)(matrices, m, force, x)
    far = call(bind(hold_far, plan), half)(x, side, c_high)
    far_low = swap(far, next_chip)
    back, n0, h0, x1, rates = call(
        bind(middle, plan), (f32(sectors, RATES, LANES), half, half, half, f32(RATES, slab)),
        products + (vmem(pad, 2 * slab), vmem(pad, slab), vmem(pad, slab), vmem(LANES, LANES)),
        flops=4_000_000_000,
    )(
        matrices, m, force, x, g, low, high, side, c_low, c_high, low_first, high_first, low_table, high_table, side_first,
        seams, weight,
    )
    returned = lax.all_to_all(back, "sector", 0, 0, tiled=True)
    sens = call(bind(collect_panels, plan), f32(fields, plan.width, insts), (vmem(insts * RATES, LANES),))(returned)
    out = call(bind(outer, plan), f32(plan.tf * cells, LANES))(down, rates, n0, h0, x1, far_low)
    sens = jnp.transpose(sens.reshape(fields, plan.panels, plan.rows, insts), (3, 0, 1, 2))
    return out.reshape(rhs.shape), sens


def solution(mesh):
    in_specs = (
        P(None, None, "sector", "span", None),
        P("sector", "span", None),
        P(None, "sector", "span", None),
        P("sector", "span", None),
        P(),
        P(),
        P("sector", "span", None),
        P(None, None, "sector", "span"),
        P(None, "sector", "span"),
        P(None, "sector", "span"),
    )
    out_specs = (P(None, None, "sector", "span", None), P(None, None, "sector", "span"))
    return jax.shard_map(
        functools.partial(on_device, mesh.shape["sector"], mesh.shape["span"]),
        mesh=mesh, in_specs=in_specs, out_specs=out_specs, check_vma=False,
    )
```

```python
import functools

import jax
import jax.numpy as jnp
import ml_dtypes
import numpy as np
from jax import lax
from jax.experimental import pallas as pl
from jax.experimental.pallas import tpu as pltpu
from jax.sharding import PartitionSpec as P

SWEEPS = 4
DEPTH = 2
LANES = 128
CHUNK = 256
WINDOW = 8
HIGHEST = lax.Precision.HIGHEST
DOWN_AZ, SPECTRAL, UP_SP, DOWN_SP, UP_AX, DOWN_AX, UP_AZ = range(7)
C_TIME, C_AZ, C_SP, C_UP, C_DOWN, C_MASK, C_OTHER = range(7)
RATES = 8
AXES = ("sector", "span")


class Plan:
    def __init__(self, rhs, stator_adj, sectors, spans):
        self.insts, self.fields, self.ct, self.rows, self.nax = rhs.shape
        self.panels = stator_adj.shape[2]
        self.sectors, self.spans = sectors, spans
        self.tf = self.insts * self.fields
        self.pad = -(-self.tf // 16) * 16
        self.cells = self.ct * self.rows
        self.slab = self.rows * LANES
        self.width = self.panels * self.rows
        self.shift = [
            ((t * sectors) // (self.insts - 1) - t // (self.insts - 1)) % sectors for t in range(self.insts)
        ]
        assert self.ct == 2 and self.nax == LANES and SWEEPS % DEPTH == 0 and spans > 1
        assert len(set(self.shift)) == self.insts and self.cells * WINDOW == LANES and self.rows >= SWEEPS
        assert self.slab % CHUNK == 0 and 3 * self.pad <= 256 and 2 * self.ct * self.width == LANES
        assert sectors % 2 == 0
        self.ends = 1 if spans == 2 else 2
        self.blocks = [-1, 0, 1]
        self.halves = [0, 1] if spans == 2 else [-1, 0, 1]
        self.tiles = [(k, x) for k in self.blocks for x in self.halves]
        self.slots = [
            [t for t in range(self.insts) if any((k + self.shift[t]) % sectors == o for k in self.blocks)]
            for o in range(sectors)
        ]
        last = LANES - self.width
        self.weight_at = [(t, last) for t in range(self.fields)] + [
            (self.fields, i * self.width) for i in range(self.insts - self.fields)
        ]
        assert max(map(len, self.slots)) * self.width <= last and 2 * self.cells == self.width
        assert self.fields == RATES - 1 and (self.insts - self.fields) * self.width <= LANES

    def spectral(self):
        t = np.arange(self.insts)
        off = t[:, None] - t[None, :]
        sines = np.where(off == 0, 1.0, np.sin(np.pi * off / self.insts))
        table = np.where(off == 0, 0.0, 0.5 * (1.0 - 2.0 * (off % 2)) / sines).astype(np.float32)
        full = np.zeros((self.pad, self.pad), np.float32)
        full[: self.tf, : self.tf] = np.kron(table.T, np.eye(self.fields, dtype=np.float32))
        hi = full.astype(ml_dtypes.bfloat16)
        lo = (full - hi.astype(np.float32)).astype(ml_dtypes.bfloat16)
        return np.concatenate([hi, lo, hi], axis=1)

    def field_rows(self):
        out = np.zeros((self.pad, self.fields), np.float32)
        out[np.arange(self.tf), np.arange(self.tf) % self.fields] = 1.0
        return out

    def field_lanes(self):
        return np.tile(self.field_rows().T, (1, 3))

    def block_diagonal(self):
        block = np.full(self.pad, -1)
        block[: self.tf] = np.arange(self.tf) // self.fields
        same = (block[:, None] == block[None, :]) & (block[:, None] >= 0)
        return np.tile(same.astype(np.float32), (1, 3))


    def inst_rows(self):
        row, inst = table_index(self.pad, 16)
        return ((row >= inst * self.fields) & (row < (inst + 1) * self.fields)).astype(jnp.float32)

    def cell_of(self, lane):
        return lax.div(lane, self.width) * self.rows + lax.rem(lane, self.rows)

    def window_lanes(self):
        lane, to = table_index(LANES, LANES)
        return (lane < self.ct * self.width) & (to == self.cell_of(lane) * WINDOW)

    def window_spread(self):
        to, lane = table_index(LANES, LANES)
        return (lane < self.ct * self.width) & (to == self.cell_of(lane) * WINDOW)

    def weight_lanes(self):
        cell, lane = table_index(LANES, LANES)
        half = self.ct * self.width
        wanted = jnp.where(lane < half, self.cell_of(lane), self.cells + self.cell_of(lane - half))
        return cell == wanted

    def panel_lanes(self):
        lane = lane_index(1)
        panel = lax.rem(lax.div(lane, self.rows), self.panels)
        return jnp.where(lane < self.ct * self.width, panel, -9).astype(jnp.float32)


def table_index(rows, columns):
    return [lax.broadcasted_iota(jnp.int32, (rows, columns), axis) for axis in (0, 1)]


def call(kernel, out, scratch=(), flops=2_000_000, nbytes=1_000_000):
    return pl.pallas_call(
        kernel,
        out_shape=out,
        scratch_shapes=list(scratch),
        compiler_params=pltpu.CompilerParams(vmem_limit_bytes=20 * 1024 * 1024),
        cost_estimate=pl.CostEstimate(flops=flops, bytes_accessed=nbytes, transcendentals=0),
    )


def f32(*shape):
    return jax.ShapeDtypeStruct(shape, jnp.float32)


def vmem(*shape):
    return pltpu.VMEM(shape, jnp.float32)


def halves_of(x):
    hi = x.astype(jnp.bfloat16)
    return hi, (x - hi.astype(jnp.float32)).astype(jnp.bfloat16)


def dot3(w, x):
    hi, lo = halves_of(x)
    return jnp.dot(w, jnp.concatenate([hi, hi, lo], axis=0), preferred_element_type=jnp.float32)


def pick(x, table):
    table = table.astype(jnp.float32).astype(jnp.bfloat16)
    table = jnp.concatenate([table, table], axis=0)
    return jnp.dot(jnp.concatenate(halves_of(x), axis=1), table, preferred_element_type=jnp.float32)


def dot_full(a, b):
    return jnp.dot(a, b, precision=HIGHEST, preferred_element_type=jnp.float32)


def lane_index(rows):
    return lax.broadcasted_iota(jnp.int32, (rows, LANES), 1)


def rolled(x, by):
    by %= LANES
    return pltpu.roll(x, by, axis=1) if by else x


def at(r, count=1, start=0):
    return slice(start + r * LANES, start + (r + count) * LANES)


def parity():
    return lax.rem(lax.axis_index("sector"), 2)


def has_sides(plan):
    span = lax.axis_index("span")
    return jnp.where(span < plan.spans - 1, 1.0, 0.0), jnp.where(span > 0, 1.0, 0.0)


class Layer:
    def __init__(self, plan, ref, start=0, rates=None, seam=None, layer=0):
        self.plan, self.ref, self.start, self.seam, self.layer = plan, ref, start, seam, layer
        self.rates = rates or (ref, start)

    def rate(self, which, r, count=1):
        if isinstance(self.rates, Layer):
            return self.rates.rate(which, r, count)
        ref, start = self.rates
        row = self.plan.pad + which
        return ref[row : row + 1, at(r, count, start)]

    def row(self, r):
        value = self.ref[: self.plan.pad, at(r, 1, self.start)]
        if self.seam is None:
            return value
        return value + placed(self.seam, self.layer * self.plan.rows + r) * self.rate(C_MASK, r)

    def chunk(self, c):
        count = CHUNK // LANES
        if self.seam is None:
            return self.ref[: self.plan.pad, at(c * count, count, self.start)]
        return jnp.concatenate([self.row(c * count + part) for part in range(count)], axis=1)


class Native(Layer):
    def __init__(self, plan, ref, table, seam, layer, near):
        super().__init__(plan, ref, 0, None, seam, layer)
        self.table, self.near = table, near

    def rate(self, which, r, count=1):
        row = which if self.near else C_OTHER
        return self.table[row : row + 1, at(r, count)]

    def row(self, r):
        plan = self.plan
        there = jnp.where(parity() == 1, self.layer, plan.ct - 1 - self.layer) * plan.rows + r
        field = self.ref[pl.ds(there, plan.tf, stride=plan.cells), :]
        field = jnp.concatenate([field, jnp.zeros((plan.pad - plan.tf, LANES), jnp.float32)], axis=0)
        if self.seam is not None:
            field = field + placed(self.seam, self.layer * plan.rows + r)
        return field * self.rate(C_MASK, r)


def placed(tile, cell):
    return jnp.where(lane_index(tile.shape[0]) == 0, rolled(tile, -cell * WINDOW), 0.0)


class Products:
    def __init__(self, plan, w_ref, p_ref, first):
        self.plan, self.w, self.p, self.first = plan, w_ref, p_ref, first

    def fill(self, layer):
        for c in range(self.plan.slab // CHUNK):
            self.p[:, c * CHUNK : (c + 1) * CHUNK] = dot3(matrix(self.plan, self.w, self.first, 6), layer.chunk(c))
        self.layer = layer
        return self

    def get(self, block, r):
        row = (block - self.first) * self.plan.pad
        return self.p[row : row + self.plan.pad, at(r)]

    def own_terms(self, r):
        rate = self.layer.rate
        total = rate(C_TIME, r) * self.get(SPECTRAL, r)
        beside = []
        if r + 1 < self.plan.rows:
            beside.append(self.get(UP_SP, r + 1))
        if r > 0:
            beside.append(self.get(DOWN_SP, r - 1))
        total = total + rate(C_SP, r) * sum(beside[1:], beside[0])
        total = total + rate(C_UP, r) * rolled(self.get(UP_AX, r), -1)
        return total + rate(C_DOWN, r) * rolled(self.get(DOWN_AX, r), 1)


def matrix(plan, w_ref, block, count=1):
    return w_ref[block * plan.pad : (block + count) * plan.pad, :]


def two_layers(plan, ref, rates=None, seam=None):
    return [
        Layer(plan, ref, a * plan.slab, (rates, a * plan.slab) if rates is not None else None, seam, a)
        for a in range(plan.ct)
    ]


def inner_rows(plan, w_ref, p_refs, layers, force, g_ref):
    first = Products(plan, w_ref, p_refs[0], DOWN_AZ).fill(layers[0])
    second = Products(plan, w_ref, p_refs[1], SPECTRAL).fill(layers[1])
    for r in range(plan.rows):
        other = second.get(UP_AZ, r), first.get(DOWN_AZ, r)
        for a, products in enumerate((first, second)):
            total = products.own_terms(r) + layers[a].rate(C_AZ, r) * other[a]
            if isinstance(g_ref, tuple):
                g_ref[a][:, at(r)] = force[a].row(r) - total
            else:
                g_ref[:, at(r, 1, a * plan.slab)] = force[a].row(r) - total


def azimuthal(plan, w_ref, block, chunk_of, take):
    for c in range(plan.slab // CHUNK):
        terms = dot3(matrix(plan, w_ref, block), chunk_of(c))
        for part in range(CHUNK // LANES):
            take(c * (CHUNK // LANES) + part, terms[:, at(part)])


def middle_rows(plan, w_ref, p_refs, own, own_force, g_ref, near, near_force, side, corner, y_ref, h_refs, n_refs):
    pad, rows, ct = plan.pad, plan.rows, plan.ct
    last = (rows - 1, 0)
    edge_terms, edge_new, corner_terms = [], [], []
    is_first = lax.axis_index("span") == 0

    def choose(n, above, below):
        return jnp.where(is_first, above, below) if plan.ends == 1 else (above, below)[n]

    for n in range(plan.ends):
        outward = choose(n, matrix(plan, w_ref, UP_SP), matrix(plan, w_ref, DOWN_SP))
        inward = choose(n, matrix(plan, w_ref, DOWN_SP), matrix(plan, w_ref, UP_SP))
        first, second, edge_force, edge_rate = side(n)
        corners = corner(n)
        every = dot3(w_ref[...], first)
        beyond = dot3(outward, second)
        within = [choose(n, x.row(last[0]), x.row(last[1])) for x in own]
        within = dot3(inward, jnp.concatenate(within, axis=1))
        from_low = dot3(matrix(plan, w_ref, DOWN_AZ), corners[0])
        from_high = dot3(matrix(plan, w_ref, UP_AZ), corners[1])
        new = []
        for a in range(ct):

            def part(block, b=a):
                return every[block * pad : (block + 1) * pad, at(b)]

            around = part(UP_AZ, 1) + from_low if a == 0 else from_high + part(DOWN_AZ, 0)
            total = edge_rate(C_TIME, a) * part(SPECTRAL) + edge_rate(C_AZ, a) * around
            total = total + edge_rate(C_SP, a) * (beyond[:, at(a)] + within[:, at(a)])
            total = total + edge_rate(C_UP, a) * rolled(part(UP_AX), -1)
            total = total + edge_rate(C_DOWN, a) * rolled(part(DOWN_AX), 1)
            new.append(edge_force[:, at(a)] - total)
        of_edge = choose(n, *(every[block * pad : (block + 1) * pad] for block in (UP_SP, DOWN_SP)))
        of_new = dot3(outward, jnp.concatenate(new, axis=1))
        of_corners = dot3(outward, jnp.concatenate(corners, axis=1))
        for keep in has_sides(plan) if plan.ends == 1 else (1.0,):
            edge_terms.append(of_edge * keep)
            edge_new.append(of_new * keep)
            corner_terms.append([of_corners[:, at(a)] * keep for a in range(ct)])

    products = (
        Products(plan, w_ref, p_refs[0], DOWN_AZ).fill(near[0]), Products(plan, w_ref, p_refs[1], SPECTRAL).fill(near[1]),
    )
    for a, (to_own, to_near) in enumerate(((DOWN_AZ, UP_AZ), (UP_AZ, DOWN_AZ))):

        def take(r, terms):
            total = products[a].own_terms(r) + near[a].rate(C_AZ, r) * terms
            mine = own[a].rate(C_AZ, r) * products[a].get(to_own, r)
            for n in range(2):
                if r == last[n]:
                    total = total + near[a].rate(C_SP, r) * corner_terms[n][a]
                    mine = mine + own[a].rate(C_SP, r) * edge_terms[n][:, at(a)]
            n_refs[a][:, at(r)] = near_force[a].row(r) - total
            lanes = at(r, 1, a * plan.slab)
            y_ref[:, lanes] = g_ref[:, lanes] - mine

        azimuthal(plan, w_ref, to_near, own[a].chunk, take)

    after = [Layer(plan, y_ref, a * plan.slab, own[a].rates) for a in range(ct)]
    inner_rows(plan, w_ref, p_refs, after, own_force, h_refs)
    for a in range(ct):
        for n in range(2):
            h_refs[a][:, at(last[n])] -= own[a].rate(C_SP, last[n]) * edge_new[n][:, at(a)]


def outer_rows(plan, w_ref, own, near, far_chunks, n_refs, h_refs, put, layers=(0, 1)):
    count = CHUNK // LANES
    for a in layers:
        block = (DOWN_AZ, UP_AZ)[a]

        def near_chunk(c):
            terms = dot3(matrix(plan, w_ref, block), far_chunks[a](c))
            return n_refs[a][:, at(c * count, count)] - near[a].rate(C_AZ, c * count, count) * terms

        def take(r, terms):
            put(a, r, h_refs[a][:, at(r)] - own[a].rate(C_AZ, r) * terms)

        azimuthal(plan, w_ref, block, near_chunk, take)


def sides_of(plan, side_ref, force_ref, seams_ref):
    pad, ct = plan.pad, plan.ct
    keeps = (1.0,) if plan.ends == 1 else has_sides(plan)
    is_first = lax.axis_index("span") == 0

    def inlet(n, e, a):
        above, below = a * plan.rows + e, a * plan.rows + plan.rows - 1 - e
        tile = seams_ref[1, 1 + n]
        if plan.ends == 1:
            return jnp.where(is_first, placed(tile, above), placed(tile, below))
        return placed(tile, (above, below)[n])

    def read(n, ref, e, seam):
        value = ref[n, :pad, at(e * ct, ct)]
        if seam:
            scale = ref[n, pad + C_MASK : pad + C_MASK + 1, at(e * ct, ct)]
            value = value + jnp.concatenate([inlet(n, e, a) for a in range(ct)], axis=1) * scale
        return value * keeps[n]

    def side(n):
        same = side_ref is force_ref

        def rate(which, a):
            return force_ref[n, pad + which : pad + which + 1, at(a)] * keeps[n]

        force = read(n, force_ref, 0, True)
        first = force if same else read(n, side_ref, 0, False)
        return first, read(n, side_ref, 1, same), force, rate

    return side


def corners_of(plan, c_refs, seams_ref):
    keeps = (1.0,) if plan.ends == 1 else has_sides(plan)
    is_first = lax.axis_index("span") == 0

    def corner(n):
        out = []
        for a in range(plan.ct):
            if seams_ref is None:
                value = c_refs[a][n, : plan.pad]
            else:
                value = c_refs[n, : plan.pad, at(a)]
                tile = seams_ref[2 * a, 1 + n]
                above, below = (placed(tile, a * plan.rows + r) for r in (0, plan.rows - 1))
                inlet = jnp.where(is_first, above, below) if plan.ends == 1 else (above, below)[n]
                value = value + inlet * c_refs[n, plan.pad + C_MASK : plan.pad + C_MASK + 1, at(a)]
            out.append(value * keeps[n])
        return out

    return corner


def prepare(plan, rhs_ref, coef_ref, m_ref, table0_ref, table1_ref, side_ref, rates_ref):
    pad, cells = plan.pad, plan.cells
    mask, diag, time, *face = [coef_ref[cells * i : cells * (i + 1), :] for i in range(6)]
    scale = mask / diag
    lane = lane_index(cells)
    axial = scale * face[2]
    rates = (
        scale * time, scale * face[0], scale * face[1],
        jnp.where(lane < LANES - 1, axial, 0.0), jnp.where(lane > 0, axial, 0.0), scale,
    )
    for i, rate in enumerate(rates):
        rates_ref[i] = rate
    tail = jnp.zeros((pad - plan.tf, LANES), jnp.float32)
    rest = jnp.zeros((RATES - 6, LANES), jnp.float32)
    mirror = parity()
    for cell in range(cells):
        a, r = divmod(cell, plan.rows)
        there = jnp.where(mirror == 0, a, plan.ct - 1 - a) * plan.rows + r
        table = [rates_ref[i, pl.ds(there, 1), :] for i in range(6)]
        field = jnp.concatenate([rhs_ref[pl.ds(there, plan.tf, stride=cells), :], tail], axis=0)
        m_ref[:pad, at(cell)] = field * table[C_MASK]
        m_ref[pad:, at(cell)] = jnp.concatenate(table + [rest], axis=0)
        other = jnp.where(mirror == 0, plan.ct - 1 - a, a) * plan.rows + r
        table = table + [rates_ref[C_MASK, pl.ds(other, 1), :], rest[:1]]
        (table0_ref, table1_ref)[a][:, at(r)] = jnp.concatenate(table, axis=0)
    write_edges(plan, m_ref, side_ref, None)


def write_edges(plan, x_ref, side_ref, c_refs):
    first = lax.axis_index("span") == 0
    for a in range(plan.ct):
        for e in range(DEPTH):
            low, high = x_ref[:, at(a * plan.rows + e)], x_ref[:, at((a + 1) * plan.rows - 1 - e)]
            ends = [jnp.where(first, high, low)] if plan.ends == 1 else [low, high]
            for n, end in enumerate(ends):
                side_ref[n, :, at(e * plan.ct + a)] = end
                if e == 0 and c_refs:
                    c_refs[a][n] = end


def corner_rows(plan, low_ref, high_ref, low_table, high_table, c_ref):
    first = lax.axis_index("span") == 0
    near = Native(plan, low_ref, low_table, None, 0, True), Native(plan, high_ref, high_table, None, 1, True)
    for a, layer in enumerate(near):
        ends = []
        for r in (0, plan.rows - 1):
            rates = [layer.rate(C_MASK, r) if i == C_MASK else jnp.zeros((1, LANES), jnp.float32) for i in range(RATES)]
            ends.append(jnp.concatenate([layer.row(r)] + rates, axis=0))
        if plan.ends == 1:
            ends = [jnp.where(first, ends[1], ends[0])]
        for n, end in enumerate(ends):
            c_ref[n, :, at(a)] = end


def stack_matrices(plan, up_ref, down_ref, spectral_ref, rows_ref, lanes_ref, diagonal_ref, out_ref, down_out):
    pad = plan.pad
    lane = lax.broadcasted_iota(jnp.int32, (pad, 3 * pad), 1)
    second = (lane >= pad) & (lane < 2 * pad)
    out_ref[SPECTRAL * pad : (SPECTRAL + 1) * pad, :] = spectral_ref[...]
    even = parity() == 0
    for block, small in (
        (DOWN_AZ, jnp.where(even, down_ref[0], up_ref[0])), (UP_AZ, jnp.where(even, up_ref[0], down_ref[0])),
        (UP_SP, up_ref[1]), (DOWN_SP, down_ref[1]), (UP_AX, up_ref[2]), (DOWN_AX, down_ref[2]),
    ):
        full = dot_full(dot_full(rows_ref[...], small), lanes_ref[...]) * diagonal_ref[...]
        hi = full.astype(jnp.bfloat16).astype(jnp.float32)
        out_ref[block * pad : (block + 1) * pad, :] = jnp.where(second, full - hi, hi).astype(jnp.bfloat16)
    down_out[...] = matrix(plan, out_ref, DOWN_AZ)


def send_panels(plan, stator_ref, both_ref, table_ref, out_ref, panels_ref):
    me = lax.axis_index("sector")
    for f in range(plan.fields):
        panels_ref[pl.ds(f, plan.insts, stride=RATES), : plan.width] = jnp.transpose(stator_ref[f])
    out_ref[...] = jnp.zeros_like(out_ref)
    for t, (row, start) in enumerate(plan.weight_at):
        both = both_ref[t : t + 1, :] + 0.0 * table_ref[0:1, 0:1]
        both = jnp.broadcast_to(both[None], (out_ref.shape[0], 1, plan.width))
        out_ref[:, row : row + 1, start : start + plan.width] = both
    for o, slots in enumerate(plan.slots):
        to = lax.rem(me + (plan.sectors - o), plan.sectors) * plan.spans
        for slot, t in enumerate(slots):
            lanes = slice(slot * plan.width, (slot + 1) * plan.width)
            panels = panels_ref[t * RATES : t * RATES + plan.fields, : plan.width]
            for x in range(plan.spans):
                out_ref[to + x, : plan.fields, lanes] = panels


def begin(
    plan, w_ref, m_ref, got_ref,
    seams_ref, weight_ref, x_ref, g_ref, panels_ref, terms_ref, rows_ref, p0_ref, p1_ref,
):
    pad, insts, fields = plan.pad, plan.insts, plan.fields
    me, span = lax.axis_index("sector"), lax.axis_index("span")
    even, is_first = parity() == 0, span == 0
    tiles = plan.tiles
    panels_ref[...] = jnp.zeros_like(panels_ref)
    rows_ref[...] = jnp.zeros_like(rows_ref)
    for n, (k, x) in enumerate(tiles):
        at_span = x if plan.spans == 2 else jnp.clip(span + x, 0, plan.spans - 1)
        for t in range(insts):
            o = (k + plan.shift[t]) % plan.sectors
            source = lax.rem(me + o, plan.sectors) * plan.spans + at_span
            tile = rolled(got_ref[source], -plan.slots[o].index(t) * plan.width)
            panels_ref[t * fields : (t + 1) * fields, n * LANES : n * LANES + plan.width] = tile[:fields, : plan.width]
        tile = got_ref[lax.rem(me + k + plan.sectors, plan.sectors) * plan.spans + at_span]
        lanes = slice(n * LANES, n * LANES + plan.width)
        rows_ref[:fields, lanes] = rolled(tile, -plan.weight_at[0][1])[:fields, : plan.width]
        for t in range(fields, insts):
            row, start = plan.weight_at[t]
            rows_ref[t : t + 1, lanes] = rolled(tile, -start)[row : row + 1, : plan.width]
    spread = dot_full(plan.inst_rows(), rows_ref[...])
    spread = pick(jnp.concatenate([spread[:, at(n)] for n in range(len(tiles))], axis=0), plan.weight_lanes())
    first, share, panel = spread, rolled(spread, plan.ct * plan.width), plan.panel_lanes()
    lower = (jnp.abs(first - panel) < 0.5).astype(jnp.float32)
    upper = (jnp.abs(first + 1.0 - panel) < 0.5).astype(jnp.float32)
    weights = share * lower + (1.0 - share) * upper
    for n in range(len(tiles)):
        panels = panels_ref[:, at(n)]
        terms_ref[n * pad : (n + 1) * pad, :] = panels + rolled(panels, plan.width)
    seams = pick(terms_ref[...] * weights, plan.window_lanes())

    def tile(values, k, x):
        n = tiles.index((k, x))
        return values[n * pad : (n + 1) * pad]

    def around(values, k):
        if plan.spans == 2:
            pair = tile(values, k, 0), tile(values, k, 1)
            return [jnp.where(is_first, pair[0], pair[1]), jnp.where(is_first, pair[1], pair[0])]
        return [tile(values, k, x) for x in (0, 1, -1)]

    def mirrored(value):
        return rolled(value, LANES // 2)

    here = around(seams, 0)
    behind, ahead = around(seams, -1), around(seams, 1)
    for i in range(1 + plan.ends):
        seams_ref[0, i] = jnp.where(even, mirrored(behind[i]), ahead[i])
        seams_ref[1, i] = jnp.where(even, here[i], mirrored(here[i]))
        seams_ref[2, i] = jnp.where(even, mirrored(ahead[i]), behind[i])
    weight_ref[...] = around(weights, 0)[0]

    for layer in two_layers(plan, m_ref, seam=seams_ref[1, 0]):
        for r in range(plan.rows):
            x_ref[:, at(r, 1, layer.start)] = layer.row(r)
    layers = two_layers(plan, x_ref, m_ref)
    inner_rows(plan, w_ref, (p0_ref, p1_ref), layers, layers, g_ref)


def first_half(
    plan, w_ref, m_ref, f_ref, g_ref, low_ref, high_ref, low_table, high_table, side_ref, corner_ref, seams_ref,
    x_ref, near_ref, side_out, c0_ref, c1_ref, p0_ref, p1_ref, y_ref, h0_ref, h1_ref, n0_ref, n1_ref, inlet_ref,
):
    own = two_layers(plan, f_ref, m_ref)
    low = [Native(plan, low_ref, low_table, seams_ref[0, 0], a, a == 0) for a in range(plan.ct)]
    high = [Native(plan, high_ref, high_table, seams_ref[2, 0], a, a == 1) for a in range(plan.ct)]
    near = low[0], high[1]
    n_refs = n0_ref, n1_ref
    middle_rows(
        plan, w_ref, (p0_ref, p1_ref), own, own, g_ref, near, near, sides_of(plan, side_ref, side_ref, seams_ref),
        corners_of(plan, corner_ref, seams_ref), y_ref, (h0_ref, h1_ref), n_refs,
    )
    lane = lane_index(plan.pad)
    inlet_ref[...] = jnp.zeros_like(inlet_ref)

    def put(a, r, value):
        x_ref[:, at(r, 1, a * plan.slab)] = value
        if a == 0:
            near_ref[:, at(r)] = value
        else:
            inlet_ref[: plan.pad, :] = jnp.where(lane == r, rolled(value, r), inlet_ref[: plan.pad, :])

    outer_rows(plan, w_ref, own, near, (low[1].chunk, high[0].chunk), n_refs, (h0_ref, h1_ref), put)
    turned = jnp.transpose(inlet_ref[...])
    for r in range(plan.rows):
        near_ref[plan.tf : plan.tf + 1, at(r)] = turned[r : r + 1, :]
    write_edges(plan, x_ref, side_out, (c0_ref, c1_ref))


def hold_far(plan, x_ref, side_ref, c_high, far_ref):
    come = side_ref[0, 0:1, 0:1] + c_high[0, 0:1, 0:1]
    far_ref[...] = x_ref[:, plan.slab :] + 0.0 * come


def inner(plan, w_ref, m_ref, f_ref, x_ref, g_ref, p0_ref, p1_ref):
    inner_rows(plan, w_ref, (p0_ref, p1_ref), two_layers(plan, x_ref, m_ref), two_layers(plan, f_ref, m_ref), g_ref)


def middle(
    plan, w_ref, m_ref, f_ref, x_ref, g_ref, low_ref, high_ref, side_ref, c_low, c_high,
    low_first, high_first, low_table, high_table, side_first, seams_ref, weight_ref,
    send_ref, n0_ref, h0_ref, x1_ref, rates_ref, p0_ref, p1_ref, y_ref, h1_ref, n1_ref, turn_ref,
):
    pad = plan.pad
    own, force = two_layers(plan, x_ref, m_ref), two_layers(plan, f_ref, m_ref)
    low_force = Native(plan, low_first, low_table, seams_ref[0, 0], 0, True)
    high_force = Native(plan, high_first, high_table, seams_ref[2, 0], 1, True)
    near = Layer(plan, low_ref, 0, low_force), Layer(plan, high_ref, plan.slab, high_force)
    n_refs = n0_ref, n1_ref
    middle_rows(
        plan, w_ref, (p0_ref, p1_ref), own, force, g_ref, near, (low_force, high_force),
        sides_of(plan, side_ref, side_first, seams_ref), corners_of(plan, (c_low, c_high), None), y_ref,
        (h0_ref, h1_ref), n_refs,
    )

    def put(a, r, value):
        x1_ref[:, at(r)] = value

    outer_rows(plan, w_ref, own, near, (None, Layer(plan, high_ref).chunk), n_refs, (h0_ref, h1_ref), put, (1,))
    for r in range(plan.rows):
        last = [near[0].rate(C_AZ, r), own[0].rate(C_AZ, r), jnp.zeros((RATES - 2, LANES), jnp.float32)]
        rates_ref[:, at(r)] = jnp.concatenate(last, axis=0)

    turn_ref[...] = jnp.zeros_like(turn_ref)
    for r in range(plan.rows):
        turn_ref[r : r + 1, :] = low_ref[plan.tf : plan.tf + 1, at(r)]
    far = jnp.transpose(turn_ref[...])[:pad]

    def packed(read, count, first=0, step=1):
        lane = lane_index(count)
        out = jnp.zeros((count, LANES), jnp.float32)
        for r in range(plan.rows):
            to = first + r * step
            out = jnp.where(lane == to, rolled(read(r), to), out)
        return out

    rates = packed(lambda r: rates_ref[:, at(r)], RATES)
    inlet = packed(lambda r: n0_ref[:, at(r)], pad) - rates[0:1] * dot3(matrix(plan, w_ref, DOWN_AZ), far)
    inlet = packed(lambda r: h0_ref[:, at(r)], pad) - rates[1:2] * dot3(matrix(plan, w_ref, DOWN_AZ), inlet)
    lane = lane_index(pad)
    spread = packed(lambda r: x1_ref[:, at(r)], pad, plan.rows * WINDOW, WINDOW)
    for r in range(plan.rows):
        spread = jnp.where(lane == r * WINDOW, rolled(inlet, r * (WINDOW - 1)), spread)
    inlet = jnp.where(parity() == 0, spread, rolled(spread, LANES // 2))
    back = pick(inlet, plan.window_spread()) * weight_ref[...]
    back = back + rolled(back, -plan.width)
    me = lax.axis_index("sector")
    send_ref[...] = jnp.zeros_like(send_ref)
    for t in range(plan.insts):
        to = lax.rem(me + plan.shift[t], plan.sectors)
        send_ref[to, : plan.fields, : plan.width] = back[t * plan.fields : (t + 1) * plan.fields, : plan.width]


def outer(plan, w_ref, rates_ref, n0_ref, h0_ref, x1_ref, far_ref, out_ref):
    mirror = parity()

    def put(a, r, value):
        there = jnp.where(mirror == 0, a, plan.ct - 1 - a) * plan.rows + r
        out_ref[pl.ds(there, plan.tf, stride=plan.cells), :] = value[: plan.tf]

    for r in range(plan.rows):
        put(1, r, x1_ref[:, at(r)])

    def near_chunk(c):
        lanes = slice(c * CHUNK, (c + 1) * CHUNK)
        return n0_ref[:, lanes] - rates_ref[0:1, lanes] * dot3(w_ref[...], far_ref[:, lanes])

    azimuthal(plan, w_ref, 0, near_chunk, lambda r, terms: put(0, r, h0_ref[:, at(r)] - rates_ref[1:2, at(r)] * terms))


def collect_panels(plan, got_ref, out_ref, panels_ref):
    me = lax.axis_index("sector")
    for t in range(plan.insts):
        source = lax.rem(me + (plan.sectors - plan.shift[t]), plan.sectors)
        panels_ref[t * RATES : (t + 1) * RATES, :] = got_ref[source]
    for f in range(plan.fields):
        tile = panels_ref[pl.ds(f, plan.insts, stride=RATES), : plan.width]
        out_ref[f] = jnp.transpose(tile)


def sibling(plan):
    return [s ^ 1 for s in range(plan.sectors)]


def outside(plan):
    return [(s - 1 if s % 2 == 0 else s + 1) % plan.sectors for s in range(plan.sectors)]


def swap(array, partner):
    return lax.ppermute(array, "sector", list(enumerate(partner)))


def beside(plan, array, partner):
    def pairs(step):
        out = []
        for s in range(plan.sectors):
            for x in range(plan.spans):
                to = 1 - x if plan.ends == 1 else x + step
                if 0 <= to < plan.spans:
                    out.append((s * plan.spans + x, partner[s] * plan.spans + to))
        return out

    if plan.ends == 1:
        return lax.ppermute(array, AXES, pairs(0))
    return jnp.concatenate([lax.ppermute(array[:1], AXES, pairs(-1)), lax.ppermute(array[1:], AXES, pairs(1))])


def on_device(
    sectors, spans,
    rhs, diag_coef, face_coef, time_coef, jac_up, jac_down, wall_mask, stator_adj, owner, first_panel_share,
):
    plan = Plan(rhs, stator_adj, sectors, spans)
    pad, cells, slab, insts, fields, ends = plan.pad, plan.cells, plan.slab, plan.insts, plan.fields, plan.ends
    bind = functools.partial
    whole, half = f32(pad, plan.ct * slab), f32(pad, slab)
    products = (vmem(6 * pad, slab),) * 2
    alone, next_chip, next_core = list(range(sectors)), outside(plan), sibling(plan)

    def edges(rows):
        return f32(ends, rows, DEPTH * plan.ct * LANES), f32(ends, rows, LANES), f32(ends, rows, LANES)

    native = rhs.reshape(plan.tf * cells, LANES)
    low_first, high_first = swap(native, next_chip), swap(native, next_core)
    m, table0, table1, side = call(
        bind(prepare, plan),
        (f32(pad + RATES, plan.ct * slab), f32(RATES, slab), f32(RATES, slab)) + edges(pad + RATES)[:1],
        (vmem(6, cells, LANES),),
    )(
        native,
        jnp.concatenate([
            wall_mask.astype(jnp.float32).reshape(cells, LANES), diag_coef.reshape(cells, LANES),
            time_coef.reshape(cells, LANES), face_coef.reshape(3 * cells, LANES),
        ]),
    )
    low_table, high_table = swap(table0, next_chip), swap(table1, next_core)
    stator = jnp.transpose(stator_adj, (1, 2, 3, 0)).reshape(fields, plan.width, insts)
    sent = call(bind(send_panels, plan), f32(sectors * spans, RATES, LANES), (vmem(insts * RATES, LANES),))(
        stator,
        jnp.concatenate([
            lax.rem(owner, plan.panels).astype(jnp.float32).reshape(insts, cells), first_panel_share.reshape(insts, cells),
        ], axis=1),
        high_table,
    )
    got = lax.all_to_all(sent, AXES, 0, 0, tiled=True)
    side_first = beside(plan, side, alone)
    corner = call(bind(corner_rows, plan), f32(ends, pad + RATES, plan.ct * LANES))(
        low_first, high_first, low_table, high_table
    )
    corner = beside(plan, corner, alone)
    matrices, down = call(
        bind(stack_matrices, plan),
        [jax.ShapeDtypeStruct((count * pad, 3 * pad), jnp.bfloat16) for count in (7, 1)],
    )(jac_up, jac_down, plan.spectral(), plan.field_rows(), plan.field_lanes(), plan.block_diagonal())
    tiles = len(plan.tiles)
    seams, weight, force, g = call(
        bind(begin, plan), (f32(3, 1 + ends, pad, LANES), f32(pad, LANES), whole, whole),
        (vmem(pad, tiles * LANES), vmem(tiles * pad, LANES), vmem(16, tiles * LANES)) + products,
        flops=2_000_000_000,
    )(matrices, m, got)
    x, near, side, c0, c1 = call(
        bind(first_half, plan), (whole, half) + edges(pad),
        products + (vmem(pad, 2 * slab),) + (vmem(pad, slab),) * 4 + (vmem(LANES, LANES),),
        flops=4_000_000_000,
    )(matrices, m, force, g, low_first, high_first, low_table, high_table, side_first, corner, seams)

    low, high = swap(near, next_chip), swap(x, next_core)
    side = beside(plan, side, alone)
    c_low, c_high = beside(plan, c0, next_chip), beside(plan, c1, next_core)
    (g,) = call(bind(inner, plan), (whole,), products, flops=2_000_000_000)(matrices, m, force, x)
    far = call(bind(hold_far, plan), half)(x, side, c_high)
    far_low = swap(far, next_chip)
    back, n0, h0, x1, rates = call(
        bind(middle, plan), (f32(sectors, RATES, LANES), half, half, half, f32(RATES, slab)),
        products + (vmem(pad, 2 * slab), vmem(pad, slab), vmem(pad, slab), vmem(LANES, LANES)),
        flops=4_000_000_000,
    )(
        matrices, m, force, x, g, low, high, side, c_low, c_high, low_first, high_first, low_table, high_table, side_first,
        seams, weight,
    )
    returned = lax.all_to_all(back, "sector", 0, 0, tiled=True)
    sens = call(bind(collect_panels, plan), f32(fields, plan.width, insts), (vmem(insts * RATES, LANES),))(returned)
    out = call(bind(outer, plan), f32(plan.tf * cells, LANES))(down, rates, n0, h0, x1, far_low)
    sens = jnp.transpose(sens.reshape(fields, plan.panels, plan.rows, insts), (3, 0, 1, 2))
    return out.reshape(rhs.shape), sens


def solution(mesh):
    in_specs = (
        P(None, None, "sector", "span", None),
        P("sector", "span", None),
        P(None, "sector", "span", None),
        P("sector", "span", None),
        P(),
        P(),
        P("sector", "span", None),
        P(None, None, "sector", "span"),
        P(None, "sector", "span"),
        P(None, "sector", "span"),
    )
    out_specs = (P(None, None, "sector", "span", None), P(None, None, "sector", "span"))
    return jax.shard_map(
        functools.partial(on_device, mesh.shape["sector"], mesh.shape["span"]),
        mesh=mesh, in_specs=in_specs, out_specs=out_specs, check_vma=False,
    )
```

```python
import functools

import jax
import jax.numpy as jnp
import ml_dtypes
import numpy as np
from jax import lax
from jax.experimental import pallas as pl
from jax.experimental.pallas import tpu as pltpu
from jax.sharding import PartitionSpec as P

SWEEPS = 4
DEPTH = 2
LANES = 128
CHUNK = 256
WINDOW = 8
HIGHEST = lax.Precision.HIGHEST
DOWN_AZ, SPECTRAL, UP_SP, DOWN_SP, UP_AX, DOWN_AX, UP_AZ = range(7)
C_TIME, C_AZ, C_SP, C_UP, C_DOWN, C_MASK, C_OTHER = range(7)
RATES = 8
AXES = ("sector", "span")


class Plan:
    def __init__(self, rhs, stator_adj, sectors, spans):
        self.insts, self.fields, self.ct, self.rows, self.nax = rhs.shape
        self.panels = stator_adj.shape[2]
        self.sectors, self.spans = sectors, spans
        self.tf = self.insts * self.fields
        self.pad = -(-self.tf // 16) * 16
        self.cells = self.ct * self.rows
        self.slab = self.rows * LANES
        self.width = self.panels * self.rows
        self.shift = [
            ((t * sectors) // (self.insts - 1) - t // (self.insts - 1)) % sectors for t in range(self.insts)
        ]
        assert self.ct == 2 and self.nax == LANES and SWEEPS % DEPTH == 0 and spans > 1
        assert len(set(self.shift)) == self.insts and self.cells * WINDOW == LANES and self.rows >= SWEEPS
        assert self.slab % CHUNK == 0 and 3 * self.pad <= 256 and 2 * self.ct * self.width == LANES
        assert sectors % 2 == 0
        self.ends = 1 if spans == 2 else 2
        self.blocks = [-1, 0, 1]
        self.halves = [0, 1] if spans == 2 else [-1, 0, 1]
        self.tiles = [(k, x) for k in self.blocks for x in self.halves]
        self.slots = [
            [t for t in range(self.insts) if any((k + self.shift[t]) % sectors == o for k in self.blocks)]
            for o in range(sectors)
        ]
        last = LANES - self.width
        self.weight_at = [(t, last) for t in range(self.fields)] + [
            (self.fields, i * self.width) for i in range(self.insts - self.fields)
        ]
        assert max(map(len, self.slots)) * self.width <= last and 2 * self.cells == self.width
        assert self.fields == RATES - 1 and (self.insts - self.fields) * self.width <= LANES

    def spectral(self):
        t = np.arange(self.insts)
        off = t[:, None] - t[None, :]
        sines = np.where(off == 0, 1.0, np.sin(np.pi * off / self.insts))
        table = np.where(off == 0, 0.0, 0.5 * (1.0 - 2.0 * (off % 2)) / sines).astype(np.float32)
        full = np.zeros((self.pad, self.pad), np.float32)
        full[: self.tf, : self.tf] = np.kron(table.T, np.eye(self.fields, dtype=np.float32))
        hi = full.astype(ml_dtypes.bfloat16)
        lo = (full - hi.astype(np.float32)).astype(ml_dtypes.bfloat16)
        return np.concatenate([hi, lo, hi], axis=1)

    def field_rows(self):
        out = np.zeros((self.pad, self.fields), np.float32)
        out[np.arange(self.tf), np.arange(self.tf) % self.fields] = 1.0
        return out

    def field_lanes(self):
        return np.tile(self.field_rows().T, (1, 3))

    def block_diagonal(self):
        block = np.full(self.pad, -1)
        block[: self.tf] = np.arange(self.tf) // self.fields
        same = (block[:, None] == block[None, :]) & (block[:, None] >= 0)
        return np.tile(same.astype(np.float32), (1, 3))


    def inst_rows(self):
        row, inst = table_index(self.pad, 16)
        return ((row >= inst * self.fields) & (row < (inst + 1) * self.fields)).astype(jnp.float32)

    def cell_of(self, lane):
        return lax.div(lane, self.width) * self.rows + lax.rem(lane, self.rows)

    def window_lanes(self):
        lane, to = table_index(LANES, LANES)
        return (lane < self.ct * self.width) & (to == self.cell_of(lane) * WINDOW)

    def window_spread(self):
        to, lane = table_index(LANES, LANES)
        return (lane < self.ct * self.width) & (to == self.cell_of(lane) * WINDOW)

    def weight_lanes(self):
        cell, lane = table_index(LANES, LANES)
        half = self.ct * self.width
        wanted = jnp.where(lane < half, self.cell_of(lane), self.cells + self.cell_of(lane - half))
        return cell == wanted

    def panel_lanes(self):
        lane = lane_index(1)
        panel = lax.rem(lax.div(lane, self.rows), self.panels)
        return jnp.where(lane < self.ct * self.width, panel, -9).astype(jnp.float32)


def table_index(rows, columns):
    return [lax.broadcasted_iota(jnp.int32, (rows, columns), axis) for axis in (0, 1)]


def call(kernel, out, scratch=(), flops=2_000_000, nbytes=1_000_000):
    return pl.pallas_call(
        kernel,
        out_shape=out,
        scratch_shapes=list(scratch),
        compiler_params=pltpu.CompilerParams(vmem_limit_bytes=20 * 1024 * 1024),
        cost_estimate=pl.CostEstimate(flops=flops, bytes_accessed=nbytes, transcendentals=0),
    )


def f32(*shape):
    return jax.ShapeDtypeStruct(shape, jnp.float32)


def vmem(*shape):
    return pltpu.VMEM(shape, jnp.float32)


def halves_of(x):
    hi = x.astype(jnp.bfloat16)
    return hi, (x - hi.astype(jnp.float32)).astype(jnp.bfloat16)


def dot3(w, x):
    hi, lo = halves_of(x)
    return jnp.dot(w, jnp.concatenate([hi, hi, lo], axis=0), preferred_element_type=jnp.float32)


def pick(x, table):
    table = table.astype(jnp.float32).astype(jnp.bfloat16)
    table = jnp.concatenate([table, table], axis=0)
    return jnp.dot(jnp.concatenate(halves_of(x), axis=1), table, preferred_element_type=jnp.float32)


def dot_full(a, b):
    return jnp.dot(a, b, precision=HIGHEST, preferred_element_type=jnp.float32)


def cell_rows(plan, ref, there):
    whole = plan.tf // 8 * 8
    rest = [ref[pl.ds(there + plan.cells * i, 1), :] for i in range(whole, plan.tf)]
    return jnp.concatenate([ref[pl.ds(there, whole, stride=plan.cells), :]] + rest, axis=0)


def lane_index(rows):
    return lax.broadcasted_iota(jnp.int32, (rows, LANES), 1)


def rolled(x, by):
    by %= LANES
    return pltpu.roll(x, by, axis=1) if by else x


def at(r, count=1, start=0):
    return slice(start + r * LANES, start + (r + count) * LANES)


def parity():
    return lax.rem(lax.axis_index("sector"), 2)


def has_sides(plan):
    span = lax.axis_index("span")
    return jnp.where(span < plan.spans - 1, 1.0, 0.0), jnp.where(span > 0, 1.0, 0.0)


class Layer:
    def __init__(self, plan, ref, start=0, rates=None, seam=None, layer=0):
        self.plan, self.ref, self.start, self.seam, self.layer = plan, ref, start, seam, layer
        self.rates = rates or (ref, start)

    def rate(self, which, r, count=1):
        if isinstance(self.rates, Layer):
            return self.rates.rate(which, r, count)
        ref, start = self.rates
        row = self.plan.pad + which
        return ref[row : row + 1, at(r, count, start)]

    def row(self, r):
        value = self.ref[: self.plan.pad, at(r, 1, self.start)]
        if self.seam is None:
            return value
        return value + placed(self.seam, self.layer * self.plan.rows + r) * self.rate(C_MASK, r)

    def chunk(self, c):
        count = CHUNK // LANES
        if self.seam is None:
            return self.ref[: self.plan.pad, at(c * count, count, self.start)]
        return jnp.concatenate([self.row(c * count + part) for part in range(count)], axis=1)


class Native(Layer):
    def __init__(self, plan, ref, table, seam, layer, near):
        super().__init__(plan, ref, 0, None, seam, layer)
        self.table, self.near = table, near

    def rate(self, which, r, count=1):
        row = which if self.near else C_OTHER
        return self.table[row : row + 1, at(r, count)]

    def row(self, r):
        plan = self.plan
        there = jnp.where(parity() == 1, self.layer, plan.ct - 1 - self.layer) * plan.rows + r
        field = cell_rows(plan, self.ref, there)
        field = jnp.concatenate([field, jnp.zeros((plan.pad - plan.tf, LANES), jnp.float32)], axis=0)
        if self.seam is not None:
            field = field + placed(self.seam, self.layer * plan.rows + r)
        return field * self.rate(C_MASK, r)


def placed(tile, cell):
    return jnp.where(lane_index(tile.shape[0]) == 0, rolled(tile, -cell * WINDOW), 0.0)


class Products:
    def __init__(self, plan, w_ref, p_ref, first):
        self.plan, self.w, self.p, self.first = plan, w_ref, p_ref, first

    def fill(self, layer):
        for c in range(self.plan.slab // CHUNK):
            self.p[:, c * CHUNK : (c + 1) * CHUNK] = dot3(matrix(self.plan, self.w, self.first, 6), layer.chunk(c))
        self.layer = layer
        return self

    def get(self, block, r):
        row = (block - self.first) * self.plan.pad
        return self.p[row : row + self.plan.pad, at(r)]

    def own_terms(self, r):
        rate = self.layer.rate
        total = rate(C_TIME, r) * self.get(SPECTRAL, r)
        beside = []
        if r + 1 < self.plan.rows:
            beside.append(self.get(UP_SP, r + 1))
        if r > 0:
            beside.append(self.get(DOWN_SP, r - 1))
        total = total + rate(C_SP, r) * sum(beside[1:], beside[0])
        total = total + rate(C_UP, r) * rolled(self.get(UP_AX, r), -1)
        return total + rate(C_DOWN, r) * rolled(self.get(DOWN_AX, r), 1)


def matrix(plan, w_ref, block, count=1):
    return w_ref[block * plan.pad : (block + count) * plan.pad, :]


def two_layers(plan, ref, rates=None, seam=None):
    return [
        Layer(plan, ref, a * plan.slab, (rates, a * plan.slab) if rates is not None else None, seam, a)
        for a in range(plan.ct)
    ]


def inner_rows(plan, w_ref, p_refs, layers, force, g_ref):
    first = Products(plan, w_ref, p_refs[0], DOWN_AZ).fill(layers[0])
    second = Products(plan, w_ref, p_refs[1], SPECTRAL).fill(layers[1])
    for r in range(plan.rows):
        other = second.get(UP_AZ, r), first.get(DOWN_AZ, r)
        for a, products in enumerate((first, second)):
            total = products.own_terms(r) + layers[a].rate(C_AZ, r) * other[a]
            if isinstance(g_ref, tuple):
                g_ref[a][:, at(r)] = force[a].row(r) - total
            else:
                g_ref[:, at(r, 1, a * plan.slab)] = force[a].row(r) - total


def azimuthal(plan, w_ref, block, chunk_of, take):
    for c in range(plan.slab // CHUNK):
        terms = dot3(matrix(plan, w_ref, block), chunk_of(c))
        for part in range(CHUNK // LANES):
            take(c * (CHUNK // LANES) + part, terms[:, at(part)])


def middle_rows(plan, w_ref, p_refs, own, own_force, g_ref, near, near_force, side, corner, y_ref, h_refs, n_refs):
    pad, rows, ct = plan.pad, plan.rows, plan.ct
    last = (rows - 1, 0)
    edge_terms, edge_new, corner_terms = [], [], []
    is_first = lax.axis_index("span") == 0

    def choose(n, above, below):
        return jnp.where(is_first, above, below) if plan.ends == 1 else (above, below)[n]

    for n in range(plan.ends):
        outward = choose(n, matrix(plan, w_ref, UP_SP), matrix(plan, w_ref, DOWN_SP))
        inward = choose(n, matrix(plan, w_ref, DOWN_SP), matrix(plan, w_ref, UP_SP))
        first, second, edge_force, edge_rate = side(n)
        corners = corner(n)
        every = dot3(w_ref[...], first)
        beyond = dot3(outward, second)
        within = [choose(n, x.row(last[0]), x.row(last[1])) for x in own]
        within = dot3(inward, jnp.concatenate(within, axis=1))
        from_low = dot3(matrix(plan, w_ref, DOWN_AZ), corners[0])
        from_high = dot3(matrix(plan, w_ref, UP_AZ), corners[1])
        new = []
        for a in range(ct):

            def part(block, b=a):
                return every[block * pad : (block + 1) * pad, at(b)]

            around = part(UP_AZ, 1) + from_low if a == 0 else from_high + part(DOWN_AZ, 0)
            total = edge_rate(C_TIME, a) * part(SPECTRAL) + edge_rate(C_AZ, a) * around
            total = total + edge_rate(C_SP, a) * (beyond[:, at(a)] + within[:, at(a)])
            total = total + edge_rate(C_UP, a) * rolled(part(UP_AX), -1)
            total = total + edge_rate(C_DOWN, a) * rolled(part(DOWN_AX), 1)
            new.append(edge_force[:, at(a)] - total)
        of_edge = choose(n, *(every[block * pad : (block + 1) * pad] for block in (UP_SP, DOWN_SP)))
        of_new = dot3(outward, jnp.concatenate(new, axis=1))
        of_corners = dot3(outward, jnp.concatenate(corners, axis=1))
        for keep in has_sides(plan) if plan.ends == 1 else (1.0,):
            edge_terms.append(of_edge * keep)
            edge_new.append(of_new * keep)
            corner_terms.append([of_corners[:, at(a)] * keep for a in range(ct)])

    products = (
        Products(plan, w_ref, p_refs[0], DOWN_AZ).fill(near[0]), Products(plan, w_ref, p_refs[1], SPECTRAL).fill(near[1]),
    )
    for a, (to_own, to_near) in enumerate(((DOWN_AZ, UP_AZ), (UP_AZ, DOWN_AZ))):

        def take(r, terms):
            total = products[a].own_terms(r) + near[a].rate(C_AZ, r) * terms
            mine = own[a].rate(C_AZ, r) * products[a].get(to_own, r)
            for n in range(2):
                if r == last[n]:
                    total = total + near[a].rate(C_SP, r) * corner_terms[n][a]
                    mine = mine + own[a].rate(C_SP, r) * edge_terms[n][:, at(a)]
            n_refs[a][:, at(r)] = near_force[a].row(r) - total
            lanes = at(r, 1, a * plan.slab)
            y_ref[:, lanes] = g_ref[:, lanes] - mine

        azimuthal(plan, w_ref, to_near, own[a].chunk, take)

    after = [Layer(plan, y_ref, a * plan.slab, own[a].rates) for a in range(ct)]
    inner_rows(plan, w_ref, p_refs, after, own_force, h_refs)
    for a in range(ct):
        for n in range(2):
            h_refs[a][:, at(last[n])] -= own[a].rate(C_SP, last[n]) * edge_new[n][:, at(a)]


def outer_rows(plan, w_ref, own, near, far_chunks, n_refs, h_refs, put, layers=(0, 1)):
    count = CHUNK // LANES
    for a in layers:
        block = (DOWN_AZ, UP_AZ)[a]

        def near_chunk(c):
            terms = dot3(matrix(plan, w_ref, block), far_chunks[a](c))
            return n_refs[a][:, at(c * count, count)] - near[a].rate(C_AZ, c * count, count) * terms

        def take(r, terms):
            put(a, r, h_refs[a][:, at(r)] - own[a].rate(C_AZ, r) * terms)

        azimuthal(plan, w_ref, block, near_chunk, take)


def sides_of(plan, side_ref, force_ref, seams_ref):
    pad, ct = plan.pad, plan.ct
    keeps = (1.0,) if plan.ends == 1 else has_sides(plan)
    is_first = lax.axis_index("span") == 0

    def inlet(n, e, a):
        above, below = a * plan.rows + e, a * plan.rows + plan.rows - 1 - e
        tile = seams_ref[1, 1 + n]
        if plan.ends == 1:
            return jnp.where(is_first, placed(tile, above), placed(tile, below))
        return placed(tile, (above, below)[n])

    def read(n, ref, e, seam):
        value = ref[n, :pad, at(e * ct, ct)]
        if seam:
            scale = ref[n, pad + C_MASK : pad + C_MASK + 1, at(e * ct, ct)]
            value = value + jnp.concatenate([inlet(n, e, a) for a in range(ct)], axis=1) * scale
        return value * keeps[n]

    def side(n):
        same = side_ref is force_ref

        def rate(which, a):
            return force_ref[n, pad + which : pad + which + 1, at(a)] * keeps[n]

        force = read(n, force_ref, 0, True)
        first = force if same else read(n, side_ref, 0, False)
        return first, read(n, side_ref, 1, same), force, rate

    return side


def corners_of(plan, c_refs, seams_ref):
    keeps = (1.0,) if plan.ends == 1 else has_sides(plan)
    is_first = lax.axis_index("span") == 0

    def corner(n):
        out = []
        for a in range(plan.ct):
            if seams_ref is None:
                value = c_refs[a][n, : plan.pad]
            else:
                value = c_refs[n, : plan.pad, at(a)]
                tile = seams_ref[2 * a, 1 + n]
                above, below = (placed(tile, a * plan.rows + r) for r in (0, plan.rows - 1))
                inlet = jnp.where(is_first, above, below) if plan.ends == 1 else (above, below)[n]
                value = value + inlet * c_refs[n, plan.pad + C_MASK : plan.pad + C_MASK + 1, at(a)]
            out.append(value * keeps[n])
        return out

    return corner


def prepare(plan, rhs_ref, coef_ref, m_ref, table0_ref, table1_ref, side_ref, rates_ref):
    pad, cells = plan.pad, plan.cells
    mask, diag, time, *face = [coef_ref[cells * i : cells * (i + 1), :] for i in range(6)]
    scale = mask / diag
    lane = lane_index(cells)
    axial = scale * face[2]
    rates = (
        scale * time, scale * face[0], scale * face[1],
        jnp.where(lane < LANES - 1, axial, 0.0), jnp.where(lane > 0, axial, 0.0), scale,
    )
    for i, rate in enumerate(rates):
        rates_ref[i] = rate
    tail = jnp.zeros((pad - plan.tf, LANES), jnp.float32)
    rest = jnp.zeros((RATES - 6, LANES), jnp.float32)
    mirror = parity()
    for cell in range(cells):
        a, r = divmod(cell, plan.rows)
        there = jnp.where(mirror == 0, a, plan.ct - 1 - a) * plan.rows + r
        table = [rates_ref[i, pl.ds(there, 1), :] for i in range(6)]
        field = jnp.concatenate([cell_rows(plan, rhs_ref, there), tail], axis=0)
        m_ref[:pad, at(cell)] = field * table[C_MASK]
        m_ref[pad:, at(cell)] = jnp.concatenate(table + [rest], axis=0)
        other = jnp.where(mirror == 0, plan.ct - 1 - a, a) * plan.rows + r
        table = table + [rates_ref[C_MASK, pl.ds(other, 1), :], rest[:1]]
        (table0_ref, table1_ref)[a][:, at(r)] = jnp.concatenate(table, axis=0)
    write_edges(plan, m_ref, side_ref, None)


def write_edges(plan, x_ref, side_ref, c_refs):
    first = lax.axis_index("span") == 0
    for a in range(plan.ct):
        for e in range(DEPTH):
            low, high = x_ref[:, at(a * plan.rows + e)], x_ref[:, at((a + 1) * plan.rows - 1 - e)]
            ends = [jnp.where(first, high, low)] if plan.ends == 1 else [low, high]
            for n, end in enumerate(ends):
                side_ref[n, :, at(e * plan.ct + a)] = end
                if e == 0 and c_refs:
                    c_refs[a][n] = end


def corner_rows(plan, low_ref, high_ref, low_table, high_table, c_ref):
    first = lax.axis_index("span") == 0
    near = Native(plan, low_ref, low_table, None, 0, True), Native(plan, high_ref, high_table, None, 1, True)
    for a, layer in enumerate(near):
        ends = []
        for r in (0, plan.rows - 1):
            rates = [layer.rate(C_MASK, r) if i == C_MASK else jnp.zeros((1, LANES), jnp.float32) for i in range(RATES)]
            ends.append(jnp.concatenate([layer.row(r)] + rates, axis=0))
        if plan.ends == 1:
            ends = [jnp.where(first, ends[1], ends[0])]
        for n, end in enumerate(ends):
            c_ref[n, :, at(a)] = end


def stack_matrices(plan, up_ref, down_ref, spectral_ref, rows_ref, lanes_ref, diagonal_ref, out_ref, down_out):
    pad = plan.pad
    lane = lax.broadcasted_iota(jnp.int32, (pad, 3 * pad), 1)
    second = (lane >= pad) & (lane < 2 * pad)
    out_ref[SPECTRAL * pad : (SPECTRAL + 1) * pad, :] = spectral_ref[...]
    even = parity() == 0
    for block, small in (
        (DOWN_AZ, jnp.where(even, down_ref[0], up_ref[0])), (UP_AZ, jnp.where(even, up_ref[0], down_ref[0])),
        (UP_SP, up_ref[1]), (DOWN_SP, down_ref[1]), (UP_AX, up_ref[2]), (DOWN_AX, down_ref[2]),
    ):
        full = dot_full(dot_full(rows_ref[...], small), lanes_ref[...]) * diagonal_ref[...]
        hi = full.astype(jnp.bfloat16).astype(jnp.float32)
        out_ref[block * pad : (block + 1) * pad, :] = jnp.where(second, full - hi, hi).astype(jnp.bfloat16)
    down_out[...] = matrix(plan, out_ref, DOWN_AZ)


def send_panels(plan, stator_ref, both_ref, out_ref, panels_ref):
    me = lax.axis_index("sector")
    for f in range(plan.fields):
        panels_ref[pl.ds(f, plan.insts, stride=RATES), : plan.width] = jnp.transpose(stator_ref[f])
    out_ref[...] = jnp.zeros_like(out_ref)
    for t, (row, start) in enumerate(plan.weight_at):
        both = jnp.broadcast_to(both_ref[t : t + 1, :][None], (out_ref.shape[0], 1, plan.width))
        out_ref[:, row : row + 1, start : start + plan.width] = both
    for o, slots in enumerate(plan.slots):
        to = lax.rem(me + (plan.sectors - o), plan.sectors) * plan.spans
        for slot, t in enumerate(slots):
            lanes = slice(slot * plan.width, (slot + 1) * plan.width)
            panels = panels_ref[t * RATES : t * RATES + plan.fields, : plan.width]
            for x in range(plan.spans):
                out_ref[to + x, : plan.fields, lanes] = panels


def begin(
    plan, w_ref, m_ref, got_ref,
    seams_ref, weight_ref, x_ref, g_ref, panels_ref, terms_ref, rows_ref, p0_ref, p1_ref,
):
    pad, insts, fields = plan.pad, plan.insts, plan.fields
    me, span = lax.axis_index("sector"), lax.axis_index("span")
    even, is_first = parity() == 0, span == 0
    tiles = plan.tiles
    panels_ref[...] = jnp.zeros_like(panels_ref)
    rows_ref[...] = jnp.zeros_like(rows_ref)
    for n, (k, x) in enumerate(tiles):
        at_span = x if plan.spans == 2 else jnp.clip(span + x, 0, plan.spans - 1)
        for t in range(insts):
            o = (k + plan.shift[t]) % plan.sectors
            source = lax.rem(me + o, plan.sectors) * plan.spans + at_span
            tile = rolled(got_ref[source], -plan.slots[o].index(t) * plan.width)
            panels_ref[t * fields : (t + 1) * fields, n * LANES : n * LANES + plan.width] = tile[:fields, : plan.width]
        tile = got_ref[lax.rem(me + k + plan.sectors, plan.sectors) * plan.spans + at_span]
        lanes = slice(n * LANES, n * LANES + plan.width)
        rows_ref[:fields, lanes] = rolled(tile, -plan.weight_at[0][1])[:fields, : plan.width]
        for t in range(fields, insts):
            row, start = plan.weight_at[t]
            rows_ref[t : t + 1, lanes] = rolled(tile, -start)[row : row + 1, : plan.width]
    spread = dot_full(plan.inst_rows(), rows_ref[...])
    spread = pick(jnp.concatenate([spread[:, at(n)] for n in range(len(tiles))], axis=0), plan.weight_lanes())
    first, share, panel = spread, rolled(spread, plan.ct * plan.width), plan.panel_lanes()
    lower = (jnp.abs(first - panel) < 0.5).astype(jnp.float32)
    upper = (jnp.abs(first + 1.0 - panel) < 0.5).astype(jnp.float32)
    weights = share * lower + (1.0 - share) * upper
    for n in range(len(tiles)):
        panels = panels_ref[:, at(n)]
        terms_ref[n * pad : (n + 1) * pad, :] = panels + rolled(panels, plan.width)
    seams = pick(terms_ref[...] * weights, plan.window_lanes())

    def tile(values, k, x):
        n = tiles.index((k, x))
        return values[n * pad : (n + 1) * pad]

    def around(values, k):
        if plan.spans == 2:
            pair = tile(values, k, 0), tile(values, k, 1)
            return [jnp.where(is_first, pair[0], pair[1]), jnp.where(is_first, pair[1], pair[0])]
        return [tile(values, k, x) for x in (0, 1, -1)]

    def mirrored(value):
        return rolled(value, LANES // 2)

    here = around(seams, 0)
    behind, ahead = around(seams, -1), around(seams, 1)
    for i in range(1 + plan.ends):
        seams_ref[0, i] = jnp.where(even, mirrored(behind[i]), ahead[i])
        seams_ref[1, i] = jnp.where(even, here[i], mirrored(here[i]))
        seams_ref[2, i] = jnp.where(even, mirrored(ahead[i]), behind[i])
    weight_ref[...] = around(weights, 0)[0]

    for layer in two_layers(plan, m_ref, seam=seams_ref[1, 0]):
        for r in range(plan.rows):
            x_ref[:, at(r, 1, layer.start)] = layer.row(r)
    layers = two_layers(plan, x_ref, m_ref)
    inner_rows(plan, w_ref, (p0_ref, p1_ref), layers, layers, g_ref)


def first_half(
    plan, w_ref, m_ref, f_ref, g_ref, low_ref, high_ref, low_table, high_table, side_ref, corner_ref, seams_ref,
    x_ref, near_ref, side_out, c0_ref, c1_ref, p0_ref, p1_ref, y_ref, h0_ref, h1_ref, n0_ref, n1_ref, inlet_ref,
):
    own = two_layers(plan, f_ref, m_ref)
    low = [Native(plan, low_ref, low_table, seams_ref[0, 0], a, a == 0) for a in range(plan.ct)]
    high = [Native(plan, high_ref, high_table, seams_ref[2, 0], a, a == 1) for a in range(plan.ct)]
    near = low[0], high[1]
    n_refs = n0_ref, n1_ref
    middle_rows(
        plan, w_ref, (p0_ref, p1_ref), own, own, g_ref, near, near, sides_of(plan, side_ref, side_ref, seams_ref),
        corners_of(plan, corner_ref, seams_ref), y_ref, (h0_ref, h1_ref), n_refs,
    )
    lane = lane_index(plan.pad)
    inlet_ref[...] = jnp.zeros_like(inlet_ref)

    def put(a, r, value):
        x_ref[:, at(r, 1, a * plan.slab)] = value
        if a == 0:
            near_ref[:, at(r)] = value
        else:
            inlet_ref[: plan.pad, :] = jnp.where(lane == r, rolled(value, r), inlet_ref[: plan.pad, :])

    outer_rows(plan, w_ref, own, near, (low[1].chunk, high[0].chunk), n_refs, (h0_ref, h1_ref), put)
    turned = jnp.transpose(inlet_ref[...])
    for r in range(plan.rows):
        near_ref[plan.tf : plan.tf + 1, at(r)] = turned[r : r + 1, :]
    write_edges(plan, x_ref, side_out, (c0_ref, c1_ref))


def hold_far(plan, x_ref, side_ref, c_high, far_ref):
    come = side_ref[0, 0:1, 0:1] + c_high[0, 0:1, 0:1]
    far_ref[...] = x_ref[:, plan.slab :] + 0.0 * come


def inner(plan, w_ref, m_ref, f_ref, x_ref, g_ref, p0_ref, p1_ref):
    inner_rows(plan, w_ref, (p0_ref, p1_ref), two_layers(plan, x_ref, m_ref), two_layers(plan, f_ref, m_ref), g_ref)


def middle(
    plan, w_ref, m_ref, f_ref, x_ref, g_ref, low_ref, high_ref, side_ref, c_low, c_high,
    low_first, high_first, low_table, high_table, side_first, seams_ref, weight_ref,
    send_ref, n0_ref, h0_ref, x1_ref, rates_ref, p0_ref, p1_ref, y_ref, h1_ref, n1_ref, turn_ref,
):
    pad = plan.pad
    own, force = two_layers(plan, x_ref, m_ref), two_layers(plan, f_ref, m_ref)
    low_force = Native(plan, low_first, low_table, seams_ref[0, 0], 0, True)
    high_force = Native(plan, high_first, high_table, seams_ref[2, 0], 1, True)
    near = Layer(plan, low_ref, 0, low_force), Layer(plan, high_ref, plan.slab, high_force)
    n_refs = n0_ref, n1_ref
    middle_rows(
        plan, w_ref, (p0_ref, p1_ref), own, force, g_ref, near, (low_force, high_force),
        sides_of(plan, side_ref, side_first, seams_ref), corners_of(plan, (c_low, c_high), None), y_ref,
        (h0_ref, h1_ref), n_refs,
    )

    def put(a, r, value):
        x1_ref[:, at(r)] = value

    outer_rows(plan, w_ref, own, near, (None, Layer(plan, high_ref).chunk), n_refs, (h0_ref, h1_ref), put, (1,))
    for r in range(plan.rows):
        last = [near[0].rate(C_AZ, r), own[0].rate(C_AZ, r), jnp.zeros((RATES - 2, LANES), jnp.float32)]
        rates_ref[:, at(r)] = jnp.concatenate(last, axis=0)

    turn_ref[...] = jnp.zeros_like(turn_ref)
    for r in range(plan.rows):
        turn_ref[r : r + 1, :] = low_ref[plan.tf : plan.tf + 1, at(r)]
    far = jnp.transpose(turn_ref[...])[:pad]

    def packed(read, count, first=0, step=1):
        lane = lane_index(count)
        out = jnp.zeros((count, LANES), jnp.float32)
        for r in range(plan.rows):
            to = first + r * step
            out = jnp.where(lane == to, rolled(read(r), to), out)
        return out

    rates = packed(lambda r: rates_ref[:, at(r)], RATES)
    inlet = packed(lambda r: n0_ref[:, at(r)], pad) - rates[0:1] * dot3(matrix(plan, w_ref, DOWN_AZ), far)
    inlet = packed(lambda r: h0_ref[:, at(r)], pad) - rates[1:2] * dot3(matrix(plan, w_ref, DOWN_AZ), inlet)
    lane = lane_index(pad)
    spread = packed(lambda r: x1_ref[:, at(r)], pad, plan.rows * WINDOW, WINDOW)
    for r in range(plan.rows):
        spread = jnp.where(lane == r * WINDOW, rolled(inlet, r * (WINDOW - 1)), spread)
    inlet = jnp.where(parity() == 0, spread, rolled(spread, LANES // 2))
    back = pick(inlet, plan.window_spread()) * weight_ref[...]
    back = back + rolled(back, -plan.width)
    me = lax.axis_index("sector")
    send_ref[...] = jnp.zeros_like(send_ref)
    for t in range(plan.insts):
        to = lax.rem(me + plan.shift[t], plan.sectors)
        send_ref[to, : plan.fields, : plan.width] = back[t * plan.fields : (t + 1) * plan.fields, : plan.width]


def outer(plan, w_ref, rates_ref, n0_ref, h0_ref, x1_ref, far_ref, out_ref):
    mirror = parity()

    def put(a, r, value):
        there = jnp.where(mirror == 0, a, plan.ct - 1 - a) * plan.rows + r
        whole = plan.tf // 8 * 8
        out_ref[pl.ds(there, whole, stride=plan.cells), :] = value[:whole]
        for i in range(whole, plan.tf):
            out_ref[pl.ds(there + plan.cells * i, 1), :] = value[i : i + 1]

    for r in range(plan.rows):
        put(1, r, x1_ref[:, at(r)])

    def near_chunk(c):
        lanes = slice(c * CHUNK, (c + 1) * CHUNK)
        return n0_ref[:, lanes] - rates_ref[0:1, lanes] * dot3(w_ref[...], far_ref[:, lanes])

    azimuthal(plan, w_ref, 0, near_chunk, lambda r, terms: put(0, r, h0_ref[:, at(r)] - rates_ref[1:2, at(r)] * terms))


def collect_panels(plan, got_ref, out_ref, panels_ref):
    me = lax.axis_index("sector")
    for t in range(plan.insts):
        source = lax.rem(me + (plan.sectors - plan.shift[t]), plan.sectors)
        panels_ref[t * RATES : (t + 1) * RATES, :] = got_ref[source]
    for f in range(plan.fields):
        tile = panels_ref[pl.ds(f, plan.insts, stride=RATES), : plan.width]
        out_ref[f] = jnp.transpose(tile)


def sibling(plan):
    return [s ^ 1 for s in range(plan.sectors)]


def outside(plan):
    return [(s - 1 if s % 2 == 0 else s + 1) % plan.sectors for s in range(plan.sectors)]


def swap(array, partner):
    return lax.ppermute(array, "sector", list(enumerate(partner)))


def beside(plan, array, partner):
    def pairs(step):
        out = []
        for s in range(plan.sectors):
            for x in range(plan.spans):
                to = 1 - x if plan.ends == 1 else x + step
                if 0 <= to < plan.spans:
                    out.append((s * plan.spans + x, partner[s] * plan.spans + to))
        return out

    if plan.ends == 1:
        return lax.ppermute(array, AXES, pairs(0))
    return jnp.concatenate([lax.ppermute(array[:1], AXES, pairs(-1)), lax.ppermute(array[1:], AXES, pairs(1))])


def on_device(
    sectors, spans,
    rhs, diag_coef, face_coef, time_coef, jac_up, jac_down, wall_mask, stator_adj, owner, first_panel_share,
):
    plan = Plan(rhs, stator_adj, sectors, spans)
    pad, cells, slab, insts, fields, ends = plan.pad, plan.cells, plan.slab, plan.insts, plan.fields, plan.ends
    bind = functools.partial
    whole, half = f32(pad, plan.ct * slab), f32(pad, slab)
    products = (vmem(6 * pad, slab),) * 2
    alone, next_chip, next_core = list(range(sectors)), outside(plan), sibling(plan)

    def edges(rows):
        return f32(ends, rows, DEPTH * plan.ct * LANES), f32(ends, rows, LANES), f32(ends, rows, LANES)

    stator = jnp.transpose(stator_adj, (1, 2, 3, 0)).reshape(fields, plan.width, insts)
    sent = call(bind(send_panels, plan), f32(sectors * spans, RATES, LANES), (vmem(insts * RATES, LANES),))(
        stator,
        jnp.concatenate([
            lax.rem(owner, plan.panels).astype(jnp.float32).reshape(insts, cells), first_panel_share.reshape(insts, cells),
        ], axis=1),
    )
    got = lax.all_to_all(sent, AXES, 0, 0, tiled=True)
    native = rhs.reshape(plan.tf * cells, LANES)
    low_first, high_first = swap(native, next_chip), swap(native, next_core)
    m, table0, table1, side = call(
        bind(prepare, plan),
        (f32(pad + RATES, plan.ct * slab), f32(RATES, slab), f32(RATES, slab)) + edges(pad + RATES)[:1],
        (vmem(6, cells, LANES),),
    )(
        native,
        jnp.concatenate([
            wall_mask.astype(jnp.float32).reshape(cells, LANES), diag_coef.reshape(cells, LANES),
            time_coef.reshape(cells, LANES), face_coef.reshape(3 * cells, LANES),
        ]),
    )
    low_table, high_table = swap(table0, next_chip), swap(table1, next_core)
    side_first = beside(plan, side, alone)
    corner = call(bind(corner_rows, plan), f32(ends, pad + RATES, plan.ct * LANES))(
        low_first, high_first, low_table, high_table
    )
    corner = beside(plan, corner, alone)
    matrices, down = call(
        bind(stack_matrices, plan),
        [jax.ShapeDtypeStruct((count * pad, 3 * pad), jnp.bfloat16) for count in (7, 1)],
    )(jac_up, jac_down, plan.spectral(), plan.field_rows(), plan.field_lanes(), plan.block_diagonal())
    tiles = len(plan.tiles)
    seams, weight, force, g = call(
        bind(begin, plan), (f32(3, 1 + ends, pad, LANES), f32(pad, LANES), whole, whole),
        (vmem(pad, tiles * LANES), vmem(tiles * pad, LANES), vmem(16, tiles * LANES)) + products,
        flops=2_000_000_000,
    )(matrices, m, got)
    x, near, side, c0, c1 = call(
        bind(first_half, plan), (whole, half) + edges(pad),
        products + (vmem(pad, 2 * slab),) + (vmem(pad, slab),) * 4 + (vmem(LANES, LANES),),
        flops=4_000_000_000,
    )(matrices, m, force, g, low_first, high_first, low_table, high_table, side_first, corner, seams)

    low, high = swap(near, next_chip), swap(x, next_core)
    side = beside(plan, side, alone)
    c_low, c_high = beside(plan, c0, next_chip), beside(plan, c1, next_core)
    (g,) = call(bind(inner, plan), (whole,), products, flops=2_000_000_000)(matrices, m, force, x)
    far = call(bind(hold_far, plan), half)(x, side, c_high)
    far_low = swap(far, next_chip)
    back, n0, h0, x1, rates = call(
        bind(middle, plan), (f32(sectors, RATES, LANES), half, half, half, f32(RATES, slab)),
        products + (vmem(pad, 2 * slab), vmem(pad, slab), vmem(pad, slab), vmem(LANES, LANES)),
        flops=4_000_000_000,
    )(
        matrices, m, force, x, g, low, high, side, c_low, c_high, low_first, high_first, low_table, high_table, side_first,
        seams, weight,
    )
    returned = lax.all_to_all(back, "sector", 0, 0, tiled=True)
    sens = call(bind(collect_panels, plan), f32(fields, plan.width, insts), (vmem(insts * RATES, LANES),))(returned)
    out = call(bind(outer, plan), f32(plan.tf * cells, LANES))(down, rates, n0, h0, x1, far_low)
    sens = jnp.transpose(sens.reshape(fields, plan.panels, plan.rows, insts), (3, 0, 1, 2))
    return out.reshape(rhs.shape), sens


def solution(mesh):
    in_specs = (
        P(None, None, "sector", "span", None),
        P("sector", "span", None),
        P(None, "sector", "span", None),
        P("sector", "span", None),
        P(),
        P(),
        P("sector", "span", None),
        P(None, None, "sector", "span"),
        P(None, "sector", "span"),
        P(None, "sector", "span"),
    )
    out_specs = (P(None, None, "sector", "span", None), P(None, None, "sector", "span"))
    return jax.shard_map(
        functools.partial(on_device, mesh.shape["sector"], mesh.shape["span"]),
        mesh=mesh, in_specs=in_specs, out_specs=out_specs, check_vma=False,
    )
```
